32 devices in a mesh: head: 2 (over x), blk: 16 (over z, y, core).
Axes of the slice: x: 2, y: 2, z: 4, core: 2. Of those that a mesh axis runs over, the one named last changes fastest.
Arguments:
- hidden: bfloat16 [8192, 1536], P(('head', 'blk')), may hold values from -6 to 6
- cotangent: bfloat16 [8192, 1536], P(('head', 'blk')), may hold values from -6 to 6
- block_order: int32 [1, 32], replicated, may hold values from 0 to 31, as said below
- norm1: float32 [1536], P(('head', 'blk')), may hold values from 0.1 to 1.9
- q_weight: float32 [1536, 1536], P(('head', 'blk')), may hold values from -0.15625 to 0.15625
- q_bias: float32 [1536], P(('head', 'blk')), may hold values from -3 to 3
- k_weight: float32 [1536, 256], P(('head', 'blk')), may hold values from -0.15625 to 0.15625
- k_bias: float32 [256], P(('head', 'blk')), may hold values from -3 to 3
- v_weight: float32 [1536, 256], P(('head', 'blk')), may hold values from -0.15625 to 0.15625
- v_bias: float32 [256], P(('head', 'blk')), may hold values from -3 to 3
- o_weight: float32 [1536, 1536], P(('head', 'blk')), may hold values from -6 to 6
- norm2: float32 [1536], P(('head', 'blk')), may hold values from 0.1 to 1.9
- gate_weight: float32 [1536, 8960], P('blk', 'head'), may hold values from -0.15625 to 0.15625
- up_weight: float32 [1536, 8960], P('blk', 'head'), may hold values from -0.15625 to 0.15625
- down_weight: float32 [1536, 8960], P('blk', 'head'), may hold values from -0.0625 to 0.0625
Outputs:
- output: bfloat16 [8192, 1536], P(('head', 'blk'))
- hidden_grad: bfloat16 [8192, 1536], P(('head', 'blk'))
- norm1_grad: float32 [1536], P(('head', 'blk'))
- q_weight_grad: float32 [1536, 1536], P(('head', 'blk'))
- q_bias_grad: float32 [1536], P(('head', 'blk'))
- k_weight_grad: float32 [1536, 256], P(('head', 'blk'))
- k_bias_grad: float32 [256], P(('head', 'blk'))
- v_weight_grad: float32 [1536, 256], P(('head', 'blk'))
- v_bias_grad: float32 [256], P(('head', 'blk'))
- o_weight_grad: float32 [1536, 1536], P(('head', 'blk'))
- norm2_grad: float32 [1536], P(('head', 'blk'))
- gate_weight_grad: float32 [1536, 8960], P('blk', 'head')
- up_weight_grad: float32 [1536, 8960], P('blk', 'head')
- down_weight_grad: float32 [1536, 8960], P('blk', 'head')
The draws below stay inside these ranges and needn't reach their ends.
Inputs may be any that keep to these rules, and one draw needn't show every extreme that they name: `block_order`: each row names every block 0 to 31 once, and entries 2 k and 2 k + 1 of a row add up to 31.
All inputs are finite; a program needn't handle non-finite values.
Results may differ from the reference program's by a relative error of at most 0.03.
Values may be sent and summed in bfloat16 or wider, within the bound.
A program may use at most 704 MiB of HBM per device.

```python
import jax
import jax.numpy as jnp
from jax import lax

D = 1536
QHEADS = 12
KVHEADS = 2
HEAD_DIM = 128
FF = 8960
SEQ_SPAN = 16
BLOCK = 256
TOK_DEV = 256
SEQS = 1
TOKENS = 8192
N_HEAD = 2


def draw_block_order(key, part):

    def one_sequence(seq_key):
        order_key, flip_key = jax.random.split(seq_key)
        pairs = jax.random.permutation(order_key, SEQ_SPAN).astype(jnp.int32)
        flips = jax.random.randint(flip_key, (SEQ_SPAN,), 0, 2, dtype=jnp.int32)
        upper = 2 * SEQ_SPAN - 1 - pairs
        first = jnp.where(flips == 0, pairs, upper)
        second = jnp.where(flips == 0, upper, pairs)
        return jnp.stack([first, second], axis=1).reshape(2 * SEQ_SPAN)
    return jax.vmap(one_sequence)(jax.random.split(key, SEQS)).astype(jnp.int32)


def steps_of(own_key, dims, cuts, least, largest):
    def one(position, shards_of):
        steps = jax.random.uniform(jax.random.fold_in(jax.random.fold_in(own_key, 6), position), (shards_of,), jnp.float32, least / len(cuts), largest / len(cuts))
        return jnp.repeat(jnp.exp(steps), dims[position] // shards_of).reshape((-1,) + (1,) * (len(dims) - position - 1))

    factor_of = one(*cuts[0])
    for cut in cuts[1:]:
        factor_of = factor_of * one(*cut)
    return factor_of


def normal_values(own_key, shape, scale, limit, cuts=(), kind=jnp.bfloat16):
    entries = scale * jax.random.normal(own_key, shape, jnp.float32)
    if cuts:
        entries = entries * steps_of(own_key, shape, cuts, -0.22, 0.18)
    return jnp.clip(entries, -limit, limit).astype(kind)


def setup_inputs(seed: int = 0) -> dict:
    arg_keys = jax.random.split(jax.random.key(seed), 16)
    hidden = normal_values(arg_keys[0], (TOKENS, D), 1.0, 6.0, ((0, 32),))
    cotangent = normal_values(arg_keys[1], (TOKENS, D), 1.0, 6.0, ((0, 32),))
    block_order = draw_block_order(jax.random.fold_in(arg_keys[15], 71), 0)
    norm1 = jnp.clip(1.0 + 0.18 * jax.random.normal(arg_keys[3], (D,), jnp.float32), 0.1, 1.9)
    q_weight = normal_values(arg_keys[4], (D, QHEADS * HEAD_DIM), D ** -0.5, 0.15625, ((0, 32),), jnp.float32)
    q_bias = normal_values(arg_keys[5], (QHEADS * HEAD_DIM,), 0.5, 3.0, ((0, 32),), jnp.float32)
    k_weight = normal_values(arg_keys[6], (D, KVHEADS * HEAD_DIM), D ** -0.5, 0.15625, ((0, 32),), jnp.float32)
    k_bias = normal_values(arg_keys[7], (KVHEADS * HEAD_DIM,), 0.5, 3.0, ((0, 32),), jnp.float32)
    v_weight = normal_values(arg_keys[8], (D, KVHEADS * HEAD_DIM), D ** -0.5, 0.15625, ((0, 32),), jnp.float32)
    v_bias = normal_values(arg_keys[9], (KVHEADS * HEAD_DIM,), 0.5, 3.0, ((0, 32),), jnp.float32)
    o_weight = normal_values(arg_keys[10], (QHEADS * HEAD_DIM, D), 1.0, 6.0, ((0, 32),), jnp.float32)
    norm2 = jnp.clip(1.0 + 0.18 * jax.random.normal(arg_keys[11], (D,), jnp.float32), 0.1, 1.9)
    gate_weight = normal_values(arg_keys[12], (D, FF), D ** -0.5, 0.15625, ((0, 16), (1, 2)), jnp.float32)
    up_weight = normal_values(arg_keys[13], (D, FF), D ** -0.5, 0.15625, ((0, 16), (1, 2)), jnp.float32)
    down_weight = normal_values(arg_keys[14], (D, FF), FF ** -0.5, 0.0625, ((0, 16), (1, 2)), jnp.float32)
    return {"hidden": hidden, "cotangent": cotangent, "block_order": block_order, "norm1": norm1, "q_weight": q_weight, "q_bias": q_bias, "k_weight": k_weight, "k_bias": k_bias, "v_weight": v_weight, "v_bias": v_bias, "o_weight": o_weight, "norm2": norm2, "gate_weight": gate_weight, "up_weight": up_weight, "down_weight": down_weight}


@jax.custom_vjp
def low(v):
    return lax.optimization_barrier(v.astype(jnp.bfloat16)).astype(jnp.float32)

@jax.custom_vjp
def low_back(v):
    return v

def low_keep(v):
    return (low(v), None)

def low_pass(kept, grad):
    return (grad,)

def back_keep(v):
    return (v, None)

def back_low(kept, grad):
    return (low(grad),)
low.defvjp(low_keep, low_pass)
low_back.defvjp(back_keep, back_low)
EPS = 1e-06
THETA = 1000000.0
NEG = -1e+30
HIGH = lax.Precision.HIGHEST

def matmul(left, right):
    return jnp.dot(left, right, precision=HIGH, preferred_element_type=jnp.float32)

def rms_scale(value, gain):
    return value * lax.rsqrt(lax.optimization_barrier(jnp.mean(value * value, axis=-1, keepdims=True)) + EPS) * gain

def angles_of(positions, head_size):
    frequency = THETA ** (-(jnp.arange(head_size // 2, dtype=jnp.float32) * 2.0) / head_size)
    return positions.astype(jnp.float32)[:, None] * frequency[None, :]

def rotate(value, angles, sign):
    half = value.shape[-1] // 2
    cosine = jnp.cos(angles)[:, None, :]
    sine = jnp.sin(angles)[:, None, :] * sign
    first = value[..., :half]
    second = value[..., half:]
    return jnp.concatenate([first * cosine - second * sine, second * cosine + first * sine], axis=-1)

def attend_block(query_part, key_rows, values, query_blocks, key_blocks):
    scale = HEAD_DIM ** (-0.5)
    scores = low_back(jnp.einsum('qhgd,chd->hgqc', query_part, key_rows, precision=HIGH) * scale)
    allowed = key_blocks[None, :] <= query_blocks[:, None]
    scores = jnp.where(allowed[None, None], scores, NEG)
    log_total = jax.nn.logsumexp(scores, axis=-1, keepdims=True)
    shares = low(jnp.exp(scores - log_total))
    return jnp.einsum('hgqc,chd->qhgd', shares, values, precision=HIGH)

def layer(inputs, positions, params):
    norm1, q_weight, q_bias, k_weight, k_bias, v_weight, v_bias, o_weight, norm2, gate_weight, up_weight, down_weight = params
    seq_len = inputs.shape[0]
    group = QHEADS // KVHEADS
    row_count = 2 * TOK_DEV
    normed = low(rms_scale(inputs, norm1))
    angles = angles_of(positions, HEAD_DIM)
    queries = low_back(matmul(normed, q_weight) + q_bias).reshape(seq_len, QHEADS, HEAD_DIM)
    key_rows = low_back(matmul(normed, k_weight) + k_bias).reshape(seq_len, KVHEADS, HEAD_DIM)
    values = low(low_back(matmul(normed, v_weight) + v_bias)).reshape(seq_len, KVHEADS, HEAD_DIM)
    queries = low(low_back(rotate(queries, angles, 1.0)))
    key_rows = low(low_back(rotate(key_rows, angles, 1.0)))
    blocks = positions // BLOCK
    query_parts = queries.reshape(seq_len // row_count, row_count, KVHEADS, group, HEAD_DIM)
    block_parts = blocks.reshape(seq_len // row_count, row_count)

    def one_block(items):
        return attend_block(items[0], key_rows, values, items[1], blocks)
    attended = lax.map(jax.checkpoint(one_block), (query_parts, block_parts))
    attended = low(low_back(attended.reshape(seq_len, QHEADS * HEAD_DIM)))
    mixed = inputs + low_back(matmul(attended, o_weight))
    normed_two = low(rms_scale(mixed, norm2))
    gate_act = low_back(matmul(normed_two, gate_weight))
    up_act = low_back(matmul(normed_two, up_weight))
    hidden_act = low(jax.nn.silu(gate_act) * up_act)
    branch = low_back(lax.dot_general(hidden_act, down_weight, (((1,), (1,)), ((), ())), precision=HIGH, preferred_element_type=jnp.float32))
    return mixed + branch

def reference(hidden, cotangent, block_order, norm1, q_weight, q_bias, k_weight, k_bias, v_weight, v_bias, o_weight, norm2, gate_weight, up_weight, down_weight):
    seq_len = 2 * SEQ_SPAN * TOK_DEV

    def arrange(value):
        return value.astype(jnp.float32).reshape(N_HEAD, SEQ_SPAN, SEQS, TOK_DEV, D).transpose(2, 1, 0, 3, 4).reshape(SEQS, seq_len, D)

    def restore(value):
        return value.reshape(SEQS, SEQ_SPAN, N_HEAD, TOK_DEV, D).transpose(2, 1, 0, 3, 4).reshape(TOKENS, D)
    positions = (block_order[:, :, None] * TOK_DEV + jnp.arange(TOK_DEV, dtype=jnp.int32)[None, None, :]).reshape(SEQS, seq_len).astype(jnp.int32)
    params = (norm1, q_weight, q_bias, k_weight, k_bias, v_weight, v_bias, o_weight, norm2, gate_weight, up_weight, down_weight)

    def forward(inputs, weights):
        rounded = tuple((low(item) for item in weights))

        def per_sequence(carry, items):
            return (carry, jax.checkpoint(layer)(items[0], items[1], rounded))
        _, results = lax.scan(per_sequence, jnp.zeros((), jnp.float32), (inputs, positions))
        return results
    results, pullback = jax.vjp(forward, arrange(hidden), params)
    input_grad, weight_grads = pullback(arrange(cotangent))
    return (restore(results).astype(jnp.bfloat16), restore(input_grad).astype(jnp.bfloat16), weight_grads[0], weight_grads[1], weight_grads[2], weight_grads[3], weight_grads[4], weight_grads[5], weight_grads[6], weight_grads[7], weight_grads[8], weight_grads[9], weight_grads[10], weight_grads[11])
```

```python
import functools

import jax
import jax.numpy as jnp
import numpy as np
from jax import lax
from jax.experimental import pallas as pl
from jax.experimental.pallas import tpu as pltpu
from jax.sharding import PartitionSpec as P

D = 1536
QHEADS = 12
KVHEADS = 2
HEAD_DIM = 128
SEQ_SPAN = 16
BLOCK = 256

EPS = 1e-06
THETA = 1000000.0
SCALE = HEAD_DIM**-0.5
LOG2E = 1.4426950408889634
SCALE2 = SCALE * LOG2E
BF = jnp.bfloat16
F32 = jnp.float32
MESH = pl.DeviceIdType.MESH
VMEM_LIMIT = 56 * 2**20
AXES = ("head", "g", "z", "y", "c")
BLK = ("g", "z", "y", "c")
LANES = 128


def dot_nn(a, b):
    return lax.dot_general(a, b, (((1,), (0,)), ((), ())), preferred_element_type=F32)


def dot_nt(a, b):
    return lax.dot_general(a, b, (((1,), (1,)), ((), ())), preferred_element_type=F32)


def dot_tn(a, b):
    return lax.dot_general(a, b, (((0,), (0,)), ((), ())), preferred_element_type=F32)


def live(axes, sizes):
    return tuple(a for a in axes if sizes[a] > 1)


def greet(axes, sizes):
    barrier = pltpu.get_barrier_semaphore()
    count = 0
    for a in axes:
        me = lax.axis_index(a)
        for d in range(1, sizes[a]):
            pl.semaphore_signal(
                barrier,
                inc=1,
                device_id={a: lax.rem(me + d, sizes[a])},
                device_id_type=MESH,
            )
            count += 1
    pl.semaphore_wait(barrier, count)


def place_of(offsets, axes, sizes):
    value = 0
    for a in axes:
        me = lax.axis_index(a)
        off = offsets.get(a, 0)
        value = value * sizes[a] + (lax.rem(me + off, sizes[a]) if off else me)
    return value


def remote(src, dst, send, recv, axis, distance, sizes):
    to = lax.rem(lax.axis_index(axis) + distance, sizes[axis])
    return pltpu.make_async_remote_copy(
        src_ref=src,
        dst_ref=dst,
        send_sem=send,
        recv_sem=recv,
        device_id={axis: to},
        device_id_type=MESH,
    )


def gather_kernel(plans, sizes, *refs):
    count = len(plans)
    xs, outs = refs[:count], refs[count : 2 * count]
    send_sems, recv_sems, local_sems = refs[2 * count :]
    greet(live(AXES, {a: (sizes[a] if any(a in p[0] for p in plans) else 1) for a in AXES}), sizes)
    sends, locals_, queue = [], [], []
    sem = 0
    for i, (axes, split) in enumerate(plans):
        mine = xs[i].at[lax.axis_index(axes[0])] if split else xs[i]
        copy = pltpu.make_async_copy(mine, outs[i].at[place_of({}, axes, sizes)], local_sems.at[i])
        copy.start()
        locals_.append(copy)
        queue.append((i, {}, -1, None))
    at = 0
    while at < len(queue):
        i, offsets, phase, arrived = queue[at]
        at += 1
        axes, split = plans[i]
        slot = outs[i].at[place_of(offsets, axes, sizes)]
        if arrived is None:
            src = xs[i].at[lax.axis_index(axes[0])] if split else xs[i]
        else:
            src = slot
            remote(
                slot, slot, send_sems.at[arrived], recv_sems.at[arrived], axes[0], 0, sizes
            ).wait_recv()
        for p in range(phase + 1, len(axes)):
            a = axes[p]
            for d in range(1, sizes[a]):
                piece = src
                if split and p == 0:
                    piece = xs[i].at[lax.rem(lax.axis_index(a) + d, sizes[a])]
                copy = remote(piece, slot, send_sems.at[sem], recv_sems.at[sem], a, d, sizes)
                copy.start()
                sends.append(copy)
                later = dict(offsets)
                later[a] = sizes[a] - d
                queue.append((i, later, p, sem))
                sem += 1
    for copy in locals_:
        copy.wait()
    for copy in sends:
        copy.wait_send()


def gather(arrays, plans, sizes, collective_id):
    plans = [(live(axes, sizes), split) for axes, split in plans]
    counts = [int(np.prod([sizes[a] for a in axes])) for axes, _ in plans]
    total = sum(counts) - len(counts)
    shapes = [
        jax.ShapeDtypeStruct((n,) + (x.shape[1:] if split else x.shape), x.dtype)
        for n, x, (_, split) in zip(counts, arrays, plans)
    ]
    spec = pl.BlockSpec(memory_space=pltpu.VMEM)
    return pl.pallas_call(
        functools.partial(gather_kernel, plans, sizes),
        out_shape=shapes,
        in_specs=[spec] * len(arrays),
        out_specs=[spec] * len(arrays),
        scratch_shapes=[
            pltpu.SemaphoreType.DMA((total,)),
            pltpu.SemaphoreType.DMA((total,)),
            pltpu.SemaphoreType.DMA((len(arrays),)),
        ],
        compiler_params=pltpu.CompilerParams(
            collective_id=collective_id, has_side_effects=True, vmem_limit_bytes=VMEM_LIMIT
        ),
        cost_estimate=pl.CostEstimate(flops=0, bytes_accessed=60 * 2**20, transcendentals=0),
    )(*arrays)


def offset_keys(axes, sizes):
    keys = [{}]
    for a in axes:
        keys = [dict(k, **{a: d}) for k in keys for d in list(range(1, sizes[a])) + [0]]
    return keys


def scatter_kernel(plans, sizes, *refs):
    count = len(plans)
    xs, outs = refs[:count], refs[count : 2 * count]
    at = 2 * count
    bufs = []
    for axes, swap in plans:
        phases = len(axes)
        bufs.append((refs[at : at + phases], refs[at + phases : at + 2 * phases]))
        at += 2 * phases
    send_sems, recv_sems, local_sems = refs[at:]
    used = {
        a: (
            sizes[a]
            if any(a in axes or (swap and a == "head") for axes, swap in plans)
            else 1
        )
        for a in AXES
    }
    greet(live(AXES, used), sizes)
    sem = 0
    sends = []
    arrivals = [dict() for _ in plans]

    def number(offsets, axes):
        value = 0
        for a in axes:
            value = value * sizes[a] + offsets.get(a, 0)
        return value

    def total_of(i, offsets, phase):
        axes = plans[i][0]
        order = axes[::-1]
        total = xs[i][place_of(offsets, axes, sizes)].astype(F32)
        for q in range(phase):
            rest = axes[: len(axes) - 1 - q]
            for d in range(1, sizes[order[q]]):
                key = (q, d, number(offsets, rest))
                s = arrivals[i].pop(key)
                buf = bufs[i][1][q].at[d - 1, number(offsets, rest)]
                remote(buf, buf, send_sems.at[s], recv_sems.at[s], order[q], 0, sizes).wait_recv()
                total = total + buf[...].astype(F32)
        return total

    depth = max(len(axes) for axes, _ in plans)
    for phase in range(depth):
        for i, (axes, swap) in enumerate(plans):
            if phase >= len(axes):
                continue
            order = axes[::-1]
            a = order[phase]
            rest = axes[: len(axes) - 1 - phase]
            for d in range(1, sizes[a]):
                for key in offset_keys(rest, sizes):
                    offsets = dict(key)
                    offsets[a] = d
                    where = number(key, rest)
                    if phase == 0:
                        src = xs[i].at[place_of(offsets, axes, sizes)]
                    else:
                        src = bufs[i][0][phase].at[d - 1, where]
                        src[...] = total_of(i, offsets, phase).astype(src.dtype)
                    dst = bufs[i][1][phase].at[d - 1, where]
                    copy = remote(src, dst, send_sems.at[sem], recv_sems.at[sem], a, d, sizes)
                    copy.start()
                    sends.append(copy)
                    arrivals[i][(phase, d, where)] = sem
                    sem += 1
    swaps = []
    for i, (axes, swap) in enumerate(plans):
        total = total_of(i, {}, len(axes))
        if swap:
            hold, out = bufs[i][0][0], outs[i]
            hold[...] = total.astype(hold.dtype)
            me = lax.axis_index("head")
            copy = pltpu.make_async_copy(hold.at[me], out.at[me], local_sems.at[i])
            copy.start()
            for d in range(1, sizes["head"]):
                to = lax.rem(me + d, sizes["head"])
                copy2 = remote(
                    hold.at[to], out.at[me], send_sems.at[sem], recv_sems.at[sem], "head", d, sizes
                )
                copy2.start()
                sends.append(copy2)
                source = out.at[lax.rem(me + sizes["head"] - d, sizes["head"])]
                swaps.append((source, sem))
                sem += 1
            swaps.append((copy, None))
        else:
            outs[i][...] = total.astype(outs[i].dtype)
    for item, s in swaps:
        if s is None:
            item.wait()
        else:
            remote(item, item, send_sems.at[s], recv_sems.at[s], "head", 0, sizes).wait_recv()
    for copy in sends:
        copy.wait_send()


def scatter(arrays, plans, out_types, sizes, collective_id):
    plans = [(live(axes, sizes), swap) for axes, swap in plans]
    scratch, total = [], 0
    for x, (axes, swap), kind in zip(arrays, plans, out_types):
        block = x.shape[1:]
        order = axes[::-1]
        send_bufs, recv_bufs = [], []
        for p, a in enumerate(order):
            rest = int(np.prod([sizes[b] for b in axes[: len(axes) - 1 - p]], dtype=int))
            shape = (sizes[a] - 1, rest) + block
            recv_bufs.append(pltpu.VMEM(shape, x.dtype))
            if p == 0:
                send_bufs.append(pltpu.VMEM(block if swap else (8, LANES), kind if swap else F32))
            else:
                send_bufs.append(pltpu.VMEM(shape, x.dtype))
            total += (sizes[a] - 1) * rest
        scratch += send_bufs + recv_bufs
        if swap:
            total += sizes["head"] - 1
    shapes = [jax.ShapeDtypeStruct(x.shape[1:], kind) for x, kind in zip(arrays, out_types)]
    spec = pl.BlockSpec(memory_space=pltpu.VMEM)
    return pl.pallas_call(
        functools.partial(scatter_kernel, plans, sizes),
        out_shape=shapes,
        in_specs=[spec] * len(arrays),
        out_specs=[spec] * len(arrays),
        scratch_shapes=scratch
        + [
            pltpu.SemaphoreType.DMA((total,)),
            pltpu.SemaphoreType.DMA((total,)),
            pltpu.SemaphoreType.DMA((len(arrays),)),
        ],
        compiler_params=pltpu.CompilerParams(
            collective_id=collective_id, has_side_effects=True, vmem_limit_bytes=VMEM_LIMIT
        ),
        cost_estimate=pl.CostEstimate(flops=0, bytes_accessed=60 * 2**20, transcendentals=0),
    )(*arrays)


def forward_kernel(heads, slots, tops, q_ref, kv_ref, o_ref, lse_ref, top_s, sum_s, acc_s):
    def score(keys, a, h):
        return dot_nt(keys, q_ref[a * BLOCK : (a + 1) * BLOCK, h * HEAD_DIM : (h + 1) * HEAD_DIM])

    for a in range(2):
        top_s[...] = jnp.full(top_s.shape, -1e30, F32)
        sum_s[...] = jnp.zeros(sum_s.shape, F32)
        acc_s[...] = jnp.zeros(acc_s.shape, F32)
        count = tops[a] + 1

        def step(keys, values_t):
            ahead = min(3, heads)
            ready = [score(keys, a, h) for h in range(ahead)]
            for h in range(heads):
                s = ready[h]
                if h + ahead < heads:
                    ready.append(score(keys, a, h + ahead))
                old = top_s[h : h + 1, :]
                new = jnp.maximum(old, jnp.max(s, axis=0, keepdims=True))
                p = jnp.exp2((s - new) * SCALE2)
                fade = jnp.exp2((old - new) * SCALE2)
                sum_s[h : h + 1, :] = sum_s[h : h + 1, :] * fade + jnp.sum(p, axis=0, keepdims=True)
                top_s[h : h + 1, :] = new
                acc_s[h] = acc_s[h] * fade + dot_nn(values_t, p.astype(BF))

        def two(i, carry):
            first, second = slots[2 * i], slots[2 * i + 1]
            both = jnp.concatenate([kv_ref[first], kv_ref[second]], axis=0)
            step(both[:, :HEAD_DIM], both[:, HEAD_DIM:].T)
            return carry

        lax.fori_loop(0, count // 2, two, 0)

        @pl.when(count % 2 == 1)
        def _():
            last = kv_ref[slots[count - 1]]
            step(last[:, :HEAD_DIM], last[:, HEAD_DIM:].T)

        for h in range(heads):
            total = sum_s[h : h + 1, :]
            o_ref[a * BLOCK : (a + 1) * BLOCK, h * HEAD_DIM : (h + 1) * HEAD_DIM] = (
                acc_s[h] / total
            ).T
            lse_ref[a, h : h + 1, :] = top_s[h : h + 1, :] * SCALE2 + jnp.log2(total)


def attend(slots, tops, q, kv):
    heads = q.shape[1] // HEAD_DIM
    spec = pl.BlockSpec(memory_space=pltpu.VMEM)
    pairs = 33 * BLOCK * BLOCK * heads
    return pl.pallas_call(
        functools.partial(forward_kernel, heads),
        grid_spec=pltpu.PrefetchScalarGridSpec(
            num_scalar_prefetch=2,
            grid=(1,),
            in_specs=[spec] * 2,
            out_specs=[spec] * 2,
            scratch_shapes=[
                pltpu.VMEM((8, BLOCK), F32),
                pltpu.VMEM((8, BLOCK), F32),
                pltpu.VMEM((heads, HEAD_DIM, BLOCK), F32),
            ],
        ),
        out_shape=(
            jax.ShapeDtypeStruct(q.shape, F32),
            jax.ShapeDtypeStruct((2, 8, BLOCK), F32),
        ),
        compiler_params=pltpu.CompilerParams(vmem_limit_bytes=VMEM_LIMIT),
        cost_estimate=pl.CostEstimate(
            flops=pairs * 4 * HEAD_DIM, bytes_accessed=80 * 2**20, transcendentals=pairs
        ),
    )(slots, tops, q, kv)


def backward_kernel(
    heads, slots, tops, q_ref, kv_ref, do_ref, lse_ref, delta_ref, dq_ref, dkv_ref, dq_s, dkv_s
):
    dkv_s[...] = jnp.zeros(dkv_s.shape, F32)
    for a in range(2):
        dq_s[...] = jnp.zeros(dq_s.shape, F32)

        def part(ref, h):
            return ref[a * BLOCK : (a + 1) * BLOCK, h * HEAD_DIM : (h + 1) * HEAD_DIM]

        def one(n, carry):
            slot = slots[n]
            keys, values = kv_ref[slot, :, :HEAD_DIM], kv_ref[slot, :, HEAD_DIM:]
            keys_t = keys.T

            def products(h):
                return dot_nt(keys, part(q_ref, h)), dot_nt(values, part(do_ref, h))

            dk = jnp.zeros((BLOCK, HEAD_DIM), F32)
            dv = jnp.zeros((BLOCK, HEAD_DIM), F32)
            ahead = min(2, heads)
            ready = [products(h) for h in range(ahead)]
            for h in range(heads):
                s, dp = ready[h]
                if h + ahead < heads:
                    ready.append(products(h + ahead))
                p = jnp.exp2(s * SCALE2 - lse_ref[a, h : h + 1, :])
                dv = dv + dot_nn(p.astype(BF), part(do_ref, h))
                ds = (p * (dp - delta_ref[a, h : h + 1, :])).astype(BF)
                dk = dk + dot_nn(ds, part(q_ref, h))
                dq_s[h] = dq_s[h] + dot_nn(keys_t, ds)
            dkv_s[slot, :, :HEAD_DIM] = dkv_s[slot, :, :HEAD_DIM] + dk
            dkv_s[slot, :, HEAD_DIM:] = dkv_s[slot, :, HEAD_DIM:] + dv
            return carry

        lax.fori_loop(0, tops[a] + 1, one, 0)
        for h in range(heads):
            dq_ref[a * BLOCK : (a + 1) * BLOCK, h * HEAD_DIM : (h + 1) * HEAD_DIM] = (
                (dq_s[h] * SCALE).T
            ).astype(BF)
    dkv_ref[:, :, :HEAD_DIM] = (dkv_s[:, :, :HEAD_DIM] * SCALE).astype(BF)
    dkv_ref[:, :, HEAD_DIM:] = dkv_s[:, :, HEAD_DIM:].astype(BF)


def attend_back(slots, tops, q, kv, do, lse, delta):
    heads = q.shape[1] // HEAD_DIM
    spec = pl.BlockSpec(memory_space=pltpu.VMEM)
    pairs = 33 * BLOCK * BLOCK * heads
    return pl.pallas_call(
        functools.partial(backward_kernel, heads),
        grid_spec=pltpu.PrefetchScalarGridSpec(
            num_scalar_prefetch=2,
            grid=(1,),
            in_specs=[spec] * 5,
            out_specs=[spec] * 2,
            scratch_shapes=[
                pltpu.VMEM((heads, HEAD_DIM, BLOCK), F32),
                pltpu.VMEM(kv.shape, F32),
            ],
        ),
        out_shape=(
            jax.ShapeDtypeStruct(q.shape, BF),
            jax.ShapeDtypeStruct(kv.shape, BF),
        ),
        compiler_params=pltpu.CompilerParams(vmem_limit_bytes=VMEM_LIMIT),
        cost_estimate=pl.CostEstimate(
            flops=pairs * 10 * HEAD_DIM, bytes_accessed=120 * 2**20, transcendentals=pairs
        ),
    )(slots, tops, q, kv, do, lse, delta)


def inverse_rms(value):
    return lax.rsqrt(jnp.mean(value * value, axis=-1, keepdims=True) + EPS)


def rotate(value, cosine, sine):
    rows, width = value.shape
    half = HEAD_DIM // 2
    parts = value.reshape(rows, width // HEAD_DIM, HEAD_DIM)
    first, second = parts[..., :half], parts[..., half:]
    cosine, sine = cosine[:, None, :], sine[:, None, :]
    return jnp.concatenate(
        [first * cosine - second * sine, second * cosine + first * sine], axis=-1
    ).reshape(rows, width)


def shift(value, axis, distance, sizes):
    n = sizes[axis]
    return lax.ppermute(value, axis, [(i, (i + distance) % n) for i in range(n)])


def small_rows(*rows):
    return jnp.stack(
        [jnp.pad(r.astype(F32), ((0, LANES - r.shape[0]),)) for r in rows]
        + [jnp.zeros((LANES,), F32)] * (8 - len(rows))
    )


def shards(
    sizes,
    hidden,
    cotangent,
    block_order,
    norm1,
    q_weight,
    q_bias,
    k_weight,
    k_bias,
    v_weight,
    v_bias,
    o_weight,
    norm2,
    gate_weight,
    up_weight,
    down_weight,
):
    tok = hidden.shape[0]
    pair = sizes["head"] * tok
    blk = int(np.prod([sizes[a] for a in BLK]))
    seqs = blk // SEQ_SPAN
    place_axes = {1: BLK, 2: BLK[:3], 4: BLK[:2]}[seqs]
    seq_axes = BLK[len(place_axes) :]
    head = lax.axis_index("head")
    place = place_of({}, place_axes, sizes)
    seq = place_of({}, seq_axes, sizes) if seq_axes else 0
    order = lax.dynamic_index_in_dim(block_order, seq, 0, keepdims=False)
    tops = lax.dynamic_slice_in_dim(order, place * 2, 2)
    slots = jnp.argsort(order).astype(jnp.int32)
    positions = (tops[:, None] * tok + jnp.arange(tok, dtype=jnp.int32)[None, :]).reshape(pair)
    frequency = THETA ** (-(jnp.arange(HEAD_DIM // 2, dtype=F32) * 2.0) / HEAD_DIM)
    angles = positions.astype(F32)[:, None] * frequency[None, :]
    cosine, sine = jnp.cos(angles), jnp.sin(angles)

    q_cols = D // 2
    kv_cols = HEAD_DIM
    rows = q_weight.shape[0]
    halves = [
        jnp.concatenate(
            [
                q_weight[:, i * q_cols : (i + 1) * q_cols],
                k_weight[:, i * kv_cols : (i + 1) * kv_cols],
                v_weight[:, i * kv_cols : (i + 1) * kv_cols],
            ],
            axis=1,
        ).astype(BF)
        for i in range(2)
    ]
    small = small_rows(
        *[v.astype(BF) for v in (norm1, norm2, q_bias, k_bias, v_bias)]
    )
    w_qkv, x_pair, small_all = gather(
        [jnp.stack(halves), hidden, small],
        [(AXES, True), (("head",), False), (AXES, False)],
        sizes,
        1,
    )
    w_qkv = w_qkv.reshape(D, q_cols + 2 * kv_cols)
    x_pair = x_pair.reshape(pair, D).astype(F32)
    gain_one = small_all[:, 0, :rows].reshape(D)
    gain_two = small_all[:, 1, :rows].reshape(D)
    bias_q = lax.dynamic_slice_in_dim(small_all[:, 2, :rows].reshape(D), head * q_cols, q_cols)
    bias_k, bias_v = (
        lax.dynamic_slice_in_dim(
            small_all[:, i, : k_bias.shape[0]].reshape(2 * kv_cols), head * kv_cols, kv_cols
        )
        for i in (3, 4)
    )

    nz = sizes["z"]
    width = gate_weight.shape[1]
    lanes = -(-width // (LANES * nz)) * LANES
    wide = lanes * nz
    z = lax.axis_index("z")
    core = lax.axis_index("c")
    ff_rows = gate_weight.shape[0]

    def quarters(weight):
        padded = jnp.pad(weight.astype(BF), ((0, 0), (0, wide - width)))
        return padded.reshape(ff_rows, nz, lanes).transpose(1, 0, 2)

    def spread(packed):
        got = [lax.dynamic_index_in_dim(packed, z, 0, keepdims=False)]
        for d in range(1, nz):
            piece = lax.dynamic_index_in_dim(packed, (z + d) % nz, 0, keepdims=False)
            got.append(shift(piece, "z", d, sizes))
        mine = jnp.stack(got)
        over = ("head", "g", "y")
        everything = lax.all_gather(mine, live(over, sizes), axis=0, tiled=False)
        everything = everything.reshape((2, sizes["g"], sizes["y"]) + mine.shape)
        other = lax.dynamic_index_in_dim(everything, 1 - core, 0, keepdims=False)
        keep = lax.dynamic_index_in_dim(everything, core, 0, keepdims=False)
        swapped = shift(other, "c", 1, sizes)
        both = jnp.where(core == 0, jnp.stack([keep, swapped]), jnp.stack([swapped, keep]))
        by_z = jnp.stack(
            [lax.dynamic_index_in_dim(both, (z - i) % nz, 3, keepdims=False) for i in range(nz)]
        )
        full = by_z.transpose(4, 2, 0, 3, 1, 5, 6)
        return full.reshape(full.shape[0], D, lanes)

    tied = lax.optimization_barrier((gate_weight, up_weight, down_weight, w_qkv))
    w_gate, w_up = spread(jnp.stack([quarters(tied[0]), quarters(tied[1])], axis=1))
    (w_down,) = spread(quarters(tied[2])[:, None])

    w_out = lax.all_gather(o_weight.astype(BF), live(AXES, sizes), axis=0, tiled=True)
    cot_all = lax.all_gather(cotangent, ("z", "c"), axis=0, tiled=True)

    scale_one = inverse_rms(x_pair)
    normed = (x_pair * scale_one * gain_one).astype(BF)
    qkv = dot_nn(normed, w_qkv)
    queries = rotate(qkv[:, :q_cols] + bias_q, cosine, sine).astype(BF)
    keys = rotate(qkv[:, q_cols : q_cols + kv_cols] + bias_k, cosine, sine).astype(BF)
    values = (qkv[:, q_cols + kv_cols :] + bias_v).astype(BF)
    (kv,) = gather(
        [jnp.concatenate([keys, values], axis=1)], [(place_axes, False)], sizes, 2
    )
    kv = kv.reshape(2 * SEQ_SPAN, tok, 2 * HEAD_DIM)
    attended, lse = attend(slots, tops, queries, kv)
    attn_local = attended.astype(BF)
    (attn_halves,) = gather([attn_local.reshape(2, tok, q_cols)], [(("head",), True)], sizes, 3)
    inputs = lax.dynamic_slice_in_dim(x_pair, head * tok, tok)
    mixed = inputs + (
        dot_nn(attn_halves[0], w_out[:q_cols]) + dot_nn(attn_halves[1], w_out[q_cols:])
    )
    scale_two = inverse_rms(mixed)
    normed_two = (mixed * scale_two * gain_two).astype(BF)
    (tokens,) = gather([normed_two], [(("z", "c"), False)], sizes, 4)
    tokens = tokens.reshape(-1, D)

    gate = dot_nn(tokens, w_gate)
    up = dot_nn(tokens, w_up)
    sig = jax.nn.sigmoid(gate)
    act = (gate * sig * up).astype(BF)
    dact = dot_nn(cot_all, w_down)
    dgate = (dact * up * sig * (1.0 + gate * (1.0 - sig))).astype(BF)
    dup = (dact * gate * sig).astype(BF)
    dtokens = (dot_nt(dgate, w_gate) + dot_nt(dup, w_up)).astype(BF)
    (dnormed_two,) = scatter(
        [dtokens.reshape(-1, tok, D)], [(("z", "c"), False)], [F32], sizes, 5
    )
    branch = dot_nt(act, w_down).astype(BF)
    branch_sum = lax.psum_scatter(branch, ("z", "c"), scatter_dimension=0, tiled=True)
    output = (mixed + branch_sum.astype(F32)).astype(BF)

    def collect(grad):
        mats = grad.shape[0]
        parts = grad.reshape(
            (mats, sizes["g"], nz, sizes["y"], sizes["c"], ff_rows, lanes)
        ).transpose(4, 1, 3, 2, 0, 5, 6)
        other = lax.dynamic_index_in_dim(parts, 1 - core, 0, keepdims=False)
        keep = lax.dynamic_index_in_dim(parts, core, 0, keepdims=False)
        swapped = shift(other, "c", 1, sizes)
        both = jnp.where(core == 0, jnp.stack([keep, swapped]), jnp.stack([swapped, keep]))
        both = both.reshape((-1,) + both.shape[3:])
        mine = lax.psum_scatter(
            both, live(("head", "g", "y"), sizes), scatter_dimension=0, tiled=True
        )[0]
        got = [lax.dynamic_index_in_dim(mine, z, 0, keepdims=False)]
        for d in range(1, nz):
            piece = lax.dynamic_index_in_dim(mine, (z + d) % nz, 0, keepdims=False)
            got.append(shift(piece, "z", d, sizes))
        held = jnp.stack(got)
        by_z = jnp.stack(
            [lax.dynamic_index_in_dim(held, (z - i) % nz, 0, keepdims=False) for i in range(nz)]
        )
        return by_z.transpose(1, 2, 0, 3).reshape(mats, ff_rows, wide)[:, :, :width].astype(F32)

    d_gate_up = collect(
        jnp.stack([dot_tn(tokens, dgate).astype(BF), dot_tn(tokens, dup).astype(BF)])
    )
    d_down = collect(dot_tn(cot_all, act).astype(BF)[None])

    z_two = mixed * scale_two
    u_two = gain_two * dnormed_two
    norm2_part = jnp.sum(dnormed_two * z_two, axis=0)
    dmixed = cotangent.astype(F32) + scale_two * (
        u_two - z_two * jnp.mean(z_two * u_two, axis=-1, keepdims=True)
    )
    dproj = dmixed.astype(BF)
    dattn = dot_nt(dproj, w_out).astype(BF)
    (dout,) = gather(
        [dattn.reshape(tok, 2, q_cols).transpose(1, 0, 2)], [(("head",), True)], sizes, 6
    )
    dout = dout.reshape(pair, q_cols)
    delta = jnp.sum(
        (dout.astype(F32) * attended).reshape(2, tok, q_cols // HEAD_DIM, HEAD_DIM), axis=-1
    ).transpose(0, 2, 1)
    delta = jnp.pad(delta, ((0, 0), (0, 8 - delta.shape[1]), (0, 0)))

    dproj_other = shift(dproj, "head", 1, sizes)
    own_attn = lax.dynamic_slice_in_dim(attn_local, head * tok, tok)
    other_attn = lax.dynamic_slice_in_dim(attn_local, (1 - head) * tok, tok)
    o_part = (dot_tn(own_attn, dproj) + dot_tn(other_attn, dproj_other)).astype(BF)
    d_out_weight = lax.psum_scatter(
        o_part, live(BLK, sizes), scatter_dimension=0, tiled=True
    ).astype(F32)

    dq, dkv_parts = attend_back(slots, tops, queries, kv, dout, lse, delta)
    (dkv,) = scatter(
        [dkv_parts.reshape(SEQ_SPAN, pair, 2 * HEAD_DIM)],
        [(place_axes, False)],
        [BF],
        sizes,
        7,
    )
    dq_pre = rotate(dq.astype(F32), cosine, -sine).astype(BF)
    dk_pre = rotate(dkv[:, :HEAD_DIM].astype(F32), cosine, -sine).astype(BF)
    dv = dkv[:, HEAD_DIM:]
    dpre = jnp.concatenate([dq_pre, dk_pre, dv], axis=1)
    w_part = dot_tn(normed, dpre).astype(BF)
    bias_part = jnp.sum(dpre.astype(F32), axis=0)
    dnormed = dot_nt(dpre, w_qkv)
    norm1_part = jnp.sum(dnormed * (x_pair * scale_one), axis=0)
    own = (jnp.arange(2) == head).astype(F32)[:, None]

    def owners(vector):
        return vector.reshape(2, blk, -1).transpose(1, 0, 2)

    def owned(vector):
        return owners((own * vector[None, :]).reshape(-1))

    small_grads = jnp.stack(
        [
            jnp.pad(part, ((0, 0), (0, 0), (0, LANES - part.shape[2])))
            for part in (
                owners(norm1_part),
                owners(norm2_part),
                owned(bias_part[:q_cols]),
                owned(bias_part[q_cols : q_cols + kv_cols]),
                owned(bias_part[q_cols + kv_cols :]),
            )
        ]
        + [jnp.zeros((blk, 2, LANES), F32)] * 3,
        axis=2,
    )
    small_grads = small_grads.transpose(1, 0, 2, 3).reshape(2 * blk, 8, LANES)
    w_grads, small_sum, dnormed_sum = scatter(
        [
            w_part.reshape(2, blk, rows, -1).transpose(1, 0, 2, 3),
            small_grads,
            dnormed.astype(BF).reshape(2, tok, D),
        ],
        [(BLK, True), (AXES, False), (("head",), False)],
        [F32, F32, F32],
        sizes,
        8,
    )
    own_scale = lax.dynamic_slice_in_dim(scale_one, head * tok, tok)
    z_one = inputs * own_scale
    u_one = gain_one * dnormed_sum
    hidden_grad = (
        dmixed + own_scale * (u_one - z_one * jnp.mean(z_one * u_one, axis=-1, keepdims=True))
    ).astype(BF)
    kn = k_bias.shape[0]
    return (
        output,
        hidden_grad,
        small_sum[0, :rows],
        jnp.concatenate([w_grads[0, :, :q_cols], w_grads[1, :, :q_cols]], axis=1),
        small_sum[2, :rows],
        jnp.concatenate([w_grads[i, :, q_cols : q_cols + kv_cols] for i in range(2)], axis=1),
        small_sum[3, :kn],
        jnp.concatenate([w_grads[i, :, q_cols + kv_cols :] for i in range(2)], axis=1),
        small_sum[4, :kn],
        d_out_weight,
        small_sum[1, :rows],
        d_gate_up[0],
        d_gate_up[1],
        d_down[0],
    )


def solution(mesh):
    heads, blk = mesh.devices.shape
    split = jax.sharding.Mesh(mesh.devices.reshape(heads, blk // 16, 4, 2, 2), AXES)
    sizes = dict(split.shape)
    rows = P(AXES, None)
    vector = P(AXES)
    feed = P(BLK, "head")
    return jax.shard_map(
        functools.partial(shards, sizes),
        mesh=split,
        in_specs=(
            rows,
            rows,
            P(),
            vector,
            rows,
            vector,
            rows,
            vector,
            rows,
            vector,
            rows,
            vector,
            feed,
            feed,
            feed,
        ),
        out_specs=(
            rows,
            rows,
            vector,
            rows,
            vector,
            rows,
            vector,
            rows,
            vector,
            rows,
            vector,
            feed,
            feed,
            feed,
        ),
        check_vma=False,
    )
```

```python
import functools

import jax
import jax.numpy as jnp
import numpy as np
from jax import lax
from jax.experimental import pallas as pl
from jax.experimental.pallas import tpu as pltpu
from jax.sharding import PartitionSpec as P

D = 1536
QHEADS = 12
KVHEADS = 2
HEAD_DIM = 128
SEQ_SPAN = 16
BLOCK = 256

EPS = 1e-06
THETA = 1000000.0
SCALE = HEAD_DIM**-0.5
LOG2E = 1.4426950408889634
SCALE2 = SCALE * LOG2E
BF = jnp.bfloat16
F32 = jnp.float32
MESH = pl.DeviceIdType.MESH
VMEM_LIMIT = 56 * 2**20
AXES = ("head", "g", "z", "y", "c")
BLK = ("g", "z", "y", "c")
LANES = 128


def dot_nn(a, b):
    return lax.dot_general(a, b, (((1,), (0,)), ((), ())), preferred_element_type=F32)


def dot_nt(a, b):
    return lax.dot_general(a, b, (((1,), (1,)), ((), ())), preferred_element_type=F32)


def dot_tn(a, b):
    return lax.dot_general(a, b, (((0,), (0,)), ((), ())), preferred_element_type=F32)


def live(axes, sizes):
    return tuple(a for a in axes if sizes[a] > 1)


def greet(axes, sizes):
    barrier = pltpu.get_barrier_semaphore()
    count = 0
    for a in axes:
        me = lax.axis_index(a)
        for d in range(1, sizes[a]):
            pl.semaphore_signal(
                barrier,
                inc=1,
                device_id={a: lax.rem(me + d, sizes[a])},
                device_id_type=MESH,
            )
            count += 1
    pl.semaphore_wait(barrier, count)


def place_of(offsets, axes, sizes):
    value = 0
    for a in axes:
        me = lax.axis_index(a)
        off = offsets.get(a, 0)
        value = value * sizes[a] + (lax.rem(me + off, sizes[a]) if off else me)
    return value


def remote(src, dst, send, recv, axis, distance, sizes):
    to = lax.rem(lax.axis_index(axis) + distance, sizes[axis])
    return pltpu.make_async_remote_copy(
        src_ref=src,
        dst_ref=dst,
        send_sem=send,
        recv_sem=recv,
        device_id={axis: to},
        device_id_type=MESH,
    )


def gather_kernel(plans, sizes, *refs):
    count = max(p[0] for p in plans) + 1
    xs, outs = refs[:count], refs[count : 2 * count]
    send_sems, recv_sems, local_sems = refs[2 * count :]
    used = {a: (sizes[a] if any(a in p[3] for p in plans) else 1) for a in AXES}
    greet(live(AXES, used), sizes)

    def cut(ref, rows):
        return ref if rows is None else ref.at[pl.ds(*rows)]

    def source(plan, place):
        i, rows, layout, phases, split = plan
        return cut(xs[i].at[place] if split else xs[i], rows)

    sends, kept, queue = [], [], []
    sem = 0
    for j, plan in enumerate(plans):
        i, rows, layout, phases, split = plan
        mine = source(plan, lax.axis_index(phases[0]))
        slot = cut(outs[i].at[place_of({}, layout, sizes)], rows)
        copy = pltpu.make_async_copy(mine, slot, local_sems.at[j])
        queue.append((plan, {}, -1, None))
        kept.append(copy)
    at = 0
    while at < len(queue):
        plan, offsets, phase, arrived = queue[at]
        at += 1
        i, rows, layout, phases, split = plan
        slot = cut(outs[i].at[place_of(offsets, layout, sizes)], rows)
        if arrived is None:
            src = source(plan, lax.axis_index(phases[0]))
        else:
            src = slot
            remote(
                slot, slot, send_sems.at[arrived], recv_sems.at[arrived], phases[0], 0, sizes
            ).wait_recv()
        for p in range(phase + 1, len(phases)):
            a = phases[p]
            for d in range(1, sizes[a]):
                piece = src
                if split and p == 0:
                    piece = source(plan, lax.rem(lax.axis_index(a) + d, sizes[a]))
                copy = remote(piece, slot, send_sems.at[sem], recv_sems.at[sem], a, d, sizes)
                copy.start()
                sends.append(copy)
                later = dict(offsets)
                later[a] = sizes[a] - d
                queue.append((plan, later, p, sem))
                sem += 1
        if at == len(plans):
            for copy in kept:
                copy.start()
    for copy in kept:
        copy.wait()
    for copy in sends:
        copy.wait_send()


def gather(arrays, plans, sizes, collective_id):
    plans = [
        (i, rows, live(layout, sizes), live(phases, sizes), split)
        for i, rows, layout, phases, split in plans
    ]
    counts = [int(np.prod([sizes[a] for a in p[2]])) for p in plans]
    total = sum(counts) - len(counts)
    shapes = []
    for i, x in enumerate(arrays):
        n, split = next((c, p[4]) for c, p in zip(counts, plans) if p[0] == i)
        shapes.append(jax.ShapeDtypeStruct((n,) + (x.shape[1:] if split else x.shape), x.dtype))
    spec = pl.BlockSpec(memory_space=pltpu.VMEM)
    moved = sum(int(np.prod(s.shape)) * s.dtype.itemsize for s in shapes)
    return pl.pallas_call(
        functools.partial(gather_kernel, plans, sizes),
        out_shape=shapes,
        in_specs=[spec] * len(arrays),
        out_specs=[spec] * len(arrays),
        scratch_shapes=[
            pltpu.SemaphoreType.DMA((total,)),
            pltpu.SemaphoreType.DMA((total,)),
            pltpu.SemaphoreType.DMA((len(plans),)),
        ],
        compiler_params=pltpu.CompilerParams(
            collective_id=collective_id, has_side_effects=True, vmem_limit_bytes=VMEM_LIMIT
        ),
        cost_estimate=pl.CostEstimate(flops=0, bytes_accessed=20 * moved, transcendentals=0),
    )(*arrays)


def offset_keys(axes, sizes):
    keys = [{}]
    for a in axes:
        keys = [dict(k, **{a: d}) for k in keys for d in list(range(1, sizes[a])) + [0]]
    return keys


def scatter_kernel(plans, sizes, *refs, between=None):
    count = max(p[0] for p in plans) + 1
    xs, outs = refs[:count], refs[count : 2 * count]
    at = 2 * count
    bufs = []
    for _, _, _, phases, swap in plans:
        n = len(phases)
        bufs.append((refs[at : at + n], refs[at + n : at + 2 * n]))
        at += 2 * n
    send_sems, recv_sems, local_sems = refs[at:]
    used = {
        a: (sizes[a] if any(a in p[3] or (p[4] and a == "head") for p in plans) else 1)
        for a in AXES
    }
    greet(live(AXES, used), sizes)
    sem = 0
    sends = []
    arrivals = [dict() for _ in plans]

    def number(offsets, axes):
        value = 0
        for a in axes:
            value = value * sizes[a] + offsets.get(a, 0)
        return value

    def block_of(j, offsets):
        i, rows, layout, phases, swap = plans[j]
        block = xs[i].at[place_of(offsets, layout, sizes)]
        return block if rows is None else block.at[pl.ds(*rows)]

    def total_of(j, offsets, phase):
        phases = plans[j][3]
        total = block_of(j, offsets)[...].astype(F32)
        for q in range(phase):
            rest = phases[q + 1 :]
            for d in range(1, sizes[phases[q]]):
                s = arrivals[j].pop((q, d, number(offsets, rest)))
                buf = bufs[j][1][q].at[d - 1, number(offsets, rest)]
                remote(buf, buf, send_sems.at[s], recv_sems.at[s], phases[q], 0, sizes).wait_recv()
                total = total + buf[...].astype(F32)
        return total

    depth = max(len(p[3]) for p in plans)
    for phase in range(depth):
        for j, (i, rows, layout, phases, swap) in enumerate(plans):
            if phase >= len(phases):
                continue
            a, rest = phases[phase], phases[phase + 1 :]
            for d in range(1, sizes[a]):
                for key in offset_keys(rest, sizes):
                    offsets = dict(key)
                    offsets[a] = d
                    where = number(key, rest)
                    if phase == 0:
                        src = block_of(j, offsets)
                    else:
                        src = bufs[j][0][phase].at[d - 1, where]
                        src[...] = total_of(j, offsets, phase).astype(src.dtype)
                    dst = bufs[j][1][phase].at[d - 1, where]
                    copy = remote(src, dst, send_sems.at[sem], recv_sems.at[sem], a, d, sizes)
                    copy.start()
                    sends.append(copy)
                    arrivals[j][(phase, d, where)] = sem
                    sem += 1
        if between is not None:
            between(phase)
    swaps = []
    for j, (i, rows, layout, phases, swap) in enumerate(plans):
        total = total_of(j, {}, len(phases))
        if swap:
            hold, out = bufs[j][0][0], outs[i]
            hold[...] = total.astype(hold.dtype)
            me = lax.axis_index("head")
            copy = pltpu.make_async_copy(hold.at[me], out.at[me], local_sems.at[j])
            copy.start()
            swaps.append((copy, None))
            for d in range(1, sizes["head"]):
                to = lax.rem(me + d, sizes["head"])
                copy = remote(
                    hold.at[to], out.at[me], send_sems.at[sem], recv_sems.at[sem], "head", d, sizes
                )
                copy.start()
                sends.append(copy)
                swaps.append((out.at[lax.rem(me + sizes["head"] - d, sizes["head"])], sem))
                sem += 1
        elif rows is None:
            outs[i][...] = total.astype(outs[i].dtype)
        else:
            outs[i][pl.ds(*rows)] = total.astype(outs[i].dtype)
    for item, s in swaps:
        if s is None:
            item.wait()
        else:
            remote(item, item, send_sems.at[s], recv_sems.at[s], "head", 0, sizes).wait_recv()
    for copy in sends:
        copy.wait_send()


def scatter_scratch(arrays, plans, out_types, sizes):
    scratch, total = [], 0
    for i, rows, layout, phases, swap in plans:
        x, kind = arrays[i], out_types[i]
        block = x.shape[1:] if rows is None else (rows[1],) + x.shape[2:]
        send_bufs, recv_bufs = [], []
        for p, a in enumerate(phases):
            rest = int(np.prod([sizes[b] for b in phases[p + 1 :]], dtype=int))
            shape = (sizes[a] - 1, rest) + block
            recv_bufs.append(pltpu.VMEM(shape, x.dtype))
            if p == 0:
                send_bufs.append(pltpu.VMEM(block if swap else (8, LANES), kind if swap else F32))
            else:
                send_bufs.append(pltpu.VMEM(shape, x.dtype))
            total += (sizes[a] - 1) * rest
        scratch += send_bufs + recv_bufs
        if swap:
            total += sizes["head"] - 1
    return scratch + [
        pltpu.SemaphoreType.DMA((total,)),
        pltpu.SemaphoreType.DMA((total,)),
        pltpu.SemaphoreType.DMA((len(plans),)),
    ]


def alive(plans, sizes):
    return [
        (i, rows, live(layout, sizes), live(phases, sizes), flag)
        for i, rows, layout, phases, flag in plans
    ]


def scatter(arrays, plans, out_types, sizes, collective_id):
    plans = alive(plans, sizes)
    shapes = [jax.ShapeDtypeStruct(x.shape[1:], kind) for x, kind in zip(arrays, out_types)]
    spec = pl.BlockSpec(memory_space=pltpu.VMEM)
    moved = sum(int(np.prod(x.shape)) * x.dtype.itemsize for x in arrays)
    return pl.pallas_call(
        functools.partial(scatter_kernel, plans, sizes),
        out_shape=shapes,
        in_specs=[spec] * len(arrays),
        out_specs=[spec] * len(arrays),
        scratch_shapes=scatter_scratch(arrays, plans, out_types, sizes),
        compiler_params=pltpu.CompilerParams(
            collective_id=collective_id, has_side_effects=True, vmem_limit_bytes=VMEM_LIMIT
        ),
        cost_estimate=pl.CostEstimate(flops=0, bytes_accessed=20 * moved, transcendentals=0),
    )(*arrays)


def feed_kernel(chunks, t_ref, c_ref, w_ref, *refs):
    act_ref, dgate_ref, dup_ref, branch_ref, dtok_ref = refs[-5:]
    before = refs[:-5]
    tokens, cot = t_ref[...], c_ref[...]
    places, _, rows, width = w_ref.shape
    per = max(1, LANES * 3 // rows)

    def products(j):
        low, n = chunks[j]

        def weight(m):
            return w_ref[:, m, :, low : low + n].reshape(D, n)

        return dot_nn(tokens, weight(1)), dot_nn(tokens, weight(2)), dot_nn(cot, weight(0))

    ready = [products(0)]
    for j, (low, n) in enumerate(chunks):
        gate, up, dact = ready[j]
        if j + 1 < len(chunks):
            ready.append(products(j + 1))
        sig = 1.0 / (1.0 + jnp.exp(-gate))
        silu = gate * sig
        act_ref[:, low : low + n] = (silu * up).astype(BF)
        dgate_ref[:, low : low + n] = (dact * up * (sig + silu * (1.0 - sig))).astype(BF)
        dup_ref[:, low : low + n] = (dact * silu).astype(BF)
    for z in range(0, places, per):
        cols = slice(z * rows, (z + per) * rows)

        def weight(m):
            return w_ref[z : z + per, m].reshape(per * rows, width)

        dtok = dot_nt(dgate_ref[...], weight(1)) + dot_nt(dup_ref[...], weight(2))
        branch = dot_nt(act_ref[...], weight(0))
        if before:
            branch = branch + before[0][:, cols].astype(F32)
            dtok = dtok + before[1][:, cols].astype(F32)
        dtok_ref[:, cols] = dtok.astype(BF)
        branch_ref[:, cols] = branch.astype(BF)


def feed(tokens, cot, weights, *before):
    n, width, tile = tokens.shape[0], weights.shape[-1], 256
    chunks = [(i, min(256, width - i)) for i in range(0, width, 256)]
    wide = pl.BlockSpec((tile, D), lambda i: (i, 0))
    inner = pl.BlockSpec((tile, width), lambda i: (i, 0))
    return pl.pallas_call(
        functools.partial(feed_kernel, chunks),
        grid=(n // tile,),
        in_specs=[wide, wide, pl.BlockSpec(memory_space=pltpu.VMEM)] + [wide] * len(before),
        out_specs=[inner, inner, inner, wide, wide],
        out_shape=[jax.ShapeDtypeStruct((n, k), BF) for k in (width, width, width, D, D)],
        compiler_params=pltpu.CompilerParams(vmem_limit_bytes=VMEM_LIMIT),
        cost_estimate=pl.CostEstimate(
            flops=12 * n * D * width, bytes_accessed=40 * 2**20, transcendentals=n * width
        ),
    )(tokens, cot, weights, *before)


def plain_grads_kernel(t_ref, c_ref, act_ref, dgate_ref, dup_ref, grad_ref):
    per, _, rows, width = grad_ref.shape
    for m, (left, right) in enumerate(((c_ref, act_ref), (t_ref, dgate_ref), (t_ref, dup_ref))):
        made = dot_tn(left[...], right[...]).astype(BF)
        grad_ref[:, m] = made.reshape(per, rows, width)


def plain_grads(tokens, cot, act, dgate, dup, places):
    n, width = act.shape
    rows = D // places
    per = max(1, LANES * 3 // rows)
    left = pl.BlockSpec((n, per * rows), lambda k: (0, k))
    right = pl.BlockSpec(memory_space=pltpu.VMEM)
    return pl.pallas_call(
        plain_grads_kernel,
        grid=(places // per,),
        in_specs=[left, left, right, right, right],
        out_specs=pl.BlockSpec((per, 3, rows, width), lambda k: (k, 0, 0, 0)),
        out_shape=jax.ShapeDtypeStruct((places, 3, rows, width), BF),
        compiler_params=pltpu.CompilerParams(vmem_limit_bytes=VMEM_LIMIT),
        cost_estimate=pl.CostEstimate(
            flops=6 * n * D * width, bytes_accessed=40 * 2**20, transcendentals=0
        ),
    )(tokens, cot, act, dgate, dup)


def grads_kernel(plans, sizes, dtok_ref, t_hbm, c_hbm, act_hbm, dgate_hbm, dup_hbm, *refs):
    sum_ref, grad_hbm, left_s, right_s, made_s, load_sems, made_sems = refs[:7]
    per, rows = made_s.shape[1:3]
    cols = per * rows
    loads = [
        pltpu.make_async_copy(c_hbm, left_s.at[0], load_sems.at[0]),
        pltpu.make_async_copy(act_hbm, right_s.at[0], load_sems.at[1]),
        pltpu.make_async_copy(t_hbm, left_s.at[1], load_sems.at[2]),
        pltpu.make_async_copy(dgate_hbm, right_s.at[1], load_sems.at[3]),
        pltpu.make_async_copy(dup_hbm, right_s.at[0], load_sems.at[4]),
    ]
    for copy in loads[:4]:
        copy.start()

    def stored(m, k, slot):
        return pltpu.make_async_copy(
            made_s.at[slot], grad_hbm.at[pl.ds(k * per, per), m], made_sems.at[slot]
        )

    def some(m, low, high, left, right, fresh):
        def one(k, carry):
            slot = lax.rem(k, 2)
            if fresh:
                pl.when(k >= 2)(lambda: stored(m, k, slot).wait())
            else:
                stored(m, k, slot).wait()
            part = left_s[left, :, pl.ds(pl.multiple_of(k * cols, LANES), cols)]
            made_s[slot] = dot_tn(part, right_s[right]).astype(BF).reshape(made_s.shape[1:])
            stored(m, k, slot).start()
            return carry

        lax.fori_loop(low, high, one, 0)

    chunks = D // cols

    def between(phase):
        if phase == 0:
            loads[0].wait()
            loads[1].wait()
            some(0, 0, chunks // 2, 0, 0, True)
        elif phase == 1:
            some(0, chunks // 2, chunks, 0, 0, False)
            loads[4].start()
            loads[2].wait()
            loads[3].wait()
            some(1, 0, chunks, 1, 1, False)
        else:
            loads[4].wait()
            some(2, 0, chunks, 1, 0, False)

    scatter_kernel(plans, sizes, dtok_ref, sum_ref, *refs[7:], between=between)
    for slot in range(2):
        stored(2, slot, slot).wait()


def feed_grads(dtok, tokens, cot, act, dgate, dup, places, plans, sizes, collective_id):
    plans = alive(plans, sizes)
    n, width = act.shape
    rows = D // places
    per = max(1, LANES * 3 // rows)
    spec = pl.BlockSpec(memory_space=pltpu.VMEM)
    far = pl.BlockSpec(memory_space=pl.ANY)
    return pl.pallas_call(
        functools.partial(grads_kernel, plans, sizes),
        out_shape=[
            jax.ShapeDtypeStruct(dtok.shape[1:], F32),
            jax.ShapeDtypeStruct((places, 3, rows, width), BF),
        ],
        in_specs=[spec] + [far] * 5,
        out_specs=[spec, far],
        scratch_shapes=[
            pltpu.VMEM((2, n, D), BF),
            pltpu.VMEM((2, n, width), BF),
            pltpu.VMEM((2, per, rows, width), BF),
            pltpu.SemaphoreType.DMA((5,)),
            pltpu.SemaphoreType.DMA((2,)),
        ]
        + scatter_scratch([dtok], plans, [F32], sizes),
        compiler_params=pltpu.CompilerParams(
            collective_id=collective_id, has_side_effects=True, vmem_limit_bytes=VMEM_LIMIT
        ),
        cost_estimate=pl.CostEstimate(
            flops=6 * n * D * width, bytes_accessed=100 * 2**20, transcendentals=0
        ),
    )(dtok, tokens, cot, act, dgate, dup)


def forward_kernel(heads, slots, tops, q_ref, kv_ref, o_ref, lse_ref, top_s, sum_s, acc_s):
    def score(keys, a, h):
        return dot_nt(keys, q_ref[a * BLOCK : (a + 1) * BLOCK, h * HEAD_DIM : (h + 1) * HEAD_DIM])

    for a in range(2):
        top_s[...] = jnp.full(top_s.shape, -1e30, F32)
        sum_s[...] = jnp.zeros(sum_s.shape, F32)
        acc_s[...] = jnp.zeros(acc_s.shape, F32)
        count = tops[a] + 1

        def step(keys, values_t):
            ahead = min(3, heads)
            ready = [score(keys, a, h) for h in range(ahead)]
            for h in range(heads):
                s = ready[h]
                if h + ahead < heads:
                    ready.append(score(keys, a, h + ahead))
                old = top_s[h : h + 1, :]
                new = jnp.maximum(old, jnp.max(s, axis=0, keepdims=True))
                p = jnp.exp2((s - new) * SCALE2)
                fade = jnp.exp2((old - new) * SCALE2)
                sum_s[h : h + 1, :] = sum_s[h : h + 1, :] * fade + jnp.sum(p, axis=0, keepdims=True)
                top_s[h : h + 1, :] = new
                acc_s[h] = acc_s[h] * fade + dot_nn(values_t, p.astype(BF))

        def two(i, carry):
            first, second = slots[2 * i], slots[2 * i + 1]
            both = jnp.concatenate([kv_ref[first], kv_ref[second]], axis=0)
            step(both[:, :HEAD_DIM], both[:, HEAD_DIM:].T)
            return carry

        lax.fori_loop(0, count // 2, two, 0)

        @pl.when(count % 2 == 1)
        def _():
            last = kv_ref[slots[count - 1]]
            step(last[:, :HEAD_DIM], last[:, HEAD_DIM:].T)

        for h in range(heads):
            total = sum_s[h : h + 1, :]
            o_ref[a * BLOCK : (a + 1) * BLOCK, h * HEAD_DIM : (h + 1) * HEAD_DIM] = (
                acc_s[h] / total
            ).T
            lse_ref[a, h : h + 1, :] = top_s[h : h + 1, :] * SCALE2 + jnp.log2(total)
        lse_ref[a, heads:8, :] = jnp.zeros((8 - heads, BLOCK), F32)


def attend(slots, tops, q, kv):
    heads = q.shape[1] // HEAD_DIM
    spec = pl.BlockSpec(memory_space=pltpu.VMEM)
    pairs = 33 * BLOCK * BLOCK * heads
    return pl.pallas_call(
        functools.partial(forward_kernel, heads),
        grid_spec=pltpu.PrefetchScalarGridSpec(
            num_scalar_prefetch=2,
            grid=(1,),
            in_specs=[spec] * 2,
            out_specs=[spec] * 2,
            scratch_shapes=[
                pltpu.VMEM((8, BLOCK), F32),
                pltpu.VMEM((8, BLOCK), F32),
                pltpu.VMEM((heads, HEAD_DIM, BLOCK), F32),
            ],
        ),
        out_shape=(
            jax.ShapeDtypeStruct(q.shape, F32),
            jax.ShapeDtypeStruct((2, 8, BLOCK), F32),
        ),
        compiler_params=pltpu.CompilerParams(vmem_limit_bytes=VMEM_LIMIT),
        cost_estimate=pl.CostEstimate(
            flops=pairs * 4 * HEAD_DIM, bytes_accessed=80 * 2**20, transcendentals=pairs
        ),
    )(slots, tops, q, kv)


def backward_kernel(
    heads, slots, tops, q_ref, kv_ref, do_ref, lse_ref, delta_ref, dq_ref, dkv_ref, dq_s, dkv_s
):
    dkv_s[...] = jnp.zeros(dkv_s.shape, F32)
    for a in range(2):
        dq_s[...] = jnp.zeros(dq_s.shape, F32)

        def part(ref, h):
            return ref[a * BLOCK : (a + 1) * BLOCK, h * HEAD_DIM : (h + 1) * HEAD_DIM]

        def one(n, carry):
            slot = slots[n]
            keys, values = kv_ref[slot, :, :HEAD_DIM], kv_ref[slot, :, HEAD_DIM:]
            keys_t = keys.T

            def products(h):
                return dot_nt(keys, part(q_ref, h)), dot_nt(values, part(do_ref, h))

            dk = jnp.zeros((BLOCK, HEAD_DIM), F32)
            dv = jnp.zeros((BLOCK, HEAD_DIM), F32)
            ahead = min(2, heads)
            ready = [products(h) for h in range(ahead)]
            for h in range(heads):
                s, dp = ready[h]
                if h + ahead < heads:
                    ready.append(products(h + ahead))
                p = jnp.exp2(s * SCALE2 - lse_ref[a, h : h + 1, :])
                dv = dv + dot_nn(p.astype(BF), part(do_ref, h))
                ds = (p * (dp - delta_ref[a, h : h + 1, :])).astype(BF)
                dk = dk + dot_nn(ds, part(q_ref, h))
                dq_s[h] = dq_s[h] + dot_nn(keys_t, ds)
            dkv_s[slot, :, :HEAD_DIM] = dkv_s[slot, :, :HEAD_DIM] + dk
            dkv_s[slot, :, HEAD_DIM:] = dkv_s[slot, :, HEAD_DIM:] + dv
            return carry

        lax.fori_loop(0, tops[a] + 1, one, 0)
        for h in range(heads):
            dq_ref[a * BLOCK : (a + 1) * BLOCK, h * HEAD_DIM : (h + 1) * HEAD_DIM] = (
                (dq_s[h] * SCALE).T
            ).astype(BF)
    dkv_ref[:, :, :HEAD_DIM] = (dkv_s[:, :, :HEAD_DIM] * SCALE).astype(BF)
    dkv_ref[:, :, HEAD_DIM:] = dkv_s[:, :, HEAD_DIM:].astype(BF)


def attend_back(slots, tops, q, kv, do, lse, delta):
    heads = q.shape[1] // HEAD_DIM
    spec = pl.BlockSpec(memory_space=pltpu.VMEM)
    pairs = 33 * BLOCK * BLOCK * heads
    return pl.pallas_call(
        functools.partial(backward_kernel, heads),
        grid_spec=pltpu.PrefetchScalarGridSpec(
            num_scalar_prefetch=2,
            grid=(1,),
            in_specs=[spec] * 5,
            out_specs=[spec] * 2,
            scratch_shapes=[
                pltpu.VMEM((heads, HEAD_DIM, BLOCK), F32),
                pltpu.VMEM(kv.shape, F32),
            ],
        ),
        out_shape=(
            jax.ShapeDtypeStruct(q.shape, BF),
            jax.ShapeDtypeStruct(kv.shape, BF),
        ),
        compiler_params=pltpu.CompilerParams(vmem_limit_bytes=VMEM_LIMIT),
        cost_estimate=pl.CostEstimate(
            flops=pairs * 10 * HEAD_DIM, bytes_accessed=120 * 2**20, transcendentals=pairs
        ),
    )(slots, tops, q, kv, do, lse, delta)


def inverse_rms(value):
    return lax.rsqrt(jnp.mean(value * value, axis=-1, keepdims=True) + EPS)


def rotate(value, cosine, sine):
    rows, width = value.shape
    half = HEAD_DIM // 2
    parts = value.reshape(rows, width // HEAD_DIM, HEAD_DIM)
    first, second = parts[..., :half], parts[..., half:]
    cosine, sine = cosine[:, None, :], sine[:, None, :]
    return jnp.concatenate(
        [first * cosine - second * sine, second * cosine + first * sine], axis=-1
    ).reshape(rows, width)


def shift(value, axis, distance, sizes):
    n = sizes[axis]
    return lax.ppermute(value, axis, [(i, (i + distance) % n) for i in range(n)])


def small_rows(*rows):
    return jnp.stack(
        [jnp.pad(r.astype(F32), ((0, LANES - r.shape[0]),)) for r in rows]
        + [jnp.zeros((LANES,), F32)] * (8 - len(rows))
    )


def shards(
    sizes,
    hidden,
    cotangent,
    block_order,
    norm1,
    q_weight,
    q_bias,
    k_weight,
    k_bias,
    v_weight,
    v_bias,
    o_weight,
    norm2,
    gate_weight,
    up_weight,
    down_weight,
):
    tok = hidden.shape[0]
    pair = sizes["head"] * tok
    blk = int(np.prod([sizes[a] for a in BLK]))
    seqs = blk // SEQ_SPAN
    place_axes = {1: BLK, 2: BLK[:3], 4: BLK[:2]}[seqs]
    seq_axes = BLK[len(place_axes) :]
    head = lax.axis_index("head")
    place = place_of({}, place_axes, sizes)
    seq = place_of({}, seq_axes, sizes) if seq_axes else 0
    order = lax.dynamic_index_in_dim(block_order, seq, 0, keepdims=False)
    tops = lax.dynamic_slice_in_dim(order, place * 2, 2)
    slots = jnp.argsort(order).astype(jnp.int32)
    positions = (tops[:, None] * tok + jnp.arange(tok, dtype=jnp.int32)[None, :]).reshape(pair)
    frequency = THETA ** (-(jnp.arange(HEAD_DIM // 2, dtype=F32) * 2.0) / HEAD_DIM)
    angles = positions.astype(F32)[:, None] * frequency[None, :]
    cosine, sine = jnp.cos(angles), jnp.sin(angles)

    q_cols = D // 2
    kv_cols = HEAD_DIM
    rows = q_weight.shape[0]
    halves = [
        jnp.concatenate(
            [
                q_weight[:, i * q_cols : (i + 1) * q_cols],
                k_weight[:, i * kv_cols : (i + 1) * kv_cols],
                v_weight[:, i * kv_cols : (i + 1) * kv_cols],
            ],
            axis=1,
        ).astype(BF)
        for i in range(2)
    ]
    small = small_rows(
        *[v.astype(BF) for v in (norm1, norm2, q_bias, k_bias, v_bias)]
    )
    w_qkv, x_pair, small_all, w_out = gather(
        [jnp.stack(halves), hidden, small, o_weight.astype(BF)],
        [
            (0, None, AXES, AXES, True),
            (1, None, ("head",), ("head",), False),
            (2, None, AXES, AXES, False),
            (3, None, BLK, BLK, False),
        ],
        sizes,
        1,
    )
    w_out = w_out.reshape(q_cols, D)
    w_qkv = w_qkv.reshape(D, q_cols + 2 * kv_cols)
    x_pair = x_pair.reshape(pair, D).astype(F32)
    gain_one = small_all[:, 0, :rows].reshape(D)
    gain_two = small_all[:, 1, :rows].reshape(D)
    bias_q = lax.dynamic_slice_in_dim(small_all[:, 2, :rows].reshape(D), head * q_cols, q_cols)
    bias_k, bias_v = (
        lax.dynamic_slice_in_dim(
            small_all[:, i, : k_bias.shape[0]].reshape(2 * kv_cols), head * kv_cols, kv_cols
        )
        for i in (3, 4)
    )

    near = ("y", "c")
    parts = sizes["y"] * sizes["c"]
    width = gate_weight.shape[1]
    lanes = -(-width // (LANES * parts)) * LANES
    wide = lanes * parts
    corner = place_of({}, near, sizes)
    ff_rows = gate_weight.shape[0]

    def corner_send(blocks):
        got = [lax.dynamic_index_in_dim(blocks, corner, 0, keepdims=False)]
        for d in range(1, parts):
            piece = lax.dynamic_index_in_dim(blocks, corner ^ d, 0, keepdims=False)
            got.append(lax.ppermute(piece, near, [(i, i ^ d) for i in range(parts)]))
        return got

    def corner_sort(got):
        held = jnp.stack(got)
        return [lax.dynamic_index_in_dim(held, corner ^ i, 0, keepdims=False) for i in range(parts)]

    def quarters(weight):
        padded = jnp.pad(weight.astype(BF), ((0, 0), (0, wide - width)))
        return padded.reshape(ff_rows, parts, lanes).transpose(1, 0, 2)

    packed = jnp.stack([quarters(w) for w in (down_weight, gate_weight, up_weight)], axis=1)
    mine = jnp.stack(corner_sort(corner_send(packed)), axis=1)
    mine = mine.reshape(1, 3, parts * ff_rows, lanes)
    first = lanes * 4 // 9 // LANES * LANES

    def along_z(part, zero):
        part = (part.astype(F32) + zero).astype(BF)
        return lax.all_gather(part, live(("g", "z"), sizes), axis=0, tiled=True)

    w_feed_one = along_z(mine[..., :first], small_all[0, 7, 0])

    def halved(value, axis, dim, kind=BF):
        me = lax.axis_index(axis)
        away = lax.dynamic_index_in_dim(value, 1 - me, dim, keepdims=False)
        keep = lax.dynamic_index_in_dim(value, me, dim, keepdims=False)
        return (keep.astype(F32) + shift(away, axis, 1, sizes).astype(F32)).astype(kind)

    def group_sum(value, kind):
        near_sum = halved(value.reshape(2, 2, 2, tok, D), "c", 2)
        one = halved(near_sum[:, :, :half], "head", 0)
        two = halved(near_sum[:, :, half:], "y", 1)
        return jnp.concatenate([halved(one, "y", 0, kind), halved(two, "head", 0, kind)])

    scale_one = inverse_rms(x_pair)
    normed = (x_pair * scale_one * gain_one).astype(BF)
    qkv = dot_nn(normed, w_qkv)
    queries = rotate(qkv[:, :q_cols] + bias_q, cosine, sine).astype(BF)
    keys = rotate(qkv[:, q_cols : q_cols + kv_cols] + bias_k, cosine, sine).astype(BF)
    values = (qkv[:, q_cols + kv_cols :] + bias_v).astype(BF)
    group = ("head", "y", "c")
    half = tok // 2
    crossed = [
        ((0, half), group, ("head", "y", "c"), False),
        ((half, half), group, ("y", "head", "c"), False),
    ]
    kv, cot_all = gather(
        [jnp.concatenate([keys, values], axis=1), cotangent],
        [
            (0, None, place_axes, place_axes, False),
            (1, None, group, ("y", "head", "c"), False),
        ],
        sizes,
        2,
    )
    cot_all = cot_all.reshape(-1, D)
    kv = kv.reshape(2 * SEQ_SPAN, tok, 2 * HEAD_DIM)
    attended, lse = attend(slots, tops, queries, kv)
    w_feed_two = along_z(mine[..., first:], lse[0, 7, 0])
    attn_local = attended.astype(BF)
    inputs = lax.dynamic_slice_in_dim(x_pair, head * tok, tok)
    mixed_part = dot_nn(attn_local, w_out).astype(BF).reshape(2, tok, D)
    (mixed_sum,) = scatter(
        [mixed_part], [(0, None, ("head",), ("head",), False)], [F32], sizes, 3
    )
    mixed = inputs + mixed_sum
    scale_two = inverse_rms(mixed)
    normed_two = (mixed * scale_two * gain_two).astype(BF)
    (tokens,) = gather([normed_two], [(0,) + c for c in crossed], sizes, 4)
    tokens = tokens.reshape(-1, D)

    places = w_feed_one.shape[0]
    act, dgate, dup, branch, dtokens = feed(tokens, cot_all, w_feed_one)
    parts_one = plain_grads(tokens, cot_all, act, dgate, dup, places)
    act, dgate, dup, branch, dtokens = feed(tokens, cot_all, w_feed_two, branch, dtokens)
    dnormed_two, parts_two = feed_grads(
        dtokens.reshape(-1, tok, D),
        tokens,
        cot_all,
        act,
        dgate,
        dup,
        places,
        [
            (0, (0, half), group, ("c", "head", "y"), False),
            (0, (half, half), group, ("c", "y", "head"), False),
        ],
        sizes,
        5,
    )
    branch_sum = group_sum(branch, F32)
    output = (mixed + branch_sum).astype(BF)

    def collect(grad):
        total = lax.psum_scatter(grad, live(("g", "z"), sizes), scatter_dimension=0, tiled=True)
        total = total.reshape(3, parts, ff_rows, grad.shape[-1])
        return corner_sort(corner_send(total.transpose(1, 0, 2, 3)))

    back = list(zip(collect(parts_one), collect(parts_two)))
    d_down, d_gate, d_up = (
        jnp.concatenate([half[m] for pair_ in back for half in pair_], axis=1)[:, :width].astype(
            F32
        )
        for m in range(3)
    )

    z_two = mixed * scale_two
    u_two = gain_two * dnormed_two
    norm2_part = jnp.sum(dnormed_two * z_two, axis=0)
    dmixed = cotangent.astype(F32) + scale_two * (
        u_two - z_two * jnp.mean(z_two * u_two, axis=-1, keepdims=True)
    )
    dproj = dmixed.astype(BF)
    (dproj_pair,) = gather([dproj], [(0, None, ("head",), ("head",), False)], sizes, 6)
    dproj_pair = dproj_pair.reshape(pair, D)
    dout = dot_nt(dproj_pair, w_out).astype(BF)
    delta = jnp.sum(
        (dout.astype(F32) * attended).reshape(2, tok, q_cols // HEAD_DIM, HEAD_DIM), axis=-1
    ).transpose(0, 2, 1)
    delta = jnp.pad(delta, ((0, 0), (0, 8 - delta.shape[1]), (0, 0)))

    o_part = dot_tn(attn_local, dproj_pair).astype(BF)

    dq, dkv_parts = attend_back(slots, tops, queries, kv, dout, lse, delta)
    (dkv,) = scatter(
        [dkv_parts.reshape(SEQ_SPAN, pair, 2 * HEAD_DIM)],
        [(0, None, place_axes, place_axes[::-1], False)],
        [BF],
        sizes,
        7,
    )
    dq_pre = rotate(dq.astype(F32), cosine, -sine).astype(BF)
    dk_pre = rotate(dkv[:, :HEAD_DIM].astype(F32), cosine, -sine).astype(BF)
    dv = dkv[:, HEAD_DIM:]
    dpre = jnp.concatenate([dq_pre, dk_pre, dv], axis=1)
    w_part = dot_tn(normed, dpre).astype(BF)
    bias_part = jnp.sum(dpre.astype(F32), axis=0)
    dnormed = dot_nt(dpre, w_qkv)
    norm1_part = jnp.sum(dnormed * (x_pair * scale_one), axis=0)
    own = (jnp.arange(2) == head).astype(F32)[:, None]

    def owners(vector):
        return vector.reshape(2, blk, -1).transpose(1, 0, 2)

    def owned(vector):
        return owners((own * vector[None, :]).reshape(-1))

    small_grads = jnp.stack(
        [
            jnp.pad(part, ((0, 0), (0, 0), (0, LANES - part.shape[2])))
            for part in (
                owners(norm1_part),
                owners(norm2_part),
                owned(bias_part[:q_cols]),
                owned(bias_part[q_cols : q_cols + kv_cols]),
                owned(bias_part[q_cols + kv_cols :]),
            )
        ]
        + [jnp.zeros((blk, 2, LANES), F32)] * 3,
        axis=2,
    )
    small_grads = small_grads.transpose(1, 0, 2, 3).reshape(2 * blk, 8, LANES)
    w_grads, small_sum, dnormed_sum, d_out_weight = scatter(
        [
            w_part.reshape(2, blk, rows, -1).transpose(1, 0, 2, 3),
            small_grads,
            dnormed.astype(BF).reshape(2, tok, D),
            o_part.reshape(blk, -1, D),
        ],
        [
            (0, None, BLK, BLK[::-1], True),
            (1, None, AXES, AXES[::-1], False),
            (2, None, ("head",), ("head",), False),
            (3, None, BLK, BLK[::-1], False),
        ],
        [F32, F32, F32, F32],
        sizes,
        8,
    )
    own_scale = lax.dynamic_slice_in_dim(scale_one, head * tok, tok)
    z_one = inputs * own_scale
    u_one = gain_one * dnormed_sum
    hidden_grad = (
        dmixed + own_scale * (u_one - z_one * jnp.mean(z_one * u_one, axis=-1, keepdims=True))
    ).astype(BF)
    kn = k_bias.shape[0]
    return (
        output,
        hidden_grad,
        small_sum[0, :rows],
        jnp.concatenate([w_grads[0, :, :q_cols], w_grads[1, :, :q_cols]], axis=1),
        small_sum[2, :rows],
        jnp.concatenate([w_grads[i, :, q_cols : q_cols + kv_cols] for i in range(2)], axis=1),
        small_sum[3, :kn],
        jnp.concatenate([w_grads[i, :, q_cols + kv_cols :] for i in range(2)], axis=1),
        small_sum[4, :kn],
        d_out_weight,
        small_sum[1, :rows],
        d_gate,
        d_up,
        d_down,
    )


def solution(mesh):
    heads, blk = mesh.devices.shape
    split = jax.sharding.Mesh(mesh.devices.reshape(heads, blk // 16, 4, 2, 2), AXES)
    sizes = dict(split.shape)
    rows = P(AXES, None)
    vector = P(AXES)
    feed = P(BLK, "head")
    return jax.shard_map(
        functools.partial(shards, sizes),
        mesh=split,
        in_specs=(
            rows,
            rows,
            P(),
            vector,
            rows,
            vector,
            rows,
            vector,
            rows,
            vector,
            rows,
            vector,
            feed,
            feed,
            feed,
        ),
        out_specs=(
            rows,
            rows,
            vector,
            rows,
            vector,
            rows,
            vector,
            rows,
            vector,
            rows,
            vector,
            feed,
            feed,
            feed,
        ),
        check_vma=False,
    )
```

```python
import functools

import jax
import jax.numpy as jnp
import numpy as np
from jax import lax
from jax.experimental import pallas as pl
from jax.experimental.pallas import tpu as pltpu
from jax.sharding import PartitionSpec as P

D = 1536
QHEADS = 12
KVHEADS = 2
HEAD_DIM = 128
SEQ_SPAN = 16
BLOCK = 256

EPS = 1e-06
THETA = 1000000.0
SCALE = HEAD_DIM**-0.5
LOG2E = 1.4426950408889634
SCALE2 = SCALE * LOG2E
BF = jnp.bfloat16
F32 = jnp.float32
MESH = pl.DeviceIdType.MESH
VMEM_LIMIT = 56 * 2**20
AXES = ("head", "g", "z", "y", "c")
BLK = ("g", "z", "y", "c")
LANES = 128


def dot_nn(a, b):
    return lax.dot_general(a, b, (((1,), (0,)), ((), ())), preferred_element_type=F32)


def dot_nt(a, b):
    return lax.dot_general(a, b, (((1,), (1,)), ((), ())), preferred_element_type=F32)


def dot_tn(a, b):
    return lax.dot_general(a, b, (((0,), (0,)), ((), ())), preferred_element_type=F32)


def live(axes, sizes):
    return tuple(a for a in axes if sizes[a] > 1)


def greet(axes, sizes, diagonal=False):
    barrier = pltpu.get_barrier_semaphore()
    count = 0
    if diagonal:
        pl.semaphore_signal(barrier, inc=1, device_id=across(3), device_id_type=MESH)
        count += 1
    for a in axes:
        me = lax.axis_index(a)
        for d in range(1, sizes[a]):
            pl.semaphore_signal(
                barrier,
                inc=1,
                device_id={a: lax.rem(me + d, sizes[a])},
                device_id_type=MESH,
            )
            count += 1
    pl.semaphore_wait(barrier, count)


def across(d):
    y, c = lax.axis_index("y"), lax.axis_index("c")
    return {"y": 1 - y if d & 2 else y, "c": 1 - c if d & 1 else c}


class Swap:
    def __init__(self, x, out, send_sems, recv_sems, local_sem):
        me = lax.axis_index("y") * 2 + lax.axis_index("c")
        self.kept = pltpu.make_async_copy(x.at[:, me], out.at[:, me], local_sem)
        self.copies = []
        for d in range(1, 4):
            to = across(d)
            self.copies.append(
                pltpu.make_async_remote_copy(
                    src_ref=x.at[:, to["y"] * 2 + to["c"]],
                    dst_ref=out.at[:, me],
                    send_sem=send_sems.at[d - 1],
                    recv_sem=recv_sems.at[d - 1],
                    device_id=to,
                    device_id_type=MESH,
                )
            )

    def start(self):
        for copy in self.copies:
            copy.start()
        self.kept.start()

    def wait(self):
        self.kept.wait()
        for copy in self.copies:
            copy.wait()


def swap_scratch(swaps):
    if not swaps:
        return []
    return [pltpu.SemaphoreType.DMA((3 * len(swaps),))] * 2 + [
        pltpu.SemaphoreType.DMA((len(swaps),))
    ]


def swaps_of(xs, outs, sems):
    return [
        Swap(
            x,
            out,
            sems[0].at[pl.ds(3 * i, 3)],
            sems[1].at[pl.ds(3 * i, 3)],
            sems[2].at[i],
        )
        for i, (x, out) in enumerate(zip(xs, outs))
    ]


def place_of(offsets, axes, sizes):
    value = 0
    for a in axes:
        me = lax.axis_index(a)
        off = offsets.get(a, 0)
        value = value * sizes[a] + (lax.rem(me + off, sizes[a]) if off else me)
    return value


def remote(src, dst, send, recv, axis, distance, sizes):
    to = lax.rem(lax.axis_index(axis) + distance, sizes[axis])
    return pltpu.make_async_remote_copy(
        src_ref=src,
        dst_ref=dst,
        send_sem=send,
        recv_sem=recv,
        device_id={axis: to},
        device_id_type=MESH,
    )


def gather_kernel(plans, sizes, swap_count, *refs, ahead=None):
    count = max(p[0] for p in plans) + 1
    xs, refs = refs[:count], refs[count:]
    swap_xs, refs = refs[:swap_count], refs[swap_count:]
    outs, refs = refs[:count], refs[count:]
    swap_outs, refs = refs[:swap_count], refs[swap_count:]
    send_sems, recv_sems, local_sems = refs[:3]
    swaps = swaps_of(swap_xs, swap_outs, refs[3:])
    used = {a: (sizes[a] if any(a in p[3] for p in plans) else 1) for a in AXES}
    greet(live(AXES, used), sizes, bool(swaps))

    def cut(ref, rows):
        return ref if rows is None else ref.at[pl.ds(*rows)]

    def source(plan, place):
        i, rows, layout, phases, split = plan
        return cut(xs[i].at[place] if split else xs[i], rows)

    sends, kept, queue = [], [], []
    sem = 0
    for j, plan in enumerate(plans):
        i, rows, layout, phases, split = plan
        mine = source(plan, lax.axis_index(phases[0]))
        slot = cut(outs[i].at[place_of({}, layout, sizes)], rows)
        copy = pltpu.make_async_copy(mine, slot, local_sems.at[j])
        queue.append((plan, {}, -1, None))
        kept.append(copy)
    at = 0
    while at < len(queue):
        plan, offsets, phase, arrived = queue[at]
        at += 1
        i, rows, layout, phases, split = plan
        slot = cut(outs[i].at[place_of(offsets, layout, sizes)], rows)
        if arrived is None:
            src = source(plan, lax.axis_index(phases[0]))
        else:
            src = slot
            remote(
                slot, slot, send_sems.at[arrived], recv_sems.at[arrived], phases[0], 0, sizes
            ).wait_recv()
        for p in range(phase + 1, len(phases)):
            a = phases[p]
            for d in range(1, sizes[a]):
                piece = src
                if split and p == 0:
                    piece = source(plan, lax.rem(lax.axis_index(a) + d, sizes[a]))
                copy = remote(piece, slot, send_sems.at[sem], recv_sems.at[sem], a, d, sizes)
                copy.start()
                sends.append(copy)
                later = dict(offsets)
                later[a] = sizes[a] - d
                queue.append((plan, later, p, sem))
                sem += 1
        if at == len(plans):
            if ahead is not None:
                ahead()
            for copy in kept + swaps:
                copy.start()
    for copy in kept + swaps:
        copy.wait()
    for copy in sends:
        copy.wait_send()


def gather(arrays, plans, sizes, collective_id, swaps=()):
    plans = [
        (i, rows, live(layout, sizes), live(phases, sizes), split)
        for i, rows, layout, phases, split in plans
    ]
    counts = [int(np.prod([sizes[a] for a in p[2]])) for p in plans]
    total = sum(counts) - len(counts)
    shapes = []
    for i, x in enumerate(arrays):
        n, split = next((c, p[4]) for c, p in zip(counts, plans) if p[0] == i)
        shapes.append(jax.ShapeDtypeStruct((n,) + (x.shape[1:] if split else x.shape), x.dtype))
    spec = pl.BlockSpec(memory_space=pltpu.VMEM)
    far = pl.BlockSpec(memory_space=pl.ANY)
    specs = [spec] * len(arrays) + [far] * len(swaps)
    moved = sum(int(np.prod(s.shape)) * s.dtype.itemsize for s in shapes)
    return pl.pallas_call(
        functools.partial(gather_kernel, plans, sizes, len(swaps)),
        out_shape=shapes + [jax.ShapeDtypeStruct(x.shape, x.dtype) for x in swaps],
        in_specs=specs,
        out_specs=specs,
        scratch_shapes=[
            pltpu.SemaphoreType.DMA((total,)),
            pltpu.SemaphoreType.DMA((total,)),
            pltpu.SemaphoreType.DMA((len(plans),)),
        ]
        + swap_scratch(swaps),
        compiler_params=pltpu.CompilerParams(
            collective_id=collective_id, has_side_effects=True, vmem_limit_bytes=VMEM_LIMIT
        ),
        cost_estimate=pl.CostEstimate(flops=0, bytes_accessed=20 * moved, transcendentals=0),
    )(*arrays, *swaps)


def front_kernel(plans, sizes, *refs):
    q_ref, k_ref, v_ref, o_ref, hidden_ref, small_ref = refs[:6]
    feeds, refs = refs[6:9], refs[9:]
    outs, swapped, second_ref, refs = refs[:4], refs[4], refs[5], refs[6:]
    halves_s, o_s, first_s = refs[:3]
    heads = halves_s.shape[0]
    q_cols, kv_cols = q_ref.shape[1] // heads, k_ref.shape[1] // heads
    for i in range(heads):
        halves_s[i, :, :q_cols] = q_ref[:, i * q_cols : (i + 1) * q_cols].astype(BF)
        cols = slice(i * kv_cols, (i + 1) * kv_cols)
        halves_s[i, :, q_cols : q_cols + kv_cols] = k_ref[:, cols].astype(BF)
        halves_s[i, :, q_cols + kv_cols :] = v_ref[:, cols].astype(BF)
    o_s[...] = o_ref[...].astype(BF)

    def pack():
        first, second = first_s.shape[-1], second_ref.shape[-1]
        for m, feed_ref in enumerate(feeds):
            rows, width = feed_ref.shape
            for i in range(first_s.shape[1]):
                low = i * (first + second)
                for ref, n in ((first_s, first), (second_ref, second)):
                    real = min(n, width - low)
                    ref[m, i, :, :real] = feed_ref[:, low : low + real].astype(BF)
                    if real < n:
                        ref[m, i, :, real:] = jnp.zeros((rows, n - real), BF)
                    low += n

    gather_kernel(
        plans,
        sizes,
        1,
        halves_s,
        hidden_ref,
        small_ref,
        o_s,
        first_s,
        *outs,
        swapped,
        *refs[3:],
        ahead=pack,
    )


def front(weights, hidden, small, feeds, first, second, plans, sizes, collective_id):
    plans = alive(plans, sizes)
    heads, rows = sizes["head"], weights[0].shape[0]
    halves = jax.ShapeDtypeStruct((heads, rows, sum(w.shape[1] for w in weights[:3]) // heads), BF)
    out = jax.ShapeDtypeStruct(weights[3].shape, BF)
    arrays = [halves, hidden, small, out]
    counts = [int(np.prod([sizes[a] for a in p[2]])) for p in plans]
    total = sum(counts) - len(counts)
    shapes = [
        jax.ShapeDtypeStruct((n,) + (x.shape[1:] if p[4] else x.shape), x.dtype)
        for n, x, p in zip(counts, arrays, plans)
    ]
    ff_rows = feeds[0].shape[0]
    blocks = [jax.ShapeDtypeStruct((3, 4, ff_rows, n), BF) for n in (first, second)]
    spec = pl.BlockSpec(memory_space=pltpu.VMEM)
    far = pl.BlockSpec(memory_space=pl.ANY)
    return pl.pallas_call(
        functools.partial(front_kernel, plans, sizes),
        out_shape=shapes + blocks,
        in_specs=[spec] * 9,
        out_specs=[spec] * 4 + [far, spec],
        scratch_shapes=[
            pltpu.VMEM(halves.shape, BF),
            pltpu.VMEM(out.shape, BF),
            pltpu.VMEM(blocks[0].shape, BF),
            pltpu.SemaphoreType.DMA((total,)),
            pltpu.SemaphoreType.DMA((total,)),
            pltpu.SemaphoreType.DMA((len(plans),)),
        ]
        + swap_scratch(blocks[:1]),
        compiler_params=pltpu.CompilerParams(
            collective_id=collective_id, has_side_effects=True, vmem_limit_bytes=VMEM_LIMIT
        ),
        cost_estimate=pl.CostEstimate(flops=0, bytes_accessed=100 * 2**20, transcendentals=0),
    )(*weights, hidden, small, *feeds)


def offset_keys(axes, sizes):
    keys = [{}]
    for a in axes:
        keys = [dict(k, **{a: d}) for k in keys for d in list(range(1, sizes[a])) + [0]]
    return keys


def scatter_kernel(plans, sizes, *refs, between=None, swaps=(), delays=None):
    count = max(p[0] for p in plans) + 1
    xs, outs = refs[:count], refs[count : 2 * count]
    at = 2 * count
    bufs = []
    for _, _, _, phases, swap in plans:
        n = len(phases)
        bufs.append((refs[at : at + n], refs[at + n : at + 2 * n]))
        at += 2 * n
    send_sems, recv_sems, local_sems = refs[at:]
    used = {
        a: (sizes[a] if any(a in p[3] or (p[4] and a == "head") for p in plans) else 1)
        for a in AXES
    }
    greet(live(AXES, used), sizes, bool(swaps))
    sem = 0
    sends = []
    arrivals = [dict() for _ in plans]

    def number(offsets, axes):
        value = 0
        for a in axes:
            value = value * sizes[a] + offsets.get(a, 0)
        return value

    def block_of(j, offsets):
        i, rows, layout, phases, swap = plans[j]
        block = xs[i].at[place_of(offsets, layout, sizes)]
        return block if rows is None else block.at[pl.ds(*rows)]

    def total_of(j, offsets, phase):
        phases = plans[j][3]
        total = block_of(j, offsets)[...].astype(F32)
        for q in range(phase):
            rest = phases[q + 1 :]
            for d in range(1, sizes[phases[q]]):
                s = arrivals[j].pop((q, d, number(offsets, rest)))
                buf = bufs[j][1][q].at[d - 1, number(offsets, rest)]
                remote(buf, buf, send_sems.at[s], recv_sems.at[s], phases[q], 0, sizes).wait_recv()
                total = total + buf[...].astype(F32)
        return total

    delays = delays or [0] * len(plans)
    depth = max(len(p[3]) + delay for p, delay in zip(plans, delays))
    for step in range(depth):
        for j, (i, rows, layout, phases, swap) in enumerate(plans):
            phase = step - delays[j]
            if phase < 0 or phase >= len(phases):
                continue
            a, rest = phases[phase], phases[phase + 1 :]
            for d in range(1, sizes[a]):
                for key in offset_keys(rest, sizes):
                    offsets = dict(key)
                    offsets[a] = d
                    where = number(key, rest)
                    if phase == 0:
                        src = block_of(j, offsets)
                    else:
                        src = bufs[j][0][phase].at[d - 1, where]
                        src[...] = total_of(j, offsets, phase).astype(src.dtype)
                    dst = bufs[j][1][phase].at[d - 1, where]
                    copy = remote(src, dst, send_sems.at[sem], recv_sems.at[sem], a, d, sizes)
                    copy.start()
                    sends.append(copy)
                    arrivals[j][(phase, d, where)] = sem
                    sem += 1
        if step == min(2, depth - 1):
            for item in swaps:
                item.start()
        if between is not None:
            between(step)
    late = []
    for j, (i, rows, layout, phases, swap) in enumerate(plans):
        total = total_of(j, {}, len(phases))
        if swap:
            hold, out = bufs[j][0][0], outs[i]
            hold[...] = total.astype(hold.dtype)
            me = lax.axis_index("head")
            copy = pltpu.make_async_copy(hold.at[me], out.at[me], local_sems.at[j])
            copy.start()
            late.append((copy, None))
            for d in range(1, sizes["head"]):
                to = lax.rem(me + d, sizes["head"])
                copy = remote(
                    hold.at[to], out.at[me], send_sems.at[sem], recv_sems.at[sem], "head", d, sizes
                )
                copy.start()
                sends.append(copy)
                late.append((out.at[lax.rem(me + sizes["head"] - d, sizes["head"])], sem))
                sem += 1
        elif rows is None:
            outs[i][...] = total.astype(outs[i].dtype)
        else:
            outs[i][pl.ds(*rows)] = total.astype(outs[i].dtype)
    for item, s in late:
        if s is None:
            item.wait()
        else:
            remote(item, item, send_sems.at[s], recv_sems.at[s], "head", 0, sizes).wait_recv()
    for item in swaps:
        item.wait()
    for copy in sends:
        copy.wait_send()


def scatter_scratch(arrays, plans, out_types, sizes):
    scratch, total = [], 0
    for i, rows, layout, phases, swap in plans:
        x, kind = arrays[i], out_types[i]
        block = x.shape[1:] if rows is None else (rows[1],) + x.shape[2:]
        send_bufs, recv_bufs = [], []
        for p, a in enumerate(phases):
            rest = int(np.prod([sizes[b] for b in phases[p + 1 :]], dtype=int))
            shape = (sizes[a] - 1, rest) + block
            recv_bufs.append(pltpu.VMEM(shape, x.dtype))
            if p == 0:
                send_bufs.append(pltpu.VMEM(block if swap else (8, LANES), kind if swap else F32))
            else:
                send_bufs.append(pltpu.VMEM(shape, x.dtype))
            total += (sizes[a] - 1) * rest
        scratch += send_bufs + recv_bufs
        if swap:
            total += sizes["head"] - 1
    return scratch + [
        pltpu.SemaphoreType.DMA((total,)),
        pltpu.SemaphoreType.DMA((total,)),
        pltpu.SemaphoreType.DMA((len(plans),)),
    ]


def alive(plans, sizes):
    return [
        (i, rows, live(layout, sizes), live(phases, sizes), flag)
        for i, rows, layout, phases, flag in plans
    ]


def scatter_and_swap_kernel(plans, sizes, arrays, carried, swap_count, delays, *refs):
    xs, refs = refs[:arrays], refs[arrays:]
    swap_xs, refs = refs[:swap_count], refs[swap_count + carried :]
    outs, refs = refs[:arrays], refs[arrays:]
    swap_outs, refs = refs[:swap_count], refs[swap_count + carried :]
    held = 3 if swap_count else 0
    swaps = swaps_of(swap_xs, swap_outs, refs[len(refs) - held :])
    rest = refs[: len(refs) - held]
    scatter_kernel(plans, sizes, *xs, *outs, *rest, swaps=swaps, delays=delays)


def scatter(arrays, plans, out_types, sizes, collective_id, swaps=(), carried=(), delays=None):
    plans = alive(plans, sizes)
    shapes = [jax.ShapeDtypeStruct(x.shape[1:], kind) for x, kind in zip(arrays, out_types)]
    spec = pl.BlockSpec(memory_space=pltpu.VMEM)
    far = pl.BlockSpec(memory_space=pl.ANY)
    specs = [spec] * len(arrays) + [far] * (len(swaps) + len(carried))
    moved = sum(int(np.prod(x.shape)) * x.dtype.itemsize for x in arrays)
    return pl.pallas_call(
        functools.partial(
            scatter_and_swap_kernel, plans, sizes, len(arrays), len(carried), len(swaps), delays
        ),
        out_shape=shapes + [jax.ShapeDtypeStruct(x.shape, x.dtype) for x in (*swaps, *carried)],
        in_specs=specs,
        out_specs=specs,
        input_output_aliases={
            len(arrays) + len(swaps) + i: len(arrays) + len(swaps) + i for i in range(len(carried))
        },
        scratch_shapes=scatter_scratch(arrays, plans, out_types, sizes) + swap_scratch(swaps),
        compiler_params=pltpu.CompilerParams(
            collective_id=collective_id, has_side_effects=True, vmem_limit_bytes=VMEM_LIMIT
        ),
        cost_estimate=pl.CostEstimate(flops=0, bytes_accessed=20 * moved, transcendentals=0),
    )(*arrays, *swaps, *carried)


def finish_kernel(count, *refs):
    xs, refs = refs[:count], refs[count + 1 :]
    outs, got, sems = refs[:3], refs[3 : 3 + count], refs[3 + count :]
    items = swaps_of(xs, got, sems)
    greet(("y", "c"), {"y": 2, "c": 2}, True)
    for item in items:
        item.start()
    width = outs[0].shape[1]
    lanes = sum(x.shape[-1] for x in xs)
    start = 0
    for item, part in zip(items, got):
        item.wait()
        n = part.shape[-1]
        for m, out in enumerate(outs):
            for i in range(part.shape[1]):
                low = i * lanes + start
                high = min(low + n, width)
                if high > low:
                    out[:, low:high] = part[m, i, :, : high - low].astype(F32)
        start += n


def finish(xs, width, last, collective_id):
    far = pl.BlockSpec(memory_space=pl.ANY)
    spec = pl.BlockSpec(memory_space=pltpu.VMEM)
    n = len(xs)
    return pl.pallas_call(
        functools.partial(finish_kernel, n),
        out_shape=[jax.ShapeDtypeStruct((xs[0].shape[2], width), F32)] * 3,
        in_specs=[far] * (n + 1),
        out_specs=[spec] * 3,
        scratch_shapes=[pltpu.VMEM(x.shape, x.dtype) for x in xs] + swap_scratch(xs),
        compiler_params=pltpu.CompilerParams(
            collective_id=collective_id, has_side_effects=True, vmem_limit_bytes=VMEM_LIMIT
        ),
    )(*xs, last)


def feed_kernel(chunks, added, t_ref, c_ref, w_ref, *refs):
    act_ref, dgate_ref, dup_ref, branch_ref, dtok_ref = refs[-5:]
    before = refs[:added]
    tokens, cot = t_ref[...], c_ref[...]
    places, _, rows, width = w_ref.shape
    per = max(1, LANES * 3 // rows)

    def products(j):
        low, n = chunks[j]

        def weight(m):
            return w_ref[:, m, :, low : low + n].reshape(D, n)

        return dot_nn(tokens, weight(1)), dot_nn(tokens, weight(2)), dot_nn(cot, weight(0))

    ready = [products(0)]
    for j, (low, n) in enumerate(chunks):
        gate, up, dact = ready[j]
        if j + 1 < len(chunks):
            ready.append(products(j + 1))
        sig = 1.0 / (1.0 + jnp.exp(-gate))
        silu = gate * sig
        act_ref[:, low : low + n] = (silu * up).astype(BF)
        dgate_ref[:, low : low + n] = (dact * up * (sig + silu * (1.0 - sig))).astype(BF)
        dup_ref[:, low : low + n] = (dact * silu).astype(BF)
    for z in range(0, places, per):
        cols = slice(z * rows, (z + per) * rows)

        def weight(m):
            return w_ref[z : z + per, m].reshape(per * rows, width)

        dtok = dot_nt(dgate_ref[...], weight(1)) + dot_nt(dup_ref[...], weight(2))
        branch = dot_nt(act_ref[...], weight(0))
        if before:
            branch = branch + before[0][:, cols].astype(F32)
            dtok = dtok + before[1][:, cols].astype(F32)
        dtok_ref[:, cols] = dtok.astype(BF)
        branch_ref[:, cols] = branch.astype(BF)


def feed(tokens, cot, weights, before=(), after=()):
    n, width, tile = tokens.shape[0], weights.shape[-1], 256
    chunks = [(i, min(256, width - i)) for i in range(0, width, 256)]
    wide = pl.BlockSpec((tile, D), lambda i: (i, 0))
    inner = pl.BlockSpec((tile, width), lambda i: (i, 0))
    return pl.pallas_call(
        functools.partial(feed_kernel, chunks, len(before)),
        grid=(n // tile,),
        in_specs=[wide, wide, pl.BlockSpec(memory_space=pltpu.VMEM)]
        + [wide] * len(before)
        + [pl.BlockSpec(memory_space=pl.ANY)] * len(after),
        out_specs=[inner, inner, inner, wide, wide],
        out_shape=[jax.ShapeDtypeStruct((n, k), BF) for k in (width, width, width, D, D)],
        compiler_params=pltpu.CompilerParams(vmem_limit_bytes=VMEM_LIMIT),
        cost_estimate=pl.CostEstimate(
            flops=12 * n * D * width, bytes_accessed=40 * 2**20, transcendentals=n * width
        ),
    )(tokens, cot, weights, *before, *after)


def plain_grads_kernel(t_ref, c_ref, act_ref, dgate_ref, dup_ref, grad_ref):
    per, _, rows, width = grad_ref.shape
    for m, (left, right) in enumerate(((c_ref, act_ref), (t_ref, dgate_ref), (t_ref, dup_ref))):
        made = dot_tn(left[...], right[...]).astype(BF)
        grad_ref[:, m] = made.reshape(per, rows, width)


def plain_grads(tokens, cot, act, dgate, dup, places):
    n, width = act.shape
    rows = D // places
    per = max(1, LANES * 3 // rows)
    left = pl.BlockSpec((n, per * rows), lambda k: (0, k))
    right = pl.BlockSpec(memory_space=pltpu.VMEM)
    return pl.pallas_call(
        plain_grads_kernel,
        grid=(places // per,),
        in_specs=[left, left, right, right, right],
        out_specs=pl.BlockSpec((per, 3, rows, width), lambda k: (k, 0, 0, 0)),
        out_shape=jax.ShapeDtypeStruct((places, 3, rows, width), BF),
        compiler_params=pltpu.CompilerParams(vmem_limit_bytes=VMEM_LIMIT),
        cost_estimate=pl.CostEstimate(
            flops=6 * n * D * width, bytes_accessed=40 * 2**20, transcendentals=0
        ),
    )(tokens, cot, act, dgate, dup)


def grads_kernel(plans, sizes, dtok_ref, t_hbm, c_hbm, act_hbm, dgate_hbm, dup_hbm, *refs):
    sum_ref, grad_hbm, left_s, right_s, made_s, load_sems, made_sems = refs[:7]
    per, rows = made_s.shape[1:3]
    cols = per * rows
    loads = [
        pltpu.make_async_copy(c_hbm, left_s.at[0], load_sems.at[0]),
        pltpu.make_async_copy(act_hbm, right_s.at[0], load_sems.at[1]),
        pltpu.make_async_copy(t_hbm, left_s.at[1], load_sems.at[2]),
        pltpu.make_async_copy(dgate_hbm, right_s.at[1], load_sems.at[3]),
        pltpu.make_async_copy(dup_hbm, right_s.at[0], load_sems.at[4]),
    ]
    for copy in loads[:4]:
        copy.start()

    def stored(m, k, slot):
        return pltpu.make_async_copy(
            made_s.at[slot], grad_hbm.at[pl.ds(k * per, per), m], made_sems.at[slot]
        )

    def some(m, low, high, left, right, fresh):
        def one(k, carry):
            slot = lax.rem(k, 2)
            if fresh:
                pl.when(k >= 2)(lambda: stored(m, k, slot).wait())
            else:
                stored(m, k, slot).wait()
            part = left_s[left, :, pl.ds(pl.multiple_of(k * cols, LANES), cols)]
            made_s[slot] = dot_tn(part, right_s[right]).astype(BF).reshape(made_s.shape[1:])
            stored(m, k, slot).start()
            return carry

        lax.fori_loop(low, high, one, 0)

    chunks = D // cols

    def between(phase):
        if phase == 0:
            loads[0].wait()
            loads[1].wait()
            some(0, 0, chunks // 2, 0, 0, True)
        elif phase == 1:
            some(0, chunks // 2, chunks, 0, 0, False)
            loads[4].start()
            loads[2].wait()
            loads[3].wait()
            some(1, 0, chunks, 1, 1, False)
        else:
            loads[4].wait()
            some(2, 0, chunks, 1, 0, False)

    scatter_kernel(plans, sizes, dtok_ref, sum_ref, *refs[7:], between=between)
    for slot in range(2):
        stored(2, slot, slot).wait()


def feed_grads(dtok, tokens, cot, act, dgate, dup, places, plans, sizes, collective_id):
    plans = alive(plans, sizes)
    n, width = act.shape
    rows = D // places
    per = max(1, LANES * 3 // rows)
    spec = pl.BlockSpec(memory_space=pltpu.VMEM)
    far = pl.BlockSpec(memory_space=pl.ANY)
    return pl.pallas_call(
        functools.partial(grads_kernel, plans, sizes),
        out_shape=[
            jax.ShapeDtypeStruct(dtok.shape[1:], F32),
            jax.ShapeDtypeStruct((places, 3, rows, width), BF),
        ],
        in_specs=[spec] + [far] * 5,
        out_specs=[spec, far],
        scratch_shapes=[
            pltpu.VMEM((2, n, D), BF),
            pltpu.VMEM((2, n, width), BF),
            pltpu.VMEM((2, per, rows, width), BF),
            pltpu.SemaphoreType.DMA((5,)),
            pltpu.SemaphoreType.DMA((2,)),
        ]
        + scatter_scratch([dtok], plans, [F32], sizes),
        compiler_params=pltpu.CompilerParams(
            collective_id=collective_id, has_side_effects=True, vmem_limit_bytes=VMEM_LIMIT
        ),
        cost_estimate=pl.CostEstimate(
            flops=6 * n * D * width, bytes_accessed=100 * 2**20, transcendentals=0
        ),
    )(dtok, tokens, cot, act, dgate, dup)


def forward_kernel(heads, slots, tops, q_ref, kv_ref, o_ref, lse_ref, top_s, sum_s, acc_s):
    def score(keys, a, h):
        return dot_nt(keys, q_ref[a * BLOCK : (a + 1) * BLOCK, h * HEAD_DIM : (h + 1) * HEAD_DIM])

    for a in range(2):
        top_s[...] = jnp.full(top_s.shape, -1e30, F32)
        sum_s[...] = jnp.zeros(sum_s.shape, F32)
        acc_s[...] = jnp.zeros(acc_s.shape, F32)
        count = tops[a] + 1

        def step(keys, values_t):
            ahead = min(3, heads)
            ready = [score(keys, a, h) for h in range(ahead)]
            for h in range(heads):
                s = ready[h]
                if h + ahead < heads:
                    ready.append(score(keys, a, h + ahead))
                old = top_s[h : h + 1, :]
                new = jnp.maximum(old, jnp.max(s, axis=0, keepdims=True))
                p = jnp.exp2((s - new) * SCALE2)
                fade = jnp.exp2((old - new) * SCALE2)
                sum_s[h : h + 1, :] = sum_s[h : h + 1, :] * fade + jnp.sum(p, axis=0, keepdims=True)
                top_s[h : h + 1, :] = new
                acc_s[h] = acc_s[h] * fade + dot_nn(values_t, p.astype(BF))

        def two(i, carry):
            first, second = slots[2 * i], slots[2 * i + 1]
            both = jnp.concatenate([kv_ref[first], kv_ref[second]], axis=0)
            step(both[:, :HEAD_DIM], both[:, HEAD_DIM:].T)
            return carry

        lax.fori_loop(0, count // 2, two, 0)

        @pl.when(count % 2 == 1)
        def _():
            last = kv_ref[slots[count - 1]]
            step(last[:, :HEAD_DIM], last[:, HEAD_DIM:].T)

        for h in range(heads):
            total = sum_s[h : h + 1, :]
            o_ref[a * BLOCK : (a + 1) * BLOCK, h * HEAD_DIM : (h + 1) * HEAD_DIM] = (
                acc_s[h] / total
            ).T
            lse_ref[a, h : h + 1, :] = top_s[h : h + 1, :] * SCALE2 + jnp.log2(total)
        lse_ref[a, heads:8, :] = jnp.zeros((8 - heads, BLOCK), F32)


def attend(slots, tops, q, kv):
    heads = q.shape[1] // HEAD_DIM
    spec = pl.BlockSpec(memory_space=pltpu.VMEM)
    pairs = 33 * BLOCK * BLOCK * heads
    return pl.pallas_call(
        functools.partial(forward_kernel, heads),
        grid_spec=pltpu.PrefetchScalarGridSpec(
            num_scalar_prefetch=2,
            grid=(1,),
            in_specs=[spec] * 2,
            out_specs=[spec] * 2,
            scratch_shapes=[
                pltpu.VMEM((8, BLOCK), F32),
                pltpu.VMEM((8, BLOCK), F32),
                pltpu.VMEM((heads, HEAD_DIM, BLOCK), F32),
            ],
        ),
        out_shape=(
            jax.ShapeDtypeStruct(q.shape, F32),
            jax.ShapeDtypeStruct((2, 8, BLOCK), F32),
        ),
        compiler_params=pltpu.CompilerParams(vmem_limit_bytes=VMEM_LIMIT),
        cost_estimate=pl.CostEstimate(
            flops=pairs * 4 * HEAD_DIM, bytes_accessed=80 * 2**20, transcendentals=pairs
        ),
    )(slots, tops, q, kv)


def backward_kernel(
    heads,
    slots,
    tops,
    q_ref,
    kv_ref,
    do_ref,
    lse_ref,
    o_ref,
    dq_ref,
    dkv_ref,
    dq_s,
    dkv_s,
    delta_s,
):
    dkv_s[...] = jnp.zeros(dkv_s.shape, F32)
    for a in range(2):
        dq_s[...] = jnp.zeros(dq_s.shape, F32)

        def part(ref, h):
            return ref[a * BLOCK : (a + 1) * BLOCK, h * HEAD_DIM : (h + 1) * HEAD_DIM]

        for h in range(heads):
            product = part(do_ref, h).astype(F32) * part(o_ref, h)
            delta_s[h : h + 1, :] = jnp.sum(product.T, axis=0, keepdims=True)

        def one(n, carry):
            slot = slots[n]
            keys, values = kv_ref[slot, :, :HEAD_DIM], kv_ref[slot, :, HEAD_DIM:]
            keys_t = keys.T

            def products(h):
                return dot_nt(keys, part(q_ref, h)), dot_nt(values, part(do_ref, h))

            dk = jnp.zeros((BLOCK, HEAD_DIM), F32)
            dv = jnp.zeros((BLOCK, HEAD_DIM), F32)
            ahead = min(2, heads)
            ready = [products(h) for h in range(ahead)]
            for h in range(heads):
                s, dp = ready[h]
                if h + ahead < heads:
                    ready.append(products(h + ahead))
                p = jnp.exp2(s * SCALE2 - lse_ref[a, h : h + 1, :])
                dv = dv + dot_nn(p.astype(BF), part(do_ref, h))
                ds = (p * (dp - delta_s[h : h + 1, :])).astype(BF)
                dk = dk + dot_nn(ds, part(q_ref, h))
                dq_s[h] = dq_s[h] + dot_nn(keys_t, ds)
            dkv_s[slot, :, :HEAD_DIM] = dkv_s[slot, :, :HEAD_DIM] + dk
            dkv_s[slot, :, HEAD_DIM:] = dkv_s[slot, :, HEAD_DIM:] + dv
            return carry

        lax.fori_loop(0, tops[a] + 1, one, 0)
        for h in range(heads):
            dq_ref[a * BLOCK : (a + 1) * BLOCK, h * HEAD_DIM : (h + 1) * HEAD_DIM] = (
                (dq_s[h] * SCALE).T
            ).astype(BF)
    dkv_ref[:, :, :HEAD_DIM] = (dkv_s[:, :, :HEAD_DIM] * SCALE).astype(BF)
    dkv_ref[:, :, HEAD_DIM:] = dkv_s[:, :, HEAD_DIM:].astype(BF)


def attend_back(slots, tops, q, kv, do, lse, attended):
    heads = q.shape[1] // HEAD_DIM
    spec = pl.BlockSpec(memory_space=pltpu.VMEM)
    pairs = 33 * BLOCK * BLOCK * heads
    return pl.pallas_call(
        functools.partial(backward_kernel, heads),
        grid_spec=pltpu.PrefetchScalarGridSpec(
            num_scalar_prefetch=2,
            grid=(1,),
            in_specs=[spec] * 5,
            out_specs=[spec] * 2,
            scratch_shapes=[
                pltpu.VMEM((heads, HEAD_DIM, BLOCK), F32),
                pltpu.VMEM(kv.shape, F32),
                pltpu.VMEM((8, BLOCK), F32),
            ],
        ),
        out_shape=(
            jax.ShapeDtypeStruct(q.shape, BF),
            jax.ShapeDtypeStruct(kv.shape, BF),
        ),
        compiler_params=pltpu.CompilerParams(vmem_limit_bytes=VMEM_LIMIT),
        cost_estimate=pl.CostEstimate(
            flops=pairs * 10 * HEAD_DIM, bytes_accessed=120 * 2**20, transcendentals=pairs
        ),
    )(slots, tops, q, kv, do, lse, attended)


def inverse_rms(value):
    return lax.rsqrt(jnp.mean(value * value, axis=-1, keepdims=True) + EPS)


def turned(value, cosine, sine):
    return value * cosine + pltpu.roll(value, HEAD_DIM // 2, 1) * sine


def project_kernel(x_ref, w_ref, gain_ref, bias_ref, cos_ref, sin_ref, q_ref, kv_ref, normed_ref):
    x = x_ref[...].astype(F32)
    normed_ref[...] = (x * inverse_rms(x) * gain_ref[...]).astype(BF)
    cosine, sine = cos_ref[...], sin_ref[...]
    heads = q_ref.shape[1] // HEAD_DIM

    def product(low, n):
        cols = slice(low * HEAD_DIM, (low + n) * HEAD_DIM)
        return dot_nn(normed_ref[...], w_ref[:, cols]) + bias_ref[:, cols]

    for low in range(0, heads, 2):
        made = product(low, 2)
        for i in range(2):
            part = made[:, i * HEAD_DIM : (i + 1) * HEAD_DIM]
            q_ref[:, (low + i) * HEAD_DIM : (low + i + 1) * HEAD_DIM] = turned(
                part, cosine, sine
            ).astype(BF)
    made = product(heads, 2)
    kv_ref[:, :HEAD_DIM] = turned(made[:, :HEAD_DIM], cosine, sine).astype(BF)
    kv_ref[:, HEAD_DIM:] = made[:, HEAD_DIM:].astype(BF)


def project(x, w, gain, bias, cosine, sine):
    n, width = x.shape[0], w.shape[1]
    spec = pl.BlockSpec(memory_space=pltpu.VMEM)
    return pl.pallas_call(
        project_kernel,
        in_specs=[spec] * 6,
        out_specs=[spec] * 3,
        out_shape=[
            jax.ShapeDtypeStruct((n, k), BF)
            for k in (width - 2 * HEAD_DIM, 2 * HEAD_DIM, D)
        ],
        compiler_params=pltpu.CompilerParams(vmem_limit_bytes=VMEM_LIMIT),
        cost_estimate=pl.CostEstimate(
            flops=2 * n * D * width, bytes_accessed=12 * 2**20, transcendentals=0
        ),
    )(x, w, gain, bias, cosine, sine)


def project_back_kernel(
    dq_ref,
    dkv_ref,
    normed_ref,
    x_ref,
    w_ref,
    cos_ref,
    sin_ref,
    grad_ref,
    dnormed_ref,
    gain_grad_ref,
    bias_grad_ref,
    dpre_s,
):
    cosine, sine = cos_ref[...], -sin_ref[...]
    heads = dq_ref.shape[1] // HEAD_DIM
    for h in range(heads + 1):
        cols = slice(h * HEAD_DIM, (h + 1) * HEAD_DIM)
        part = dq_ref[:, cols] if h < heads else dkv_ref[:, :HEAD_DIM]
        dpre_s[:, cols] = turned(part.astype(F32), cosine, sine).astype(BF)
    dpre_s[:, (heads + 1) * HEAD_DIM :] = dkv_ref[:, HEAD_DIM:]
    bias_grad_ref[...] = jnp.sum(dpre_s[...].astype(F32), axis=0, keepdims=True)
    x = x_ref[...].astype(F32)
    scale = inverse_rms(x)
    step = 2 * HEAD_DIM
    for low in range(0, D, step):
        cols = slice(low, low + step)
        dnormed = dot_nt(dpre_s[...], w_ref[cols, :])
        dnormed_ref[:, cols] = dnormed.astype(BF)
        gain_grad_ref[:, cols] = jnp.sum(
            dnormed * (x[:, cols] * scale), axis=0, keepdims=True
        )
        if len(grad_ref.shape) == 2:
            grad_ref[cols, :] = dot_tn(normed_ref[:, cols], dpre_s[...]).astype(BF)
    if len(grad_ref.shape) == 4:
        blk, heads, rows, width = grad_ref.shape
        step = 3 * LANES
        for low in range(0, D, step):
            made = dot_tn(normed_ref[:, low : low + step], dpre_s[...]).astype(BF)
            half, start = divmod(low // rows, blk)
            grad_ref[start : start + step // rows, half] = made.reshape(step // rows, rows, width)


def project_back(dq, dkv, normed, x, w, cosine, sine, blk, rows):
    n, width = x.shape[0], w.shape[1]
    split = rows % 16 == 0
    made = (blk, 2, rows, width) if split else (D, width)
    spec = pl.BlockSpec(memory_space=pltpu.VMEM)
    return pl.pallas_call(
        project_back_kernel,
        in_specs=[spec] * 7,
        out_specs=[spec] * 4,
        out_shape=[
            jax.ShapeDtypeStruct(made, BF),
            jax.ShapeDtypeStruct((n, D), BF),
            jax.ShapeDtypeStruct((1, D), F32),
            jax.ShapeDtypeStruct((1, width), F32),
        ],
        scratch_shapes=[pltpu.VMEM((n, width), BF)],
        compiler_params=pltpu.CompilerParams(vmem_limit_bytes=VMEM_LIMIT),
        cost_estimate=pl.CostEstimate(
            flops=4 * n * D * width, bytes_accessed=16 * 2**20, transcendentals=0
        ),
    )(dq, dkv, normed, x, w, cosine, sine)


def last_kernel(plans, sizes, delays, *refs):
    xs, refs = refs[:4], refs[4:]
    dmixed_ref, x_ref, mixed_ref, gain_ref, _ = refs[:5]
    q_ref, k_ref, v_ref, small_ref, out_ref, hidden_ref = refs[5:11]
    w_s, dnormed_s, branch_s = refs[11:14]
    outs = (w_s, small_ref, dnormed_s, branch_s)
    scatter_kernel(plans, sizes, *xs, *outs, *refs[14:], delays=delays)
    heads = w_s.shape[0]
    q_cols = q_ref.shape[1] // heads
    for i in range(heads):
        cols = slice(i * HEAD_DIM, (i + 1) * HEAD_DIM)
        q_ref[:, i * q_cols : (i + 1) * q_cols] = w_s[i, :, :q_cols]
        k_ref[:, cols] = w_s[i, :, q_cols : q_cols + HEAD_DIM]
        v_ref[:, cols] = w_s[i, :, q_cols + HEAD_DIM :]
    out_ref[...] = (mixed_ref[...] + branch_s[...]).astype(BF)
    x = x_ref[...].astype(F32)
    scale = inverse_rms(x)
    z = x * scale
    u = gain_ref[...] * dnormed_s[...]
    hidden_ref[...] = (
        dmixed_ref[...] + scale * (u - z * jnp.mean(z * u, axis=-1, keepdims=True))
    ).astype(BF)


def last_sums(arrays, plans, delays, dmixed, x, mixed, gain, after, sizes, collective_id):
    plans = alive(plans, sizes)
    kinds = [F32] * 4
    spec = pl.BlockSpec(memory_space=pltpu.VMEM)
    heads, rows, width = arrays[0].shape[1:]
    q_cols = heads * (width - 2 * HEAD_DIM)
    tok = x.shape[0]
    shapes = [
        ((rows, q_cols), F32),
        ((rows, heads * HEAD_DIM), F32),
        ((rows, heads * HEAD_DIM), F32),
        (arrays[1].shape[1:], F32),
        ((tok, D), BF),
        ((tok, D), BF),
    ]
    return pl.pallas_call(
        functools.partial(last_kernel, plans, sizes, delays),
        out_shape=[jax.ShapeDtypeStruct(*s) for s in shapes],
        in_specs=[spec] * 8 + [pl.BlockSpec(memory_space=pl.ANY)],
        out_specs=[spec] * 6,
        scratch_shapes=[
            pltpu.VMEM((heads, rows, width), F32),
            pltpu.VMEM((tok, D), F32),
            pltpu.VMEM((tok, D), F32),
        ]
        + scatter_scratch(arrays, plans, kinds, sizes),
        compiler_params=pltpu.CompilerParams(
            collective_id=collective_id, has_side_effects=True, vmem_limit_bytes=VMEM_LIMIT
        ),
        cost_estimate=pl.CostEstimate(
            flops=0, bytes_accessed=200 * 2**20, transcendentals=0
        ),
    )(*arrays, dmixed, x, mixed, gain, after)


def small_rows(*rows):
    return jnp.stack(
        [jnp.pad(r.astype(F32), ((0, LANES - r.shape[0]),)) for r in rows]
        + [jnp.zeros((LANES,), F32)] * (8 - len(rows))
    )


def shards(
    sizes,
    hidden,
    cotangent,
    block_order,
    norm1,
    q_weight,
    q_bias,
    k_weight,
    k_bias,
    v_weight,
    v_bias,
    o_weight,
    norm2,
    gate_weight,
    up_weight,
    down_weight,
):
    tok = hidden.shape[0]
    pair = sizes["head"] * tok
    blk = int(np.prod([sizes[a] for a in BLK]))
    seqs = blk // SEQ_SPAN
    place_axes = {1: BLK, 2: BLK[:3], 4: BLK[:2]}[seqs]
    seq_axes = BLK[len(place_axes) :]
    head = lax.axis_index("head")
    place = place_of({}, place_axes, sizes)
    seq = place_of({}, seq_axes, sizes) if seq_axes else 0
    order = lax.dynamic_index_in_dim(block_order, seq, 0, keepdims=False)
    tops = lax.dynamic_slice_in_dim(order, place * 2, 2)
    slots = jnp.argsort(order).astype(jnp.int32)
    positions = (tops[:, None] * tok + jnp.arange(tok, dtype=jnp.int32)[None, :]).reshape(pair)
    frequency = THETA ** (-(jnp.arange(HEAD_DIM // 2, dtype=F32) * 2.0) / HEAD_DIM)
    angles = positions.astype(F32)[:, None] * frequency[None, :]
    cosine, sine = jnp.cos(angles), jnp.sin(angles)
    cosine = jnp.concatenate([cosine, cosine], axis=1)
    sine = jnp.concatenate([-sine, sine], axis=1)

    q_cols = D // 2
    kv_cols = HEAD_DIM
    rows = q_weight.shape[0]
    small = small_rows(
        *[v.astype(BF) for v in (norm1, norm2, q_bias, k_bias, v_bias)]
    )
    parts = sizes["y"] * sizes["c"]
    width = gate_weight.shape[1]
    lanes = -(-width // (LANES * parts)) * LANES
    first = lanes * 6 // 9 // LANES * LANES
    ff_rows = gate_weight.shape[0]

    def along_z(part):
        part = part.reshape(1, 3, parts * ff_rows, part.shape[-1])
        return lax.all_gather(part, live(("g", "z"), sizes), axis=0, tiled=True)

    w_qkv, x_pair, small_all, w_out, mine_one, packed_two = front(
        (q_weight, k_weight, v_weight, o_weight),
        hidden,
        small,
        (down_weight, gate_weight, up_weight),
        first,
        lanes - first,
        [
            (0, None, AXES, AXES, True),
            (1, None, ("head",), ("head",), False),
            (2, None, AXES, AXES, False),
            (3, None, BLK, ("y", "z", "g", "c"), False),
        ],
        sizes,
        1,
    )
    w_feed_one = along_z(mine_one)
    w_out = w_out.reshape(q_cols, D)
    w_qkv = w_qkv.reshape(D, q_cols + 2 * kv_cols)
    x_pair = x_pair.reshape(pair, D)
    gain_one = small_all[:, 0, :rows].reshape(D)
    gain_two = small_all[:, 1, :rows].reshape(D)
    bias_q = lax.dynamic_slice_in_dim(small_all[:, 2, :rows].reshape(D), head * q_cols, q_cols)
    bias_k, bias_v = (
        lax.dynamic_slice_in_dim(
            small_all[:, i, : k_bias.shape[0]].reshape(2 * kv_cols), head * kv_cols, kv_cols
        )
        for i in (3, 4)
    )

    queries, kv_local, normed = project(
        x_pair,
        w_qkv,
        gain_one[None],
        jnp.concatenate([bias_q, bias_k, bias_v])[None],
        cosine,
        sine,
    )
    group = ("head", "y", "c")
    half = tok // 2
    crossed = [
        ((0, half), group, ("head", "y", "c"), False),
        ((half, half), group, ("y", "head", "c"), False),
    ]
    summed = [
        ((0, half), group, ("c", "head", "y"), False),
        ((half, half), group, ("c", "y", "head"), False),
    ]
    kv, cot_all, mine_two = gather(
        [kv_local, cotangent],
        [
            (0, None, place_axes, place_axes, False),
            (1, None, group, ("y", "head", "c"), False),
        ],
        sizes,
        2,
        [packed_two],
    )
    cot_all = cot_all.reshape(-1, D)
    kv = kv.reshape(2 * SEQ_SPAN, tok, 2 * HEAD_DIM)
    attended, lse = attend(slots, tops, queries, kv)
    w_feed_two = along_z((mine_two.astype(F32) + lse[0, 7, 0]).astype(BF))
    attn_local = attended.astype(BF)
    inputs = hidden.astype(F32)
    mixed_part = dot_nn(attn_local, w_out).reshape(2, tok, D)
    (mixed_got,) = gather(
        [mixed_part.astype(BF)], [(0, None, ("head",), ("head",), True)], sizes, 3
    )
    mixed = (
        inputs
        + lax.dynamic_index_in_dim(mixed_part, head, 0, keepdims=False)
        + lax.dynamic_index_in_dim(mixed_got, 1 - head, 0, keepdims=False).astype(F32)
    )
    scale_two = inverse_rms(mixed)
    normed_two = (mixed * scale_two * gain_two).astype(BF)
    (tokens,) = gather([normed_two], [(0,) + c for c in crossed], sizes, 4)
    tokens = tokens.reshape(-1, D)

    places = w_feed_one.shape[0]
    act, dgate, dup, branch, dtokens = feed(tokens, cot_all, w_feed_one)
    parts_one = plain_grads(tokens, cot_all, act, dgate, dup, places)
    act, dgate, dup, branch, dtokens = feed(
        tokens, cot_all, w_feed_two, (branch, dtokens), (parts_one,)
    )
    dnormed_two, parts_two = feed_grads(
        dtokens.reshape(-1, tok, D),
        tokens,
        cot_all,
        act,
        dgate,
        dup,
        places,
        [(0,) + c for c in summed],
        sizes,
        5,
    )
    def collect(grad):
        total = lax.psum_scatter(grad, live(("g", "z"), sizes), scatter_dimension=0, tiled=True)
        return total.reshape(3, parts, ff_rows, grad.shape[-1])

    back_one = collect(parts_one)

    z_two = mixed * scale_two
    u_two = gain_two * dnormed_two
    norm2_part = jnp.sum(dnormed_two * z_two, axis=0)
    dmixed = cotangent.astype(F32) + scale_two * (
        u_two - z_two * jnp.mean(z_two * u_two, axis=-1, keepdims=True)
    )
    dproj = dmixed.astype(BF)
    (dproj_pair,) = gather([dproj], [(0, None, ("head",), ("head",), False)], sizes, 6)
    dproj_pair = dproj_pair.reshape(pair, D)
    dout = dot_nt(dproj_pair, w_out).astype(BF)
    o_part = dot_tn(attn_local, dproj_pair).astype(BF)

    dq, dkv_parts = attend_back(slots, tops, queries, kv, dout, lse, attended)
    dkv, d_out_weight, parts_two = scatter(
        [dkv_parts.reshape(SEQ_SPAN, pair, 2 * HEAD_DIM), o_part.reshape(blk, -1, D)],
        [
            (0, None, place_axes, place_axes[::-1], False),
            (1, None, BLK, BLK[::-1], False),
        ],
        [BF, F32],
        sizes,
        7,
        [],
        [parts_two],
    )
    back_two = collect(parts_two)
    w_part, dnormed, norm1_part, bias_part = project_back(
        dq, dkv, normed, x_pair, w_qkv, cosine, sine, blk, rows
    )
    if w_part.ndim == 2:
        w_part = w_part.reshape(2, blk, rows, -1).transpose(1, 0, 2, 3)
    norm1_part, bias_part = norm1_part[0], bias_part[0]
    own = (jnp.arange(2) == head).astype(F32)[:, None]

    def owners(vector):
        return vector.reshape(2, blk, -1).transpose(1, 0, 2)

    def owned(vector):
        return owners((own * vector[None, :]).reshape(-1))

    small_grads = jnp.stack(
        [
            jnp.pad(part, ((0, 0), (0, 0), (0, LANES - part.shape[2])))
            for part in (
                owners(norm1_part),
                owners(norm2_part),
                owned(bias_part[:q_cols]),
                owned(bias_part[q_cols : q_cols + kv_cols]),
                owned(bias_part[q_cols + kv_cols :]),
            )
        ]
        + [jnp.zeros((blk, 2, LANES), F32)] * 3,
        axis=2,
    )
    small_grads = small_grads.transpose(1, 0, 2, 3).reshape(2 * blk, 8, LANES)
    d_query, d_key, d_value, small_sum, output, hidden_grad = last_sums(
        [
            w_part,
            small_grads,
            dnormed.reshape(2, tok, D),
            branch.reshape(-1, tok, D),
        ],
        [
            (0, None, BLK, BLK[::-1], True),
            (1, None, AXES, AXES[::-1], False),
            (2, None, ("head",), ("head",), False),
        ]
        + [(3,) + c for c in summed],
        [0, 0, 0, 0, 0],
        dmixed,
        hidden,
        mixed,
        gain_one[None],
        back_one,
        sizes,
        8,
    )
    d_down, d_gate, d_up = finish([back_one, back_two], width, d_query, 9)
    kn = k_bias.shape[0]
    return (
        output,
        hidden_grad,
        small_sum[0, :rows],
        d_query,
        small_sum[2, :rows],
        d_key,
        small_sum[3, :kn],
        d_value,
        small_sum[4, :kn],
        d_out_weight,
        small_sum[1, :rows],
        d_gate,
        d_up,
        d_down,
    )


def solution(mesh):
    heads, blk = mesh.devices.shape
    split = jax.sharding.Mesh(mesh.devices.reshape(heads, blk // 16, 4, 2, 2), AXES)
    sizes = dict(split.shape)
    rows = P(AXES, None)
    vector = P(AXES)
    feed = P(BLK, "head")
    return jax.shard_map(
        functools.partial(shards, sizes),
        mesh=split,
        in_specs=(
            rows,
            rows,
            P(),
            vector,
            rows,
            vector,
            rows,
            vector,
            rows,
            vector,
            rows,
            vector,
            feed,
            feed,
            feed,
        ),
        out_specs=(
            rows,
            rows,
            vector,
            rows,
            vector,
            rows,
            vector,
            rows,
            vector,
            rows,
            vector,
            feed,
            feed,
            feed,
        ),
        check_vma=False,
    )
```

```python
import functools

import jax
import jax.numpy as jnp
import numpy as np
from jax import lax
from jax.experimental import pallas as pl
from jax.experimental.pallas import tpu as pltpu
from jax.sharding import PartitionSpec as P

D = 1536
QHEADS = 12
KVHEADS = 2
HEAD_DIM = 128
SEQ_SPAN = 16
BLOCK = 256

EPS = 1e-06
THETA = 1000000.0
SCALE = HEAD_DIM**-0.5
LOG2E = 1.4426950408889634
SCALE2 = SCALE * LOG2E
BF = jnp.bfloat16
F32 = jnp.float32
MESH = pl.DeviceIdType.MESH
VMEM_LIMIT = 56 * 2**20
AXES = ("head", "g", "z", "y", "c")
BLK = ("g", "z", "y", "c")
LANES = 128


def dot_nn(a, b):
    return lax.dot_general(a, b, (((1,), (0,)), ((), ())), preferred_element_type=F32)


def dot_nt(a, b):
    return lax.dot_general(a, b, (((1,), (1,)), ((), ())), preferred_element_type=F32)


def dot_tn(a, b):
    return lax.dot_general(a, b, (((0,), (0,)), ((), ())), preferred_element_type=F32)


def live(axes, sizes):
    return tuple(a for a in axes if sizes[a] > 1)


def greet(axes, sizes, diagonal=False):
    barrier = pltpu.get_barrier_semaphore()
    count = 0
    if diagonal:
        pl.semaphore_signal(barrier, inc=1, device_id=across(3), device_id_type=MESH)
        count += 1
    for a in axes:
        me = lax.axis_index(a)
        for d in range(1, sizes[a]):
            pl.semaphore_signal(
                barrier,
                inc=1,
                device_id={a: lax.rem(me + d, sizes[a])},
                device_id_type=MESH,
            )
            count += 1
    pl.semaphore_wait(barrier, count)


def across(d):
    y, c = lax.axis_index("y"), lax.axis_index("c")
    return {"y": 1 - y if d & 2 else y, "c": 1 - c if d & 1 else c}


class Swap:
    def __init__(self, x, out, send_sems, recv_sems, local_sem):
        me = lax.axis_index("y") * 2 + lax.axis_index("c")
        self.kept = pltpu.make_async_copy(x.at[:, me], out.at[:, me], local_sem)
        self.copies = []
        for d in range(1, 4):
            to = across(d)
            self.copies.append(
                pltpu.make_async_remote_copy(
                    src_ref=x.at[:, to["y"] * 2 + to["c"]],
                    dst_ref=out.at[:, me],
                    send_sem=send_sems.at[d - 1],
                    recv_sem=recv_sems.at[d - 1],
                    device_id=to,
                    device_id_type=MESH,
                )
            )

    def start(self):
        for copy in self.copies:
            copy.start()
        self.kept.start()

    def wait(self):
        self.kept.wait()
        for copy in self.copies:
            copy.wait()


def swap_scratch(swaps):
    if not swaps:
        return []
    return [pltpu.SemaphoreType.DMA((3 * len(swaps),))] * 2 + [
        pltpu.SemaphoreType.DMA((len(swaps),))
    ]


def swaps_of(xs, outs, sems):
    return [
        Swap(
            x,
            out,
            sems[0].at[pl.ds(3 * i, 3)],
            sems[1].at[pl.ds(3 * i, 3)],
            sems[2].at[i],
        )
        for i, (x, out) in enumerate(zip(xs, outs))
    ]


def place_of(offsets, axes, sizes):
    value = 0
    for a in axes:
        me = lax.axis_index(a)
        off = offsets.get(a, 0)
        value = value * sizes[a] + (lax.rem(me + off, sizes[a]) if off else me)
    return value


def remote(src, dst, send, recv, axis, distance, sizes):
    to = lax.rem(lax.axis_index(axis) + distance, sizes[axis])
    return pltpu.make_async_remote_copy(
        src_ref=src,
        dst_ref=dst,
        send_sem=send,
        recv_sem=recv,
        device_id={axis: to},
        device_id_type=MESH,
    )


def gather_kernel(plans, sizes, swap_count, waited, carried, *refs, ahead=None):
    count = max(p[0] for p in plans) + 1
    xs, refs = refs[:count], refs[count:]
    swap_xs, refs = refs[:swap_count], refs[swap_count + waited :]
    outs, refs = refs[:count], refs[count:]
    swap_outs, refs = refs[:swap_count], refs[swap_count + carried :]
    send_sems, recv_sems, local_sems = refs[:3]
    swaps = swaps_of(swap_xs, swap_outs, refs[3:])
    used = {a: (sizes[a] if any(a in p[3] for p in plans) else 1) for a in AXES}
    if swaps:
        used.update(y=sizes["y"], c=sizes["c"])
    greet(live(AXES, used), sizes, bool(swaps))

    def cut(ref, rows):
        return ref if rows is None else ref.at[pl.ds(*rows)]

    def source(plan, place):
        i, rows, layout, phases, split = plan
        return cut(xs[i].at[place] if split else xs[i], rows)

    sends, kept, queue = [], [], []
    sem = 0
    for j, plan in enumerate(plans):
        i, rows, layout, phases, split = plan
        mine = source(plan, lax.axis_index(phases[0]))
        slot = cut(outs[i].at[place_of({}, layout, sizes)], rows)
        copy = pltpu.make_async_copy(mine, slot, local_sems.at[j])
        queue.append((plan, {}, -1, None))
        kept.append(copy)
    at = 0
    while at < len(queue):
        plan, offsets, phase, arrived = queue[at]
        at += 1
        i, rows, layout, phases, split = plan
        slot = cut(outs[i].at[place_of(offsets, layout, sizes)], rows)
        if arrived is None:
            src = source(plan, lax.axis_index(phases[0]))
        else:
            src = slot
            remote(
                slot, slot, send_sems.at[arrived], recv_sems.at[arrived], phases[0], 0, sizes
            ).wait_recv()
        for p in range(phase + 1, len(phases)):
            a = phases[p]
            for d in range(1, sizes[a]):
                piece = src
                if split and p == 0:
                    piece = source(plan, lax.rem(lax.axis_index(a) + d, sizes[a]))
                copy = remote(piece, slot, send_sems.at[sem], recv_sems.at[sem], a, d, sizes)
                copy.start()
                sends.append(copy)
                later = dict(offsets)
                later[a] = sizes[a] - d
                queue.append((plan, later, p, sem))
                sem += 1
        if at == len(plans):
            if ahead is not None:
                ahead()
            for copy in kept + swaps:
                copy.start()
    for copy in kept + swaps:
        copy.wait()
    for copy in sends:
        copy.wait_send()


def gather(arrays, plans, sizes, collective_id, swaps=(), after=(), carried=()):
    plans = [
        (i, rows, live(layout, sizes), live(phases, sizes), split)
        for i, rows, layout, phases, split in plans
    ]
    counts = [int(np.prod([sizes[a] for a in p[2]])) for p in plans]
    total = sum(counts) - len(counts)
    shapes = []
    for i, x in enumerate(arrays):
        n, split = next((c, p[4]) for c, p in zip(counts, plans) if p[0] == i)
        shapes.append(jax.ShapeDtypeStruct((n,) + (x.shape[1:] if split else x.shape), x.dtype))
    spec = pl.BlockSpec(memory_space=pltpu.VMEM)
    far = pl.BlockSpec(memory_space=pl.ANY)
    specs = [spec] * len(arrays) + [far] * len(swaps)
    moved = sum(int(np.prod(s.shape)) * s.dtype.itemsize for s in shapes)
    return pl.pallas_call(
        functools.partial(
            gather_kernel, plans, sizes, len(swaps), len(after) + len(carried), len(carried)
        ),
        out_shape=shapes + [jax.ShapeDtypeStruct(x.shape, x.dtype) for x in (*swaps, *carried)],
        in_specs=specs + [far] * (len(after) + len(carried)),
        out_specs=specs + [far] * len(carried),
        input_output_aliases={
            len(specs) + len(after) + i: len(specs) + i for i in range(len(carried))
        },
        scratch_shapes=[
            pltpu.SemaphoreType.DMA((total,)),
            pltpu.SemaphoreType.DMA((total,)),
            pltpu.SemaphoreType.DMA((len(plans),)),
        ]
        + swap_scratch(swaps),
        compiler_params=pltpu.CompilerParams(
            collective_id=collective_id, has_side_effects=True, vmem_limit_bytes=VMEM_LIMIT
        ),
        cost_estimate=pl.CostEstimate(flops=0, bytes_accessed=20 * moved, transcendentals=0),
    )(*arrays, *swaps, *after, *carried)


def front_kernel(plans, sizes, *refs):
    q_ref, k_ref, v_ref, o_ref, hidden_ref, small_ref = refs[:6]
    feeds, refs = refs[6:9], refs[9:]
    outs, first_ref, second_ref, refs = refs[:4], refs[4], refs[5], refs[6:]
    halves_s, o_s = refs[:2]
    heads = halves_s.shape[0]
    q_cols, kv_cols = q_ref.shape[1] // heads, k_ref.shape[1] // heads
    for i in range(heads):
        halves_s[i, :, :q_cols] = q_ref[:, i * q_cols : (i + 1) * q_cols].astype(BF)
        cols = slice(i * kv_cols, (i + 1) * kv_cols)
        halves_s[i, :, q_cols : q_cols + kv_cols] = k_ref[:, cols].astype(BF)
        halves_s[i, :, q_cols + kv_cols :] = v_ref[:, cols].astype(BF)
    o_s[...] = o_ref[...].astype(BF)

    def pack():
        first, second = first_ref.shape[-1], second_ref.shape[-1]
        for m, feed_ref in enumerate(feeds):
            rows, width = feed_ref.shape
            for i in range(first_ref.shape[1]):
                low = i * (first + second)
                for ref, n in ((first_ref, first), (second_ref, second)):
                    real = min(n, width - low)
                    ref[m, i, :, :real] = feed_ref[:, low : low + real].astype(BF)
                    if real < n:
                        ref[m, i, :, real:] = jnp.zeros((rows, n - real), BF)
                    low += n

    gather_kernel(
        plans,
        sizes,
        0,
        0,
        0,
        halves_s,
        hidden_ref,
        small_ref,
        o_s,
        *outs,
        *refs[2:],
        ahead=pack,
    )


def front(weights, hidden, small, feeds, first, second, plans, sizes, collective_id):
    plans = alive(plans, sizes)
    heads, rows = sizes["head"], weights[0].shape[0]
    halves = jax.ShapeDtypeStruct((heads, rows, sum(w.shape[1] for w in weights[:3]) // heads), BF)
    out = jax.ShapeDtypeStruct(weights[3].shape, BF)
    arrays = [halves, hidden, small, out]
    counts = [int(np.prod([sizes[a] for a in p[2]])) for p in plans]
    total = sum(counts) - len(counts)
    shapes = [
        jax.ShapeDtypeStruct((n,) + (x.shape[1:] if p[4] else x.shape), x.dtype)
        for n, x, p in zip(counts, arrays, plans)
    ]
    ff_rows = feeds[0].shape[0]
    blocks = [jax.ShapeDtypeStruct((3, 4, ff_rows, n), BF) for n in (first, second)]
    spec = pl.BlockSpec(memory_space=pltpu.VMEM)
    return pl.pallas_call(
        functools.partial(front_kernel, plans, sizes),
        out_shape=shapes + blocks,
        in_specs=[spec] * 9,
        out_specs=[spec] * 6,
        scratch_shapes=[
            pltpu.VMEM(halves.shape, BF),
            pltpu.VMEM(out.shape, BF),
            pltpu.SemaphoreType.DMA((total,)),
            pltpu.SemaphoreType.DMA((total,)),
            pltpu.SemaphoreType.DMA((len(plans),)),
        ],
        compiler_params=pltpu.CompilerParams(
            collective_id=collective_id, has_side_effects=True, vmem_limit_bytes=VMEM_LIMIT
        ),
        cost_estimate=pl.CostEstimate(flops=0, bytes_accessed=100 * 2**20, transcendentals=0),
    )(*weights, hidden, small, *feeds)


def offset_keys(axes, sizes):
    keys = [{}]
    for a in axes:
        keys = [dict(k, **{a: d}) for k in keys for d in list(range(1, sizes[a])) + [0]]
    return keys


def scatter_kernel(plans, sizes, *refs, between=None):
    count = max(p[0] for p in plans) + 1
    xs, outs = refs[:count], refs[count : 2 * count]
    at = 2 * count
    bufs = []
    for _, _, _, phases, swap in plans:
        n = len(phases)
        bufs.append((refs[at : at + n], refs[at + n : at + 2 * n]))
        at += 2 * n
    send_sems, recv_sems, local_sems = refs[at:]
    used = {
        a: (sizes[a] if any(a in p[3] or (p[4] and a == "head") for p in plans) else 1)
        for a in AXES
    }
    greet(live(AXES, used), sizes)
    sem = 0
    sends = []
    arrivals = [dict() for _ in plans]

    def number(offsets, axes):
        value = 0
        for a in axes:
            value = value * sizes[a] + offsets.get(a, 0)
        return value

    def block_of(j, offsets):
        i, rows, layout, phases, swap = plans[j]
        block = xs[i].at[place_of(offsets, layout, sizes)]
        return block if rows is None else block.at[pl.ds(*rows)]

    def total_of(j, offsets, phase):
        phases = plans[j][3]
        total = block_of(j, offsets)[...].astype(F32)
        for q in range(phase):
            rest = phases[q + 1 :]
            for d in range(1, sizes[phases[q]]):
                s = arrivals[j].pop((q, d, number(offsets, rest)))
                buf = bufs[j][1][q].at[d - 1, number(offsets, rest)]
                remote(buf, buf, send_sems.at[s], recv_sems.at[s], phases[q], 0, sizes).wait_recv()
                total = total + buf[...].astype(F32)
        return total

    depth = max(len(p[3]) for p in plans)
    for phase in range(depth):
        for j, (i, rows, layout, phases, swap) in enumerate(plans):
            if phase >= len(phases):
                continue
            a, rest = phases[phase], phases[phase + 1 :]
            for d in range(1, sizes[a]):
                for key in offset_keys(rest, sizes):
                    offsets = dict(key)
                    offsets[a] = d
                    where = number(key, rest)
                    if phase == 0:
                        src = block_of(j, offsets)
                    else:
                        src = bufs[j][0][phase].at[d - 1, where]
                        src[...] = total_of(j, offsets, phase).astype(src.dtype)
                    dst = bufs[j][1][phase].at[d - 1, where]
                    copy = remote(src, dst, send_sems.at[sem], recv_sems.at[sem], a, d, sizes)
                    copy.start()
                    sends.append(copy)
                    arrivals[j][(phase, d, where)] = sem
                    sem += 1
        if between is not None:
            between(phase)
    late = []
    for j, (i, rows, layout, phases, swap) in enumerate(plans):
        total = total_of(j, {}, len(phases))
        if swap:
            hold, out = bufs[j][0][0], outs[i]
            hold[...] = total.astype(hold.dtype)
            me = lax.axis_index("head")
            copy = pltpu.make_async_copy(hold.at[me], out.at[me], local_sems.at[j])
            copy.start()
            late.append((copy, None))
            for d in range(1, sizes["head"]):
                to = lax.rem(me + d, sizes["head"])
                copy = remote(
                    hold.at[to], out.at[me], send_sems.at[sem], recv_sems.at[sem], "head", d, sizes
                )
                copy.start()
                sends.append(copy)
                late.append((out.at[lax.rem(me + sizes["head"] - d, sizes["head"])], sem))
                sem += 1
        elif rows is None:
            outs[i][...] = total.astype(outs[i].dtype)
        else:
            outs[i][pl.ds(*rows)] = total.astype(outs[i].dtype)
    for item, s in late:
        if s is None:
            item.wait()
        else:
            remote(item, item, send_sems.at[s], recv_sems.at[s], "head", 0, sizes).wait_recv()
    for copy in sends:
        copy.wait_send()


def scatter_scratch(arrays, plans, out_types, sizes):
    scratch, total = [], 0
    for i, rows, layout, phases, swap in plans:
        x, kind = arrays[i], out_types[i]
        block = x.shape[1:] if rows is None else (rows[1],) + x.shape[2:]
        send_bufs, recv_bufs = [], []
        for p, a in enumerate(phases):
            rest = int(np.prod([sizes[b] for b in phases[p + 1 :]], dtype=int))
            shape = (sizes[a] - 1, rest) + block
            recv_bufs.append(pltpu.VMEM(shape, x.dtype))
            if p == 0:
                send_bufs.append(pltpu.VMEM(block if swap else (8, LANES), kind if swap else F32))
            else:
                send_bufs.append(pltpu.VMEM(shape, x.dtype))
            total += (sizes[a] - 1) * rest
        scratch += send_bufs + recv_bufs
        if swap:
            total += sizes["head"] - 1
    return scratch + [
        pltpu.SemaphoreType.DMA((total,)),
        pltpu.SemaphoreType.DMA((total,)),
        pltpu.SemaphoreType.DMA((len(plans),)),
    ]


def alive(plans, sizes):
    return [
        (i, rows, live(layout, sizes), live(phases, sizes), flag)
        for i, rows, layout, phases, flag in plans
    ]


def scatter_and_wait_kernel(plans, sizes, arrays, waited, carried, *refs):
    xs, refs = refs[:arrays], refs[arrays + waited :]
    scatter_kernel(plans, sizes, *xs, *refs[:arrays], *refs[arrays + carried :])


def scatter(arrays, plans, out_types, sizes, collective_id, after=(), carried=()):
    plans = alive(plans, sizes)
    shapes = [jax.ShapeDtypeStruct(x.shape[1:], kind) for x, kind in zip(arrays, out_types)]
    spec = pl.BlockSpec(memory_space=pltpu.VMEM)
    far = pl.BlockSpec(memory_space=pl.ANY)
    moved = sum(int(np.prod(x.shape)) * x.dtype.itemsize for x in arrays)
    return pl.pallas_call(
        functools.partial(
            scatter_and_wait_kernel,
            plans,
            sizes,
            len(arrays),
            len(after) + len(carried),
            len(carried),
        ),
        out_shape=shapes + [jax.ShapeDtypeStruct(x.shape, x.dtype) for x in carried],
        in_specs=[spec] * len(arrays) + [far] * (len(after) + len(carried)),
        out_specs=[spec] * len(arrays) + [far] * len(carried),
        input_output_aliases={
            len(arrays) + len(after) + i: len(arrays) + i for i in range(len(carried))
        },
        scratch_shapes=scatter_scratch(arrays, plans, out_types, sizes),
        compiler_params=pltpu.CompilerParams(
            collective_id=collective_id, has_side_effects=True, vmem_limit_bytes=VMEM_LIMIT
        ),
        cost_estimate=pl.CostEstimate(flops=0, bytes_accessed=20 * moved, transcendentals=0),
    )(*arrays, *after, *carried)


def swap_kernel(count, *refs):
    items = swaps_of(refs[:count], refs[count + 1 : 2 * count + 1], refs[2 * count + 1 :])
    greet(("y", "c"), {"y": 2, "c": 2}, True)
    for item in items:
        item.start()
    for item in items:
        item.wait()


def swap(xs, last, collective_id):
    far = pl.BlockSpec(memory_space=pl.ANY)
    n = len(xs)
    return pl.pallas_call(
        functools.partial(swap_kernel, n),
        out_shape=[jax.ShapeDtypeStruct(x.shape, x.dtype) for x in xs],
        in_specs=[far] * (n + 1),
        out_specs=[far] * n,
        scratch_shapes=swap_scratch(xs),
        compiler_params=pltpu.CompilerParams(
            collective_id=collective_id, has_side_effects=True, vmem_limit_bytes=VMEM_LIMIT
        ),
    )(*xs, last)


def outputs_kernel(*refs):
    w_ref, dnormed_ref, branch_ref, dmixed_ref, x_ref, mixed_ref, gain_ref = refs[:7]
    parts, refs = refs[7:9], refs[9:]
    q_ref, k_ref, v_ref, out_ref, hidden_ref = refs[:5]
    feeds = refs[5:]
    heads = w_ref.shape[0]
    q_cols = q_ref.shape[1] // heads
    for i in range(heads):
        cols = slice(i * HEAD_DIM, (i + 1) * HEAD_DIM)
        q_ref[:, i * q_cols : (i + 1) * q_cols] = w_ref[i, :, :q_cols]
        k_ref[:, cols] = w_ref[i, :, q_cols : q_cols + HEAD_DIM]
        v_ref[:, cols] = w_ref[i, :, q_cols + HEAD_DIM :]
    out_ref[...] = (mixed_ref[...] + branch_ref[...]).astype(BF)
    x = x_ref[...].astype(F32)
    scale = inverse_rms(x)
    z = x * scale
    u = gain_ref[...] * dnormed_ref[...]
    hidden_ref[...] = (
        dmixed_ref[...] + scale * (u - z * jnp.mean(z * u, axis=-1, keepdims=True))
    ).astype(BF)
    width = feeds[0].shape[1]
    lanes = sum(part.shape[-1] for part in parts)
    for m, feed_ref in enumerate(feeds):
        for i in range(parts[0].shape[1]):
            low = i * lanes
            for part in parts:
                n = part.shape[-1]
                real = min(n, width - low)
                if real > 0:
                    feed_ref[:, low : low + real] = part[m, i, :, :real].astype(F32)
                low += n


def write_outputs(w, dnormed, branch, dmixed, x, mixed, gain, parts, width):
    spec = pl.BlockSpec(memory_space=pltpu.VMEM)
    heads, rows, inner = w.shape
    kinds = [
        ((rows, heads * (inner - 2 * HEAD_DIM)), F32),
        ((rows, heads * HEAD_DIM), F32),
        ((rows, heads * HEAD_DIM), F32),
        (x.shape, BF),
        (x.shape, BF),
    ] + [((parts[0].shape[2], width), F32)] * 3
    return pl.pallas_call(
        outputs_kernel,
        out_shape=[jax.ShapeDtypeStruct(*k) for k in kinds],
        in_specs=[spec] * 9,
        out_specs=[spec] * len(kinds),
        compiler_params=pltpu.CompilerParams(vmem_limit_bytes=VMEM_LIMIT),
        cost_estimate=pl.CostEstimate(flops=0, bytes_accessed=20 * 2**20, transcendentals=0),
    )(w, dnormed, branch, dmixed, x, mixed, gain, *parts)


def feed_kernel(chunks, added, t_ref, c_ref, w_ref, *refs):
    act_ref, dgate_ref, dup_ref, branch_ref, dtok_ref = refs[-5:]
    before = refs[:added]
    tokens, cot = t_ref[...], c_ref[...]
    places, _, rows, width = w_ref.shape
    per = max(1, LANES * 3 // rows)

    def products(j):
        low, n = chunks[j]

        def weight(m):
            return w_ref[:, m, :, low : low + n].reshape(D, n)

        return dot_nn(tokens, weight(1)), dot_nn(tokens, weight(2)), dot_nn(cot, weight(0))

    ready = [products(0)]
    for j, (low, n) in enumerate(chunks):
        gate, up, dact = ready[j]
        if j + 1 < len(chunks):
            ready.append(products(j + 1))
        sig = 1.0 / (1.0 + jnp.exp(-gate))
        silu = gate * sig
        act_ref[:, low : low + n] = (silu * up).astype(BF)
        dgate_ref[:, low : low + n] = (dact * up * (sig + silu * (1.0 - sig))).astype(BF)
        dup_ref[:, low : low + n] = (dact * silu).astype(BF)
    for z in range(0, places, per):
        cols = slice(z * rows, (z + per) * rows)

        def weight(m):
            return w_ref[z : z + per, m].reshape(per * rows, width)

        dtok = dot_nt(dgate_ref[...], weight(1)) + dot_nt(dup_ref[...], weight(2))
        branch = dot_nt(act_ref[...], weight(0))
        if before:
            branch = branch + before[0][:, cols].astype(F32)
            dtok = dtok + before[1][:, cols].astype(F32)
        dtok_ref[:, cols] = dtok.astype(BF)
        branch_ref[:, cols] = branch.astype(BF)


def feed(tokens, cot, weights, before=(), after=()):
    n, width, tile = tokens.shape[0], weights.shape[-1], 256
    chunks = [(i, min(256, width - i)) for i in range(0, width, 256)]
    wide = pl.BlockSpec((tile, D), lambda i: (i, 0))
    inner = pl.BlockSpec((tile, width), lambda i: (i, 0))
    return pl.pallas_call(
        functools.partial(feed_kernel, chunks, len(before)),
        grid=(n // tile,),
        in_specs=[wide, wide, pl.BlockSpec(memory_space=pltpu.VMEM)]
        + [wide] * len(before)
        + [pl.BlockSpec(memory_space=pl.ANY)] * len(after),
        out_specs=[inner, inner, inner, wide, wide],
        out_shape=[jax.ShapeDtypeStruct((n, k), BF) for k in (width, width, width, D, D)],
        compiler_params=pltpu.CompilerParams(vmem_limit_bytes=VMEM_LIMIT),
        cost_estimate=pl.CostEstimate(
            flops=12 * n * D * width, bytes_accessed=40 * 2**20, transcendentals=n * width
        ),
    )(tokens, cot, weights, *before, *after)


def plain_grads_kernel(t_ref, c_ref, act_ref, dgate_ref, dup_ref, grad_ref):
    per, _, rows, width = grad_ref.shape
    for m, (left, right) in enumerate(((c_ref, act_ref), (t_ref, dgate_ref), (t_ref, dup_ref))):
        made = dot_tn(left[...], right[...]).astype(BF)
        grad_ref[:, m] = made.reshape(per, rows, width)


def plain_grads(tokens, cot, act, dgate, dup, places):
    n, width = act.shape
    rows = D // places
    per = max(1, LANES * 3 // rows)
    left = pl.BlockSpec((n, per * rows), lambda k: (0, k))
    right = pl.BlockSpec(memory_space=pltpu.VMEM)
    return pl.pallas_call(
        plain_grads_kernel,
        grid=(places // per,),
        in_specs=[left, left, right, right, right],
        out_specs=pl.BlockSpec((per, 3, rows, width), lambda k: (k, 0, 0, 0)),
        out_shape=jax.ShapeDtypeStruct((places, 3, rows, width), BF),
        compiler_params=pltpu.CompilerParams(vmem_limit_bytes=VMEM_LIMIT),
        cost_estimate=pl.CostEstimate(
            flops=6 * n * D * width, bytes_accessed=40 * 2**20, transcendentals=0
        ),
    )(tokens, cot, act, dgate, dup)


def grads_kernel(plans, sizes, dtok_ref, t_hbm, c_hbm, act_hbm, dgate_hbm, dup_hbm, *refs):
    sum_ref, grad_hbm, left_s, right_s, made_s, load_sems, made_sems = refs[:7]
    per, rows = made_s.shape[1:3]
    cols = per * rows
    loads = [
        pltpu.make_async_copy(c_hbm, left_s.at[0], load_sems.at[0]),
        pltpu.make_async_copy(act_hbm, right_s.at[0], load_sems.at[1]),
        pltpu.make_async_copy(t_hbm, left_s.at[1], load_sems.at[2]),
        pltpu.make_async_copy(dgate_hbm, right_s.at[1], load_sems.at[3]),
        pltpu.make_async_copy(dup_hbm, right_s.at[0], load_sems.at[4]),
    ]
    for copy in loads[:4]:
        copy.start()

    def stored(m, k, slot):
        return pltpu.make_async_copy(
            made_s.at[slot], grad_hbm.at[pl.ds(k * per, per), m], made_sems.at[slot]
        )

    def some(m, low, high, left, right, fresh):
        def one(k, carry):
            slot = lax.rem(k, 2)
            if fresh:
                pl.when(k >= 2)(lambda: stored(m, k, slot).wait())
            else:
                stored(m, k, slot).wait()
            part = left_s[left, :, pl.ds(pl.multiple_of(k * cols, LANES), cols)]
            made_s[slot] = dot_tn(part, right_s[right]).astype(BF).reshape(made_s.shape[1:])
            stored(m, k, slot).start()
            return carry

        lax.fori_loop(low, high, one, 0)

    chunks = D // cols

    def between(phase):
        if phase == 0:
            loads[0].wait()
            loads[1].wait()
            some(0, 0, chunks // 2, 0, 0, True)
        elif phase == 1:
            some(0, chunks // 2, chunks, 0, 0, False)
            loads[4].start()
            loads[2].wait()
            loads[3].wait()
            some(1, 0, chunks, 1, 1, False)
        else:
            loads[4].wait()
            some(2, 0, chunks, 1, 0, False)

    scatter_kernel(plans, sizes, dtok_ref, sum_ref, *refs[7:], between=between)
    for slot in range(2):
        stored(2, slot, slot).wait()


def feed_grads(dtok, tokens, cot, act, dgate, dup, places, plans, sizes, collective_id):
    plans = alive(plans, sizes)
    n, width = act.shape
    rows = D // places
    per = max(1, LANES * 3 // rows)
    spec = pl.BlockSpec(memory_space=pltpu.VMEM)
    far = pl.BlockSpec(memory_space=pl.ANY)
    return pl.pallas_call(
        functools.partial(grads_kernel, plans, sizes),
        out_shape=[
            jax.ShapeDtypeStruct(dtok.shape[1:], F32),
            jax.ShapeDtypeStruct((places, 3, rows, width), BF),
        ],
        in_specs=[spec] + [far] * 5,
        out_specs=[spec, far],
        scratch_shapes=[
            pltpu.VMEM((2, n, D), BF),
            pltpu.VMEM((2, n, width), BF),
            pltpu.VMEM((2, per, rows, width), BF),
            pltpu.SemaphoreType.DMA((5,)),
            pltpu.SemaphoreType.DMA((2,)),
        ]
        + scatter_scratch([dtok], plans, [F32], sizes),
        compiler_params=pltpu.CompilerParams(
            collective_id=collective_id, has_side_effects=True, vmem_limit_bytes=VMEM_LIMIT
        ),
        cost_estimate=pl.CostEstimate(
            flops=6 * n * D * width, bytes_accessed=100 * 2**20, transcendentals=0
        ),
    )(dtok, tokens, cot, act, dgate, dup)


def forward_kernel(heads, slots, tops, q_ref, kv_ref, o_ref, lse_ref, top_s, sum_s, acc_s):
    def score(keys, a, h):
        return dot_nt(keys, q_ref[a * BLOCK : (a + 1) * BLOCK, h * HEAD_DIM : (h + 1) * HEAD_DIM])

    for a in range(2):
        top_s[...] = jnp.full(top_s.shape, -1e30, F32)
        sum_s[...] = jnp.zeros(sum_s.shape, F32)
        acc_s[...] = jnp.zeros(acc_s.shape, F32)
        count = tops[a] + 1

        def step(keys, values_t):
            ahead = min(3, heads)
            ready = [score(keys, a, h) for h in range(ahead)]
            for h in range(heads):
                s = ready[h]
                if h + ahead < heads:
                    ready.append(score(keys, a, h + ahead))
                old = top_s[h : h + 1, :]
                new = jnp.maximum(old, jnp.max(s, axis=0, keepdims=True))
                p = jnp.exp2((s - new) * SCALE2)
                fade = jnp.exp2((old - new) * SCALE2)
                sum_s[h : h + 1, :] = sum_s[h : h + 1, :] * fade + jnp.sum(p, axis=0, keepdims=True)
                top_s[h : h + 1, :] = new
                acc_s[h] = acc_s[h] * fade + dot_nn(values_t, p.astype(BF))

        def two(i, carry):
            first, second = slots[2 * i], slots[2 * i + 1]
            both = jnp.concatenate([kv_ref[first], kv_ref[second]], axis=0)
            step(both[:, :HEAD_DIM], both[:, HEAD_DIM:].T)
            return carry

        lax.fori_loop(0, count // 2, two, 0)

        @pl.when(count % 2 == 1)
        def _():
            last = kv_ref[slots[count - 1]]
            step(last[:, :HEAD_DIM], last[:, HEAD_DIM:].T)

        for h in range(heads):
            total = sum_s[h : h + 1, :]
            o_ref[a * BLOCK : (a + 1) * BLOCK, h * HEAD_DIM : (h + 1) * HEAD_DIM] = (
                acc_s[h] / total
            ).T
            lse_ref[a, h : h + 1, :] = top_s[h : h + 1, :] * SCALE2 + jnp.log2(total)
        lse_ref[a, heads:8, :] = jnp.zeros((8 - heads, BLOCK), F32)


def attend(slots, tops, q, kv):
    heads = q.shape[1] // HEAD_DIM
    spec = pl.BlockSpec(memory_space=pltpu.VMEM)
    pairs = 33 * BLOCK * BLOCK * heads
    return pl.pallas_call(
        functools.partial(forward_kernel, heads),
        grid_spec=pltpu.PrefetchScalarGridSpec(
            num_scalar_prefetch=2,
            grid=(1,),
            in_specs=[spec] * 2,
            out_specs=[spec] * 2,
            scratch_shapes=[
                pltpu.VMEM((8, BLOCK), F32),
                pltpu.VMEM((8, BLOCK), F32),
                pltpu.VMEM((heads, HEAD_DIM, BLOCK), F32),
            ],
        ),
        out_shape=(
            jax.ShapeDtypeStruct(q.shape, F32),
            jax.ShapeDtypeStruct((2, 8, BLOCK), F32),
        ),
        compiler_params=pltpu.CompilerParams(vmem_limit_bytes=VMEM_LIMIT),
        cost_estimate=pl.CostEstimate(
            flops=pairs * 4 * HEAD_DIM, bytes_accessed=80 * 2**20, transcendentals=pairs
        ),
    )(slots, tops, q, kv)


def backward_kernel(
    heads,
    slots,
    tops,
    q_ref,
    kv_ref,
    do_ref,
    lse_ref,
    o_ref,
    dq_ref,
    dkv_ref,
    dq_s,
    dkv_s,
    delta_s,
):
    dkv_s[...] = jnp.zeros(dkv_s.shape, F32)
    for a in range(2):
        dq_s[...] = jnp.zeros(dq_s.shape, F32)

        def part(ref, h):
            return ref[a * BLOCK : (a + 1) * BLOCK, h * HEAD_DIM : (h + 1) * HEAD_DIM]

        for h in range(heads):
            product = part(do_ref, h).astype(F32) * part(o_ref, h)
            delta_s[h : h + 1, :] = jnp.sum(product.T, axis=0, keepdims=True)

        def one(n, carry):
            slot = slots[n]
            keys, values = kv_ref[slot, :, :HEAD_DIM], kv_ref[slot, :, HEAD_DIM:]
            keys_t = keys.T

            def products(h):
                return dot_nt(keys, part(q_ref, h)), dot_nt(values, part(do_ref, h))

            dk = jnp.zeros((BLOCK, HEAD_DIM), F32)
            dv = jnp.zeros((BLOCK, HEAD_DIM), F32)
            ahead = min(2, heads)
            ready = [products(h) for h in range(ahead)]
            for h in range(heads):
                s, dp = ready[h]
                if h + ahead < heads:
                    ready.append(products(h + ahead))
                p = jnp.exp2(s * SCALE2 - lse_ref[a, h : h + 1, :])
                dv = dv + dot_nn(p.astype(BF), part(do_ref, h))
                ds = (p * (dp - delta_s[h : h + 1, :])).astype(BF)
                dk = dk + dot_nn(ds, part(q_ref, h))
                dq_s[h] = dq_s[h] + dot_nn(keys_t, ds)
            dkv_s[slot, :, :HEAD_DIM] = dkv_s[slot, :, :HEAD_DIM] + dk
            dkv_s[slot, :, HEAD_DIM:] = dkv_s[slot, :, HEAD_DIM:] + dv
            return carry

        lax.fori_loop(0, tops[a] + 1, one, 0)
        for h in range(heads):
            dq_ref[a * BLOCK : (a + 1) * BLOCK, h * HEAD_DIM : (h + 1) * HEAD_DIM] = (
                (dq_s[h] * SCALE).T
            ).astype(BF)
    dkv_ref[:, :, :HEAD_DIM] = (dkv_s[:, :, :HEAD_DIM] * SCALE).astype(BF)
    dkv_ref[:, :, HEAD_DIM:] = dkv_s[:, :, HEAD_DIM:].astype(BF)


def attend_back(slots, tops, q, kv, do, lse, attended):
    heads = q.shape[1] // HEAD_DIM
    spec = pl.BlockSpec(memory_space=pltpu.VMEM)
    pairs = 33 * BLOCK * BLOCK * heads
    return pl.pallas_call(
        functools.partial(backward_kernel, heads),
        grid_spec=pltpu.PrefetchScalarGridSpec(
            num_scalar_prefetch=2,
            grid=(1,),
            in_specs=[spec] * 5,
            out_specs=[spec] * 2,
            scratch_shapes=[
                pltpu.VMEM((heads, HEAD_DIM, BLOCK), F32),
                pltpu.VMEM(kv.shape, F32),
                pltpu.VMEM((8, BLOCK), F32),
            ],
        ),
        out_shape=(
            jax.ShapeDtypeStruct(q.shape, BF),
            jax.ShapeDtypeStruct(kv.shape, BF),
        ),
        compiler_params=pltpu.CompilerParams(vmem_limit_bytes=VMEM_LIMIT),
        cost_estimate=pl.CostEstimate(
            flops=pairs * 10 * HEAD_DIM, bytes_accessed=120 * 2**20, transcendentals=pairs
        ),
    )(slots, tops, q, kv, do, lse, attended)


def inverse_rms(value):
    return lax.rsqrt(jnp.mean(value * value, axis=-1, keepdims=True) + EPS)


def turned(value, cosine, sine):
    return value * cosine + pltpu.roll(value, HEAD_DIM // 2, 1) * sine


def project_kernel(x_ref, w_ref, gain_ref, bias_ref, cos_ref, sin_ref, q_ref, kv_ref, normed_ref):
    x = x_ref[...].astype(F32)
    normed_ref[...] = (x * inverse_rms(x) * gain_ref[...]).astype(BF)
    cosine, sine = cos_ref[...], sin_ref[...]
    heads = q_ref.shape[1] // HEAD_DIM

    def product(low, n):
        cols = slice(low * HEAD_DIM, (low + n) * HEAD_DIM)
        return dot_nn(normed_ref[...], w_ref[:, cols]) + bias_ref[:, cols]

    for low in range(0, heads, 2):
        made = product(low, 2)
        for i in range(2):
            part = made[:, i * HEAD_DIM : (i + 1) * HEAD_DIM]
            q_ref[:, (low + i) * HEAD_DIM : (low + i + 1) * HEAD_DIM] = turned(
                part, cosine, sine
            ).astype(BF)
    made = product(heads, 2)
    kv_ref[:, :HEAD_DIM] = turned(made[:, :HEAD_DIM], cosine, sine).astype(BF)
    kv_ref[:, HEAD_DIM:] = made[:, HEAD_DIM:].astype(BF)


def project(x, w, gain, bias, cosine, sine):
    n, width = x.shape[0], w.shape[1]
    spec = pl.BlockSpec(memory_space=pltpu.VMEM)
    return pl.pallas_call(
        project_kernel,
        in_specs=[spec] * 6,
        out_specs=[spec] * 3,
        out_shape=[
            jax.ShapeDtypeStruct((n, k), BF)
            for k in (width - 2 * HEAD_DIM, 2 * HEAD_DIM, D)
        ],
        compiler_params=pltpu.CompilerParams(vmem_limit_bytes=VMEM_LIMIT),
        cost_estimate=pl.CostEstimate(
            flops=2 * n * D * width, bytes_accessed=12 * 2**20, transcendentals=0
        ),
    )(x, w, gain, bias, cosine, sine)


def project_back_kernel(
    dq_ref,
    dkv_ref,
    normed_ref,
    x_ref,
    w_ref,
    cos_ref,
    sin_ref,
    grad_ref,
    dnormed_ref,
    gain_grad_ref,
    bias_grad_ref,
    dpre_s,
):
    cosine, sine = cos_ref[...], -sin_ref[...]
    heads = dq_ref.shape[1] // HEAD_DIM
    for h in range(heads + 1):
        cols = slice(h * HEAD_DIM, (h + 1) * HEAD_DIM)
        part = dq_ref[:, cols] if h < heads else dkv_ref[:, :HEAD_DIM]
        dpre_s[:, cols] = turned(part.astype(F32), cosine, sine).astype(BF)
    dpre_s[:, (heads + 1) * HEAD_DIM :] = dkv_ref[:, HEAD_DIM:]
    bias_grad_ref[...] = jnp.sum(dpre_s[...].astype(F32), axis=0, keepdims=True)
    x = x_ref[...].astype(F32)
    scale = inverse_rms(x)
    step = 2 * HEAD_DIM
    for low in range(0, D, step):
        cols = slice(low, low + step)
        dnormed = dot_nt(dpre_s[...], w_ref[cols, :])
        dnormed_ref[:, cols] = dnormed.astype(BF)
        gain_grad_ref[:, cols] = jnp.sum(
            dnormed * (x[:, cols] * scale), axis=0, keepdims=True
        )
        if len(grad_ref.shape) == 2:
            grad_ref[cols, :] = dot_tn(normed_ref[:, cols], dpre_s[...]).astype(BF)
    if len(grad_ref.shape) == 4:
        blk, heads, rows, width = grad_ref.shape
        step = 3 * LANES
        for low in range(0, D, step):
            made = dot_tn(normed_ref[:, low : low + step], dpre_s[...]).astype(BF)
            half, start = divmod(low // rows, blk)
            grad_ref[start : start + step // rows, half] = made.reshape(step // rows, rows, width)


def project_back(dq, dkv, normed, x, w, cosine, sine, blk, rows):
    n, width = x.shape[0], w.shape[1]
    split = rows % 16 == 0
    made = (blk, 2, rows, width) if split else (D, width)
    spec = pl.BlockSpec(memory_space=pltpu.VMEM)
    return pl.pallas_call(
        project_back_kernel,
        in_specs=[spec] * 7,
        out_specs=[spec] * 4,
        out_shape=[
            jax.ShapeDtypeStruct(made, BF),
            jax.ShapeDtypeStruct((n, D), BF),
            jax.ShapeDtypeStruct((1, D), F32),
            jax.ShapeDtypeStruct((1, width), F32),
        ],
        scratch_shapes=[pltpu.VMEM((n, width), BF)],
        compiler_params=pltpu.CompilerParams(vmem_limit_bytes=VMEM_LIMIT),
        cost_estimate=pl.CostEstimate(
            flops=4 * n * D * width, bytes_accessed=16 * 2**20, transcendentals=0
        ),
    )(dq, dkv, normed, x, w, cosine, sine)


def small_rows(*rows):
    return jnp.stack(
        [jnp.pad(r.astype(F32), ((0, LANES - r.shape[0]),)) for r in rows]
        + [jnp.zeros((LANES,), F32)] * (8 - len(rows))
    )


def shards(
    sizes,
    hidden,
    cotangent,
    block_order,
    norm1,
    q_weight,
    q_bias,
    k_weight,
    k_bias,
    v_weight,
    v_bias,
    o_weight,
    norm2,
    gate_weight,
    up_weight,
    down_weight,
):
    tok = hidden.shape[0]
    pair = sizes["head"] * tok
    blk = int(np.prod([sizes[a] for a in BLK]))
    seqs = blk // SEQ_SPAN
    place_axes = {1: BLK, 2: BLK[:3], 4: BLK[:2]}[seqs]
    seq_axes = BLK[len(place_axes) :]
    head = lax.axis_index("head")
    place = place_of({}, place_axes, sizes)
    seq = place_of({}, seq_axes, sizes) if seq_axes else 0
    order = lax.dynamic_index_in_dim(block_order, seq, 0, keepdims=False)
    tops = lax.dynamic_slice_in_dim(order, place * 2, 2)
    slots = jnp.argsort(order).astype(jnp.int32)
    positions = (tops[:, None] * tok + jnp.arange(tok, dtype=jnp.int32)[None, :]).reshape(pair)
    frequency = THETA ** (-(jnp.arange(HEAD_DIM // 2, dtype=F32) * 2.0) / HEAD_DIM)
    angles = positions.astype(F32)[:, None] * frequency[None, :]
    cosine, sine = jnp.cos(angles), jnp.sin(angles)
    cosine = jnp.concatenate([cosine, cosine], axis=1)
    sine = jnp.concatenate([-sine, sine], axis=1)

    q_cols = D // 2
    kv_cols = HEAD_DIM
    rows = q_weight.shape[0]
    small = small_rows(
        *[v.astype(BF) for v in (norm1, norm2, q_bias, k_bias, v_bias)]
    )
    parts = sizes["y"] * sizes["c"]
    width = gate_weight.shape[1]
    lanes = -(-width // (LANES * parts)) * LANES
    first = lanes * 6 // 9 // LANES * LANES
    ff_rows = gate_weight.shape[0]

    def along_z(part):
        part = part.reshape(1, 3, parts * ff_rows, part.shape[-1])
        return lax.all_gather(part, live(("g", "z"), sizes), axis=0, tiled=True)

    w_qkv, x_pair, small_all, w_out, packed_one, packed_two = front(
        (q_weight, k_weight, v_weight, o_weight),
        hidden,
        small,
        (down_weight, gate_weight, up_weight),
        first,
        lanes - first,
        [
            (0, None, AXES, AXES, True),
            (1, None, ("head",), ("head",), False),
            (2, None, AXES, AXES, False),
            (3, None, BLK, ("y", "z", "g", "c"), False),
        ],
        sizes,
        1,
    )
    w_out = w_out.reshape(q_cols, D)
    w_qkv = w_qkv.reshape(D, q_cols + 2 * kv_cols)
    x_pair = x_pair.reshape(pair, D)
    gain_one = small_all[:, 0, :rows].reshape(D)
    gain_two = small_all[:, 1, :rows].reshape(D)
    bias_q = lax.dynamic_slice_in_dim(small_all[:, 2, :rows].reshape(D), head * q_cols, q_cols)
    bias_k, bias_v = (
        lax.dynamic_slice_in_dim(
            small_all[:, i, : k_bias.shape[0]].reshape(2 * kv_cols), head * kv_cols, kv_cols
        )
        for i in (3, 4)
    )

    queries, kv_local, normed = project(
        x_pair,
        w_qkv,
        gain_one[None],
        jnp.concatenate([bias_q, bias_k, bias_v])[None],
        cosine,
        sine,
    )
    group = ("head", "y", "c")
    half = tok // 2
    crossed = [
        ((0, half), group, ("head", "y", "c"), False),
        ((half, half), group, ("y", "head", "c"), False),
    ]
    summed = [
        ((0, half), group, ("c", "head", "y"), False),
        ((half, half), group, ("c", "y", "head"), False),
    ]
    far_axes, near_axes = place_axes[:2], place_axes[2:]
    cot_all = lax.all_gather(cotangent, group, axis=0, tiled=True)
    kv, mine_one = gather(
        [kv_local],
        [(0, None, far_axes, far_axes, False)],
        sizes,
        2,
        [packed_one],
        [cot_all],
    )
    w_feed_one = along_z(mine_one)
    if near_axes:
        (kv,) = gather([kv], [(0, None, near_axes, near_axes, False)], sizes, 10)
    near_count = int(np.prod([sizes[a] for a in near_axes], dtype=int))
    far_count = SEQ_SPAN // near_count
    where = slots // 2
    slots = ((where % near_count) * far_count + where // near_count) * 2 + slots % 2
    kv = kv.reshape(2 * SEQ_SPAN, tok, 2 * HEAD_DIM)
    attended, lse = attend(slots, tops, queries, kv)
    attn_local = attended.astype(BF)
    inputs = hidden.astype(F32)
    mixed_part = dot_nn(attn_local, w_out).reshape(2, tok, D)
    mixed_got, mine_two = gather(
        [mixed_part.astype(BF)],
        [(0, None, ("head",), ("head",), True)],
        sizes,
        3,
        [packed_two],
    )
    w_feed_two = along_z(mine_two)
    mixed = (
        inputs
        + lax.dynamic_index_in_dim(mixed_part, head, 0, keepdims=False)
        + lax.dynamic_index_in_dim(mixed_got, 1 - head, 0, keepdims=False).astype(F32)
    )
    scale_two = inverse_rms(mixed)
    normed_two = (mixed * scale_two * gain_two).astype(BF)
    (tokens,) = gather([normed_two], [(0,) + c for c in crossed], sizes, 4)
    tokens = tokens.reshape(-1, D)

    places = w_feed_one.shape[0]
    act, dgate, dup, branch, dtokens = feed(tokens, cot_all, w_feed_one)
    parts_one = plain_grads(tokens, cot_all, act, dgate, dup, places)
    act, dgate, dup, branch, dtokens = feed(
        tokens, cot_all, w_feed_two, (branch, dtokens), (parts_one,)
    )
    dnormed_two, parts_two = feed_grads(
        dtokens.reshape(-1, tok, D),
        tokens,
        cot_all,
        act,
        dgate,
        dup,
        places,
        [(0,) + c for c in summed],
        sizes,
        5,
    )
    def collect(grad):
        total = lax.psum_scatter(grad, live(("g", "z"), sizes), scatter_dimension=0, tiled=True)
        return total.reshape(3, parts, ff_rows, grad.shape[-1])

    back_one = collect(parts_one)

    z_two = mixed * scale_two
    u_two = gain_two * dnormed_two
    norm2_part = jnp.sum(dnormed_two * z_two, axis=0)
    dmixed = cotangent.astype(F32) + scale_two * (
        u_two - z_two * jnp.mean(z_two * u_two, axis=-1, keepdims=True)
    )
    dproj = dmixed.astype(BF)
    (dproj_pair,) = gather([dproj], [(0, None, ("head",), ("head",), False)], sizes, 6)
    dproj_pair = dproj_pair.reshape(pair, D)
    dout = dot_nt(dproj_pair, w_out).astype(BF)
    o_part = dot_tn(attn_local, dproj_pair).astype(BF)

    dq, dkv_parts = attend_back(slots, tops, queries, kv, dout, lse, attended)
    dkv, d_out_weight, parts_two = scatter(
        [dkv_parts.reshape(SEQ_SPAN, pair, 2 * HEAD_DIM), o_part.reshape(blk, -1, D)],
        [
            (0, None, near_axes + far_axes, place_axes[::-1], False),
            (1, None, BLK, BLK[::-1], False),
        ],
        [BF, F32],
        sizes,
        7,
        carried=[parts_two],
    )
    back_two = collect(parts_two)
    w_part, dnormed, norm1_part, bias_part = project_back(
        dq, dkv, normed, x_pair, w_qkv, cosine, sine, blk, rows
    )
    if w_part.ndim == 2:
        w_part = w_part.reshape(2, blk, rows, -1).transpose(1, 0, 2, 3)
    norm1_part, bias_part = norm1_part[0], bias_part[0]
    own = (jnp.arange(2) == head).astype(F32)[:, None]

    def owners(vector):
        return vector.reshape(2, blk, -1).transpose(1, 0, 2)

    def owned(vector):
        return owners((own * vector[None, :]).reshape(-1))

    small_grads = jnp.stack(
        [
            jnp.pad(part, ((0, 0), (0, 0), (0, LANES - part.shape[2])))
            for part in (
                owners(norm1_part),
                owners(norm2_part),
                owned(bias_part[:q_cols]),
                owned(bias_part[q_cols : q_cols + kv_cols]),
                owned(bias_part[q_cols + kv_cols :]),
            )
        ]
        + [jnp.zeros((blk, 2, LANES), F32)] * 3,
        axis=2,
    )
    small_grads = small_grads.transpose(1, 0, 2, 3).reshape(2 * blk, 8, LANES)
    w_grads, small_sum, dnormed_sum, branch_sum = scatter(
        [
            w_part,
            small_grads,
            dnormed.reshape(2, tok, D),
            branch.reshape(-1, tok, D),
        ],
        [
            (0, None, BLK, BLK[::-1], True),
            (1, None, AXES, AXES[::-1], False),
            (2, None, ("head",), ("head",), False),
        ]
        + [(3,) + c for c in summed],
        [F32] * 4,
        sizes,
        8,
        [back_one],
    )
    d_query, d_key, d_value, output, hidden_grad, d_down, d_gate, d_up = write_outputs(
        w_grads,
        dnormed_sum,
        branch_sum,
        dmixed,
        hidden,
        mixed,
        gain_one[None],
        swap([back_one, back_two], w_grads, 9),
        width,
    )
    kn = k_bias.shape[0]
    return (
        output,
        hidden_grad,
        small_sum[0, :rows],
        d_query,
        small_sum[2, :rows],
        d_key,
        small_sum[3, :kn],
        d_value,
        small_sum[4, :kn],
        d_out_weight,
        small_sum[1, :rows],
        d_gate,
        d_up,
        d_down,
    )


def solution(mesh):
    heads, blk = mesh.devices.shape
    split = jax.sharding.Mesh(mesh.devices.reshape(heads, blk // 16, 4, 2, 2), AXES)
    sizes = dict(split.shape)
    rows = P(AXES, None)
    vector = P(AXES)
    feed = P(BLK, "head")
    return jax.shard_map(
        functools.partial(shards, sizes),
        mesh=split,
        in_specs=(
            rows,
            rows,
            P(),
            vector,
            rows,
            vector,
            rows,
            vector,
            rows,
            vector,
            rows,
            vector,
            feed,
            feed,
            feed,
        ),
        out_specs=(
            rows,
            rows,
            vector,
            rows,
            vector,
            rows,
            vector,
            rows,
            vector,
            rows,
            vector,
            feed,
            feed,
            feed,
        ),
        check_vma=False,
    )
```

```python
import functools

import jax
import jax.numpy as jnp
import numpy as np
from jax import lax
from jax.experimental import pallas as pl
from jax.experimental.pallas import tpu as pltpu
from jax.sharding import PartitionSpec as P

D = 1536
QHEADS = 12
KVHEADS = 2
HEAD_DIM = 128
SEQ_SPAN = 16
BLOCK = 256

EPS = 1e-06
THETA = 1000000.0
SCALE = HEAD_DIM**-0.5
LOG2E = 1.4426950408889634
SCALE2 = SCALE * LOG2E
BF = jnp.bfloat16
F32 = jnp.float32
MESH = pl.DeviceIdType.MESH
VMEM_LIMIT = 56 * 2**20
AXES = ("head", "g", "z", "y", "c")
BLK = ("g", "z", "y", "c")
LANES = 128


def dot_nn(a, b):
    return lax.dot_general(a, b, (((1,), (0,)), ((), ())), preferred_element_type=F32)


def dot_nt(a, b):
    return lax.dot_general(a, b, (((1,), (1,)), ((), ())), preferred_element_type=F32)


def dot_tn(a, b):
    return lax.dot_general(a, b, (((0,), (0,)), ((), ())), preferred_element_type=F32)


def live(axes, sizes):
    return tuple(a for a in axes if sizes[a] > 1)


def greet(axes, sizes, diagonal=False):
    barrier = pltpu.get_barrier_semaphore()
    count = 0
    if diagonal:
        pl.semaphore_signal(barrier, inc=1, device_id=across(3), device_id_type=MESH)
        count += 1
    for a in axes:
        me = lax.axis_index(a)
        for d in range(1, sizes[a]):
            pl.semaphore_signal(
                barrier,
                inc=1,
                device_id={a: lax.rem(me + d, sizes[a])},
                device_id_type=MESH,
            )
            count += 1
    pl.semaphore_wait(barrier, count)


def across(d):
    y, c = lax.axis_index("y"), lax.axis_index("c")
    return {"y": 1 - y if d & 2 else y, "c": 1 - c if d & 1 else c}


class Swap:
    def __init__(self, x, out, send_sems, recv_sems, local_sem):
        me = lax.axis_index("y") * 2 + lax.axis_index("c")
        self.kept = pltpu.make_async_copy(x.at[:, me], out.at[:, me], local_sem)
        self.copies = []
        for d in range(1, 4):
            to = across(d)
            self.copies.append(
                pltpu.make_async_remote_copy(
                    src_ref=x.at[:, to["y"] * 2 + to["c"]],
                    dst_ref=out.at[:, me],
                    send_sem=send_sems.at[d - 1],
                    recv_sem=recv_sems.at[d - 1],
                    device_id=to,
                    device_id_type=MESH,
                )
            )

    def start(self):
        for copy in self.copies:
            copy.start()
        self.kept.start()

    def wait(self):
        self.kept.wait()
        for copy in self.copies:
            copy.wait()


def swap_scratch(swaps):
    if not swaps:
        return []
    return [pltpu.SemaphoreType.DMA((3 * len(swaps),))] * 2 + [
        pltpu.SemaphoreType.DMA((len(swaps),))
    ]


def swaps_of(xs, outs, sems):
    return [
        Swap(
            x,
            out,
            sems[0].at[pl.ds(3 * i, 3)],
            sems[1].at[pl.ds(3 * i, 3)],
            sems[2].at[i],
        )
        for i, (x, out) in enumerate(zip(xs, outs))
    ]


def place_of(offsets, axes, sizes):
    value = 0
    for a in axes:
        me = lax.axis_index(a)
        off = offsets.get(a, 0)
        value = value * sizes[a] + (lax.rem(me + off, sizes[a]) if off else me)
    return value


def remote(src, dst, send, recv, axis, distance, sizes):
    to = lax.rem(lax.axis_index(axis) + distance, sizes[axis])
    return pltpu.make_async_remote_copy(
        src_ref=src,
        dst_ref=dst,
        send_sem=send,
        recv_sem=recv,
        device_id={axis: to},
        device_id_type=MESH,
    )


def gather_kernel(plans, sizes, swap_count, waited, carried, *refs, ahead=None, behind=None):
    count = max(p[0] for p in plans) + 1
    xs, refs = refs[:count], refs[count:]
    swap_xs, refs = refs[:swap_count], refs[swap_count + waited :]
    outs, refs = refs[:count], refs[count:]
    swap_outs, refs = refs[:swap_count], refs[swap_count + carried :]
    send_sems, recv_sems, local_sems = refs[:3]
    swaps = swaps_of(swap_xs, swap_outs, refs[3:])
    used = {a: (sizes[a] if any(a in p[3] for p in plans) else 1) for a in AXES}
    if swaps:
        used.update(y=sizes["y"], c=sizes["c"])
    greet(live(AXES, used), sizes, bool(swaps))

    def cut(ref, rows):
        return ref if rows is None else ref.at[pl.ds(*rows)]

    def source(plan, place):
        i, rows, layout, phases, split = plan
        return cut(xs[i].at[place] if split else xs[i], rows)

    def landed(slot, number):
        axis = plans[0][3][0]
        return remote(slot, slot, send_sems.at[number], recv_sems.at[number], axis, 0, sizes)

    sends, kept, queue = [], [], []
    sem = 0
    for j, plan in enumerate(plans):
        i, rows, layout, phases, split = plan
        mine = source(plan, lax.axis_index(phases[0]))
        slot = cut(outs[i].at[place_of({}, layout, sizes)], rows)
        copy = pltpu.make_async_copy(mine, slot, local_sems.at[j])
        queue.append((plan, {}, -1, None))
        kept.append(copy)
    at = 0
    ends = []
    while at < len(queue):
        plan, offsets, phase, arrived = queue[at]
        at += 1
        i, rows, layout, phases, split = plan
        slot = cut(outs[i].at[place_of(offsets, layout, sizes)], rows)
        if arrived is None:
            src = source(plan, lax.axis_index(phases[0]))
        else:
            src = slot
            landed(slot, arrived).wait_recv()
        for p in range(phase + 1, len(phases)):
            a = phases[p]
            for d in range(1, sizes[a]):
                piece = src
                if split and p == 0:
                    piece = source(plan, lax.rem(lax.axis_index(a) + d, sizes[a]))
                copy = remote(piece, slot, send_sems.at[sem], recv_sems.at[sem], a, d, sizes)
                copy.start()
                sends.append(copy)
                later = dict(offsets)
                later[a] = sizes[a] - d
                if p + 1 < len(phases):
                    queue.append((plan, later, p, sem))
                else:
                    ends.append((plan, later, sem))
                sem += 1
        if at == len(plans):
            if ahead is not None:
                ahead()
            for copy in kept + swaps:
                copy.start()
            if behind is not None:
                behind()
    for (i, rows, layout, phases, split), offsets, arrived in ends:
        landed(cut(outs[i].at[place_of(offsets, layout, sizes)], rows), arrived).wait_recv()
    for copy in kept + swaps:
        copy.wait()
    for copy in sends:
        copy.wait_send()


def gather(arrays, plans, sizes, collective_id, swaps=(), after=(), carried=()):
    plans = [
        (i, rows, live(layout, sizes), live(phases, sizes), split)
        for i, rows, layout, phases, split in plans
    ]
    counts = [int(np.prod([sizes[a] for a in p[2]])) for p in plans]
    total = sum(counts) - len(counts)
    shapes = []
    for i, x in enumerate(arrays):
        n, split = next((c, p[4]) for c, p in zip(counts, plans) if p[0] == i)
        shapes.append(jax.ShapeDtypeStruct((n,) + (x.shape[1:] if split else x.shape), x.dtype))
    spec = pl.BlockSpec(memory_space=pltpu.VMEM)
    far = pl.BlockSpec(memory_space=pl.ANY)
    specs = [spec] * len(arrays) + [far] * len(swaps)
    moved = sum(int(np.prod(s.shape)) * s.dtype.itemsize for s in shapes)
    return pl.pallas_call(
        functools.partial(
            gather_kernel, plans, sizes, len(swaps), len(after) + len(carried), len(carried)
        ),
        out_shape=shapes + [jax.ShapeDtypeStruct(x.shape, x.dtype) for x in (*swaps, *carried)],
        in_specs=specs + [far] * (len(after) + len(carried)),
        out_specs=specs + [far] * len(carried),
        input_output_aliases={
            len(specs) + len(after) + i: len(specs) + i for i in range(len(carried))
        },
        scratch_shapes=[
            pltpu.SemaphoreType.DMA((total,)),
            pltpu.SemaphoreType.DMA((total,)),
            pltpu.SemaphoreType.DMA((len(plans),)),
        ]
        + swap_scratch(swaps),
        compiler_params=pltpu.CompilerParams(
            collective_id=collective_id, has_side_effects=True, vmem_limit_bytes=VMEM_LIMIT
        ),
        cost_estimate=pl.CostEstimate(flops=0, bytes_accessed=20 * moved, transcendentals=0),
    )(*arrays, *swaps, *after, *carried)


def front_kernel(plans, sizes, *refs):
    q_ref, k_ref, v_ref, o_ref, hidden_ref, small_ref = refs[:6]
    feeds, refs = refs[6:9], refs[9:]
    outs, first_ref, second_ref, refs = refs[:4], refs[4], refs[5], refs[6:]
    halves_s, o_s = refs[:2]
    heads = halves_s.shape[0]
    q_cols, kv_cols = q_ref.shape[1] // heads, k_ref.shape[1] // heads
    for i in range(heads):
        halves_s[i, :, :q_cols] = q_ref[:, i * q_cols : (i + 1) * q_cols].astype(BF)
        cols = slice(i * kv_cols, (i + 1) * kv_cols)
        halves_s[i, :, q_cols : q_cols + kv_cols] = k_ref[:, cols].astype(BF)
        halves_s[i, :, q_cols + kv_cols :] = v_ref[:, cols].astype(BF)
    o_s[...] = o_ref[...].astype(BF)

    def pack():
        first, second = first_ref.shape[-1], second_ref.shape[-1]
        for m, feed_ref in enumerate(feeds):
            rows, width = feed_ref.shape
            for i in range(first_ref.shape[1]):
                low = i * (first + second)
                for ref, n in ((first_ref, first), (second_ref, second)):
                    real = min(n, width - low)
                    ref[m, i, :, :real] = feed_ref[:, low : low + real].astype(BF)
                    if real < n:
                        ref[m, i, :, real:] = jnp.zeros((rows, n - real), BF)
                    low += n

    gather_kernel(
        plans,
        sizes,
        0,
        0,
        0,
        halves_s,
        hidden_ref,
        small_ref,
        o_s,
        *outs,
        *refs[2:],
        ahead=pack,
    )


def front(weights, hidden, small, feeds, first, second, plans, sizes, collective_id):
    plans = alive(plans, sizes)
    heads, rows = sizes["head"], weights[0].shape[0]
    halves = jax.ShapeDtypeStruct((heads, rows, sum(w.shape[1] for w in weights[:3]) // heads), BF)
    out = jax.ShapeDtypeStruct(weights[3].shape, BF)
    arrays = [halves, hidden, small, out]
    counts = [int(np.prod([sizes[a] for a in p[2]])) for p in plans]
    total = sum(counts) - len(counts)
    shapes = [
        jax.ShapeDtypeStruct((n,) + (x.shape[1:] if p[4] else x.shape), x.dtype)
        for n, x, p in zip(counts, arrays, plans)
    ]
    ff_rows = feeds[0].shape[0]
    blocks = [jax.ShapeDtypeStruct((3, 4, ff_rows, n), BF) for n in (first, second)]
    spec = pl.BlockSpec(memory_space=pltpu.VMEM)
    return pl.pallas_call(
        functools.partial(front_kernel, plans, sizes),
        out_shape=shapes + blocks,
        in_specs=[spec] * 9,
        out_specs=[spec] * 6,
        scratch_shapes=[
            pltpu.VMEM(halves.shape, BF),
            pltpu.VMEM(out.shape, BF),
            pltpu.SemaphoreType.DMA((total,)),
            pltpu.SemaphoreType.DMA((total,)),
            pltpu.SemaphoreType.DMA((len(plans),)),
        ],
        compiler_params=pltpu.CompilerParams(
            collective_id=collective_id, has_side_effects=True, vmem_limit_bytes=VMEM_LIMIT
        ),
        cost_estimate=pl.CostEstimate(flops=0, bytes_accessed=100 * 2**20, transcendentals=0),
    )(*weights, hidden, small, *feeds)


def offset_keys(axes, sizes):
    keys = [{}]
    for a in axes:
        keys = [dict(k, **{a: d}) for k in keys for d in list(range(1, sizes[a])) + [0]]
    return keys


def scatter_kernel(plans, sizes, *refs, between=None):
    count = max(p[0] for p in plans) + 1
    xs, outs = refs[:count], refs[count : 2 * count]
    at = 2 * count
    bufs = []
    for _, _, _, phases, swap in plans:
        n = len(phases)
        bufs.append((refs[at : at + n], refs[at + n : at + 2 * n]))
        at += 2 * n
    send_sems, recv_sems, local_sems = refs[at:]
    used = {
        a: (sizes[a] if any(a in p[3] or (p[4] and a == "head") for p in plans) else 1)
        for a in AXES
    }
    greet(live(AXES, used), sizes)
    sem = 0
    sends = []
    arrivals = [dict() for _ in plans]

    def number(offsets, axes):
        value = 0
        for a in axes:
            value = value * sizes[a] + offsets.get(a, 0)
        return value

    def block_of(j, offsets):
        i, rows, layout, phases, swap = plans[j]
        block = xs[i].at[place_of(offsets, layout, sizes)]
        return block if rows is None else block.at[pl.ds(*rows)]

    def total_of(j, offsets, phase):
        phases = plans[j][3]
        total = block_of(j, offsets)[...].astype(F32)
        for q in range(phase):
            rest = phases[q + 1 :]
            for d in range(1, sizes[phases[q]]):
                s = arrivals[j].pop((q, d, number(offsets, rest)))
                buf = bufs[j][1][q].at[d - 1, number(offsets, rest)]
                remote(buf, buf, send_sems.at[s], recv_sems.at[s], phases[q], 0, sizes).wait_recv()
                total = total + buf[...].astype(F32)
        return total

    depth = max(len(p[3]) for p in plans)
    for phase in range(depth):
        for j, (i, rows, layout, phases, swap) in enumerate(plans):
            if phase >= len(phases):
                continue
            a, rest = phases[phase], phases[phase + 1 :]
            for d in range(1, sizes[a]):
                for key in offset_keys(rest, sizes):
                    offsets = dict(key)
                    offsets[a] = d
                    where = number(key, rest)
                    if phase == 0:
                        src = block_of(j, offsets)
                    else:
                        src = bufs[j][0][phase].at[d - 1, where]
                        src[...] = total_of(j, offsets, phase).astype(src.dtype)
                    dst = bufs[j][1][phase].at[d - 1, where]
                    copy = remote(src, dst, send_sems.at[sem], recv_sems.at[sem], a, d, sizes)
                    copy.start()
                    sends.append(copy)
                    arrivals[j][(phase, d, where)] = sem
                    sem += 1
        if between is not None:
            between(phase)
    late = []
    for j, (i, rows, layout, phases, swap) in enumerate(plans):
        total = total_of(j, {}, len(phases))
        if swap:
            hold, out = bufs[j][0][0], outs[i]
            hold[...] = total.astype(hold.dtype)
            me = lax.axis_index("head")
            copy = pltpu.make_async_copy(hold.at[me], out.at[me], local_sems.at[j])
            copy.start()
            late.append((copy, None))
            for d in range(1, sizes["head"]):
                to = lax.rem(me + d, sizes["head"])
                copy = remote(
                    hold.at[to], out.at[me], send_sems.at[sem], recv_sems.at[sem], "head", d, sizes
                )
                copy.start()
                sends.append(copy)
                late.append((out.at[lax.rem(me + sizes["head"] - d, sizes["head"])], sem))
                sem += 1
        elif rows is None:
            outs[i][...] = total.astype(outs[i].dtype)
        else:
            outs[i][pl.ds(*rows)] = total.astype(outs[i].dtype)
    for item, s in late:
        if s is None:
            item.wait()
        else:
            remote(item, item, send_sems.at[s], recv_sems.at[s], "head", 0, sizes).wait_recv()
    for copy in sends:
        copy.wait_send()


def scatter_scratch(arrays, plans, out_types, sizes):
    scratch, total = [], 0
    for i, rows, layout, phases, swap in plans:
        x, kind = arrays[i], out_types[i]
        block = x.shape[1:] if rows is None else (rows[1],) + x.shape[2:]
        send_bufs, recv_bufs = [], []
        for p, a in enumerate(phases):
            rest = int(np.prod([sizes[b] for b in phases[p + 1 :]], dtype=int))
            shape = (sizes[a] - 1, rest) + block
            recv_bufs.append(pltpu.VMEM(shape, x.dtype))
            if p == 0:
                send_bufs.append(pltpu.VMEM(block if swap else (8, LANES), kind if swap else F32))
            else:
                send_bufs.append(pltpu.VMEM(shape, x.dtype))
            total += (sizes[a] - 1) * rest
        scratch += send_bufs + recv_bufs
        if swap:
            total += sizes["head"] - 1
    return scratch + [
        pltpu.SemaphoreType.DMA((total,)),
        pltpu.SemaphoreType.DMA((total,)),
        pltpu.SemaphoreType.DMA((len(plans),)),
    ]


def alive(plans, sizes):
    return [
        (i, rows, live(layout, sizes), live(phases, sizes), flag)
        for i, rows, layout, phases, flag in plans
    ]


def scatter_and_wait_kernel(plans, sizes, arrays, waited, carried, *refs):
    xs, refs = refs[:arrays], refs[arrays + waited :]
    scatter_kernel(plans, sizes, *xs, *refs[:arrays], *refs[arrays + carried :])


def scatter(arrays, plans, out_types, sizes, collective_id, after=(), carried=()):
    plans = alive(plans, sizes)
    shapes = [jax.ShapeDtypeStruct(x.shape[1:], kind) for x, kind in zip(arrays, out_types)]
    spec = pl.BlockSpec(memory_space=pltpu.VMEM)
    far = pl.BlockSpec(memory_space=pl.ANY)
    moved = sum(int(np.prod(x.shape)) * x.dtype.itemsize for x in arrays)
    return pl.pallas_call(
        functools.partial(
            scatter_and_wait_kernel,
            plans,
            sizes,
            len(arrays),
            len(after) + len(carried),
            len(carried),
        ),
        out_shape=shapes + [jax.ShapeDtypeStruct(x.shape, x.dtype) for x in carried],
        in_specs=[spec] * len(arrays) + [far] * (len(after) + len(carried)),
        out_specs=[spec] * len(arrays) + [far] * len(carried),
        input_output_aliases={
            len(arrays) + len(after) + i: len(arrays) + i for i in range(len(carried))
        },
        scratch_shapes=scatter_scratch(arrays, plans, out_types, sizes),
        compiler_params=pltpu.CompilerParams(
            collective_id=collective_id, has_side_effects=True, vmem_limit_bytes=VMEM_LIMIT
        ),
        cost_estimate=pl.CostEstimate(flops=0, bytes_accessed=20 * moved, transcendentals=0),
    )(*arrays, *after, *carried)


def swap_kernel(count, *refs):
    items = swaps_of(refs[:count], refs[count + 1 : 2 * count + 1], refs[2 * count + 1 :])
    greet(("y", "c"), {"y": 2, "c": 2}, True)
    for item in items:
        item.start()
    for item in items:
        item.wait()


def swap(xs, last, collective_id):
    far = pl.BlockSpec(memory_space=pl.ANY)
    n = len(xs)
    return pl.pallas_call(
        functools.partial(swap_kernel, n),
        out_shape=[jax.ShapeDtypeStruct(x.shape, x.dtype) for x in xs],
        in_specs=[far] * (n + 1),
        out_specs=[far] * n,
        scratch_shapes=swap_scratch(xs),
        compiler_params=pltpu.CompilerParams(
            collective_id=collective_id, has_side_effects=True, vmem_limit_bytes=VMEM_LIMIT
        ),
    )(*xs, last)


def outputs_kernel(*refs):
    w_ref, dnormed_ref, branch_ref, dmixed_ref, x_ref, mixed_ref, gain_ref = refs[:7]
    parts, refs = refs[7:9], refs[9:]
    q_ref, k_ref, v_ref, out_ref, hidden_ref = refs[:5]
    feeds = refs[5:]
    heads = w_ref.shape[0]
    q_cols = q_ref.shape[1] // heads
    for i in range(heads):
        cols = slice(i * HEAD_DIM, (i + 1) * HEAD_DIM)
        q_ref[:, i * q_cols : (i + 1) * q_cols] = w_ref[i, :, :q_cols]
        k_ref[:, cols] = w_ref[i, :, q_cols : q_cols + HEAD_DIM]
        v_ref[:, cols] = w_ref[i, :, q_cols + HEAD_DIM :]
    out_ref[...] = (mixed_ref[...] + branch_ref[...]).astype(BF)
    x = x_ref[...].astype(F32)
    scale = inverse_rms(x)
    z = x * scale
    u = gain_ref[...] * dnormed_ref[...]
    hidden_ref[...] = (
        dmixed_ref[...] + scale * (u - z * jnp.mean(z * u, axis=-1, keepdims=True))
    ).astype(BF)
    width = feeds[0].shape[1]
    lanes = sum(part.shape[-1] for part in parts)
    for m, feed_ref in enumerate(feeds):
        for i in range(parts[0].shape[1]):
            low = i * lanes
            for part in parts:
                n = part.shape[-1]
                real = min(n, width - low)
                if real > 0:
                    feed_ref[:, low : low + real] = part[m, i, :, :real].astype(F32)
                low += n


def write_outputs(w, dnormed, branch, dmixed, x, mixed, gain, parts, width):
    spec = pl.BlockSpec(memory_space=pltpu.VMEM)
    heads, rows, inner = w.shape
    kinds = [
        ((rows, heads * (inner - 2 * HEAD_DIM)), F32),
        ((rows, heads * HEAD_DIM), F32),
        ((rows, heads * HEAD_DIM), F32),
        (x.shape, BF),
        (x.shape, BF),
    ] + [((parts[0].shape[2], width), F32)] * 3
    return pl.pallas_call(
        outputs_kernel,
        out_shape=[jax.ShapeDtypeStruct(*k) for k in kinds],
        in_specs=[spec] * 9,
        out_specs=[spec] * len(kinds),
        compiler_params=pltpu.CompilerParams(vmem_limit_bytes=VMEM_LIMIT),
        cost_estimate=pl.CostEstimate(flops=0, bytes_accessed=20 * 2**20, transcendentals=0),
    )(w, dnormed, branch, dmixed, x, mixed, gain, *parts)


def feed_kernel(chunks, added, t_ref, c_ref, w_ref, *refs):
    act_ref, dgate_ref, dup_ref, branch_ref, dtok_ref = refs[-5:]
    before = refs[:added]
    tokens, cot = t_ref[...], c_ref[...]
    places, _, rows, width = w_ref.shape
    per = max(1, LANES * 3 // rows)

    def products(j):
        low, n = chunks[j]

        def weight(m):
            return w_ref[:, m, :, low : low + n].reshape(D, n)

        return dot_nn(tokens, weight(1)), dot_nn(tokens, weight(2)), dot_nn(cot, weight(0))

    ready = [products(0)]
    for j, (low, n) in enumerate(chunks):
        gate, up, dact = ready[j]
        if j + 1 < len(chunks):
            ready.append(products(j + 1))
        sig = 1.0 / (1.0 + jnp.exp(-gate))
        silu = gate * sig
        act_ref[:, low : low + n] = (silu * up).astype(BF)
        dgate_ref[:, low : low + n] = (dact * up * (sig + silu * (1.0 - sig))).astype(BF)
        dup_ref[:, low : low + n] = (dact * silu).astype(BF)
    for z in range(0, places, per):
        cols = slice(z * rows, (z + per) * rows)

        def weight(m):
            return w_ref[z : z + per, m].reshape(per * rows, width)

        dtok = dot_nt(dgate_ref[...], weight(1)) + dot_nt(dup_ref[...], weight(2))
        branch = dot_nt(act_ref[...], weight(0))
        if before:
            branch = branch + before[0][:, cols].astype(F32)
            dtok = dtok + before[1][:, cols].astype(F32)
        dtok_ref[:, cols] = dtok.astype(BF)
        branch_ref[:, cols] = branch.astype(BF)


def feed(tokens, cot, weights, before=(), after=()):
    n, width, tile = tokens.shape[0], weights.shape[-1], 256
    chunks = [(i, min(256, width - i)) for i in range(0, width, 256)]
    wide = pl.BlockSpec((tile, D), lambda i: (i, 0))
    inner = pl.BlockSpec((tile, width), lambda i: (i, 0))
    return pl.pallas_call(
        functools.partial(feed_kernel, chunks, len(before)),
        grid=(n // tile,),
        in_specs=[wide, wide, pl.BlockSpec(memory_space=pltpu.VMEM)]
        + [wide] * len(before)
        + [pl.BlockSpec(memory_space=pl.ANY)] * len(after),
        out_specs=[inner, inner, inner, wide, wide],
        out_shape=[jax.ShapeDtypeStruct((n, k), BF) for k in (width, width, width, D, D)],
        compiler_params=pltpu.CompilerParams(vmem_limit_bytes=VMEM_LIMIT),
        cost_estimate=pl.CostEstimate(
            flops=12 * n * D * width, bytes_accessed=40 * 2**20, transcendentals=n * width
        ),
    )(tokens, cot, weights, *before, *after)


def plain_grads_kernel(t_ref, c_ref, act_ref, dgate_ref, dup_ref, grad_ref):
    per, _, rows, width = grad_ref.shape
    for m, (left, right) in enumerate(((c_ref, act_ref), (t_ref, dgate_ref), (t_ref, dup_ref))):
        made = dot_tn(left[...], right[...]).astype(BF)
        grad_ref[:, m] = made.reshape(per, rows, width)


def plain_grads(tokens, cot, act, dgate, dup, places):
    n, width = act.shape
    rows = D // places
    per = max(1, LANES * 3 // rows)
    left = pl.BlockSpec((n, per * rows), lambda k: (0, k))
    right = pl.BlockSpec(memory_space=pltpu.VMEM)
    return pl.pallas_call(
        plain_grads_kernel,
        grid=(places // per,),
        in_specs=[left, left, right, right, right],
        out_specs=pl.BlockSpec((per, 3, rows, width), lambda k: (k, 0, 0, 0)),
        out_shape=jax.ShapeDtypeStruct((places, 3, rows, width), BF),
        compiler_params=pltpu.CompilerParams(vmem_limit_bytes=VMEM_LIMIT),
        cost_estimate=pl.CostEstimate(
            flops=6 * n * D * width, bytes_accessed=40 * 2**20, transcendentals=0
        ),
    )(tokens, cot, act, dgate, dup)


def grads_kernel(plans, sizes, dtok_ref, mixed_ref, cot_ref, gain_ref, *refs):
    t_hbm, c_hbm, act_hbm, dgate_hbm, dup_hbm = refs[:5]
    dmixed_ref, dproj_ref, gain_grad_ref, grad_hbm = refs[5:9]
    sum_ref, left_s, right_s, made_s, load_sems, made_sems = refs[9:15]
    per, rows = made_s.shape[1:3]
    cols = per * rows
    loads = [
        pltpu.make_async_copy(c_hbm, left_s.at[0], load_sems.at[0]),
        pltpu.make_async_copy(act_hbm, right_s.at[0], load_sems.at[1]),
        pltpu.make_async_copy(t_hbm, left_s.at[1], load_sems.at[2]),
        pltpu.make_async_copy(dgate_hbm, right_s.at[1], load_sems.at[3]),
        pltpu.make_async_copy(dup_hbm, right_s.at[0], load_sems.at[4]),
    ]
    for copy in loads[:4]:
        copy.start()

    def stored(m, k, slot):
        return pltpu.make_async_copy(
            made_s.at[slot], grad_hbm.at[pl.ds(k * per, per), m], made_sems.at[slot]
        )

    def some(m, low, high, left, right, fresh):
        def one(k, carry):
            slot = lax.rem(k, 2)
            if fresh:
                pl.when(k >= 2)(lambda: stored(m, k, slot).wait())
            else:
                stored(m, k, slot).wait()
            part = left_s[left, :, pl.ds(pl.multiple_of(k * cols, LANES), cols)]
            made_s[slot] = dot_tn(part, right_s[right]).astype(BF).reshape(made_s.shape[1:])
            stored(m, k, slot).start()
            return carry

        lax.fori_loop(low, high, one, 0)

    chunks = D // cols

    def between(phase):
        if phase == 0:
            loads[0].wait()
            loads[1].wait()
            some(0, 0, chunks // 2, 0, 0, True)
        elif phase == 1:
            some(0, chunks // 2, chunks, 0, 0, False)
            loads[4].start()
            loads[2].wait()
            loads[3].wait()
            some(1, 0, chunks, 1, 1, False)
        else:
            loads[4].wait()
            some(2, 0, chunks, 1, 0, False)

    scatter_kernel(plans, sizes, dtok_ref, sum_ref, *refs[15:], between=between)
    mixed, dnormed = mixed_ref[...], sum_ref[...]
    scale = inverse_rms(mixed)
    z = mixed * scale
    u = gain_ref[...] * dnormed
    gain_grad_ref[...] = jnp.sum(dnormed * z, axis=0, keepdims=True)
    dmixed = cot_ref[...].astype(F32) + scale * (
        u - z * jnp.mean(z * u, axis=-1, keepdims=True)
    )
    dmixed_ref[...] = dmixed
    dproj_ref[...] = dmixed.astype(BF)
    for slot in range(2):
        stored(2, slot, slot).wait()


def feed_grads(dtok, mixed, cot_own, gain, tokens, cot, act, dgate, dup, places, plans, sizes, collective_id):
    plans = alive(plans, sizes)
    n, width = act.shape
    rows = D // places
    per = max(1, LANES * 3 // rows)
    spec = pl.BlockSpec(memory_space=pltpu.VMEM)
    far = pl.BlockSpec(memory_space=pl.ANY)
    return pl.pallas_call(
        functools.partial(grads_kernel, plans, sizes),
        out_shape=[
            jax.ShapeDtypeStruct(dtok.shape[1:], F32),
            jax.ShapeDtypeStruct(dtok.shape[1:], BF),
            jax.ShapeDtypeStruct((1, D), F32),
            jax.ShapeDtypeStruct((places, 3, rows, width), BF),
        ],
        in_specs=[spec] * 4 + [far] * 5,
        out_specs=[spec] * 3 + [far],
        scratch_shapes=[
            pltpu.VMEM(dtok.shape[1:], F32),
            pltpu.VMEM((2, n, D), BF),
            pltpu.VMEM((2, n, width), BF),
            pltpu.VMEM((2, per, rows, width), BF),
            pltpu.SemaphoreType.DMA((5,)),
            pltpu.SemaphoreType.DMA((2,)),
        ]
        + scatter_scratch([dtok], plans, [F32], sizes),
        compiler_params=pltpu.CompilerParams(
            collective_id=collective_id, has_side_effects=True, vmem_limit_bytes=VMEM_LIMIT
        ),
        cost_estimate=pl.CostEstimate(
            flops=6 * n * D * width, bytes_accessed=100 * 2**20, transcendentals=0
        ),
    )(dtok, mixed, cot_own, gain, tokens, cot, act, dgate, dup)


def forward_kernel(heads, slots, tops, q_ref, kv_ref, o_ref, lse_ref, top_s, sum_s, acc_s):
    def score(keys, a, h):
        return dot_nt(keys, q_ref[a * BLOCK : (a + 1) * BLOCK, h * HEAD_DIM : (h + 1) * HEAD_DIM])

    for a in range(2):
        top_s[...] = jnp.full(top_s.shape, -1e30, F32)
        sum_s[...] = jnp.zeros(sum_s.shape, F32)
        acc_s[...] = jnp.zeros(acc_s.shape, F32)
        count = tops[a] + 1

        def step(keys, values_t):
            ahead = min(3, heads)
            ready = [score(keys, a, h) for h in range(ahead)]
            for h in range(heads):
                s = ready[h]
                if h + ahead < heads:
                    ready.append(score(keys, a, h + ahead))
                old = top_s[h : h + 1, :]
                new = jnp.maximum(old, jnp.max(s, axis=0, keepdims=True))
                p = jnp.exp2((s - new) * SCALE2)
                fade = jnp.exp2((old - new) * SCALE2)
                sum_s[h : h + 1, :] = sum_s[h : h + 1, :] * fade + jnp.sum(p, axis=0, keepdims=True)
                top_s[h : h + 1, :] = new
                acc_s[h] = acc_s[h] * fade + dot_nn(values_t, p.astype(BF))

        def two(i, carry):
            first, second = slots[2 * i], slots[2 * i + 1]
            both = jnp.concatenate([kv_ref[first], kv_ref[second]], axis=0)
            step(both[:, :HEAD_DIM], both[:, HEAD_DIM:].T)
            return carry

        lax.fori_loop(0, count // 2, two, 0)

        @pl.when(count % 2 == 1)
        def _():
            last = kv_ref[slots[count - 1]]
            step(last[:, :HEAD_DIM], last[:, HEAD_DIM:].T)

        for h in range(heads):
            total = sum_s[h : h + 1, :]
            o_ref[a * BLOCK : (a + 1) * BLOCK, h * HEAD_DIM : (h + 1) * HEAD_DIM] = (
                acc_s[h] / total
            ).T
            lse_ref[a, h : h + 1, :] = top_s[h : h + 1, :] * SCALE2 + jnp.log2(total)
        lse_ref[a, heads:8, :] = jnp.zeros((8 - heads, BLOCK), F32)


def attend(slots, tops, q, kv):
    heads = q.shape[1] // HEAD_DIM
    spec = pl.BlockSpec(memory_space=pltpu.VMEM)
    pairs = 33 * BLOCK * BLOCK * heads
    return pl.pallas_call(
        functools.partial(forward_kernel, heads),
        grid_spec=pltpu.PrefetchScalarGridSpec(
            num_scalar_prefetch=2,
            grid=(1,),
            in_specs=[spec] * 2,
            out_specs=[spec] * 2,
            scratch_shapes=[
                pltpu.VMEM((8, BLOCK), F32),
                pltpu.VMEM((8, BLOCK), F32),
                pltpu.VMEM((heads, HEAD_DIM, BLOCK), F32),
            ],
        ),
        out_shape=(
            jax.ShapeDtypeStruct(q.shape, F32),
            jax.ShapeDtypeStruct((2, 8, BLOCK), F32),
        ),
        compiler_params=pltpu.CompilerParams(vmem_limit_bytes=VMEM_LIMIT),
        cost_estimate=pl.CostEstimate(
            flops=pairs * 4 * HEAD_DIM, bytes_accessed=80 * 2**20, transcendentals=pairs
        ),
    )(slots, tops, q, kv)


def backward_kernel(
    heads,
    slots,
    tops,
    q_ref,
    kv_ref,
    do_ref,
    lse_ref,
    o_ref,
    dq_ref,
    dkv_ref,
    dq_s,
    dkv_s,
    delta_s,
):
    dkv_s[...] = jnp.zeros(dkv_s.shape, F32)
    for a in range(2):
        dq_s[...] = jnp.zeros(dq_s.shape, F32)

        def part(ref, h):
            return ref[a * BLOCK : (a + 1) * BLOCK, h * HEAD_DIM : (h + 1) * HEAD_DIM]

        for h in range(heads):
            product = part(do_ref, h).astype(F32) * part(o_ref, h)
            delta_s[h : h + 1, :] = jnp.sum(product.T, axis=0, keepdims=True)

        def one(n, carry):
            slot = slots[n]
            keys, values = kv_ref[slot, :, :HEAD_DIM], kv_ref[slot, :, HEAD_DIM:]
            keys_t = keys.T

            def products(h):
                return dot_nt(keys, part(q_ref, h)), dot_nt(values, part(do_ref, h))

            dk = jnp.zeros((BLOCK, HEAD_DIM), F32)
            dv = jnp.zeros((BLOCK, HEAD_DIM), F32)
            ahead = min(2, heads)
            ready = [products(h) for h in range(ahead)]
            for h in range(heads):
                s, dp = ready[h]
                if h + ahead < heads:
                    ready.append(products(h + ahead))
                p = jnp.exp2(s * SCALE2 - lse_ref[a, h : h + 1, :])
                dv = dv + dot_nn(p.astype(BF), part(do_ref, h))
                ds = (p * (dp - delta_s[h : h + 1, :])).astype(BF)
                dk = dk + dot_nn(ds, part(q_ref, h))
                dq_s[h] = dq_s[h] + dot_nn(keys_t, ds)
            dkv_s[slot, :, :HEAD_DIM] = dkv_s[slot, :, :HEAD_DIM] + dk
            dkv_s[slot, :, HEAD_DIM:] = dkv_s[slot, :, HEAD_DIM:] + dv
            return carry

        lax.fori_loop(0, tops[a] + 1, one, 0)
        for h in range(heads):
            dq_ref[a * BLOCK : (a + 1) * BLOCK, h * HEAD_DIM : (h + 1) * HEAD_DIM] = (
                (dq_s[h] * SCALE).T
            ).astype(BF)
    dkv_ref[:, :, :HEAD_DIM] = (dkv_s[:, :, :HEAD_DIM] * SCALE).astype(BF)
    dkv_ref[:, :, HEAD_DIM:] = dkv_s[:, :, HEAD_DIM:].astype(BF)


def attend_back(slots, tops, q, kv, do, lse, attended):
    heads = q.shape[1] // HEAD_DIM
    spec = pl.BlockSpec(memory_space=pltpu.VMEM)
    pairs = 33 * BLOCK * BLOCK * heads
    return pl.pallas_call(
        functools.partial(backward_kernel, heads),
        grid_spec=pltpu.PrefetchScalarGridSpec(
            num_scalar_prefetch=2,
            grid=(1,),
            in_specs=[spec] * 5,
            out_specs=[spec] * 2,
            scratch_shapes=[
                pltpu.VMEM((heads, HEAD_DIM, BLOCK), F32),
                pltpu.VMEM(kv.shape, F32),
                pltpu.VMEM((8, BLOCK), F32),
            ],
        ),
        out_shape=(
            jax.ShapeDtypeStruct(q.shape, BF),
            jax.ShapeDtypeStruct(kv.shape, BF),
        ),
        compiler_params=pltpu.CompilerParams(vmem_limit_bytes=VMEM_LIMIT),
        cost_estimate=pl.CostEstimate(
            flops=pairs * 10 * HEAD_DIM, bytes_accessed=120 * 2**20, transcendentals=pairs
        ),
    )(slots, tops, q, kv, do, lse, attended)


def inverse_rms(value):
    return lax.rsqrt(jnp.mean(value * value, axis=-1, keepdims=True) + EPS)


def turned(value, cosine, sine):
    return value * cosine + pltpu.roll(value, HEAD_DIM // 2, 1) * sine


def project_kernel(plans, sizes, x_ref, w_ref, gain_ref, bias_ref, cos_ref, sin_ref, *refs):
    packed_ref, _, kv_all_ref, swapped_ref, q_ref, normed_ref, kv_s = refs[:7]
    x = x_ref[...].astype(F32)
    normed_ref[...] = (x * inverse_rms(x) * gain_ref[...]).astype(BF)
    cosine, sine = cos_ref[...], sin_ref[...]
    heads = q_ref.shape[1] // HEAD_DIM

    def product(low, n):
        cols = slice(low * HEAD_DIM, (low + n) * HEAD_DIM)
        return dot_nn(normed_ref[...], w_ref[:, cols]) + bias_ref[:, cols]

    made = product(heads, 2)
    kv_s[:, :HEAD_DIM] = turned(made[:, :HEAD_DIM], cosine, sine).astype(BF)
    kv_s[:, HEAD_DIM:] = made[:, HEAD_DIM:].astype(BF)

    def queries():
        for low in range(0, heads, 2):
            made = product(low, 2)
            for i in range(2):
                part = made[:, i * HEAD_DIM : (i + 1) * HEAD_DIM]
                q_ref[:, (low + i) * HEAD_DIM : (low + i + 1) * HEAD_DIM] = turned(
                    part, cosine, sine
                ).astype(BF)

    gather_kernel(
        plans, sizes, 1, 0, 0, kv_s, packed_ref, kv_all_ref, swapped_ref, *refs[7:], behind=queries
    )


def project(x, w, gain, bias, cosine, sine, packed, after, plans, sizes, collective_id):
    plans = alive(plans, sizes)
    n, width = x.shape[0], w.shape[1]
    spec = pl.BlockSpec(memory_space=pltpu.VMEM)
    far = pl.BlockSpec(memory_space=pl.ANY)
    count = int(np.prod([sizes[a] for a in plans[0][2]]))
    kv = (n, 2 * HEAD_DIM)
    return pl.pallas_call(
        functools.partial(project_kernel, plans, sizes),
        in_specs=[spec] * 6 + [far] * 2,
        out_specs=[spec, far, spec, spec],
        out_shape=[
            jax.ShapeDtypeStruct(s, BF)
            for s in ((count,) + kv, packed.shape, (n, width - 2 * HEAD_DIM), (n, D))
        ],
        scratch_shapes=[
            pltpu.VMEM(kv, BF),
            pltpu.SemaphoreType.DMA((count - 1,)),
            pltpu.SemaphoreType.DMA((count - 1,)),
            pltpu.SemaphoreType.DMA((1,)),
        ]
        + swap_scratch([packed]),
        compiler_params=pltpu.CompilerParams(
            collective_id=collective_id, has_side_effects=True, vmem_limit_bytes=VMEM_LIMIT
        ),
        cost_estimate=pl.CostEstimate(
            flops=2 * n * D * width, bytes_accessed=80 * 2**20, transcendentals=0
        ),
    )(x, w, gain, bias, cosine, sine, packed, after)


def project_back_kernel(
    dq_ref,
    dkv_ref,
    normed_ref,
    x_ref,
    w_ref,
    cos_ref,
    sin_ref,
    back_ref,
    grad_ref,
    dnormed_ref,
    gain_grad_ref,
    bias_grad_ref,
    swapped_ref,
    dpre_s,
    *sems,
):
    (item,) = swaps_of([back_ref], [swapped_ref], sems)
    greet(("y", "c"), {"y": 2, "c": 2}, True)
    item.start()
    cosine, sine = cos_ref[...], -sin_ref[...]
    heads = dq_ref.shape[1] // HEAD_DIM
    for h in range(heads + 1):
        cols = slice(h * HEAD_DIM, (h + 1) * HEAD_DIM)
        part = dq_ref[:, cols] if h < heads else dkv_ref[:, :HEAD_DIM]
        dpre_s[:, cols] = turned(part.astype(F32), cosine, sine).astype(BF)
    dpre_s[:, (heads + 1) * HEAD_DIM :] = dkv_ref[:, HEAD_DIM:]
    bias_grad_ref[...] = jnp.sum(dpre_s[...].astype(F32), axis=0, keepdims=True)
    x = x_ref[...].astype(F32)
    scale = inverse_rms(x)
    step = 2 * HEAD_DIM
    for low in range(0, D, step):
        cols = slice(low, low + step)
        dnormed = dot_nt(dpre_s[...], w_ref[cols, :])
        dnormed_ref[:, cols] = dnormed.astype(BF)
        gain_grad_ref[:, cols] = jnp.sum(
            dnormed * (x[:, cols] * scale), axis=0, keepdims=True
        )
        if len(grad_ref.shape) == 2:
            grad_ref[cols, :] = dot_tn(normed_ref[:, cols], dpre_s[...]).astype(BF)
    if len(grad_ref.shape) == 4:
        blk, heads, rows, width = grad_ref.shape
        step = 3 * LANES
        for low in range(0, D, step):
            made = dot_tn(normed_ref[:, low : low + step], dpre_s[...]).astype(BF)
            half, start = divmod(low // rows, blk)
            grad_ref[start : start + step // rows, half] = made.reshape(step // rows, rows, width)
    item.wait()


def project_back(dq, dkv, normed, x, w, cosine, sine, back, blk, rows, collective_id):
    n, width = x.shape[0], w.shape[1]
    split = rows % 16 == 0
    made = (blk, 2, rows, width) if split else (D, width)
    spec = pl.BlockSpec(memory_space=pltpu.VMEM)
    far = pl.BlockSpec(memory_space=pl.ANY)
    return pl.pallas_call(
        project_back_kernel,
        in_specs=[spec] * 7 + [far],
        out_specs=[spec] * 4 + [far],
        out_shape=[
            jax.ShapeDtypeStruct(made, BF),
            jax.ShapeDtypeStruct((n, D), BF),
            jax.ShapeDtypeStruct((1, D), F32),
            jax.ShapeDtypeStruct((1, width), F32),
            jax.ShapeDtypeStruct(back.shape, back.dtype),
        ],
        scratch_shapes=[pltpu.VMEM((n, width), BF)] + swap_scratch([back]),
        compiler_params=pltpu.CompilerParams(
            collective_id=collective_id, has_side_effects=True, vmem_limit_bytes=VMEM_LIMIT
        ),
        cost_estimate=pl.CostEstimate(
            flops=4 * n * D * width, bytes_accessed=16 * 2**20, transcendentals=0
        ),
    )(dq, dkv, normed, x, w, cosine, sine, back)


def exchange_back_kernel(sizes, dproj_ref, w_ref, attn_ref, dout_ref, o_ref, pair_s, sum_s, *sems):
    send_sems, recv_sems = sems
    greet(("head",), sizes)
    me, count = lax.axis_index("head"), sizes["head"]
    tok = dproj_ref.shape[0]
    copies = []
    for d in range(1, count):
        copy = remote(
            dproj_ref, pair_s.at[me], send_sems.at[d - 1], recv_sems.at[d - 1], "head", d, sizes
        )
        copy.start()
        copies.append(copy)
    cols = 2 * LANES

    def use(place, grads, fresh, last):
        rows = pl.ds(pl.multiple_of(place * tok, tok), tok)
        for low in range(0, w_ref.shape[0], cols):
            part = slice(low, low + cols)
            dout_ref[rows, part] = dot_nt(grads, w_ref[part, :]).astype(BF)
            made = dot_tn(attn_ref[rows, part], grads)
            if not fresh:
                made = made + sum_s[part, :]
            if last:
                o_ref[part, :] = made.astype(BF)
            else:
                sum_s[part, :] = made

    use(me, dproj_ref[...], True, count == 1)
    for d in range(1, count):
        copies[d - 1].wait_recv()
        place = lax.rem(me + count - d, count)
        use(place, pair_s[place], False, d == count - 1)
    for copy in copies:
        copy.wait_send()


def exchange_back(dproj, w, attn, sizes, collective_id):
    spec = pl.BlockSpec(memory_space=pltpu.VMEM)
    count = sizes["head"]
    return pl.pallas_call(
        functools.partial(exchange_back_kernel, sizes),
        in_specs=[spec] * 3,
        out_specs=[spec] * 2,
        out_shape=[
            jax.ShapeDtypeStruct(attn.shape, BF),
            jax.ShapeDtypeStruct(w.shape, BF),
        ],
        scratch_shapes=[
            pltpu.VMEM((count,) + dproj.shape, BF),
            pltpu.VMEM(w.shape, F32),
            pltpu.SemaphoreType.DMA((count - 1,)),
            pltpu.SemaphoreType.DMA((count - 1,)),
        ],
        compiler_params=pltpu.CompilerParams(
            collective_id=collective_id, has_side_effects=True, vmem_limit_bytes=VMEM_LIMIT
        ),
        cost_estimate=pl.CostEstimate(
            flops=4 * w.size * attn.shape[0], bytes_accessed=40 * 2**20, transcendentals=0
        ),
    )(dproj, w, attn)


def shards(
    sizes,
    hidden,
    cotangent,
    block_order,
    norm1,
    q_weight,
    q_bias,
    k_weight,
    k_bias,
    v_weight,
    v_bias,
    o_weight,
    norm2,
    gate_weight,
    up_weight,
    down_weight,
):
    tok = hidden.shape[0]
    pair = sizes["head"] * tok
    blk = int(np.prod([sizes[a] for a in BLK]))
    seqs = blk // SEQ_SPAN
    place_axes = {1: BLK, 2: BLK[:3], 4: BLK[:2]}[seqs]
    seq_axes = BLK[len(place_axes) :]
    head = lax.axis_index("head")
    place = place_of({}, place_axes, sizes)
    seq = place_of({}, seq_axes, sizes) if seq_axes else 0
    order = lax.dynamic_index_in_dim(block_order, seq, 0, keepdims=False)
    tops = lax.dynamic_slice_in_dim(order, place * 2, 2)
    slots = jnp.argsort(order).astype(jnp.int32)
    positions = (tops[:, None] * tok + jnp.arange(tok, dtype=jnp.int32)[None, :]).reshape(pair)
    frequency = THETA ** (-(jnp.arange(HEAD_DIM // 2, dtype=F32) * 2.0) / HEAD_DIM)
    angles = positions.astype(F32)[:, None] * frequency[None, :]
    cosine, sine = jnp.cos(angles), jnp.sin(angles)
    cosine = jnp.concatenate([cosine, cosine], axis=1)
    sine = jnp.concatenate([-sine, sine], axis=1)

    q_cols = D // 2
    kv_cols = HEAD_DIM
    rows = q_weight.shape[0]
    small = jnp.concatenate([v.astype(BF) for v in (norm1, norm2, q_bias, k_bias, v_bias)])
    small = jnp.pad(small.astype(F32), (0, 8 * LANES - small.shape[0])).reshape(8, LANES)
    parts = sizes["y"] * sizes["c"]
    width = gate_weight.shape[1]
    lanes = -(-width // (LANES * parts)) * LANES
    first = lanes * 6 // 9 // LANES * LANES
    ff_rows = gate_weight.shape[0]

    def along_z(part):
        part = part.reshape(1, 3, parts * ff_rows, part.shape[-1])
        return lax.all_gather(part, live(("g", "z"), sizes), axis=0, tiled=True)

    w_qkv, x_pair, small_all, w_out, packed_one, packed_two = front(
        (q_weight, k_weight, v_weight, o_weight),
        hidden,
        small,
        (down_weight, gate_weight, up_weight),
        first,
        lanes - first,
        [
            (0, None, AXES, AXES, True),
            (1, None, ("head",), ("head",), False),
            (2, None, AXES, AXES, False),
            (3, None, BLK, ("y", "z", "g", "c"), False),
        ],
        sizes,
        1,
    )
    w_out = w_out.reshape(q_cols, D)
    w_qkv = w_qkv.reshape(D, q_cols + 2 * kv_cols)
    x_pair = x_pair.reshape(pair, D)
    small_all = small_all.reshape(-1, 8 * LANES)
    kn = k_bias.shape[0]
    long = small_all[:, : 3 * rows].reshape(-1, 3, rows).transpose(1, 0, 2).reshape(3, D)
    short = small_all[:, 3 * rows : 3 * rows + 2 * kn].reshape(-1, 2, kn)
    short = short.transpose(1, 0, 2).reshape(2, 2 * kv_cols)
    gain_one, gain_two = long[:1], long[1:2]
    bias = jnp.concatenate(
        [
            lax.dynamic_slice_in_dim(v, head * n, n)
            for v, n in ((long[2], q_cols), (short[0], kv_cols), (short[1], kv_cols))
        ]
    )[None]
    far_axes, near_axes = place_axes[:2], place_axes[2:]
    group = ("head", "y", "c")
    cot_all = lax.all_gather(cotangent, group, axis=0, tiled=True)
    kv, mine_one, queries, normed = project(
        x_pair,
        w_qkv,
        gain_one,
        bias,
        cosine,
        sine,
        packed_one,
        cot_all,
        [(0, None, far_axes, far_axes, False)],
        sizes,
        2,
    )
    half = tok // 2
    crossed = [
        ((0, half), group, ("head", "y", "c"), False),
        ((half, half), group, ("y", "head", "c"), False),
    ]
    summed = [
        ((0, half), group, ("c", "head", "y"), False),
        ((half, half), group, ("c", "y", "head"), False),
    ]
    w_feed_one = along_z(mine_one)
    if near_axes:
        (kv,) = gather([kv], [(0, None, near_axes, near_axes, False)], sizes, 10)
    near_count = int(np.prod([sizes[a] for a in near_axes], dtype=int))
    far_count = SEQ_SPAN // near_count
    where = slots // 2
    slots = ((where % near_count) * far_count + where // near_count) * 2 + slots % 2
    kv = kv.reshape(2 * SEQ_SPAN, tok, 2 * HEAD_DIM)
    attended, lse = attend(slots, tops, queries, kv)
    attn_local = attended.astype(BF)
    inputs = hidden.astype(F32)
    mixed_part = dot_nn(attn_local, w_out).reshape(2, tok, D)
    mixed_got, mine_two = gather(
        [mixed_part.astype(BF)],
        [(0, None, ("head",), ("head",), True)],
        sizes,
        3,
        [packed_two],
    )
    w_feed_two = along_z(mine_two)
    mixed = (
        inputs
        + lax.dynamic_index_in_dim(mixed_part, head, 0, keepdims=False)
        + lax.dynamic_index_in_dim(mixed_got, 1 - head, 0, keepdims=False).astype(F32)
    )
    scale_two = inverse_rms(mixed)
    normed_two = (mixed * scale_two * gain_two).astype(BF)
    (tokens,) = gather([normed_two], [(0,) + c for c in crossed], sizes, 4)
    tokens = tokens.reshape(-1, D)

    places = w_feed_one.shape[0]
    act, dgate, dup, branch, dtokens = feed(tokens, cot_all, w_feed_one)
    parts_one = plain_grads(tokens, cot_all, act, dgate, dup, places)
    act, dgate, dup, branch, dtokens = feed(
        tokens, cot_all, w_feed_two, (branch, dtokens), (parts_one,)
    )
    dmixed, dproj, norm2_part, parts_two = feed_grads(
        dtokens.reshape(-1, tok, D),
        mixed,
        cotangent,
        gain_two,
        tokens,
        cot_all,
        act,
        dgate,
        dup,
        places,
        [(0,) + c for c in summed],
        sizes,
        5,
    )
    def collect(grad):
        total = lax.psum_scatter(grad, live(("g", "z"), sizes), scatter_dimension=0, tiled=True)
        return total.reshape(3, parts, ff_rows, grad.shape[-1])

    back_one = collect(parts_one)

    dout, o_part = exchange_back(dproj, w_out, attn_local, sizes, 6)

    dq, dkv_parts = attend_back(slots, tops, queries, kv, dout, lse, attended)
    dkv, d_out_weight, parts_two = scatter(
        [dkv_parts.reshape(SEQ_SPAN, pair, 2 * HEAD_DIM), o_part.reshape(blk, -1, D)],
        [
            (0, None, near_axes + far_axes, place_axes[::-1], False),
            (1, None, BLK, BLK[::-1], False),
        ],
        [BF, F32],
        sizes,
        7,
        carried=[parts_two],
    )
    back_two = collect(parts_two)
    w_part, dnormed, norm1_part, bias_part, back_one = project_back(
        dq, dkv, normed, x_pair, w_qkv, cosine, sine, back_one, blk, rows, 11
    )
    if w_part.ndim == 2:
        w_part = w_part.reshape(2, blk, rows, -1).transpose(1, 0, 2, 3)
    norm1_part, bias_part = norm1_part[0], bias_part[0]
    own = (jnp.arange(2) == head).astype(F32)[:, None]

    def owners(vector):
        return vector.reshape(2, blk, -1).transpose(1, 0, 2)

    def owned(vector):
        return owners((own * vector[None, :]).reshape(-1))

    small_grads = jnp.stack(
        [
            jnp.pad(part, ((0, 0), (0, 0), (0, LANES - part.shape[2])))
            for part in (
                owners(norm1_part),
                owners(norm2_part[0]),
                owned(bias_part[:q_cols]),
                owned(bias_part[q_cols : q_cols + kv_cols]),
                owned(bias_part[q_cols + kv_cols :]),
            )
        ]
        + [jnp.zeros((blk, 2, LANES), F32)] * 3,
        axis=2,
    )
    small_grads = small_grads.transpose(1, 0, 2, 3).reshape(2 * blk, 8, LANES)
    w_grads, small_sum, dnormed_sum, branch_sum = scatter(
        [
            w_part,
            small_grads,
            dnormed.reshape(2, tok, D),
            branch.reshape(-1, tok, D),
        ],
        [
            (0, None, BLK, BLK[::-1], True),
            (1, None, AXES, AXES[::-1], False),
            (2, None, ("head",), ("head",), False),
        ]
        + [(3,) + c for c in summed],
        [F32] * 4,
        sizes,
        8,
    )
    d_query, d_key, d_value, output, hidden_grad, d_down, d_gate, d_up = write_outputs(
        w_grads,
        dnormed_sum,
        branch_sum,
        dmixed,
        hidden,
        mixed,
        gain_one,
        [back_one] + list(swap([back_two], w_grads, 9)),
        width,
    )
    return (
        output,
        hidden_grad,
        small_sum[0, :rows],
        d_query,
        small_sum[2, :rows],
        d_key,
        small_sum[3, :kn],
        d_value,
        small_sum[4, :kn],
        d_out_weight,
        small_sum[1, :rows],
        d_gate,
        d_up,
        d_down,
    )


def solution(mesh):
    heads, blk = mesh.devices.shape
    split = jax.sharding.Mesh(mesh.devices.reshape(heads, blk // 16, 4, 2, 2), AXES)
    sizes = dict(split.shape)
    rows = P(AXES, None)
    vector = P(AXES)
    feed = P(BLK, "head")
    return jax.shard_map(
        functools.partial(shards, sizes),
        mesh=split,
        in_specs=(
            rows,
            rows,
            P(),
            vector,
            rows,
            vector,
            rows,
            vector,
            rows,
            vector,
            rows,
            vector,
            feed,
            feed,
            feed,
        ),
        out_specs=(
            rows,
            rows,
            vector,
            rows,
            vector,
            rows,
            vector,
            rows,
            vector,
            rows,
            vector,
            feed,
            feed,
            feed,
        ),
        check_vma=False,
    )
```

```python
import functools

import jax
import jax.numpy as jnp
import numpy as np
from jax import lax
from jax.experimental import pallas as pl
from jax.experimental.pallas import tpu as pltpu
from jax.sharding import PartitionSpec as P

D = 1536
QHEADS = 12
KVHEADS = 2
HEAD_DIM = 128
SEQ_SPAN = 16
BLOCK = 256

EPS = 1e-06
THETA = 1000000.0
SCALE = HEAD_DIM**-0.5
LOG2E = 1.4426950408889634
SCALE2 = SCALE * LOG2E
BF = jnp.bfloat16
F32 = jnp.float32
MESH = pl.DeviceIdType.MESH
VMEM_LIMIT = 56 * 2**20
AXES = ("head", "g", "z", "y", "c")
BLK = ("g", "z", "y", "c")
LANES = 128


def dot_nn(a, b):
    return lax.dot_general(a, b, (((1,), (0,)), ((), ())), preferred_element_type=F32)


def dot_nt(a, b):
    return lax.dot_general(a, b, (((1,), (1,)), ((), ())), preferred_element_type=F32)


def dot_tn(a, b):
    return lax.dot_general(a, b, (((0,), (0,)), ((), ())), preferred_element_type=F32)


def live(axes, sizes):
    return tuple(a for a in axes if sizes[a] > 1)


def greet(axes, sizes, diagonal=False):
    barrier = pltpu.get_barrier_semaphore()
    count = 0
    if diagonal:
        pl.semaphore_signal(barrier, inc=1, device_id=across(3), device_id_type=MESH)
        count += 1
    for a in axes:
        me = lax.axis_index(a)
        for d in range(1, sizes[a]):
            pl.semaphore_signal(
                barrier,
                inc=1,
                device_id={a: lax.rem(me + d, sizes[a])},
                device_id_type=MESH,
            )
            count += 1
    pl.semaphore_wait(barrier, count)


def across(d):
    y, c = lax.axis_index("y"), lax.axis_index("c")
    return {"y": 1 - y if d & 2 else y, "c": 1 - c if d & 1 else c}


class Swap:
    def __init__(self, x, out, send_sems, recv_sems, local_sem):
        me = lax.axis_index("y") * 2 + lax.axis_index("c")
        self.kept = pltpu.make_async_copy(x.at[:, me], out.at[:, me], local_sem)
        self.copies = []
        for d in range(1, 4):
            to = across(d)
            self.copies.append(
                pltpu.make_async_remote_copy(
                    src_ref=x.at[:, to["y"] * 2 + to["c"]],
                    dst_ref=out.at[:, me],
                    send_sem=send_sems.at[d - 1],
                    recv_sem=recv_sems.at[d - 1],
                    device_id=to,
                    device_id_type=MESH,
                )
            )

    def start(self):
        for copy in self.copies:
            copy.start()
        self.kept.start()

    def wait(self):
        self.kept.wait()
        for copy in self.copies:
            copy.wait()


def swap_scratch(swaps):
    if not swaps:
        return []
    return [pltpu.SemaphoreType.DMA((3 * len(swaps),))] * 2 + [
        pltpu.SemaphoreType.DMA((len(swaps),))
    ]


def swaps_of(xs, outs, sems):
    return [
        Swap(
            x,
            out,
            sems[0].at[pl.ds(3 * i, 3)],
            sems[1].at[pl.ds(3 * i, 3)],
            sems[2].at[i],
        )
        for i, (x, out) in enumerate(zip(xs, outs))
    ]


def place_of(offsets, axes, sizes):
    value = 0
    for a in axes:
        me = lax.axis_index(a)
        off = offsets.get(a, 0)
        value = value * sizes[a] + (lax.rem(me + off, sizes[a]) if off else me)
    return value


def remote(src, dst, send, recv, axis, distance, sizes):
    to = lax.rem(lax.axis_index(axis) + distance, sizes[axis])
    return pltpu.make_async_remote_copy(
        src_ref=src,
        dst_ref=dst,
        send_sem=send,
        recv_sem=recv,
        device_id={axis: to},
        device_id_type=MESH,
    )


def gather_kernel(plans, sizes, swap_count, waited, carried, *refs, ahead=None, behind=None):
    count = max(p[0] for p in plans) + 1
    xs, refs = refs[:count], refs[count:]
    swap_xs, refs = refs[:swap_count], refs[swap_count + waited :]
    outs, refs = refs[:count], refs[count:]
    swap_outs, refs = refs[:swap_count], refs[swap_count + carried :]
    send_sems, recv_sems, local_sems = refs[:3]
    swaps = swaps_of(swap_xs, swap_outs, refs[3:])
    used = {a: (sizes[a] if any(a in p[3] for p in plans) else 1) for a in AXES}
    if swaps:
        used.update(y=sizes["y"], c=sizes["c"])
    greet(live(AXES, used), sizes, bool(swaps))

    def cut(ref, rows):
        return ref if rows is None else ref.at[pl.ds(*rows)]

    def source(plan, place):
        i, rows, layout, phases, split = plan
        return cut(xs[i].at[place] if split else xs[i], rows)

    def landed(slot, number):
        axis = plans[0][3][0]
        return remote(slot, slot, send_sems.at[number], recv_sems.at[number], axis, 0, sizes)

    sends, kept, queue = [], [], []
    sem = 0
    for j, plan in enumerate(plans):
        i, rows, layout, phases, split = plan
        mine = source(plan, lax.axis_index(phases[0]))
        slot = cut(outs[i].at[place_of({}, layout, sizes)], rows)
        copy = pltpu.make_async_copy(mine, slot, local_sems.at[j])
        queue.append((plan, {}, -1, None))
        kept.append(copy)
    at = 0
    ends = []
    while at < len(queue):
        plan, offsets, phase, arrived = queue[at]
        at += 1
        i, rows, layout, phases, split = plan
        slot = cut(outs[i].at[place_of(offsets, layout, sizes)], rows)
        if arrived is None:
            src = source(plan, lax.axis_index(phases[0]))
        else:
            src = slot
            landed(slot, arrived).wait_recv()
        for p in range(phase + 1, len(phases)):
            a = phases[p]
            for d in range(1, sizes[a]):
                piece = src
                if split and p == 0:
                    piece = source(plan, lax.rem(lax.axis_index(a) + d, sizes[a]))
                copy = remote(piece, slot, send_sems.at[sem], recv_sems.at[sem], a, d, sizes)
                copy.start()
                sends.append(copy)
                later = dict(offsets)
                later[a] = sizes[a] - d
                if p + 1 < len(phases):
                    queue.append((plan, later, p, sem))
                else:
                    ends.append((plan, later, sem))
                sem += 1
        if at == len(plans):
            if ahead is not None:
                ahead()
            for copy in kept + swaps:
                copy.start()
            if behind is not None:
                behind()
    for (i, rows, layout, phases, split), offsets, arrived in ends:
        landed(cut(outs[i].at[place_of(offsets, layout, sizes)], rows), arrived).wait_recv()
    for copy in kept + swaps:
        copy.wait()
    for copy in sends:
        copy.wait_send()


def gather(arrays, plans, sizes, collective_id, swaps=(), after=(), carried=()):
    plans = [
        (i, rows, live(layout, sizes), live(phases, sizes), split)
        for i, rows, layout, phases, split in plans
    ]
    counts = [int(np.prod([sizes[a] for a in p[2]])) for p in plans]
    total = sum(counts) - len(counts)
    shapes = []
    for i, x in enumerate(arrays):
        n, split = next((c, p[4]) for c, p in zip(counts, plans) if p[0] == i)
        shapes.append(jax.ShapeDtypeStruct((n,) + (x.shape[1:] if split else x.shape), x.dtype))
    spec = pl.BlockSpec(memory_space=pltpu.VMEM)
    far = pl.BlockSpec(memory_space=pl.ANY)
    specs = [spec] * len(arrays) + [far] * len(swaps)
    moved = sum(int(np.prod(s.shape)) * s.dtype.itemsize for s in shapes)
    return pl.pallas_call(
        functools.partial(
            gather_kernel, plans, sizes, len(swaps), len(after) + len(carried), len(carried)
        ),
        out_shape=shapes + [jax.ShapeDtypeStruct(x.shape, x.dtype) for x in (*swaps, *carried)],
        in_specs=specs + [far] * (len(after) + len(carried)),
        out_specs=specs + [far] * len(carried),
        input_output_aliases={
            len(specs) + len(after) + i: len(specs) + i for i in range(len(carried))
        },
        scratch_shapes=[
            pltpu.SemaphoreType.DMA((total,)),
            pltpu.SemaphoreType.DMA((total,)),
            pltpu.SemaphoreType.DMA((len(plans),)),
        ]
        + swap_scratch(swaps),
        compiler_params=pltpu.CompilerParams(
            collective_id=collective_id, has_side_effects=True, vmem_limit_bytes=VMEM_LIMIT
        ),
        cost_estimate=pl.CostEstimate(flops=0, bytes_accessed=20 * moved, transcendentals=0),
    )(*arrays, *swaps, *after, *carried)


def front_kernel(plans, sizes, *refs):
    q_ref, k_ref, v_ref, o_ref, hidden_ref, small_ref = refs[:6]
    feeds, refs = refs[6:9], refs[9:]
    outs, first_ref, second_ref, refs = refs[:4], refs[4], refs[5], refs[6:]
    halves_s, o_s, feed_s, feed_sems = refs[:4]
    loads = [
        pltpu.make_async_copy(feeds[m], feed_s.at[m], feed_sems.at[m]) for m in range(len(feeds))
    ]
    for copy in loads:
        copy.start()
    heads = halves_s.shape[0]
    q_cols, kv_cols = q_ref.shape[1] // heads, k_ref.shape[1] // heads
    for i in range(heads):
        halves_s[i, :, :q_cols] = q_ref[:, i * q_cols : (i + 1) * q_cols].astype(BF)
        cols = slice(i * kv_cols, (i + 1) * kv_cols)
        halves_s[i, :, q_cols : q_cols + kv_cols] = k_ref[:, cols].astype(BF)
        halves_s[i, :, q_cols + kv_cols :] = v_ref[:, cols].astype(BF)
    o_s[...] = o_ref[...].astype(BF)

    def pack():
        first, second = first_ref.shape[-1], second_ref.shape[-1]
        for m in range(len(feeds)):
            loads[m].wait()
            rows, width = feed_s.shape[1:]
            for i in range(first_ref.shape[1]):
                low = i * (first + second)
                for ref, n in ((first_ref, first), (second_ref, second)):
                    real = min(n, width - low)
                    ref[m, i, :, :real] = feed_s[m, :, low : low + real].astype(BF)
                    if real < n:
                        ref[m, i, :, real:] = jnp.zeros((rows, n - real), BF)
                    low += n

    gather_kernel(
        plans,
        sizes,
        0,
        0,
        0,
        halves_s,
        hidden_ref,
        small_ref,
        o_s,
        *outs,
        *refs[4:],
        ahead=pack,
    )


def front(weights, hidden, small, feeds, first, second, plans, sizes, collective_id):
    plans = alive(plans, sizes)
    heads, rows = sizes["head"], weights[0].shape[0]
    halves = jax.ShapeDtypeStruct((heads, rows, sum(w.shape[1] for w in weights[:3]) // heads), BF)
    out = jax.ShapeDtypeStruct(weights[3].shape, BF)
    arrays = [halves, hidden, small, out]
    counts = [int(np.prod([sizes[a] for a in p[2]])) for p in plans]
    total = sum(counts) - len(counts)
    shapes = [
        jax.ShapeDtypeStruct((n,) + (x.shape[1:] if p[4] else x.shape), x.dtype)
        for n, x, p in zip(counts, arrays, plans)
    ]
    ff_rows = feeds[0].shape[0]
    blocks = [jax.ShapeDtypeStruct((3, 4, ff_rows, n), BF) for n in (first, second)]
    spec = pl.BlockSpec(memory_space=pltpu.VMEM)
    return pl.pallas_call(
        functools.partial(front_kernel, plans, sizes),
        out_shape=shapes + blocks,
        in_specs=[spec] * 6 + [pl.BlockSpec(memory_space=pl.ANY)] * 3,
        out_specs=[spec] * 6,
        scratch_shapes=[
            pltpu.VMEM(halves.shape, BF),
            pltpu.VMEM(out.shape, BF),
            pltpu.VMEM((3,) + feeds[0].shape, F32),
            pltpu.SemaphoreType.DMA((3,)),
            pltpu.SemaphoreType.DMA((total,)),
            pltpu.SemaphoreType.DMA((total,)),
            pltpu.SemaphoreType.DMA((len(plans),)),
        ],
        compiler_params=pltpu.CompilerParams(
            collective_id=collective_id, has_side_effects=True, vmem_limit_bytes=VMEM_LIMIT
        ),
        cost_estimate=pl.CostEstimate(flops=0, bytes_accessed=100 * 2**20, transcendentals=0),
    )(*weights, hidden, small, *feeds)


def offset_keys(axes, sizes):
    keys = [{}]
    for a in axes:
        keys = [dict(k, **{a: d}) for k in keys for d in list(range(1, sizes[a])) + [0]]
    return keys


def scatter_kernel(plans, sizes, *refs, between=None, held=None, held_sems=None):
    count = max(p[0] for p in plans) + 1
    xs, outs = refs[:count], refs[count : 2 * count]
    held = held or {}
    at = 2 * count
    bufs = []
    for _, _, _, phases, swap in plans:
        n = len(phases)
        bufs.append((refs[at : at + n], refs[at + n : at + 2 * n]))
        at += 2 * n
    send_sems, recv_sems, local_sems = refs[at:]
    used = {
        a: (sizes[a] if any(a in p[3] or (p[4] and a == "head") for p in plans) else 1)
        for a in AXES
    }
    loads = {}
    for j, (i, rows, layout, phases, swap) in enumerate(plans):
        if i not in held:
            continue
        for key in offset_keys(phases[1:], sizes):
            place = place_of(key, layout, sizes)
            src, dst = xs[i].at[place], held[i].at[place]
            if rows is not None:
                src, dst = src.at[pl.ds(*rows)], dst.at[pl.ds(*rows)]
            copy = pltpu.make_async_copy(src, dst, held_sems.at[len(loads)])
            copy.start()
            loads[j, tuple(key.get(a, 0) for a in phases[1:])] = copy
    greet(live(AXES, used), sizes)
    sem = 0
    sends = []
    arrivals = [dict() for _ in plans]

    def number(offsets, axes):
        value = 0
        for a in axes:
            value = value * sizes[a] + offsets.get(a, 0)
        return value

    def block_of(j, offsets, near=False):
        i, rows, layout, phases, swap = plans[j]
        block = (held.get(i, xs[i]) if near else xs[i]).at[place_of(offsets, layout, sizes)]
        return block if rows is None else block.at[pl.ds(*rows)]

    def total_of(j, offsets, phase):
        phases = plans[j][3]
        if plans[j][0] in held:
            loads[j, tuple(offsets.get(a, 0) for a in phases[1:])].wait()
        total = block_of(j, offsets, True)[...].astype(F32)
        for q in range(phase):
            rest = phases[q + 1 :]
            for d in range(1, sizes[phases[q]]):
                s = arrivals[j].pop((q, d, number(offsets, rest)))
                buf = bufs[j][1][q].at[d - 1, number(offsets, rest)]
                remote(buf, buf, send_sems.at[s], recv_sems.at[s], phases[q], 0, sizes).wait_recv()
                total = total + buf[...].astype(F32)
        return total

    depth = max(len(p[3]) for p in plans)
    for phase in range(depth):
        for j, (i, rows, layout, phases, swap) in enumerate(plans):
            if phase >= len(phases):
                continue
            a, rest = phases[phase], phases[phase + 1 :]
            for d in range(1, sizes[a]):
                for key in offset_keys(rest, sizes):
                    offsets = dict(key)
                    offsets[a] = d
                    where = number(key, rest)
                    if phase == 0:
                        src = block_of(j, offsets)
                    else:
                        src = bufs[j][0][phase].at[d - 1, where]
                        src[...] = total_of(j, offsets, phase).astype(src.dtype)
                    dst = bufs[j][1][phase].at[d - 1, where]
                    copy = remote(src, dst, send_sems.at[sem], recv_sems.at[sem], a, d, sizes)
                    copy.start()
                    sends.append(copy)
                    arrivals[j][(phase, d, where)] = sem
                    sem += 1
        if between is not None:
            between(phase)
    late = []
    for j, (i, rows, layout, phases, swap) in enumerate(plans):
        total = total_of(j, {}, len(phases))
        if swap:
            hold, out = bufs[j][0][0], outs[i]
            hold[...] = total.astype(hold.dtype)
            me = lax.axis_index("head")
            copy = pltpu.make_async_copy(hold.at[me], out.at[me], local_sems.at[j])
            copy.start()
            late.append((copy, None))
            for d in range(1, sizes["head"]):
                to = lax.rem(me + d, sizes["head"])
                copy = remote(
                    hold.at[to], out.at[me], send_sems.at[sem], recv_sems.at[sem], "head", d, sizes
                )
                copy.start()
                sends.append(copy)
                late.append((out.at[lax.rem(me + sizes["head"] - d, sizes["head"])], sem))
                sem += 1
        elif rows is None:
            outs[i][...] = total.astype(outs[i].dtype)
        else:
            outs[i][pl.ds(*rows)] = total.astype(outs[i].dtype)
    for item, s in late:
        if s is None:
            item.wait()
        else:
            remote(item, item, send_sems.at[s], recv_sems.at[s], "head", 0, sizes).wait_recv()
    for copy in sends:
        copy.wait_send()


def scatter_scratch(arrays, plans, out_types, sizes):
    scratch, total = [], 0
    for i, rows, layout, phases, swap in plans:
        x, kind = arrays[i], out_types[i]
        block = x.shape[1:] if rows is None else (rows[1],) + x.shape[2:]
        send_bufs, recv_bufs = [], []
        for p, a in enumerate(phases):
            rest = int(np.prod([sizes[b] for b in phases[p + 1 :]], dtype=int))
            shape = (sizes[a] - 1, rest) + block
            recv_bufs.append(pltpu.VMEM(shape, x.dtype))
            if p == 0:
                send_bufs.append(pltpu.VMEM(block if swap else (8, LANES), kind if swap else F32))
            else:
                send_bufs.append(pltpu.VMEM(shape, x.dtype))
            total += (sizes[a] - 1) * rest
        scratch += send_bufs + recv_bufs
        if swap:
            total += sizes["head"] - 1
    return scratch + [
        pltpu.SemaphoreType.DMA((total,)),
        pltpu.SemaphoreType.DMA((total,)),
        pltpu.SemaphoreType.DMA((len(plans),)),
    ]


def held_scratch(arrays, plans, far, sizes):
    count = 0
    for i, _, _, phases, _ in plans:
        if i in far:
            count += int(np.prod([sizes[a] for a in phases[1:]], dtype=int))
    return [pltpu.VMEM(arrays[i].shape, arrays[i].dtype) for i in far] + [
        pltpu.SemaphoreType.DMA((count,))
    ]


def alive(plans, sizes):
    return [
        (i, rows, live(layout, sizes), live(phases, sizes), flag)
        for i, rows, layout, phases, flag in plans
    ]


def scatter_and_wait_kernel(plans, sizes, arrays, waited, carried, far, *refs):
    xs, refs = refs[:arrays], refs[arrays + waited :]
    outs, refs, held = refs[:arrays], refs[arrays + carried :], {}
    if far:
        held = dict(zip(far, refs[-len(far) - 1 : -1]))
        refs, held_sems = refs[: -len(far) - 1], refs[-1]
        scatter_kernel(plans, sizes, *xs, *outs, *refs, held=held, held_sems=held_sems)
    else:
        scatter_kernel(plans, sizes, *xs, *outs, *refs)


def scatter(arrays, plans, out_types, sizes, collective_id, after=(), carried=()):
    plans = alive(plans, sizes)
    shapes = [jax.ShapeDtypeStruct(x.shape[1:], kind) for x, kind in zip(arrays, out_types)]
    spec = pl.BlockSpec(memory_space=pltpu.VMEM)
    far = pl.BlockSpec(memory_space=pl.ANY)
    big = tuple(i for i, x in enumerate(arrays) if x.dtype == BF)
    moved = sum(int(np.prod(x.shape)) * x.dtype.itemsize for x in arrays)
    return pl.pallas_call(
        functools.partial(
            scatter_and_wait_kernel,
            plans,
            sizes,
            len(arrays),
            len(after) + len(carried),
            len(carried),
            big,
        ),
        out_shape=shapes + [jax.ShapeDtypeStruct(x.shape, x.dtype) for x in carried],
        in_specs=[far if i in big else spec for i in range(len(arrays))] + [far] * (len(after) + len(carried)),
        out_specs=[spec] * len(arrays) + [far] * len(carried),
        input_output_aliases={
            len(arrays) + len(after) + i: len(arrays) + i for i in range(len(carried))
        },
        scratch_shapes=scatter_scratch(arrays, plans, out_types, sizes)
        + (held_scratch(arrays, plans, big, sizes) if big else []),
        compiler_params=pltpu.CompilerParams(
            collective_id=collective_id, has_side_effects=True, vmem_limit_bytes=VMEM_LIMIT
        ),
        cost_estimate=pl.CostEstimate(flops=0, bytes_accessed=20 * moved, transcendentals=0),
    )(*arrays, *after, *carried)


def swap_kernel(count, *refs):
    items = swaps_of(refs[:count], refs[count + 1 : 2 * count + 1], refs[2 * count + 1 :])
    greet(("y", "c"), {"y": 2, "c": 2}, True)
    for item in items:
        item.start()
    for item in items:
        item.wait()


def swap(xs, last, collective_id):
    far = pl.BlockSpec(memory_space=pl.ANY)
    n = len(xs)
    return pl.pallas_call(
        functools.partial(swap_kernel, n),
        out_shape=[jax.ShapeDtypeStruct(x.shape, x.dtype) for x in xs],
        in_specs=[far] * (n + 1),
        out_specs=[far] * n,
        scratch_shapes=swap_scratch(xs),
        compiler_params=pltpu.CompilerParams(
            collective_id=collective_id, has_side_effects=True, vmem_limit_bytes=VMEM_LIMIT
        ),
    )(*xs, last)


def outputs_kernel(*refs):
    w_ref, dnormed_ref, branch_ref, dmixed_ref, x_ref, mixed_ref, gain_ref = refs[:7]
    parts, refs = refs[7:9], refs[9:]
    q_ref, k_ref, v_ref, out_ref, hidden_ref = refs[:5]
    feeds = refs[5:]
    heads = w_ref.shape[0]
    q_cols = q_ref.shape[1] // heads
    for i in range(heads):
        cols = slice(i * HEAD_DIM, (i + 1) * HEAD_DIM)
        q_ref[:, i * q_cols : (i + 1) * q_cols] = w_ref[i, :, :q_cols]
        k_ref[:, cols] = w_ref[i, :, q_cols : q_cols + HEAD_DIM]
        v_ref[:, cols] = w_ref[i, :, q_cols + HEAD_DIM :]
    out_ref[...] = (mixed_ref[...] + branch_ref[...]).astype(BF)
    x = x_ref[...].astype(F32)
    scale = inverse_rms(x)
    z = x * scale
    u = gain_ref[...] * dnormed_ref[...]
    hidden_ref[...] = (
        dmixed_ref[...] + scale * (u - z * jnp.mean(z * u, axis=-1, keepdims=True))
    ).astype(BF)
    width = feeds[0].shape[1]
    lanes = sum(part.shape[-1] for part in parts)
    for m, feed_ref in enumerate(feeds):
        for i in range(parts[0].shape[1]):
            low = i * lanes
            for part in parts:
                n = part.shape[-1]
                real = min(n, width - low)
                if real > 0:
                    feed_ref[:, low : low + real] = part[m, i, :, :real].astype(F32)
                low += n


def write_outputs(w, dnormed, branch, dmixed, x, mixed, gain, parts, width):
    heads, rows, inner = w.shape
    tok, ff_rows = x.shape[0], parts[0].shape[2]
    steps = 2 if rows % 16 == 0 and ff_rows % 32 == 0 else 1

    def rows_of(shape, dim):
        block = tuple(n // steps if i == dim else n for i, n in enumerate(shape))
        return pl.BlockSpec(block, lambda i: tuple(i if k == dim else 0 for k in range(len(shape))))

    kinds = [
        ((rows, heads * (inner - 2 * HEAD_DIM)), F32),
        ((rows, heads * HEAD_DIM), F32),
        ((rows, heads * HEAD_DIM), F32),
        (x.shape, BF),
        (x.shape, BF),
    ] + [((ff_rows, width), F32)] * 3
    return pl.pallas_call(
        outputs_kernel,
        grid=(steps,),
        out_shape=[jax.ShapeDtypeStruct(*k) for k in kinds],
        in_specs=[rows_of(w.shape, 1)]
        + [rows_of(x.shape, 0)] * 5
        + [pl.BlockSpec(gain.shape, lambda i: (0, 0))]
        + [rows_of(part.shape, 2) for part in parts],
        out_specs=[rows_of(shape, 0) for shape, _ in kinds],
        compiler_params=pltpu.CompilerParams(vmem_limit_bytes=VMEM_LIMIT),
        cost_estimate=pl.CostEstimate(flops=0, bytes_accessed=20 * 2**20, transcendentals=0),
    )(w, dnormed, branch, dmixed, x, mixed, gain, *parts)


def feed_kernel(chunks, added, t_ref, c_ref, w_ref, *refs):
    act_ref, dgate_ref, dup_ref, branch_ref, dtok_ref = refs[-5:]
    before = refs[:added]
    tokens, cot = t_ref[...], c_ref[...]
    places, _, rows, width = w_ref.shape
    per = max(1, LANES * 3 // rows)

    def products(j):
        low, n = chunks[j]

        def weight(m):
            return w_ref[:, m, :, low : low + n].reshape(D, n)

        return dot_nn(tokens, weight(1)), dot_nn(tokens, weight(2)), dot_nn(cot, weight(0))

    ready = [products(0)]
    for j, (low, n) in enumerate(chunks):
        gate, up, dact = ready[j]
        if j + 1 < len(chunks):
            ready.append(products(j + 1))
        sig = 1.0 / (1.0 + jnp.exp(-gate))
        silu = gate * sig
        act_ref[:, low : low + n] = (silu * up).astype(BF)
        dgate_ref[:, low : low + n] = (dact * up * (sig + silu * (1.0 - sig))).astype(BF)
        dup_ref[:, low : low + n] = (dact * silu).astype(BF)
    for z in range(0, places, per):
        cols = slice(z * rows, (z + per) * rows)

        def weight(m):
            return w_ref[z : z + per, m].reshape(per * rows, width)

        dtok = dot_nt(dgate_ref[...], weight(1)) + dot_nt(dup_ref[...], weight(2))
        branch = dot_nt(act_ref[...], weight(0))
        if before:
            branch = branch + before[0][:, cols].astype(F32)
            dtok = dtok + before[1][:, cols].astype(F32)
        dtok_ref[:, cols] = dtok.astype(BF)
        branch_ref[:, cols] = branch.astype(BF)


def feed(tokens, cot, weights, before=(), after=()):
    n, width, tile = tokens.shape[0], weights.shape[-1], 256
    chunks = [(i, min(256, width - i)) for i in range(0, width, 256)]
    wide = pl.BlockSpec((tile, D), lambda i: (i, 0))
    inner = pl.BlockSpec((tile, width), lambda i: (i, 0))
    return pl.pallas_call(
        functools.partial(feed_kernel, chunks, len(before)),
        grid=(n // tile,),
        in_specs=[wide, wide, pl.BlockSpec(memory_space=pltpu.VMEM)]
        + [wide] * len(before)
        + [pl.BlockSpec(memory_space=pl.ANY)] * len(after),
        out_specs=[inner, inner, inner, wide, wide],
        out_shape=[jax.ShapeDtypeStruct((n, k), BF) for k in (width, width, width, D, D)],
        compiler_params=pltpu.CompilerParams(vmem_limit_bytes=VMEM_LIMIT),
        cost_estimate=pl.CostEstimate(
            flops=12 * n * D * width, bytes_accessed=40 * 2**20, transcendentals=n * width
        ),
    )(tokens, cot, weights, *before, *after)


def plain_grads_kernel(t_ref, c_ref, act_ref, dgate_ref, dup_ref, grad_ref):
    per, _, rows, width = grad_ref.shape
    for m, (left, right) in enumerate(((c_ref, act_ref), (t_ref, dgate_ref), (t_ref, dup_ref))):
        made = dot_tn(left[...], right[...]).astype(BF)
        grad_ref[:, m] = made.reshape(per, rows, width)


def plain_grads(tokens, cot, act, dgate, dup, places):
    n, width = act.shape
    rows = D // places
    per = max(1, LANES * 3 // rows)
    left = pl.BlockSpec((n, per * rows), lambda k: (0, k))
    right = pl.BlockSpec(memory_space=pltpu.VMEM)
    return pl.pallas_call(
        plain_grads_kernel,
        grid=(places // per,),
        in_specs=[left, left, right, right, right],
        out_specs=pl.BlockSpec((per, 3, rows, width), lambda k: (k, 0, 0, 0)),
        out_shape=jax.ShapeDtypeStruct((places, 3, rows, width), BF),
        compiler_params=pltpu.CompilerParams(vmem_limit_bytes=VMEM_LIMIT),
        cost_estimate=pl.CostEstimate(
            flops=6 * n * D * width, bytes_accessed=40 * 2**20, transcendentals=0
        ),
    )(tokens, cot, act, dgate, dup)


def grads_kernel(plans, sizes, dtok_ref, mixed_ref, cot_ref, gain_ref, *refs):
    t_hbm, c_hbm, act_hbm, dgate_hbm, dup_hbm = refs[:5]
    dmixed_ref, dproj_ref, gain_grad_ref, grad_hbm = refs[5:9]
    sum_ref, left_s, right_s, made_s, load_sems, made_sems = refs[9:15]
    held, held_sems = {0: refs[-2]}, refs[-1]
    per, rows = made_s.shape[1:3]
    cols = per * rows
    loads = [
        pltpu.make_async_copy(c_hbm, left_s.at[0], load_sems.at[0]),
        pltpu.make_async_copy(act_hbm, right_s.at[0], load_sems.at[1]),
        pltpu.make_async_copy(t_hbm, left_s.at[1], load_sems.at[2]),
        pltpu.make_async_copy(dgate_hbm, right_s.at[1], load_sems.at[3]),
        pltpu.make_async_copy(dup_hbm, right_s.at[0], load_sems.at[4]),
    ]
    for copy in loads[:4]:
        copy.start()

    def stored(m, k, slot):
        return pltpu.make_async_copy(
            made_s.at[slot], grad_hbm.at[pl.ds(k * per, per), m], made_sems.at[slot]
        )

    def some(m, low, high, left, right, fresh):
        def one(k, carry):
            slot = lax.rem(k, 2)
            if fresh:
                pl.when(k >= 2)(lambda: stored(m, k, slot).wait())
            else:
                stored(m, k, slot).wait()
            part = left_s[left, :, pl.ds(pl.multiple_of(k * cols, LANES), cols)]
            made_s[slot] = dot_tn(part, right_s[right]).astype(BF).reshape(made_s.shape[1:])
            stored(m, k, slot).start()
            return carry

        lax.fori_loop(low, high, one, 0)

    chunks = D // cols

    def between(phase):
        if phase == 0:
            loads[0].wait()
            loads[1].wait()
            some(0, 0, chunks // 2, 0, 0, True)
        elif phase == 1:
            some(0, chunks // 2, chunks, 0, 0, False)
            loads[4].start()
            loads[2].wait()
            loads[3].wait()
            some(1, 0, chunks, 1, 1, False)
        else:
            loads[4].wait()
            some(2, 0, chunks, 1, 0, False)

    scatter_kernel(
        plans,
        sizes,
        dtok_ref,
        sum_ref,
        *refs[15:-2],
        between=between,
        held=held,
        held_sems=held_sems,
    )
    mixed, dnormed = mixed_ref[...], sum_ref[...]
    scale = inverse_rms(mixed)
    z = mixed * scale
    u = gain_ref[...] * dnormed
    gain_grad_ref[...] = jnp.sum(dnormed * z, axis=0, keepdims=True)
    dmixed = cot_ref[...].astype(F32) + scale * (
        u - z * jnp.mean(z * u, axis=-1, keepdims=True)
    )
    dmixed_ref[...] = dmixed
    dproj_ref[...] = dmixed.astype(BF)
    for slot in range(2):
        stored(2, slot, slot).wait()


def feed_grads(dtok, mixed, cot_own, gain, tokens, cot, act, dgate, dup, places, plans, sizes, collective_id):
    plans = alive(plans, sizes)
    n, width = act.shape
    rows = D // places
    per = max(1, LANES * 3 // rows)
    spec = pl.BlockSpec(memory_space=pltpu.VMEM)
    far = pl.BlockSpec(memory_space=pl.ANY)
    return pl.pallas_call(
        functools.partial(grads_kernel, plans, sizes),
        out_shape=[
            jax.ShapeDtypeStruct(dtok.shape[1:], F32),
            jax.ShapeDtypeStruct(dtok.shape[1:], BF),
            jax.ShapeDtypeStruct((1, D), F32),
            jax.ShapeDtypeStruct((places, 3, rows, width), BF),
        ],
        in_specs=[far] + [spec] * 3 + [far] * 5,
        out_specs=[spec] * 3 + [far],
        scratch_shapes=[
            pltpu.VMEM(dtok.shape[1:], F32),
            pltpu.VMEM((2, n, D), BF),
            pltpu.VMEM((2, n, width), BF),
            pltpu.VMEM((2, per, rows, width), BF),
            pltpu.SemaphoreType.DMA((5,)),
            pltpu.SemaphoreType.DMA((2,)),
        ]
        + scatter_scratch([dtok], plans, [F32], sizes)
        + held_scratch([dtok], plans, (0,), sizes),
        compiler_params=pltpu.CompilerParams(
            collective_id=collective_id, has_side_effects=True, vmem_limit_bytes=VMEM_LIMIT
        ),
        cost_estimate=pl.CostEstimate(
            flops=6 * n * D * width, bytes_accessed=100 * 2**20, transcendentals=0
        ),
    )(dtok, mixed, cot_own, gain, tokens, cot, act, dgate, dup)


def forward_kernel(heads, slots, tops, q_ref, kv_ref, o_ref, lse_ref, top_s, sum_s, acc_s):
    def score(keys, a, h):
        return dot_nt(keys, q_ref[a * BLOCK : (a + 1) * BLOCK, h * HEAD_DIM : (h + 1) * HEAD_DIM])

    for a in range(2):
        top_s[...] = jnp.full(top_s.shape, -1e30, F32)
        sum_s[...] = jnp.zeros(sum_s.shape, F32)
        acc_s[...] = jnp.zeros(acc_s.shape, F32)
        count = tops[a] + 1

        def step(keys, values_t):
            ahead = min(3, heads)
            ready = [score(keys, a, h) for h in range(ahead)]
            for h in range(heads):
                s = ready[h]
                if h + ahead < heads:
                    ready.append(score(keys, a, h + ahead))
                old = top_s[h : h + 1, :]
                new = jnp.maximum(old, jnp.max(s, axis=0, keepdims=True))
                p = jnp.exp2((s - new) * SCALE2)
                fade = jnp.exp2((old - new) * SCALE2)
                sum_s[h : h + 1, :] = sum_s[h : h + 1, :] * fade + jnp.sum(p, axis=0, keepdims=True)
                top_s[h : h + 1, :] = new
                acc_s[h] = acc_s[h] * fade + dot_nn(values_t, p.astype(BF))

        def two(i, carry):
            first, second = slots[2 * i], slots[2 * i + 1]
            both = jnp.concatenate([kv_ref[first], kv_ref[second]], axis=0)
            step(both[:, :HEAD_DIM], both[:, HEAD_DIM:].T)
            return carry

        lax.fori_loop(0, count // 2, two, 0)

        @pl.when(count % 2 == 1)
        def _():
            last = kv_ref[slots[count - 1]]
            step(last[:, :HEAD_DIM], last[:, HEAD_DIM:].T)

        for h in range(heads):
            total = sum_s[h : h + 1, :]
            o_ref[a * BLOCK : (a + 1) * BLOCK, h * HEAD_DIM : (h + 1) * HEAD_DIM] = (
                acc_s[h] / total
            ).T
            lse_ref[a, h : h + 1, :] = top_s[h : h + 1, :] * SCALE2 + jnp.log2(total)
        lse_ref[a, heads:8, :] = jnp.zeros((8 - heads, BLOCK), F32)


def attend(slots, tops, q, kv):
    heads = q.shape[1] // HEAD_DIM
    spec = pl.BlockSpec(memory_space=pltpu.VMEM)
    pairs = 33 * BLOCK * BLOCK * heads
    return pl.pallas_call(
        functools.partial(forward_kernel, heads),
        grid_spec=pltpu.PrefetchScalarGridSpec(
            num_scalar_prefetch=2,
            grid=(1,),
            in_specs=[spec] * 2,
            out_specs=[spec] * 2,
            scratch_shapes=[
                pltpu.VMEM((8, BLOCK), F32),
                pltpu.VMEM((8, BLOCK), F32),
                pltpu.VMEM((heads, HEAD_DIM, BLOCK), F32),
            ],
        ),
        out_shape=(
            jax.ShapeDtypeStruct(q.shape, F32),
            jax.ShapeDtypeStruct((2, 8, BLOCK), F32),
        ),
        compiler_params=pltpu.CompilerParams(vmem_limit_bytes=VMEM_LIMIT),
        cost_estimate=pl.CostEstimate(
            flops=pairs * 4 * HEAD_DIM, bytes_accessed=80 * 2**20, transcendentals=pairs
        ),
    )(slots, tops, q, kv)


def backward_kernel(
    heads,
    slots,
    tops,
    q_ref,
    kv_ref,
    do_ref,
    lse_ref,
    o_ref,
    dq_ref,
    dkv_ref,
    dq_s,
    dkv_s,
    delta_s,
):
    dkv_s[...] = jnp.zeros(dkv_s.shape, F32)
    for a in range(2):
        dq_s[...] = jnp.zeros(dq_s.shape, F32)

        def part(ref, h):
            return ref[a * BLOCK : (a + 1) * BLOCK, h * HEAD_DIM : (h + 1) * HEAD_DIM]

        for h in range(heads):
            product = part(do_ref, h).astype(F32) * part(o_ref, h)
            delta_s[h : h + 1, :] = jnp.sum(product.T, axis=0, keepdims=True)

        def one(n, carry):
            slot = slots[n]
            keys, values = kv_ref[slot, :, :HEAD_DIM], kv_ref[slot, :, HEAD_DIM:]
            keys_t = keys.T

            def products(h):
                return dot_nt(keys, part(q_ref, h)), dot_nt(values, part(do_ref, h))

            dk = jnp.zeros((BLOCK, HEAD_DIM), F32)
            dv = jnp.zeros((BLOCK, HEAD_DIM), F32)
            ahead = min(2, heads)
            ready = [products(h) for h in range(ahead)]
            for h in range(heads):
                s, dp = ready[h]
                if h + ahead < heads:
                    ready.append(products(h + ahead))
                p = jnp.exp2(s * SCALE2 - lse_ref[a, h : h + 1, :])
                dv = dv + dot_nn(p.astype(BF), part(do_ref, h))
                ds = (p * (dp - delta_s[h : h + 1, :])).astype(BF)
                dk = dk + dot_nn(ds, part(q_ref, h))
                dq_s[h] = dq_s[h] + dot_nn(keys_t, ds)
            dkv_s[slot, :, :HEAD_DIM] = dkv_s[slot, :, :HEAD_DIM] + dk
            dkv_s[slot, :, HEAD_DIM:] = dkv_s[slot, :, HEAD_DIM:] + dv
            return carry

        lax.fori_loop(0, tops[a] + 1, one, 0)
        for h in range(heads):
            dq_ref[a * BLOCK : (a + 1) * BLOCK, h * HEAD_DIM : (h + 1) * HEAD_DIM] = (
                (dq_s[h] * SCALE).T
            ).astype(BF)
    dkv_ref[:, :, :HEAD_DIM] = (dkv_s[:, :, :HEAD_DIM] * SCALE).astype(BF)
    dkv_ref[:, :, HEAD_DIM:] = dkv_s[:, :, HEAD_DIM:].astype(BF)


def attend_back(slots, tops, q, kv, do, lse, attended):
    heads = q.shape[1] // HEAD_DIM
    spec = pl.BlockSpec(memory_space=pltpu.VMEM)
    pairs = 33 * BLOCK * BLOCK * heads
    return pl.pallas_call(
        functools.partial(backward_kernel, heads),
        grid_spec=pltpu.PrefetchScalarGridSpec(
            num_scalar_prefetch=2,
            grid=(1,),
            in_specs=[spec] * 5,
            out_specs=[spec] * 2,
            scratch_shapes=[
                pltpu.VMEM((heads, HEAD_DIM, BLOCK), F32),
                pltpu.VMEM(kv.shape, F32),
                pltpu.VMEM((8, BLOCK), F32),
            ],
        ),
        out_shape=(
            jax.ShapeDtypeStruct(q.shape, BF),
            jax.ShapeDtypeStruct(kv.shape, BF),
        ),
        compiler_params=pltpu.CompilerParams(vmem_limit_bytes=VMEM_LIMIT),
        cost_estimate=pl.CostEstimate(
            flops=pairs * 10 * HEAD_DIM, bytes_accessed=120 * 2**20, transcendentals=pairs
        ),
    )(slots, tops, q, kv, do, lse, attended)


def inverse_rms(value):
    return lax.rsqrt(jnp.mean(value * value, axis=-1, keepdims=True) + EPS)


def turned(value, cosine, sine):
    return value * cosine + pltpu.roll(value, HEAD_DIM // 2, 1) * sine


def project_kernel(plans, sizes, x_ref, w_ref, gain_ref, bias_ref, cos_ref, sin_ref, *refs):
    packed_ref, _, kv_all_ref, swapped_ref, q_ref, normed_ref, kv_s = refs[:7]
    x = x_ref[...].astype(F32)
    normed_ref[...] = (x * inverse_rms(x) * gain_ref[...]).astype(BF)
    cosine, sine = cos_ref[...], sin_ref[...]
    heads = q_ref.shape[1] // HEAD_DIM

    def product(low, n):
        cols = slice(low * HEAD_DIM, (low + n) * HEAD_DIM)
        return dot_nn(normed_ref[...], w_ref[:, cols]) + bias_ref[:, cols]

    made = product(heads, 2)
    kv_s[:, :HEAD_DIM] = turned(made[:, :HEAD_DIM], cosine, sine).astype(BF)
    kv_s[:, HEAD_DIM:] = made[:, HEAD_DIM:].astype(BF)

    def queries():
        for low in range(0, heads, 2):
            made = product(low, 2)
            for i in range(2):
                part = made[:, i * HEAD_DIM : (i + 1) * HEAD_DIM]
                q_ref[:, (low + i) * HEAD_DIM : (low + i + 1) * HEAD_DIM] = turned(
                    part, cosine, sine
                ).astype(BF)

    gather_kernel(
        plans, sizes, 1, 0, 0, kv_s, packed_ref, kv_all_ref, swapped_ref, *refs[7:], behind=queries
    )


def project(x, w, gain, bias, cosine, sine, packed, after, plans, sizes, collective_id):
    plans = alive(plans, sizes)
    n, width = x.shape[0], w.shape[1]
    spec = pl.BlockSpec(memory_space=pltpu.VMEM)
    far = pl.BlockSpec(memory_space=pl.ANY)
    count = int(np.prod([sizes[a] for a in plans[0][2]]))
    kv = (n, 2 * HEAD_DIM)
    return pl.pallas_call(
        functools.partial(project_kernel, plans, sizes),
        in_specs=[spec] * 6 + [far] * 2,
        out_specs=[spec, far, spec, spec],
        out_shape=[
            jax.ShapeDtypeStruct(s, BF)
            for s in ((count,) + kv, packed.shape, (n, width - 2 * HEAD_DIM), (n, D))
        ],
        scratch_shapes=[
            pltpu.VMEM(kv, BF),
            pltpu.SemaphoreType.DMA((count - 1,)),
            pltpu.SemaphoreType.DMA((count - 1,)),
            pltpu.SemaphoreType.DMA((1,)),
        ]
        + swap_scratch([packed]),
        compiler_params=pltpu.CompilerParams(
            collective_id=collective_id, has_side_effects=True, vmem_limit_bytes=VMEM_LIMIT
        ),
        cost_estimate=pl.CostEstimate(
            flops=2 * n * D * width, bytes_accessed=80 * 2**20, transcendentals=0
        ),
    )(x, w, gain, bias, cosine, sine, packed, after)


def project_back_kernel(
    dq_ref,
    dkv_ref,
    normed_ref,
    x_ref,
    w_ref,
    cos_ref,
    sin_ref,
    back_ref,
    grad_ref,
    dnormed_ref,
    gain_grad_ref,
    bias_grad_ref,
    swapped_ref,
    dpre_s,
    *sems,
):
    (item,) = swaps_of([back_ref], [swapped_ref], sems)
    greet(("y", "c"), {"y": 2, "c": 2}, True)
    item.start()
    cosine, sine = cos_ref[...], -sin_ref[...]
    heads = dq_ref.shape[1] // HEAD_DIM
    for h in range(heads + 1):
        cols = slice(h * HEAD_DIM, (h + 1) * HEAD_DIM)
        part = dq_ref[:, cols] if h < heads else dkv_ref[:, :HEAD_DIM]
        dpre_s[:, cols] = turned(part.astype(F32), cosine, sine).astype(BF)
    dpre_s[:, (heads + 1) * HEAD_DIM :] = dkv_ref[:, HEAD_DIM:]
    bias_grad_ref[...] = jnp.sum(dpre_s[...].astype(F32), axis=0, keepdims=True)
    x = x_ref[...].astype(F32)
    scale = inverse_rms(x)
    step = 2 * HEAD_DIM
    for low in range(0, D, step):
        cols = slice(low, low + step)
        dnormed = dot_nt(dpre_s[...], w_ref[cols, :])
        dnormed_ref[:, cols] = dnormed.astype(BF)
        gain_grad_ref[:, cols] = jnp.sum(
            dnormed * (x[:, cols] * scale), axis=0, keepdims=True
        )
        if len(grad_ref.shape) == 2:
            grad_ref[cols, :] = dot_tn(normed_ref[:, cols], dpre_s[...]).astype(BF)
    if len(grad_ref.shape) == 4:
        blk, heads, rows, width = grad_ref.shape
        step = 3 * LANES
        for low in range(0, D, step):
            made = dot_tn(normed_ref[:, low : low + step], dpre_s[...]).astype(BF)
            half, start = divmod(low // rows, blk)
            grad_ref[start : start + step // rows, half] = made.reshape(step // rows, rows, width)
    item.wait()


def project_back(dq, dkv, normed, x, w, cosine, sine, back, blk, rows, collective_id):
    n, width = x.shape[0], w.shape[1]
    split = rows % 16 == 0
    made = (blk, 2, rows, width) if split else (D, width)
    spec = pl.BlockSpec(memory_space=pltpu.VMEM)
    far = pl.BlockSpec(memory_space=pl.ANY)
    return pl.pallas_call(
        project_back_kernel,
        in_specs=[spec] * 7 + [far],
        out_specs=[spec] * 4 + [far],
        out_shape=[
            jax.ShapeDtypeStruct(made, BF),
            jax.ShapeDtypeStruct((n, D), BF),
            jax.ShapeDtypeStruct((1, D), F32),
            jax.ShapeDtypeStruct((1, width), F32),
            jax.ShapeDtypeStruct(back.shape, back.dtype),
        ],
        scratch_shapes=[pltpu.VMEM((n, width), BF)] + swap_scratch([back]),
        compiler_params=pltpu.CompilerParams(
            collective_id=collective_id, has_side_effects=True, vmem_limit_bytes=VMEM_LIMIT
        ),
        cost_estimate=pl.CostEstimate(
            flops=4 * n * D * width, bytes_accessed=16 * 2**20, transcendentals=0
        ),
    )(dq, dkv, normed, x, w, cosine, sine, back)


def exchange_back_kernel(sizes, dproj_ref, w_ref, attn_ref, dout_ref, o_ref, pair_s, sum_s, *sems):
    send_sems, recv_sems = sems
    greet(("head",), sizes)
    me, count = lax.axis_index("head"), sizes["head"]
    tok = dproj_ref.shape[0]
    copies = []
    for d in range(1, count):
        copy = remote(
            dproj_ref, pair_s.at[me], send_sems.at[d - 1], recv_sems.at[d - 1], "head", d, sizes
        )
        copy.start()
        copies.append(copy)
    cols = 2 * LANES

    def use(place, grads, fresh, last):
        rows = pl.ds(pl.multiple_of(place * tok, tok), tok)
        for low in range(0, w_ref.shape[0], cols):
            part = slice(low, low + cols)
            dout_ref[rows, part] = dot_nt(grads, w_ref[part, :]).astype(BF)
            made = dot_tn(attn_ref[rows, part], grads)
            if not fresh:
                made = made + sum_s[part, :]
            if last:
                o_ref[part, :] = made.astype(BF)
            else:
                sum_s[part, :] = made

    use(me, dproj_ref[...], True, count == 1)
    for d in range(1, count):
        copies[d - 1].wait_recv()
        place = lax.rem(me + count - d, count)
        use(place, pair_s[place], False, d == count - 1)
    for copy in copies:
        copy.wait_send()


def exchange_back(dproj, w, attn, sizes, collective_id):
    spec = pl.BlockSpec(memory_space=pltpu.VMEM)
    count = sizes["head"]
    return pl.pallas_call(
        functools.partial(exchange_back_kernel, sizes),
        in_specs=[spec] * 3,
        out_specs=[spec] * 2,
        out_shape=[
            jax.ShapeDtypeStruct(attn.shape, BF),
            jax.ShapeDtypeStruct(w.shape, BF),
        ],
        scratch_shapes=[
            pltpu.VMEM((count,) + dproj.shape, BF),
            pltpu.VMEM(w.shape, F32),
            pltpu.SemaphoreType.DMA((count - 1,)),
            pltpu.SemaphoreType.DMA((count - 1,)),
        ],
        compiler_params=pltpu.CompilerParams(
            collective_id=collective_id, has_side_effects=True, vmem_limit_bytes=VMEM_LIMIT
        ),
        cost_estimate=pl.CostEstimate(
            flops=4 * w.size * attn.shape[0], bytes_accessed=40 * 2**20, transcendentals=0
        ),
    )(dproj, w, attn)


def shards(
    sizes,
    hidden,
    cotangent,
    block_order,
    norm1,
    q_weight,
    q_bias,
    k_weight,
    k_bias,
    v_weight,
    v_bias,
    o_weight,
    norm2,
    gate_weight,
    up_weight,
    down_weight,
):
    tok = hidden.shape[0]
    pair = sizes["head"] * tok
    blk = int(np.prod([sizes[a] for a in BLK]))
    seqs = blk // SEQ_SPAN
    place_axes = {1: BLK, 2: BLK[:3], 4: BLK[:2]}[seqs]
    seq_axes = BLK[len(place_axes) :]
    head = lax.axis_index("head")
    place = place_of({}, place_axes, sizes)
    seq = place_of({}, seq_axes, sizes) if seq_axes else 0
    order = lax.dynamic_index_in_dim(block_order, seq, 0, keepdims=False)
    tops = lax.dynamic_slice_in_dim(order, place * 2, 2)
    slots = jnp.argsort(order).astype(jnp.int32)
    positions = (tops[:, None] * tok + jnp.arange(tok, dtype=jnp.int32)[None, :]).reshape(pair)
    frequency = THETA ** (-(jnp.arange(HEAD_DIM // 2, dtype=F32) * 2.0) / HEAD_DIM)
    angles = positions.astype(F32)[:, None] * frequency[None, :]
    cosine, sine = jnp.cos(angles), jnp.sin(angles)
    cosine = jnp.concatenate([cosine, cosine], axis=1)
    sine = jnp.concatenate([-sine, sine], axis=1)

    q_cols = D // 2
    kv_cols = HEAD_DIM
    rows = q_weight.shape[0]
    small = lax.reduce_precision(jnp.concatenate([norm1, norm2, q_bias, k_bias, v_bias]), 8, 7)
    small = jnp.pad(small, (0, 8 * LANES - small.shape[0])).reshape(8, LANES)
    parts = sizes["y"] * sizes["c"]
    width = gate_weight.shape[1]
    lanes = -(-width // (LANES * parts)) * LANES
    first = lanes * 6 // 9 // LANES * LANES
    ff_rows = gate_weight.shape[0]

    def along_z(part):
        part = part.reshape(1, 3, parts * ff_rows, part.shape[-1])
        return lax.all_gather(part, live(("g", "z"), sizes), axis=0, tiled=True)

    w_qkv, x_pair, small_all, w_out, packed_one, packed_two = front(
        (q_weight, k_weight, v_weight, o_weight),
        hidden,
        small,
        (down_weight, gate_weight, up_weight),
        first,
        lanes - first,
        [
            (0, None, AXES, AXES, True),
            (1, None, ("head",), ("head",), False),
            (2, None, AXES, AXES, False),
            (3, None, BLK, ("y", "z", "g", "c"), False),
        ],
        sizes,
        1,
    )
    w_out = w_out.reshape(q_cols, D)
    w_qkv = w_qkv.reshape(D, q_cols + 2 * kv_cols)
    x_pair = x_pair.reshape(pair, D)
    small_all = small_all.reshape(-1, 8 * LANES)
    kn = k_bias.shape[0]
    long = small_all[:, : 3 * rows].reshape(-1, 3, rows).transpose(1, 0, 2).reshape(3, D)
    short = small_all[:, 3 * rows : 3 * rows + 2 * kn].reshape(-1, 2, kn)
    short = short.transpose(1, 0, 2).reshape(2, 2 * kv_cols)
    gain_one, gain_two = long[:1], long[1:2]
    bias = jnp.concatenate(
        [
            lax.dynamic_slice_in_dim(v, head * n, n)
            for v, n in ((long[2], q_cols), (short[0], kv_cols), (short[1], kv_cols))
        ]
    )[None]
    far_axes, near_axes = place_axes[:2], place_axes[2:]
    group = ("head", "y", "c")
    cot_all = lax.all_gather(cotangent, group, axis=0, tiled=True)
    kv, mine_one, queries, normed = project(
        x_pair,
        w_qkv,
        gain_one,
        bias,
        cosine,
        sine,
        packed_one,
        cot_all,
        [(0, None, far_axes, far_axes, False)],
        sizes,
        2,
    )
    half = tok // 2
    crossed = [
        ((0, half), group, ("head", "y", "c"), False),
        ((half, half), group, ("y", "head", "c"), False),
    ]
    summed = [
        ((0, half), group, ("c", "head", "y"), False),
        ((half, half), group, ("c", "y", "head"), False),
    ]
    w_feed_one = along_z(mine_one)
    if near_axes:
        (kv,) = gather([kv], [(0, None, near_axes, near_axes, False)], sizes, 10)
    near_count = int(np.prod([sizes[a] for a in near_axes], dtype=int))
    far_count = SEQ_SPAN // near_count
    where = slots // 2
    slots = ((where % near_count) * far_count + where // near_count) * 2 + slots % 2
    kv = kv.reshape(2 * SEQ_SPAN, tok, 2 * HEAD_DIM)
    attended, lse = attend(slots, tops, queries, kv)
    attn_local = attended.astype(BF)
    inputs = hidden.astype(F32)
    mixed_part = dot_nn(attn_local, w_out).reshape(2, tok, D)
    mixed_got, mine_two = gather(
        [mixed_part.astype(BF)],
        [(0, None, ("head",), ("head",), True)],
        sizes,
        3,
        [packed_two],
    )
    w_feed_two = along_z(mine_two)
    mixed = (
        inputs
        + lax.dynamic_index_in_dim(mixed_part, head, 0, keepdims=False)
        + lax.dynamic_index_in_dim(mixed_got, 1 - head, 0, keepdims=False).astype(F32)
    )
    scale_two = inverse_rms(mixed)
    normed_two = (mixed * scale_two * gain_two).astype(BF)
    (tokens,) = gather([normed_two], [(0,) + c for c in crossed], sizes, 4)
    tokens = tokens.reshape(-1, D)

    places = w_feed_one.shape[0]
    act, dgate, dup, branch, dtokens = feed(tokens, cot_all, w_feed_one)
    parts_one = plain_grads(tokens, cot_all, act, dgate, dup, places)
    act, dgate, dup, branch, dtokens = feed(
        tokens, cot_all, w_feed_two, (branch, dtokens), (parts_one,)
    )
    dmixed, dproj, norm2_part, parts_two = feed_grads(
        dtokens.reshape(-1, tok, D),
        mixed,
        cotangent,
        gain_two,
        tokens,
        cot_all,
        act,
        dgate,
        dup,
        places,
        [(0,) + c for c in summed],
        sizes,
        5,
    )
    def collect(grad):
        total = lax.psum_scatter(grad, live(("g", "z"), sizes), scatter_dimension=0, tiled=True)
        return total.reshape(3, parts, ff_rows, grad.shape[-1])

    back_one = collect(parts_one)

    dout, o_part = exchange_back(dproj, w_out, attn_local, sizes, 6)

    dq, dkv_parts = attend_back(slots, tops, queries, kv, dout, lse, attended)
    dkv, d_out_weight, parts_two = scatter(
        [dkv_parts.reshape(SEQ_SPAN, pair, 2 * HEAD_DIM), o_part.reshape(blk, -1, D)],
        [
            (0, None, near_axes + far_axes, place_axes[::-1], False),
            (1, None, BLK, BLK[::-1], False),
        ],
        [BF, F32],
        sizes,
        7,
        carried=[parts_two],
    )
    back_two = collect(parts_two)
    w_part, dnormed, norm1_part, bias_part, back_one = project_back(
        dq, dkv, normed, x_pair, w_qkv, cosine, sine, back_one, blk, rows, 11
    )
    if w_part.ndim == 2:
        w_part = w_part.reshape(2, blk, rows, -1).transpose(1, 0, 2, 3)
    norm1_part, bias_part = norm1_part[0], bias_part[0]
    own = (jnp.arange(2) == head).astype(F32)[:, None]

    def owners(vector):
        return vector.reshape(2, blk, -1).transpose(1, 0, 2)

    def owned(vector):
        return owners((own * vector[None, :]).reshape(-1))

    small_grads = jnp.stack(
        [
            jnp.pad(part, ((0, 0), (0, 0), (0, LANES - part.shape[2])))
            for part in (
                owners(norm1_part),
                owners(norm2_part[0]),
                owned(bias_part[:q_cols]),
                owned(bias_part[q_cols : q_cols + kv_cols]),
                owned(bias_part[q_cols + kv_cols :]),
            )
        ]
        + [jnp.zeros((blk, 2, LANES), F32)] * 3,
        axis=2,
    )
    small_grads = small_grads.transpose(1, 0, 2, 3).reshape(2 * blk, 8, LANES)
    w_grads, small_sum, dnormed_sum, branch_sum = scatter(
        [
            w_part,
            small_grads,
            dnormed.reshape(2, tok, D),
            branch.reshape(-1, tok, D),
        ],
        [
            (0, None, BLK, BLK[::-1], True),
            (1, None, AXES, AXES[::-1], False),
            (2, None, ("head",), ("head",), False),
        ]
        + [(3,) + c for c in summed],
        [F32] * 4,
        sizes,
        8,
    )
    d_query, d_key, d_value, output, hidden_grad, d_down, d_gate, d_up = write_outputs(
        w_grads,
        dnormed_sum,
        branch_sum,
        dmixed,
        hidden,
        mixed,
        gain_one,
        [back_one] + list(swap([back_two], w_grads, 9)),
        width,
    )
    return (
        output,
        hidden_grad,
        small_sum[0, :rows],
        d_query,
        small_sum[2, :rows],
        d_key,
        small_sum[3, :kn],
        d_value,
        small_sum[4, :kn],
        d_out_weight,
        small_sum[1, :rows],
        d_gate,
        d_up,
        d_down,
    )


def solution(mesh):
    heads, blk = mesh.devices.shape
    split = jax.sharding.Mesh(mesh.devices.reshape(heads, blk // 16, 4, 2, 2), AXES)
    sizes = dict(split.shape)
    rows = P(AXES, None)
    vector = P(AXES)
    feed = P(BLK, "head")
    return jax.shard_map(
        functools.partial(shards, sizes),
        mesh=split,
        in_specs=(
            rows,
            rows,
            P(),
            vector,
            rows,
            vector,
            rows,
            vector,
            rows,
            vector,
            rows,
            vector,
            feed,
            feed,
            feed,
        ),
        out_specs=(
            rows,
            rows,
            vector,
            rows,
            vector,
            rows,
            vector,
            rows,
            vector,
            rows,
            vector,
            feed,
            feed,
            feed,
        ),
        check_vma=False,
    )
```

```python
import functools

import jax
import jax.numpy as jnp
import numpy as np
from jax import lax
from jax.experimental import pallas as pl
from jax.experimental.pallas import tpu as pltpu
from jax.sharding import PartitionSpec as P

D = 1536
QHEADS = 12
KVHEADS = 2
HEAD_DIM = 128
SEQ_SPAN = 16
BLOCK = 256

EPS = 1e-06
THETA = 1000000.0
SCALE = HEAD_DIM**-0.5
LOG2E = 1.4426950408889634
SCALE2 = SCALE * LOG2E
BF = jnp.bfloat16
F32 = jnp.float32
MESH = pl.DeviceIdType.MESH
VMEM_LIMIT = 56 * 2**20
AXES = ("head", "g", "z", "y", "c")
BLK = ("g", "z", "y", "c")
LANES = 128


def dot_nn(a, b):
    return lax.dot_general(a, b, (((1,), (0,)), ((), ())), preferred_element_type=F32)


def dot_nt(a, b):
    return lax.dot_general(a, b, (((1,), (1,)), ((), ())), preferred_element_type=F32)


def dot_tn(a, b):
    return lax.dot_general(a, b, (((0,), (0,)), ((), ())), preferred_element_type=F32)


def live(axes, sizes):
    return tuple(a for a in axes if sizes[a] > 1)


def greet(axes, sizes, diagonal=False):
    barrier = pltpu.get_barrier_semaphore()
    count = 0
    if diagonal:
        pl.semaphore_signal(barrier, inc=1, device_id=across(3), device_id_type=MESH)
        count += 1
    for a in axes:
        me = lax.axis_index(a)
        for d in range(1, sizes[a]):
            pl.semaphore_signal(
                barrier,
                inc=1,
                device_id={a: lax.rem(me + d, sizes[a])},
                device_id_type=MESH,
            )
            count += 1
    pl.semaphore_wait(barrier, count)


def across(d):
    y, c = lax.axis_index("y"), lax.axis_index("c")
    return {"y": 1 - y if d & 2 else y, "c": 1 - c if d & 1 else c}


class Swap:
    def __init__(self, x, out, send_sems, recv_sems, local_sem):
        me = lax.axis_index("y") * 2 + lax.axis_index("c")
        self.kept = pltpu.make_async_copy(x.at[:, me], out.at[:, me], local_sem)
        self.copies = []
        for d in range(1, 4):
            to = across(d)
            self.copies.append(
                pltpu.make_async_remote_copy(
                    src_ref=x.at[:, to["y"] * 2 + to["c"]],
                    dst_ref=out.at[:, me],
                    send_sem=send_sems.at[d - 1],
                    recv_sem=recv_sems.at[d - 1],
                    device_id=to,
                    device_id_type=MESH,
                )
            )

    def start(self):
        for copy in self.copies:
            copy.start()
        self.kept.start()

    def wait(self):
        self.kept.wait()
        for copy in self.copies:
            copy.wait()


def swap_scratch(swaps):
    if not swaps:
        return []
    return [pltpu.SemaphoreType.DMA((3 * len(swaps),))] * 2 + [
        pltpu.SemaphoreType.DMA((len(swaps),))
    ]


def swaps_of(xs, outs, sems):
    return [
        Swap(
            x,
            out,
            sems[0].at[pl.ds(3 * i, 3)],
            sems[1].at[pl.ds(3 * i, 3)],
            sems[2].at[i],
        )
        for i, (x, out) in enumerate(zip(xs, outs))
    ]


def place_of(offsets, axes, sizes):
    value = 0
    for a in axes:
        me = lax.axis_index(a)
        off = offsets.get(a, 0)
        value = value * sizes[a] + (lax.rem(me + off, sizes[a]) if off else me)
    return value


def remote(src, dst, send, recv, axis, distance, sizes):
    to = lax.rem(lax.axis_index(axis) + distance, sizes[axis])
    return pltpu.make_async_remote_copy(
        src_ref=src,
        dst_ref=dst,
        send_sem=send,
        recv_sem=recv,
        device_id={axis: to},
        device_id_type=MESH,
    )


def gather_kernel(plans, sizes, swap_count, waited, carried, *refs, ahead=None, behind=None):
    count = max(p[0] for p in plans) + 1
    xs, refs = refs[:count], refs[count:]
    swap_xs, refs = refs[:swap_count], refs[swap_count + waited :]
    outs, refs = refs[:count], refs[count:]
    swap_outs, refs = refs[:swap_count], refs[swap_count + carried :]
    send_sems, recv_sems, local_sems = refs[:3]
    swaps = swaps_of(swap_xs, swap_outs, refs[3:])
    used = {a: (sizes[a] if any(a in p[3] for p in plans) else 1) for a in AXES}
    if swaps:
        used.update(y=sizes["y"], c=sizes["c"])
    greet(live(AXES, used), sizes, bool(swaps))

    def cut(ref, rows):
        return ref if rows is None else ref.at[pl.ds(*rows)]

    def source(plan, place):
        i, rows, layout, phases, split = plan
        return cut(xs[i].at[place] if split else xs[i], rows)

    def landed(slot, number):
        axis = plans[0][3][0]
        return remote(slot, slot, send_sems.at[number], recv_sems.at[number], axis, 0, sizes)

    sends, kept, queue = [], [], []
    sem = 0
    for j, plan in enumerate(plans):
        i, rows, layout, phases, split = plan
        mine = source(plan, lax.axis_index(phases[0]))
        slot = cut(outs[i].at[place_of({}, layout, sizes)], rows)
        copy = pltpu.make_async_copy(mine, slot, local_sems.at[j])
        queue.append((plan, {}, -1, None))
        kept.append(copy)
    at = 0
    ends = []
    while at < len(queue):
        plan, offsets, phase, arrived = queue[at]
        at += 1
        i, rows, layout, phases, split = plan
        slot = cut(outs[i].at[place_of(offsets, layout, sizes)], rows)
        if arrived is None:
            src = source(plan, lax.axis_index(phases[0]))
        else:
            src = slot
            landed(slot, arrived).wait_recv()
        for p in range(phase + 1, len(phases)):
            a = phases[p]
            for d in range(1, sizes[a]):
                piece = src
                if split and p == 0:
                    piece = source(plan, lax.rem(lax.axis_index(a) + d, sizes[a]))
                copy = remote(piece, slot, send_sems.at[sem], recv_sems.at[sem], a, d, sizes)
                copy.start()
                sends.append(copy)
                later = dict(offsets)
                later[a] = sizes[a] - d
                if p + 1 < len(phases):
                    queue.append((plan, later, p, sem))
                else:
                    ends.append((plan, later, sem))
                sem += 1
        if at == len(plans):
            if ahead is not None:
                ahead()
            for copy in kept + swaps:
                copy.start()
            if behind is not None:
                behind()
    for (i, rows, layout, phases, split), offsets, arrived in ends:
        landed(cut(outs[i].at[place_of(offsets, layout, sizes)], rows), arrived).wait_recv()
    for copy in kept + swaps:
        copy.wait()
    for copy in sends:
        copy.wait_send()


def gather(arrays, plans, sizes, collective_id, swaps=(), after=(), carried=()):
    plans = [
        (i, rows, live(layout, sizes), live(phases, sizes), split)
        for i, rows, layout, phases, split in plans
    ]
    counts = [int(np.prod([sizes[a] for a in p[2]])) for p in plans]
    total = sum(counts) - len(counts)
    shapes = []
    for i, x in enumerate(arrays):
        n, split = next((c, p[4]) for c, p in zip(counts, plans) if p[0] == i)
        shapes.append(jax.ShapeDtypeStruct((n,) + (x.shape[1:] if split else x.shape), x.dtype))
    spec = pl.BlockSpec(memory_space=pltpu.VMEM)
    far = pl.BlockSpec(memory_space=pl.ANY)
    specs = [spec] * len(arrays) + [far] * len(swaps)
    moved = sum(int(np.prod(s.shape)) * s.dtype.itemsize for s in shapes)
    return pl.pallas_call(
        functools.partial(
            gather_kernel, plans, sizes, len(swaps), len(after) + len(carried), len(carried)
        ),
        out_shape=shapes + [jax.ShapeDtypeStruct(x.shape, x.dtype) for x in (*swaps, *carried)],
        in_specs=specs + [far] * (len(after) + len(carried)),
        out_specs=[far] * (len(specs) + len(carried)),
        input_output_aliases={
            len(specs) + len(after) + i: len(specs) + i for i in range(len(carried))
        },
        scratch_shapes=[
            pltpu.SemaphoreType.DMA((total,)),
            pltpu.SemaphoreType.DMA((total,)),
            pltpu.SemaphoreType.DMA((len(plans),)),
        ]
        + swap_scratch(swaps),
        compiler_params=pltpu.CompilerParams(
            collective_id=collective_id, has_side_effects=True, vmem_limit_bytes=VMEM_LIMIT
        ),
        cost_estimate=pl.CostEstimate(flops=0, bytes_accessed=20 * moved, transcendentals=0),
    )(*arrays, *swaps, *after, *carried)


def front_kernel(plans, sizes, *refs):
    q_ref, k_ref, v_ref, o_ref, hidden_ref, small_ref = refs[:6]
    feeds, refs = refs[6:9], refs[9:]
    outs, first_ref, second_ref, refs = refs[:4], refs[4], refs[5], refs[6:]
    halves_s, o_s, feed_s, feed_sems = refs[:4]
    loads = [
        pltpu.make_async_copy(feeds[m], feed_s.at[m], feed_sems.at[m]) for m in range(len(feeds))
    ]
    for copy in loads:
        copy.start()
    heads = halves_s.shape[0]
    q_cols, kv_cols = q_ref.shape[1] // heads, k_ref.shape[1] // heads
    for i in range(heads):
        halves_s[i, :, :q_cols] = q_ref[:, i * q_cols : (i + 1) * q_cols].astype(BF)
        cols = slice(i * kv_cols, (i + 1) * kv_cols)
        halves_s[i, :, q_cols : q_cols + kv_cols] = k_ref[:, cols].astype(BF)
        halves_s[i, :, q_cols + kv_cols :] = v_ref[:, cols].astype(BF)
    o_s[...] = o_ref[...].astype(BF)

    def pack():
        first, second = first_ref.shape[-1], second_ref.shape[-1]
        for m in range(len(feeds)):
            loads[m].wait()
            rows, width = feed_s.shape[1:]
            for i in range(first_ref.shape[1]):
                low = i * (first + second)
                for ref, n in ((first_ref, first), (second_ref, second)):
                    real = min(n, width - low)
                    ref[m, i, :, :real] = feed_s[m, :, low : low + real].astype(BF)
                    if real < n:
                        ref[m, i, :, real:] = jnp.zeros((rows, n - real), BF)
                    low += n

    gather_kernel(
        plans,
        sizes,
        0,
        0,
        0,
        halves_s,
        hidden_ref,
        small_ref,
        o_s,
        *outs,
        *refs[4:],
        ahead=pack,
    )


def front(weights, hidden, small, feeds, first, second, plans, sizes, collective_id):
    plans = alive(plans, sizes)
    heads, rows = sizes["head"], weights[0].shape[0]
    halves = jax.ShapeDtypeStruct((heads, rows, sum(w.shape[1] for w in weights[:3]) // heads), BF)
    out = jax.ShapeDtypeStruct(weights[3].shape, BF)
    arrays = [halves, hidden, small, out]
    counts = [int(np.prod([sizes[a] for a in p[2]])) for p in plans]
    total = sum(counts) - len(counts)
    shapes = [
        jax.ShapeDtypeStruct((n,) + (x.shape[1:] if p[4] else x.shape), x.dtype)
        for n, x, p in zip(counts, arrays, plans)
    ]
    ff_rows = feeds[0].shape[0]
    blocks = [jax.ShapeDtypeStruct((3, 4, ff_rows, n), BF) for n in (first, second)]
    spec = pl.BlockSpec(memory_space=pltpu.VMEM)
    return pl.pallas_call(
        functools.partial(front_kernel, plans, sizes),
        out_shape=shapes + blocks,
        in_specs=[spec] * 6 + [pl.BlockSpec(memory_space=pl.ANY)] * 3,
        out_specs=[pl.BlockSpec(memory_space=pl.ANY)] * 4 + [spec] * 2,
        scratch_shapes=[
            pltpu.VMEM(halves.shape, BF),
            pltpu.VMEM(out.shape, BF),
            pltpu.VMEM((3,) + feeds[0].shape, F32),
            pltpu.SemaphoreType.DMA((3,)),
            pltpu.SemaphoreType.DMA((total,)),
            pltpu.SemaphoreType.DMA((total,)),
            pltpu.SemaphoreType.DMA((len(plans),)),
        ],
        compiler_params=pltpu.CompilerParams(
            collective_id=collective_id, has_side_effects=True, vmem_limit_bytes=VMEM_LIMIT
        ),
        cost_estimate=pl.CostEstimate(flops=0, bytes_accessed=100 * 2**20, transcendentals=0),
    )(*weights, hidden, small, *feeds)


def offset_keys(axes, sizes):
    keys = [{}]
    for a in axes:
        keys = [dict(k, **{a: d}) for k in keys for d in list(range(1, sizes[a])) + [0]]
    return keys


def scatter_kernel(plans, sizes, *refs, between=None, held=None, held_sems=None):
    count = max(p[0] for p in plans) + 1
    xs, outs = refs[:count], refs[count : 2 * count]
    held = held or {}
    at = 2 * count
    bufs = []
    for _, _, _, phases, swap in plans:
        n = len(phases)
        bufs.append((refs[at : at + n], refs[at + n : at + 2 * n]))
        at += 2 * n
    send_sems, recv_sems, local_sems = refs[at:]
    used = {
        a: (sizes[a] if any(a in p[3] or (p[4] and a == "head") for p in plans) else 1)
        for a in AXES
    }
    loads = {}
    for j, (i, rows, layout, phases, swap) in enumerate(plans):
        if i not in held:
            continue
        for key in offset_keys(phases[1:], sizes):
            place = place_of(key, layout, sizes)
            src, dst = xs[i].at[place], held[i].at[place]
            if rows is not None:
                src, dst = src.at[pl.ds(*rows)], dst.at[pl.ds(*rows)]
            copy = pltpu.make_async_copy(src, dst, held_sems.at[len(loads)])
            copy.start()
            loads[j, tuple(key.get(a, 0) for a in phases[1:])] = copy
    greet(live(AXES, used), sizes)
    sem = 0
    sends = []
    arrivals = [dict() for _ in plans]

    def number(offsets, axes):
        value = 0
        for a in axes:
            value = value * sizes[a] + offsets.get(a, 0)
        return value

    def block_of(j, offsets, near=False):
        i, rows, layout, phases, swap = plans[j]
        block = (held.get(i, xs[i]) if near else xs[i]).at[place_of(offsets, layout, sizes)]
        return block if rows is None else block.at[pl.ds(*rows)]

    def total_of(j, offsets, phase):
        phases = plans[j][3]
        if plans[j][0] in held:
            loads[j, tuple(offsets.get(a, 0) for a in phases[1:])].wait()
        total = block_of(j, offsets, True)[...].astype(F32)
        for q in range(phase):
            rest = phases[q + 1 :]
            for d in range(1, sizes[phases[q]]):
                s = arrivals[j].pop((q, d, number(offsets, rest)))
                buf = bufs[j][1][q].at[d - 1, number(offsets, rest)]
                remote(buf, buf, send_sems.at[s], recv_sems.at[s], phases[q], 0, sizes).wait_recv()
                total = total + buf[...].astype(F32)
        return total

    depth = max(len(p[3]) for p in plans)
    for phase in range(depth):
        for j, (i, rows, layout, phases, swap) in enumerate(plans):
            if phase >= len(phases):
                continue
            a, rest = phases[phase], phases[phase + 1 :]
            for d in range(1, sizes[a]):
                for key in offset_keys(rest, sizes):
                    offsets = dict(key)
                    offsets[a] = d
                    where = number(key, rest)
                    if phase == 0:
                        src = block_of(j, offsets)
                    else:
                        src = bufs[j][0][phase].at[d - 1, where]
                        src[...] = total_of(j, offsets, phase).astype(src.dtype)
                    dst = bufs[j][1][phase].at[d - 1, where]
                    copy = remote(src, dst, send_sems.at[sem], recv_sems.at[sem], a, d, sizes)
                    copy.start()
                    sends.append(copy)
                    arrivals[j][(phase, d, where)] = sem
                    sem += 1
        if between is not None:
            between(phase)
    late = []
    for j, (i, rows, layout, phases, swap) in enumerate(plans):
        total = total_of(j, {}, len(phases))
        if swap:
            hold, out = bufs[j][0][0], outs[i]
            hold[...] = total.astype(hold.dtype)
            me = lax.axis_index("head")
            copy = pltpu.make_async_copy(hold.at[me], out.at[me], local_sems.at[j])
            copy.start()
            late.append((copy, None))
            for d in range(1, sizes["head"]):
                to = lax.rem(me + d, sizes["head"])
                copy = remote(
                    hold.at[to], out.at[me], send_sems.at[sem], recv_sems.at[sem], "head", d, sizes
                )
                copy.start()
                sends.append(copy)
                late.append((out.at[lax.rem(me + sizes["head"] - d, sizes["head"])], sem))
                sem += 1
        elif rows is None:
            outs[i][...] = total.astype(outs[i].dtype)
        else:
            outs[i][pl.ds(*rows)] = total.astype(outs[i].dtype)
    for item, s in late:
        if s is None:
            item.wait()
        else:
            remote(item, item, send_sems.at[s], recv_sems.at[s], "head", 0, sizes).wait_recv()
    for copy in sends:
        copy.wait_send()


def scatter_scratch(arrays, plans, out_types, sizes):
    scratch, total = [], 0
    for i, rows, layout, phases, swap in plans:
        x, kind = arrays[i], out_types[i]
        block = x.shape[1:] if rows is None else (rows[1],) + x.shape[2:]
        send_bufs, recv_bufs = [], []
        for p, a in enumerate(phases):
            rest = int(np.prod([sizes[b] for b in phases[p + 1 :]], dtype=int))
            shape = (sizes[a] - 1, rest) + block
            recv_bufs.append(pltpu.VMEM(shape, x.dtype))
            if p == 0:
                send_bufs.append(pltpu.VMEM(block if swap else (8, LANES), kind if swap else F32))
            else:
                send_bufs.append(pltpu.VMEM(shape, x.dtype))
            total += (sizes[a] - 1) * rest
        scratch += send_bufs + recv_bufs
        if swap:
            total += sizes["head"] - 1
    return scratch + [
        pltpu.SemaphoreType.DMA((total,)),
        pltpu.SemaphoreType.DMA((total,)),
        pltpu.SemaphoreType.DMA((len(plans),)),
    ]


def held_scratch(arrays, plans, far, sizes):
    count = 0
    for i, _, _, phases, _ in plans:
        if i in far:
            count += int(np.prod([sizes[a] for a in phases[1:]], dtype=int))
    return [pltpu.VMEM(arrays[i].shape, arrays[i].dtype) for i in far] + [
        pltpu.SemaphoreType.DMA((count,))
    ]


def alive(plans, sizes):
    return [
        (i, rows, live(layout, sizes), live(phases, sizes), flag)
        for i, rows, layout, phases, flag in plans
    ]


def scatter_and_wait_kernel(plans, sizes, arrays, waited, carried, far, *refs):
    xs, refs = refs[:arrays], refs[arrays + waited :]
    outs, refs, held = refs[:arrays], refs[arrays + carried :], {}
    if far:
        held = dict(zip(far, refs[-len(far) - 1 : -1]))
        refs, held_sems = refs[: -len(far) - 1], refs[-1]
        scatter_kernel(plans, sizes, *xs, *outs, *refs, held=held, held_sems=held_sems)
    else:
        scatter_kernel(plans, sizes, *xs, *outs, *refs)


def scatter(arrays, plans, out_types, sizes, collective_id, after=(), carried=()):
    plans = alive(plans, sizes)
    shapes = [jax.ShapeDtypeStruct(x.shape[1:], kind) for x, kind in zip(arrays, out_types)]
    spec = pl.BlockSpec(memory_space=pltpu.VMEM)
    far = pl.BlockSpec(memory_space=pl.ANY)
    big = tuple(i for i, x in enumerate(arrays) if x.dtype == BF)
    moved = sum(int(np.prod(x.shape)) * x.dtype.itemsize for x in arrays)
    return pl.pallas_call(
        functools.partial(
            scatter_and_wait_kernel,
            plans,
            sizes,
            len(arrays),
            len(after) + len(carried),
            len(carried),
            big,
        ),
        out_shape=shapes + [jax.ShapeDtypeStruct(x.shape, x.dtype) for x in carried],
        in_specs=[far if i in big else spec for i in range(len(arrays))] + [far] * (len(after) + len(carried)),
        out_specs=[spec] * len(arrays) + [far] * len(carried),
        input_output_aliases={
            len(arrays) + len(after) + i: len(arrays) + i for i in range(len(carried))
        },
        scratch_shapes=scatter_scratch(arrays, plans, out_types, sizes)
        + (held_scratch(arrays, plans, big, sizes) if big else []),
        compiler_params=pltpu.CompilerParams(
            collective_id=collective_id, has_side_effects=True, vmem_limit_bytes=VMEM_LIMIT
        ),
        cost_estimate=pl.CostEstimate(flops=0, bytes_accessed=20 * moved, transcendentals=0),
    )(*arrays, *after, *carried)


def swap_kernel(count, *refs):
    items = swaps_of(refs[:count], refs[count + 1 : 2 * count + 1], refs[2 * count + 1 :])
    greet(("y", "c"), {"y": 2, "c": 2}, True)
    for item in items:
        item.start()
    for item in items:
        item.wait()


def swap(xs, last, collective_id):
    far = pl.BlockSpec(memory_space=pl.ANY)
    n = len(xs)
    return pl.pallas_call(
        functools.partial(swap_kernel, n),
        out_shape=[jax.ShapeDtypeStruct(x.shape, x.dtype) for x in xs],
        in_specs=[far] * (n + 1),
        out_specs=[far] * n,
        scratch_shapes=swap_scratch(xs),
        compiler_params=pltpu.CompilerParams(
            collective_id=collective_id, has_side_effects=True, vmem_limit_bytes=VMEM_LIMIT
        ),
    )(*xs, last)


def outputs_kernel(*refs):
    w_ref, dnormed_ref, branch_ref, dmixed_ref, x_ref, mixed_ref, gain_ref = refs[:7]
    parts, refs = refs[7:9], refs[9:]
    q_ref, k_ref, v_ref, out_ref, hidden_ref = refs[:5]
    feeds = refs[5:]
    heads = w_ref.shape[0]
    q_cols = q_ref.shape[1] // heads
    for i in range(heads):
        cols = slice(i * HEAD_DIM, (i + 1) * HEAD_DIM)
        q_ref[:, i * q_cols : (i + 1) * q_cols] = w_ref[i, :, :q_cols]
        k_ref[:, cols] = w_ref[i, :, q_cols : q_cols + HEAD_DIM]
        v_ref[:, cols] = w_ref[i, :, q_cols + HEAD_DIM :]
    out_ref[...] = (mixed_ref[...] + branch_ref[...]).astype(BF)
    x = x_ref[...].astype(F32)
    scale = inverse_rms(x)
    z = x * scale
    u = gain_ref[...] * dnormed_ref[...]
    hidden_ref[...] = (
        dmixed_ref[...] + scale * (u - z * jnp.mean(z * u, axis=-1, keepdims=True))
    ).astype(BF)
    width = feeds[0].shape[1]
    lanes = sum(part.shape[-1] for part in parts)
    for m, feed_ref in enumerate(feeds):
        for i in range(parts[0].shape[1]):
            low = i * lanes
            for part in parts:
                n = part.shape[-1]
                real = min(n, width - low)
                if real > 0:
                    feed_ref[:, low : low + real] = part[m, i, :, :real].astype(F32)
                low += n


def write_outputs(w, dnormed, branch, dmixed, x, mixed, gain, parts, width):
    heads, rows, inner = w.shape
    tok, ff_rows = x.shape[0], parts[0].shape[2]
    steps = 2 if rows % 16 == 0 and ff_rows % 32 == 0 else 1

    def rows_of(shape, dim):
        block = tuple(n // steps if i == dim else n for i, n in enumerate(shape))
        return pl.BlockSpec(block, lambda i: tuple(i if k == dim else 0 for k in range(len(shape))))

    kinds = [
        ((rows, heads * (inner - 2 * HEAD_DIM)), F32),
        ((rows, heads * HEAD_DIM), F32),
        ((rows, heads * HEAD_DIM), F32),
        (x.shape, BF),
        (x.shape, BF),
    ] + [((ff_rows, width), F32)] * 3
    return pl.pallas_call(
        outputs_kernel,
        grid=(steps,),
        out_shape=[jax.ShapeDtypeStruct(*k) for k in kinds],
        in_specs=[rows_of(w.shape, 1)]
        + [rows_of(x.shape, 0)] * 5
        + [pl.BlockSpec(gain.shape, lambda i: (0, 0))]
        + [rows_of(part.shape, 2) for part in parts],
        out_specs=[rows_of(shape, 0) for shape, _ in kinds],
        compiler_params=pltpu.CompilerParams(vmem_limit_bytes=VMEM_LIMIT),
        cost_estimate=pl.CostEstimate(flops=0, bytes_accessed=20 * 2**20, transcendentals=0),
    )(w, dnormed, branch, dmixed, x, mixed, gain, *parts)


def feed_kernel(chunks, added, t_ref, c_ref, w_ref, *refs):
    act_ref, dgate_ref, dup_ref, branch_ref, dtok_ref = refs[-5:]
    before = refs[:added]
    tokens, cot = t_ref[...], c_ref[...]
    places, _, rows, width = w_ref.shape
    per = max(1, LANES * 3 // rows)

    def products(j):
        low, n = chunks[j]

        def weight(m):
            return w_ref[:, m, :, low : low + n].reshape(D, n)

        return dot_nn(tokens, weight(1)), dot_nn(tokens, weight(2)), dot_nn(cot, weight(0))

    ready = [products(0)]
    for j, (low, n) in enumerate(chunks):
        gate, up, dact = ready[j]
        if j + 1 < len(chunks):
            ready.append(products(j + 1))
        sig = 1.0 / (1.0 + jnp.exp(-gate))
        silu = gate * sig
        act_ref[:, low : low + n] = (silu * up).astype(BF)
        dgate_ref[:, low : low + n] = (dact * up * (sig + silu * (1.0 - sig))).astype(BF)
        dup_ref[:, low : low + n] = (dact * silu).astype(BF)
    for z in range(0, places, per):
        cols = slice(z * rows, (z + per) * rows)

        def weight(m):
            return w_ref[z : z + per, m].reshape(per * rows, width)

        dtok = dot_nt(dgate_ref[...], weight(1)) + dot_nt(dup_ref[...], weight(2))
        branch = dot_nt(act_ref[...], weight(0))
        if before:
            branch = branch + before[0][:, cols].astype(F32)
            dtok = dtok + before[1][:, cols].astype(F32)
        dtok_ref[:, cols] = dtok.astype(BF)
        branch_ref[:, cols] = branch.astype(BF)


def feed(tokens, cot, weights, before=(), after=()):
    n, width, tile = tokens.shape[0], weights.shape[-1], 256
    chunks = [(i, min(256, width - i)) for i in range(0, width, 256)]
    wide = pl.BlockSpec((tile, D), lambda i: (i, 0))
    inner = pl.BlockSpec((tile, width), lambda i: (i, 0))
    return pl.pallas_call(
        functools.partial(feed_kernel, chunks, len(before)),
        grid=(n // tile,),
        in_specs=[wide, wide, pl.BlockSpec(memory_space=pltpu.VMEM)]
        + [wide] * len(before)
        + [pl.BlockSpec(memory_space=pl.ANY)] * len(after),
        out_specs=[inner, inner, inner, wide, wide],
        out_shape=[jax.ShapeDtypeStruct((n, k), BF) for k in (width, width, width, D, D)],
        compiler_params=pltpu.CompilerParams(vmem_limit_bytes=VMEM_LIMIT),
        cost_estimate=pl.CostEstimate(
            flops=12 * n * D * width, bytes_accessed=40 * 2**20, transcendentals=n * width
        ),
    )(tokens, cot, weights, *before, *after)


def plain_grads_kernel(t_ref, c_ref, act_ref, dgate_ref, dup_ref, grad_ref):
    per, _, rows, width = grad_ref.shape
    for m, (left, right) in enumerate(((c_ref, act_ref), (t_ref, dgate_ref), (t_ref, dup_ref))):
        made = dot_tn(left[...], right[...]).astype(BF)
        grad_ref[:, m] = made.reshape(per, rows, width)


def plain_grads(tokens, cot, act, dgate, dup, places):
    n, width = act.shape
    rows = D // places
    per = max(1, LANES * 3 // rows)
    left = pl.BlockSpec((n, per * rows), lambda k: (0, k))
    right = pl.BlockSpec(memory_space=pltpu.VMEM)
    return pl.pallas_call(
        plain_grads_kernel,
        grid=(places // per,),
        in_specs=[left, left, right, right, right],
        out_specs=pl.BlockSpec((per, 3, rows, width), lambda k: (k, 0, 0, 0)),
        out_shape=jax.ShapeDtypeStruct((places, 3, rows, width), BF),
        compiler_params=pltpu.CompilerParams(vmem_limit_bytes=VMEM_LIMIT),
        cost_estimate=pl.CostEstimate(
            flops=6 * n * D * width, bytes_accessed=40 * 2**20, transcendentals=0
        ),
    )(tokens, cot, act, dgate, dup)


def grads_kernel(plans, sizes, dtok_ref, mixed_ref, cot_ref, gain_ref, *refs):
    t_hbm, c_hbm, act_hbm, dgate_hbm, dup_hbm = refs[:5]
    dmixed_ref, dproj_ref, gain_grad_ref, grad_hbm = refs[5:9]
    sum_ref, left_s, right_s, made_s, load_sems, made_sems = refs[9:15]
    held, held_sems = {0: refs[-2]}, refs[-1]
    per, rows = made_s.shape[1:3]
    cols = per * rows
    loads = [
        pltpu.make_async_copy(c_hbm, left_s.at[0], load_sems.at[0]),
        pltpu.make_async_copy(act_hbm, right_s.at[0], load_sems.at[1]),
        pltpu.make_async_copy(t_hbm, left_s.at[1], load_sems.at[2]),
        pltpu.make_async_copy(dgate_hbm, right_s.at[1], load_sems.at[3]),
        pltpu.make_async_copy(dup_hbm, right_s.at[0], load_sems.at[4]),
    ]
    for copy in loads[:4]:
        copy.start()

    def stored(m, k, slot):
        return pltpu.make_async_copy(
            made_s.at[slot], grad_hbm.at[pl.ds(k * per, per), m], made_sems.at[slot]
        )

    def some(m, low, high, left, right, fresh):
        def one(k, carry):
            slot = lax.rem(k, 2)
            if fresh:
                pl.when(k >= 2)(lambda: stored(m, k, slot).wait())
            else:
                stored(m, k, slot).wait()
            part = left_s[left, :, pl.ds(pl.multiple_of(k * cols, LANES), cols)]
            made_s[slot] = dot_tn(part, right_s[right]).astype(BF).reshape(made_s.shape[1:])
            stored(m, k, slot).start()
            return carry

        lax.fori_loop(low, high, one, 0)

    chunks = D // cols

    def between(phase):
        if phase == 0:
            loads[0].wait()
            loads[1].wait()
            some(0, 0, chunks // 2, 0, 0, True)
        elif phase == 1:
            some(0, chunks // 2, chunks, 0, 0, False)
            loads[4].start()
            loads[2].wait()
            loads[3].wait()
            some(1, 0, chunks, 1, 1, False)
        else:
            loads[4].wait()
            some(2, 0, chunks, 1, 0, False)

    scatter_kernel(
        plans,
        sizes,
        dtok_ref,
        sum_ref,
        *refs[15:-2],
        between=between,
        held=held,
        held_sems=held_sems,
    )
    mixed, dnormed = mixed_ref[...], sum_ref[...]
    scale = inverse_rms(mixed)
    z = mixed * scale
    u = gain_ref[...] * dnormed
    gain_grad_ref[...] = jnp.sum(dnormed * z, axis=0, keepdims=True)
    dmixed = cot_ref[...].astype(F32) + scale * (
        u - z * jnp.mean(z * u, axis=-1, keepdims=True)
    )
    dmixed_ref[...] = dmixed
    dproj_ref[...] = dmixed.astype(BF)
    for slot in range(2):
        stored(2, slot, slot).wait()


def feed_grads(dtok, mixed, cot_own, gain, tokens, cot, act, dgate, dup, places, plans, sizes, collective_id):
    plans = alive(plans, sizes)
    n, width = act.shape
    rows = D // places
    per = max(1, LANES * 3 // rows)
    spec = pl.BlockSpec(memory_space=pltpu.VMEM)
    far = pl.BlockSpec(memory_space=pl.ANY)
    return pl.pallas_call(
        functools.partial(grads_kernel, plans, sizes),
        out_shape=[
            jax.ShapeDtypeStruct(dtok.shape[1:], F32),
            jax.ShapeDtypeStruct(dtok.shape[1:], BF),
            jax.ShapeDtypeStruct((1, D), F32),
            jax.ShapeDtypeStruct((places, 3, rows, width), BF),
        ],
        in_specs=[far] + [spec] * 3 + [far] * 5,
        out_specs=[spec] * 3 + [far],
        scratch_shapes=[
            pltpu.VMEM(dtok.shape[1:], F32),
            pltpu.VMEM((2, n, D), BF),
            pltpu.VMEM((2, n, width), BF),
            pltpu.VMEM((2, per, rows, width), BF),
            pltpu.SemaphoreType.DMA((5,)),
            pltpu.SemaphoreType.DMA((2,)),
        ]
        + scatter_scratch([dtok], plans, [F32], sizes)
        + held_scratch([dtok], plans, (0,), sizes),
        compiler_params=pltpu.CompilerParams(
            collective_id=collective_id, has_side_effects=True, vmem_limit_bytes=VMEM_LIMIT
        ),
        cost_estimate=pl.CostEstimate(
            flops=6 * n * D * width, bytes_accessed=100 * 2**20, transcendentals=0
        ),
    )(dtok, mixed, cot_own, gain, tokens, cot, act, dgate, dup)


def forward_kernel(heads, slots, tops, q_ref, kv_ref, o_ref, lse_ref, top_s, sum_s, acc_s):
    def score(keys, a, h):
        return dot_nt(keys, q_ref[a * BLOCK : (a + 1) * BLOCK, h * HEAD_DIM : (h + 1) * HEAD_DIM])

    for a in range(2):
        top_s[...] = jnp.full(top_s.shape, -1e30, F32)
        sum_s[...] = jnp.zeros(sum_s.shape, F32)
        acc_s[...] = jnp.zeros(acc_s.shape, F32)
        count = tops[a] + 1

        def step(keys, values_t):
            ahead = min(3, heads)
            ready = [score(keys, a, h) for h in range(ahead)]
            for h in range(heads):
                s = ready[h]
                if h + ahead < heads:
                    ready.append(score(keys, a, h + ahead))
                old = top_s[h : h + 1, :]
                new = jnp.maximum(old, jnp.max(s, axis=0, keepdims=True))
                p = jnp.exp2((s - new) * SCALE2)
                fade = jnp.exp2((old - new) * SCALE2)
                sum_s[h : h + 1, :] = sum_s[h : h + 1, :] * fade + jnp.sum(p, axis=0, keepdims=True)
                top_s[h : h + 1, :] = new
                acc_s[h] = acc_s[h] * fade + dot_nn(values_t, p.astype(BF))

        def two(i, carry):
            first, second = slots[2 * i], slots[2 * i + 1]
            both = jnp.concatenate([kv_ref[first], kv_ref[second]], axis=0)
            step(both[:, :HEAD_DIM], both[:, HEAD_DIM:].T)
            return carry

        lax.fori_loop(0, count // 2, two, 0)

        @pl.when(count % 2 == 1)
        def _():
            last = kv_ref[slots[count - 1]]
            step(last[:, :HEAD_DIM], last[:, HEAD_DIM:].T)

        for h in range(heads):
            total = sum_s[h : h + 1, :]
            o_ref[a * BLOCK : (a + 1) * BLOCK, h * HEAD_DIM : (h + 1) * HEAD_DIM] = (
                acc_s[h] / total
            ).T
            lse_ref[a, h : h + 1, :] = top_s[h : h + 1, :] * SCALE2 + jnp.log2(total)
        lse_ref[a, heads:8, :] = jnp.zeros((8 - heads, BLOCK), F32)


def attend(slots, tops, q, kv):
    heads = q.shape[1] // HEAD_DIM
    spec = pl.BlockSpec(memory_space=pltpu.VMEM)
    pairs = 33 * BLOCK * BLOCK * heads
    return pl.pallas_call(
        functools.partial(forward_kernel, heads),
        grid_spec=pltpu.PrefetchScalarGridSpec(
            num_scalar_prefetch=2,
            grid=(1,),
            in_specs=[spec] * 2,
            out_specs=[spec] * 2,
            scratch_shapes=[
                pltpu.VMEM((8, BLOCK), F32),
                pltpu.VMEM((8, BLOCK), F32),
                pltpu.VMEM((heads, HEAD_DIM, BLOCK), F32),
            ],
        ),
        out_shape=(
            jax.ShapeDtypeStruct(q.shape, F32),
            jax.ShapeDtypeStruct((2, 8, BLOCK), F32),
        ),
        compiler_params=pltpu.CompilerParams(vmem_limit_bytes=VMEM_LIMIT),
        cost_estimate=pl.CostEstimate(
            flops=pairs * 4 * HEAD_DIM, bytes_accessed=80 * 2**20, transcendentals=pairs
        ),
    )(slots, tops, q, kv)


def backward_kernel(
    heads,
    slots,
    tops,
    q_ref,
    kv_ref,
    do_ref,
    lse_ref,
    o_ref,
    dq_ref,
    dkv_ref,
    dq_s,
    dkv_s,
    delta_s,
):
    dkv_s[...] = jnp.zeros(dkv_s.shape, F32)
    for a in range(2):
        dq_s[...] = jnp.zeros(dq_s.shape, F32)

        def part(ref, h):
            return ref[a * BLOCK : (a + 1) * BLOCK, h * HEAD_DIM : (h + 1) * HEAD_DIM]

        for h in range(heads):
            product = part(do_ref, h).astype(F32) * part(o_ref, h)
            delta_s[h : h + 1, :] = jnp.sum(product.T, axis=0, keepdims=True)

        def one(n, carry):
            slot = slots[n]
            keys, values = kv_ref[slot, :, :HEAD_DIM], kv_ref[slot, :, HEAD_DIM:]
            keys_t = keys.T

            def products(h):
                return dot_nt(keys, part(q_ref, h)), dot_nt(values, part(do_ref, h))

            dk = jnp.zeros((BLOCK, HEAD_DIM), F32)
            dv = jnp.zeros((BLOCK, HEAD_DIM), F32)
            ahead = min(2, heads)
            ready = [products(h) for h in range(ahead)]
            for h in range(heads):
                s, dp = ready[h]
                if h + ahead < heads:
                    ready.append(products(h + ahead))
                p = jnp.exp2(s * SCALE2 - lse_ref[a, h : h + 1, :])
                dv = dv + dot_nn(p.astype(BF), part(do_ref, h))
                ds = (p * (dp - delta_s[h : h + 1, :])).astype(BF)
                dk = dk + dot_nn(ds, part(q_ref, h))
                dq_s[h] = dq_s[h] + dot_nn(keys_t, ds)
            dkv_s[slot, :, :HEAD_DIM] = dkv_s[slot, :, :HEAD_DIM] + dk
            dkv_s[slot, :, HEAD_DIM:] = dkv_s[slot, :, HEAD_DIM:] + dv
            return carry

        lax.fori_loop(0, tops[a] + 1, one, 0)
        for h in range(heads):
            dq_ref[a * BLOCK : (a + 1) * BLOCK, h * HEAD_DIM : (h + 1) * HEAD_DIM] = (
                (dq_s[h] * SCALE).T
            ).astype(BF)
    dkv_ref[:, :, :HEAD_DIM] = (dkv_s[:, :, :HEAD_DIM] * SCALE).astype(BF)
    dkv_ref[:, :, HEAD_DIM:] = dkv_s[:, :, HEAD_DIM:].astype(BF)


def attend_back(slots, tops, q, kv, do, lse, attended):
    heads = q.shape[1] // HEAD_DIM
    spec = pl.BlockSpec(memory_space=pltpu.VMEM)
    pairs = 33 * BLOCK * BLOCK * heads
    return pl.pallas_call(
        functools.partial(backward_kernel, heads),
        grid_spec=pltpu.PrefetchScalarGridSpec(
            num_scalar_prefetch=2,
            grid=(1,),
            in_specs=[spec] * 5,
            out_specs=[spec] * 2,
            scratch_shapes=[
                pltpu.VMEM((heads, HEAD_DIM, BLOCK), F32),
                pltpu.VMEM(kv.shape, F32),
                pltpu.VMEM((8, BLOCK), F32),
            ],
        ),
        out_shape=(
            jax.ShapeDtypeStruct(q.shape, BF),
            jax.ShapeDtypeStruct(kv.shape, BF),
        ),
        compiler_params=pltpu.CompilerParams(vmem_limit_bytes=VMEM_LIMIT),
        cost_estimate=pl.CostEstimate(
            flops=pairs * 10 * HEAD_DIM, bytes_accessed=120 * 2**20, transcendentals=pairs
        ),
    )(slots, tops, q, kv, do, lse, attended)


def inverse_rms(value):
    return lax.rsqrt(jnp.mean(value * value, axis=-1, keepdims=True) + EPS)


def turned(value, cosine, sine):
    return value * cosine + pltpu.roll(value, HEAD_DIM // 2, 1) * sine


def project_kernel(plans, sizes, x_ref, w_ref, gain_ref, bias_ref, cos_ref, sin_ref, *refs):
    packed_ref, _, kv_all_ref, swapped_ref, q_ref, normed_ref, kv_s = refs[:7]
    x = x_ref[...].astype(F32)
    normed_ref[...] = (x * inverse_rms(x) * gain_ref[...]).astype(BF)
    cosine, sine = cos_ref[...], sin_ref[...]
    heads = q_ref.shape[1] // HEAD_DIM

    def product(low, n):
        cols = slice(low * HEAD_DIM, (low + n) * HEAD_DIM)
        return dot_nn(normed_ref[...], w_ref[:, cols]) + bias_ref[:, cols]

    made = product(heads, 2)
    kv_s[:, :HEAD_DIM] = turned(made[:, :HEAD_DIM], cosine, sine).astype(BF)
    kv_s[:, HEAD_DIM:] = made[:, HEAD_DIM:].astype(BF)

    def queries():
        for low in range(0, heads, 2):
            made = product(low, 2)
            for i in range(2):
                part = made[:, i * HEAD_DIM : (i + 1) * HEAD_DIM]
                q_ref[:, (low + i) * HEAD_DIM : (low + i + 1) * HEAD_DIM] = turned(
                    part, cosine, sine
                ).astype(BF)

    gather_kernel(
        plans, sizes, 1, 0, 0, kv_s, packed_ref, kv_all_ref, swapped_ref, *refs[7:], behind=queries
    )


def project(x, w, gain, bias, cosine, sine, packed, after, plans, sizes, collective_id):
    plans = alive(plans, sizes)
    n, width = x.shape[0], w.shape[1]
    spec = pl.BlockSpec(memory_space=pltpu.VMEM)
    far = pl.BlockSpec(memory_space=pl.ANY)
    count = int(np.prod([sizes[a] for a in plans[0][2]]))
    kv = (n, 2 * HEAD_DIM)
    return pl.pallas_call(
        functools.partial(project_kernel, plans, sizes),
        in_specs=[spec] * 6 + [far] * 2,
        out_specs=[far, far, spec, spec],
        out_shape=[
            jax.ShapeDtypeStruct(s, BF)
            for s in ((count,) + kv, packed.shape, (n, width - 2 * HEAD_DIM), (n, D))
        ],
        scratch_shapes=[
            pltpu.VMEM(kv, BF),
            pltpu.SemaphoreType.DMA((count - 1,)),
            pltpu.SemaphoreType.DMA((count - 1,)),
            pltpu.SemaphoreType.DMA((1,)),
        ]
        + swap_scratch([packed]),
        compiler_params=pltpu.CompilerParams(
            collective_id=collective_id, has_side_effects=True, vmem_limit_bytes=VMEM_LIMIT
        ),
        cost_estimate=pl.CostEstimate(
            flops=2 * n * D * width, bytes_accessed=80 * 2**20, transcendentals=0
        ),
    )(x, w, gain, bias, cosine, sine, packed, after)


def project_back_kernel(
    dq_ref,
    dkv_ref,
    normed_ref,
    x_ref,
    w_ref,
    cos_ref,
    sin_ref,
    back_ref,
    grad_ref,
    dnormed_ref,
    gain_grad_ref,
    bias_grad_ref,
    swapped_ref,
    dpre_s,
    *sems,
):
    (item,) = swaps_of([back_ref], [swapped_ref], sems)
    greet(("y", "c"), {"y": 2, "c": 2}, True)
    item.start()
    cosine, sine = cos_ref[...], -sin_ref[...]
    heads = dq_ref.shape[1] // HEAD_DIM
    for h in range(heads + 1):
        cols = slice(h * HEAD_DIM, (h + 1) * HEAD_DIM)
        part = dq_ref[:, cols] if h < heads else dkv_ref[:, :HEAD_DIM]
        dpre_s[:, cols] = turned(part.astype(F32), cosine, sine).astype(BF)
    dpre_s[:, (heads + 1) * HEAD_DIM :] = dkv_ref[:, HEAD_DIM:]
    bias_grad_ref[...] = jnp.sum(dpre_s[...].astype(F32), axis=0, keepdims=True)
    x = x_ref[...].astype(F32)
    scale = inverse_rms(x)
    step = 2 * HEAD_DIM
    for low in range(0, D, step):
        cols = slice(low, low + step)
        dnormed = dot_nt(dpre_s[...], w_ref[cols, :])
        dnormed_ref[:, cols] = dnormed.astype(BF)
        gain_grad_ref[:, cols] = jnp.sum(
            dnormed * (x[:, cols] * scale), axis=0, keepdims=True
        )
        if len(grad_ref.shape) == 2:
            grad_ref[cols, :] = dot_tn(normed_ref[:, cols], dpre_s[...]).astype(BF)
    if len(grad_ref.shape) == 4:
        blk, heads, rows, width = grad_ref.shape
        step = 3 * LANES
        for low in range(0, D, step):
            made = dot_tn(normed_ref[:, low : low + step], dpre_s[...]).astype(BF)
            half, start = divmod(low // rows, blk)
            grad_ref[start : start + step // rows, half] = made.reshape(step // rows, rows, width)
    item.wait()


def project_back(dq, dkv, normed, x, w, cosine, sine, back, blk, rows, collective_id):
    n, width = x.shape[0], w.shape[1]
    split = rows % 16 == 0
    made = (blk, 2, rows, width) if split else (D, width)
    spec = pl.BlockSpec(memory_space=pltpu.VMEM)
    far = pl.BlockSpec(memory_space=pl.ANY)
    return pl.pallas_call(
        project_back_kernel,
        in_specs=[spec] * 7 + [far],
        out_specs=[spec] * 4 + [far],
        out_shape=[
            jax.ShapeDtypeStruct(made, BF),
            jax.ShapeDtypeStruct((n, D), BF),
            jax.ShapeDtypeStruct((1, D), F32),
            jax.ShapeDtypeStruct((1, width), F32),
            jax.ShapeDtypeStruct(back.shape, back.dtype),
        ],
        scratch_shapes=[pltpu.VMEM((n, width), BF)] + swap_scratch([back]),
        compiler_params=pltpu.CompilerParams(
            collective_id=collective_id, has_side_effects=True, vmem_limit_bytes=VMEM_LIMIT
        ),
        cost_estimate=pl.CostEstimate(
            flops=4 * n * D * width, bytes_accessed=16 * 2**20, transcendentals=0
        ),
    )(dq, dkv, normed, x, w, cosine, sine, back)


def exchange_back_kernel(sizes, dproj_ref, w_ref, attn_ref, dout_ref, o_ref, pair_s, sum_s, *sems):
    send_sems, recv_sems = sems
    greet(("head",), sizes)
    me, count = lax.axis_index("head"), sizes["head"]
    tok = dproj_ref.shape[0]
    copies = []
    for d in range(1, count):
        copy = remote(
            dproj_ref, pair_s.at[me], send_sems.at[d - 1], recv_sems.at[d - 1], "head", d, sizes
        )
        copy.start()
        copies.append(copy)
    cols = 2 * LANES

    def use(place, grads, fresh, last):
        rows = pl.ds(pl.multiple_of(place * tok, tok), tok)
        for low in range(0, w_ref.shape[0], cols):
            part = slice(low, low + cols)
            dout_ref[rows, part] = dot_nt(grads, w_ref[part, :]).astype(BF)
            made = dot_tn(attn_ref[rows, part], grads)
            if not fresh:
                made = made + sum_s[part, :]
            if last:
                o_ref[part, :] = made.astype(BF)
            else:
                sum_s[part, :] = made

    use(me, dproj_ref[...], True, count == 1)
    for d in range(1, count):
        copies[d - 1].wait_recv()
        place = lax.rem(me + count - d, count)
        use(place, pair_s[place], False, d == count - 1)
    for copy in copies:
        copy.wait_send()


def exchange_back(dproj, w, attn, sizes, collective_id):
    spec = pl.BlockSpec(memory_space=pltpu.VMEM)
    count = sizes["head"]
    return pl.pallas_call(
        functools.partial(exchange_back_kernel, sizes),
        in_specs=[spec] * 3,
        out_specs=[spec] * 2,
        out_shape=[
            jax.ShapeDtypeStruct(attn.shape, BF),
            jax.ShapeDtypeStruct(w.shape, BF),
        ],
        scratch_shapes=[
            pltpu.VMEM((count,) + dproj.shape, BF),
            pltpu.VMEM(w.shape, F32),
            pltpu.SemaphoreType.DMA((count - 1,)),
            pltpu.SemaphoreType.DMA((count - 1,)),
        ],
        compiler_params=pltpu.CompilerParams(
            collective_id=collective_id, has_side_effects=True, vmem_limit_bytes=VMEM_LIMIT
        ),
        cost_estimate=pl.CostEstimate(
            flops=4 * w.size * attn.shape[0], bytes_accessed=40 * 2**20, transcendentals=0
        ),
    )(dproj, w, attn)


def shards(
    sizes,
    hidden,
    cotangent,
    block_order,
    norm1,
    q_weight,
    q_bias,
    k_weight,
    k_bias,
    v_weight,
    v_bias,
    o_weight,
    norm2,
    gate_weight,
    up_weight,
    down_weight,
):
    tok = hidden.shape[0]
    pair = sizes["head"] * tok
    blk = int(np.prod([sizes[a] for a in BLK]))
    seqs = blk // SEQ_SPAN
    place_axes = {1: BLK, 2: BLK[:3], 4: BLK[:2]}[seqs]
    seq_axes = BLK[len(place_axes) :]
    head = lax.axis_index("head")
    place = place_of({}, place_axes, sizes)
    seq = place_of({}, seq_axes, sizes) if seq_axes else 0
    order = lax.dynamic_index_in_dim(block_order, seq, 0, keepdims=False)
    tops = lax.dynamic_slice_in_dim(order, place * 2, 2)
    slots = jnp.argsort(order).astype(jnp.int32)
    positions = (tops[:, None] * tok + jnp.arange(tok, dtype=jnp.int32)[None, :]).reshape(pair)
    frequency = THETA ** (-(jnp.arange(HEAD_DIM // 2, dtype=F32) * 2.0) / HEAD_DIM)
    angles = positions.astype(F32)[:, None] * frequency[None, :]
    cosine, sine = jnp.cos(angles), jnp.sin(angles)
    cosine = jnp.concatenate([cosine, cosine], axis=1)
    sine = jnp.concatenate([-sine, sine], axis=1)

    q_cols = D // 2
    kv_cols = HEAD_DIM
    rows = q_weight.shape[0]
    small = lax.reduce_precision(jnp.concatenate([norm1, norm2, q_bias, k_bias, v_bias]), 8, 7)
    small = jnp.pad(small, (0, 8 * LANES - small.shape[0])).reshape(8, LANES)
    parts = sizes["y"] * sizes["c"]
    width = gate_weight.shape[1]
    lanes = -(-width // (LANES * parts)) * LANES
    first = lanes * 6 // 9 // LANES * LANES
    ff_rows = gate_weight.shape[0]

    def along_z(part):
        part = part.reshape(1, 3, parts * ff_rows, part.shape[-1])
        return lax.all_gather(part, live(("g", "z"), sizes), axis=0, tiled=True)

    w_qkv, x_pair, small_all, w_out, packed_one, packed_two = front(
        (q_weight, k_weight, v_weight, o_weight),
        hidden,
        small,
        (down_weight, gate_weight, up_weight),
        first,
        lanes - first,
        [
            (0, None, AXES, AXES, True),
            (1, None, ("head",), ("head",), False),
            (2, None, AXES, AXES, False),
            (3, None, BLK, ("y", "z", "g", "c"), False),
        ],
        sizes,
        1,
    )
    w_out = w_out.reshape(q_cols, D)
    w_qkv = w_qkv.reshape(D, q_cols + 2 * kv_cols)
    x_pair = x_pair.reshape(pair, D)
    small_all = small_all.reshape(-1, 8 * LANES)
    kn = k_bias.shape[0]
    long = small_all[:, : 3 * rows].reshape(-1, 3, rows).transpose(1, 0, 2).reshape(3, D)
    short = small_all[:, 3 * rows : 3 * rows + 2 * kn].reshape(-1, 2, kn)
    short = short.transpose(1, 0, 2).reshape(2, 2 * kv_cols)
    gain_one, gain_two = long[:1], long[1:2]
    bias = jnp.concatenate(
        [
            lax.dynamic_slice_in_dim(v, head * n, n)
            for v, n in ((long[2], q_cols), (short[0], kv_cols), (short[1], kv_cols))
        ]
    )[None]
    far_axes, near_axes = place_axes[:2], place_axes[2:]
    group = ("head", "y", "c")
    cot_all = lax.all_gather(cotangent, group, axis=0, tiled=True)
    kv, mine_one, queries, normed = project(
        x_pair,
        w_qkv,
        gain_one,
        bias,
        cosine,
        sine,
        packed_one,
        cot_all,
        [(0, None, far_axes, far_axes, False)],
        sizes,
        2,
    )
    half = tok // 2
    crossed = [
        ((0, half), group, ("head", "y", "c"), False),
        ((half, half), group, ("y", "head", "c"), False),
    ]
    summed = [
        ((0, half), group, ("c", "head", "y"), False),
        ((half, half), group, ("c", "y", "head"), False),
    ]
    w_feed_one = along_z(mine_one)
    if near_axes:
        (kv,) = gather([kv], [(0, None, near_axes, near_axes, False)], sizes, 10)
    near_count = int(np.prod([sizes[a] for a in near_axes], dtype=int))
    far_count = SEQ_SPAN // near_count
    where = slots // 2
    slots = ((where % near_count) * far_count + where // near_count) * 2 + slots % 2
    kv = kv.reshape(2 * SEQ_SPAN, tok, 2 * HEAD_DIM)
    attended, lse = attend(slots, tops, queries, kv)
    attn_local = attended.astype(BF)
    inputs = hidden.astype(F32)
    mixed_part = dot_nn(attn_local, w_out).reshape(2, tok, D)
    mixed_got, mine_two = gather(
        [mixed_part.astype(BF)],
        [(0, None, ("head",), ("head",), True)],
        sizes,
        3,
        [packed_two],
    )
    w_feed_two = along_z(mine_two)
    mixed = (
        inputs
        + lax.dynamic_index_in_dim(mixed_part, head, 0, keepdims=False)
        + lax.dynamic_index_in_dim(mixed_got, 1 - head, 0, keepdims=False).astype(F32)
    )
    scale_two = inverse_rms(mixed)
    normed_two = (mixed * scale_two * gain_two).astype(BF)
    (tokens,) = gather([normed_two], [(0,) + c for c in crossed], sizes, 4)
    tokens = tokens.reshape(-1, D)

    places = w_feed_one.shape[0]
    act, dgate, dup, branch, dtokens = feed(tokens, cot_all, w_feed_one)
    parts_one = plain_grads(tokens, cot_all, act, dgate, dup, places)
    act, dgate, dup, branch, dtokens = feed(
        tokens, cot_all, w_feed_two, (branch, dtokens), (parts_one,)
    )
    dmixed, dproj, norm2_part, parts_two = feed_grads(
        dtokens.reshape(-1, tok, D),
        mixed,
        cotangent,
        gain_two,
        tokens,
        cot_all,
        act,
        dgate,
        dup,
        places,
        [(0,) + c for c in summed],
        sizes,
        5,
    )
    def collect(grad):
        total = lax.psum_scatter(grad, live(("g", "z"), sizes), scatter_dimension=0, tiled=True)
        return total.reshape(3, parts, ff_rows, grad.shape[-1])

    back_one = collect(parts_one)

    dout, o_part = exchange_back(dproj, w_out, attn_local, sizes, 6)

    dq, dkv_parts = attend_back(slots, tops, queries, kv, dout, lse, attended)
    dkv, d_out_weight, parts_two = scatter(
        [dkv_parts.reshape(SEQ_SPAN, pair, 2 * HEAD_DIM), o_part.reshape(blk, -1, D)],
        [
            (0, None, near_axes + far_axes, place_axes[::-1], False),
            (1, None, BLK, BLK[::-1], False),
        ],
        [BF, F32],
        sizes,
        7,
        carried=[parts_two],
    )
    back_two = collect(parts_two)
    w_part, dnormed, norm1_part, bias_part, back_one = project_back(
        dq, dkv, normed, x_pair, w_qkv, cosine, sine, back_one, blk, rows, 11
    )
    if w_part.ndim == 2:
        w_part = w_part.reshape(2, blk, rows, -1).transpose(1, 0, 2, 3)
    norm1_part, bias_part = norm1_part[0], bias_part[0]
    own = (jnp.arange(2) == head).astype(F32)[:, None]

    def owners(vector):
        return vector.reshape(2, blk, -1).transpose(1, 0, 2)

    def owned(vector):
        return owners((own * vector[None, :]).reshape(-1))

    small_grads = jnp.stack(
        [
            jnp.pad(part, ((0, 0), (0, 0), (0, LANES - part.shape[2])))
            for part in (
                owners(norm1_part),
                owners(norm2_part[0]),
                owned(bias_part[:q_cols]),
                owned(bias_part[q_cols : q_cols + kv_cols]),
                owned(bias_part[q_cols + kv_cols :]),
            )
        ]
        + [jnp.zeros((blk, 2, LANES), F32)] * 3,
        axis=2,
    )
    small_grads = small_grads.transpose(1, 0, 2, 3).reshape(2 * blk, 8, LANES)
    w_grads, small_sum, dnormed_sum, branch_sum = scatter(
        [
            w_part,
            small_grads,
            dnormed.reshape(2, tok, D),
            branch.reshape(-1, tok, D),
        ],
        [
            (0, None, BLK, BLK[::-1], True),
            (1, None, AXES, AXES[::-1], False),
            (2, None, ("head",), ("head",), False),
        ]
        + [(3,) + c for c in summed],
        [F32] * 4,
        sizes,
        8,
    )
    d_query, d_key, d_value, output, hidden_grad, d_down, d_gate, d_up = write_outputs(
        w_grads,
        dnormed_sum,
        branch_sum,
        dmixed,
        hidden,
        mixed,
        gain_one,
        [back_one] + list(swap([back_two], w_grads, 9)),
        width,
    )
    return (
        output,
        hidden_grad,
        small_sum[0, :rows],
        d_query,
        small_sum[2, :rows],
        d_key,
        small_sum[3, :kn],
        d_value,
        small_sum[4, :kn],
        d_out_weight,
        small_sum[1, :rows],
        d_gate,
        d_up,
        d_down,
    )


def solution(mesh):
    heads, blk = mesh.devices.shape
    split = jax.sharding.Mesh(mesh.devices.reshape(heads, blk // 16, 4, 2, 2), AXES)
    sizes = dict(split.shape)
    rows = P(AXES, None)
    vector = P(AXES)
    feed = P(BLK, "head")
    return jax.shard_map(
        functools.partial(shards, sizes),
        mesh=split,
        in_specs=(
            rows,
            rows,
            P(),
            vector,
            rows,
            vector,
            rows,
            vector,
            rows,
            vector,
            rows,
            vector,
            feed,
            feed,
            feed,
        ),
        out_specs=(
            rows,
            rows,
            vector,
            rows,
            vector,
            rows,
            vector,
            rows,
            vector,
            rows,
            vector,
            feed,
            feed,
            feed,
        ),
        check_vma=False,
    )
```

```python
import functools

import jax
import jax.numpy as jnp
import numpy as np
from jax import lax
from jax.experimental import pallas as pl
from jax.experimental.pallas import tpu as pltpu
from jax.sharding import PartitionSpec as P

D = 1536
QHEADS = 12
KVHEADS = 2
HEAD_DIM = 128
SEQ_SPAN = 16
BLOCK = 256

EPS = 1e-06
THETA = 1000000.0
SCALE = HEAD_DIM**-0.5
LOG2E = 1.4426950408889634
SCALE2 = SCALE * LOG2E
BF = jnp.bfloat16
F32 = jnp.float32
MESH = pl.DeviceIdType.MESH
VMEM_LIMIT = 56 * 2**20
AXES = ("head", "g", "z", "y", "c")
BLK = ("g", "z", "y", "c")
LANES = 128


def dot_nn(a, b):
    return lax.dot_general(a, b, (((1,), (0,)), ((), ())), preferred_element_type=F32)


def dot_nt(a, b):
    return lax.dot_general(a, b, (((1,), (1,)), ((), ())), preferred_element_type=F32)


def dot_tn(a, b):
    return lax.dot_general(a, b, (((0,), (0,)), ((), ())), preferred_element_type=F32)


def live(axes, sizes):
    return tuple(a for a in axes if sizes[a] > 1)


def greet(axes, sizes, diagonal=False):
    barrier = pltpu.get_barrier_semaphore()
    count = 0
    if diagonal:
        pl.semaphore_signal(barrier, inc=1, device_id=across(3), device_id_type=MESH)
        count += 1
    for a in axes:
        me = lax.axis_index(a)
        for d in range(1, sizes[a]):
            pl.semaphore_signal(
                barrier,
                inc=1,
                device_id={a: lax.rem(me + d, sizes[a])},
                device_id_type=MESH,
            )
            count += 1
    pl.semaphore_wait(barrier, count)


def across(d):
    y, c = lax.axis_index("y"), lax.axis_index("c")
    return {"y": 1 - y if d & 2 else y, "c": 1 - c if d & 1 else c}


class Swap:
    def __init__(self, x, out, send_sems, recv_sems, local_sem):
        me = lax.axis_index("y") * 2 + lax.axis_index("c")
        self.kept = pltpu.make_async_copy(x.at[:, me], out.at[:, me], local_sem)
        self.copies = []
        for d in range(1, 4):
            to = across(d)
            self.copies.append(
                pltpu.make_async_remote_copy(
                    src_ref=x.at[:, to["y"] * 2 + to["c"]],
                    dst_ref=out.at[:, me],
                    send_sem=send_sems.at[d - 1],
                    recv_sem=recv_sems.at[d - 1],
                    device_id=to,
                    device_id_type=MESH,
                )
            )

    def start(self):
        for copy in self.copies:
            copy.start()
        self.kept.start()

    def wait(self):
        self.kept.wait()
        for copy in self.copies:
            copy.wait()


def swap_scratch(swaps):
    if not swaps:
        return []
    return [pltpu.SemaphoreType.DMA((3 * len(swaps),))] * 2 + [
        pltpu.SemaphoreType.DMA((len(swaps),))
    ]


def swaps_of(xs, outs, sems):
    return [
        Swap(
            x,
            out,
            sems[0].at[pl.ds(3 * i, 3)],
            sems[1].at[pl.ds(3 * i, 3)],
            sems[2].at[i],
        )
        for i, (x, out) in enumerate(zip(xs, outs))
    ]


def place_of(offsets, axes, sizes):
    value = 0
    for a in axes:
        me = lax.axis_index(a)
        off = offsets.get(a, 0)
        value = value * sizes[a] + (lax.rem(me + off, sizes[a]) if off else me)
    return value


def remote(src, dst, send, recv, axis, distance, sizes):
    to = lax.rem(lax.axis_index(axis) + distance, sizes[axis])
    return pltpu.make_async_remote_copy(
        src_ref=src,
        dst_ref=dst,
        send_sem=send,
        recv_sem=recv,
        device_id={axis: to},
        device_id_type=MESH,
    )


def gather_kernel(plans, sizes, swap_count, waited, carried, *refs, ahead=None, behind=None):
    count = max(p[0] for p in plans) + 1
    xs, refs = refs[:count], refs[count:]
    swap_xs, refs = refs[:swap_count], refs[swap_count + waited :]
    outs, refs = refs[:count], refs[count:]
    swap_outs, refs = refs[:swap_count], refs[swap_count + carried :]
    send_sems, recv_sems, local_sems = refs[:3]
    swaps = swaps_of(swap_xs, swap_outs, refs[3:])
    used = {a: (sizes[a] if any(a in p[3] for p in plans) else 1) for a in AXES}
    if swaps:
        used.update(y=sizes["y"], c=sizes["c"])
    greet(live(AXES, used), sizes, bool(swaps))

    def cut(ref, rows):
        return ref if rows is None else ref.at[pl.ds(*rows)]

    def source(plan, place):
        i, rows, layout, phases, split = plan
        return cut(xs[i].at[place] if split else xs[i], rows)

    def landed(slot, number):
        axis = plans[0][3][0]
        return remote(slot, slot, send_sems.at[number], recv_sems.at[number], axis, 0, sizes)

    sends, kept, queue = [], [], []
    sem = 0
    for j, plan in enumerate(plans):
        i, rows, layout, phases, split = plan
        mine = source(plan, lax.axis_index(phases[0]))
        slot = cut(outs[i].at[place_of({}, layout, sizes)], rows)
        copy = pltpu.make_async_copy(mine, slot, local_sems.at[j])
        queue.append((plan, {}, -1, None))
        kept.append(copy)
    at = 0
    ends = []
    while at < len(queue):
        plan, offsets, phase, arrived = queue[at]
        at += 1
        i, rows, layout, phases, split = plan
        slot = cut(outs[i].at[place_of(offsets, layout, sizes)], rows)
        if arrived is None:
            src = source(plan, lax.axis_index(phases[0]))
        else:
            src = slot
            landed(slot, arrived).wait_recv()
        for p in range(phase + 1, len(phases)):
            a = phases[p]
            for d in range(1, sizes[a]):
                piece = src
                if split and p == 0:
                    piece = source(plan, lax.rem(lax.axis_index(a) + d, sizes[a]))
                copy = remote(piece, slot, send_sems.at[sem], recv_sems.at[sem], a, d, sizes)
                copy.start()
                sends.append(copy)
                later = dict(offsets)
                later[a] = sizes[a] - d
                if p + 1 < len(phases):
                    queue.append((plan, later, p, sem))
                else:
                    ends.append((plan, later, sem))
                sem += 1
        if at == len(plans):
            if ahead is not None:
                ahead()
            for copy in kept + swaps:
                copy.start()
            if behind is not None:
                behind()
    for (i, rows, layout, phases, split), offsets, arrived in ends:
        landed(cut(outs[i].at[place_of(offsets, layout, sizes)], rows), arrived).wait_recv()
    for copy in kept + swaps:
        copy.wait()
    for copy in sends:
        copy.wait_send()


def gather(arrays, plans, sizes, collective_id, swaps=(), after=(), carried=()):
    plans = [
        (i, rows, live(layout, sizes), live(phases, sizes), split)
        for i, rows, layout, phases, split in plans
    ]
    counts = [int(np.prod([sizes[a] for a in p[2]])) for p in plans]
    total = sum(counts) - len(counts)
    shapes = []
    for i, x in enumerate(arrays):
        n, split = next((c, p[4]) for c, p in zip(counts, plans) if p[0] == i)
        shapes.append(jax.ShapeDtypeStruct((n,) + (x.shape[1:] if split else x.shape), x.dtype))
    spec = pl.BlockSpec(memory_space=pltpu.VMEM)
    far = pl.BlockSpec(memory_space=pl.ANY)
    specs = [spec] * len(arrays) + [far] * len(swaps)
    moved = sum(int(np.prod(s.shape)) * s.dtype.itemsize for s in shapes)
    return pl.pallas_call(
        functools.partial(
            gather_kernel, plans, sizes, len(swaps), len(after) + len(carried), len(carried)
        ),
        out_shape=shapes + [jax.ShapeDtypeStruct(x.shape, x.dtype) for x in (*swaps, *carried)],
        in_specs=specs + [far] * (len(after) + len(carried)),
        out_specs=[far] * (len(specs) + len(carried)),
        input_output_aliases={
            len(specs) + len(after) + i: len(specs) + i for i in range(len(carried))
        },
        scratch_shapes=[
            pltpu.SemaphoreType.DMA((total,)),
            pltpu.SemaphoreType.DMA((total,)),
            pltpu.SemaphoreType.DMA((len(plans),)),
        ]
        + swap_scratch(swaps),
        compiler_params=pltpu.CompilerParams(
            collective_id=collective_id, has_side_effects=True, vmem_limit_bytes=VMEM_LIMIT
        ),
        cost_estimate=pl.CostEstimate(flops=0, bytes_accessed=20 * moved, transcendentals=0),
    )(*arrays, *swaps, *after, *carried)


def front_kernel(plans, sizes, *refs):
    q_ref, k_ref, v_ref, o_ref, hidden_ref, small_ref = refs[:6]
    feeds, refs = refs[6:9], refs[9:]
    outs, first_ref, second_ref, refs = refs[:4], refs[4], refs[5], refs[6:]
    halves_s, o_s, feed_s, feed_sems = refs[:4]
    loads = [
        pltpu.make_async_copy(feeds[m], feed_s.at[m], feed_sems.at[m]) for m in range(len(feeds))
    ]
    for copy in loads:
        copy.start()
    heads = halves_s.shape[0]
    q_cols, kv_cols = q_ref.shape[1] // heads, k_ref.shape[1] // heads
    for i in range(heads):
        halves_s[i, :, :q_cols] = q_ref[:, i * q_cols : (i + 1) * q_cols].astype(BF)
        cols = slice(i * kv_cols, (i + 1) * kv_cols)
        halves_s[i, :, q_cols : q_cols + kv_cols] = k_ref[:, cols].astype(BF)
        halves_s[i, :, q_cols + kv_cols :] = v_ref[:, cols].astype(BF)
    o_s[...] = o_ref[...].astype(BF)

    def pack():
        first, second = first_ref.shape[-1], second_ref.shape[-1]
        for m in range(len(feeds)):
            loads[m].wait()
            rows, width = feed_s.shape[1:]
            for i in range(first_ref.shape[1]):
                low = i * (first + second)
                for ref, n in ((first_ref, first), (second_ref, second)):
                    real = min(n, width - low)
                    ref[m, i, :, :real] = feed_s[m, :, low : low + real].astype(BF)
                    if real < n:
                        ref[m, i, :, real:] = jnp.zeros((rows, n - real), BF)
                    low += n

    gather_kernel(
        plans,
        sizes,
        0,
        0,
        0,
        halves_s,
        hidden_ref,
        small_ref,
        o_s,
        *outs,
        *refs[4:],
        ahead=pack,
    )


def front(weights, hidden, small, feeds, first, second, plans, sizes, collective_id):
    plans = alive(plans, sizes)
    heads, rows = sizes["head"], weights[0].shape[0]
    halves = jax.ShapeDtypeStruct((heads, rows, sum(w.shape[1] for w in weights[:3]) // heads), BF)
    out = jax.ShapeDtypeStruct(weights[3].shape, BF)
    arrays = [halves, hidden, small, out]
    counts = [int(np.prod([sizes[a] for a in p[2]])) for p in plans]
    total = sum(counts) - len(counts)
    shapes = [
        jax.ShapeDtypeStruct((n,) + (x.shape[1:] if p[4] else x.shape), x.dtype)
        for n, x, p in zip(counts, arrays, plans)
    ]
    ff_rows = feeds[0].shape[0]
    blocks = [jax.ShapeDtypeStruct((3, 4, ff_rows, n), BF) for n in (first, second)]
    spec = pl.BlockSpec(memory_space=pltpu.VMEM)
    return pl.pallas_call(
        functools.partial(front_kernel, plans, sizes),
        out_shape=shapes + blocks,
        in_specs=[spec] * 6 + [pl.BlockSpec(memory_space=pl.ANY)] * 3,
        out_specs=[pl.BlockSpec(memory_space=pl.ANY)] * 4 + [spec] * 2,
        scratch_shapes=[
            pltpu.VMEM(halves.shape, BF),
            pltpu.VMEM(out.shape, BF),
            pltpu.VMEM((3,) + feeds[0].shape, F32),
            pltpu.SemaphoreType.DMA((3,)),
            pltpu.SemaphoreType.DMA((total,)),
            pltpu.SemaphoreType.DMA((total,)),
            pltpu.SemaphoreType.DMA((len(plans),)),
        ],
        compiler_params=pltpu.CompilerParams(
            collective_id=collective_id, has_side_effects=True, vmem_limit_bytes=VMEM_LIMIT
        ),
        cost_estimate=pl.CostEstimate(flops=0, bytes_accessed=100 * 2**20, transcendentals=0),
    )(*weights, hidden, small, *feeds)


def offset_keys(axes, sizes):
    keys = [{}]
    for a in axes:
        keys = [dict(k, **{a: d}) for k in keys for d in list(range(1, sizes[a])) + [0]]
    return keys


def scatter_kernel(plans, sizes, *refs, between=None, held=None, held_sems=None):
    count = max(p[0] for p in plans) + 1
    xs, outs = refs[:count], refs[count : 2 * count]
    held = held or {}
    at = 2 * count
    bufs = []
    for _, _, _, phases, swap in plans:
        n = len(phases)
        bufs.append((refs[at : at + n], refs[at + n : at + 2 * n]))
        at += 2 * n
    send_sems, recv_sems, local_sems = refs[at:]
    used = {
        a: (sizes[a] if any(a in p[3] or (p[4] and a == "head") for p in plans) else 1)
        for a in AXES
    }
    loads = {}
    for j, (i, rows, layout, phases, swap) in enumerate(plans):
        if i not in held:
            continue
        for key in offset_keys(phases[1:], sizes):
            place = place_of(key, layout, sizes)
            src, dst = xs[i].at[place], held[i].at[place]
            if rows is not None:
                src, dst = src.at[pl.ds(*rows)], dst.at[pl.ds(*rows)]
            copy = pltpu.make_async_copy(src, dst, held_sems.at[len(loads)])
            copy.start()
            loads[j, tuple(key.get(a, 0) for a in phases[1:])] = copy
    greet(live(AXES, used), sizes)
    sem = 0
    sends = []
    arrivals = [dict() for _ in plans]

    def number(offsets, axes):
        value = 0
        for a in axes:
            value = value * sizes[a] + offsets.get(a, 0)
        return value

    def block_of(j, offsets, near=False):
        i, rows, layout, phases, swap = plans[j]
        block = (held.get(i, xs[i]) if near else xs[i]).at[place_of(offsets, layout, sizes)]
        return block if rows is None else block.at[pl.ds(*rows)]

    def total_of(j, offsets, phase):
        phases = plans[j][3]
        if plans[j][0] in held:
            loads[j, tuple(offsets.get(a, 0) for a in phases[1:])].wait()
        total = block_of(j, offsets, True)[...].astype(F32)
        for q in range(phase):
            rest = phases[q + 1 :]
            for d in range(1, sizes[phases[q]]):
                s = arrivals[j].pop((q, d, number(offsets, rest)))
                buf = bufs[j][1][q].at[d - 1, number(offsets, rest)]
                remote(buf, buf, send_sems.at[s], recv_sems.at[s], phases[q], 0, sizes).wait_recv()
                total = total + buf[...].astype(F32)
        return total

    depth = max(len(p[3]) for p in plans)
    for phase in range(depth):
        for j, (i, rows, layout, phases, swap) in enumerate(plans):
            if phase >= len(phases):
                continue
            a, rest = phases[phase], phases[phase + 1 :]
            for d in range(1, sizes[a]):
                for key in offset_keys(rest, sizes):
                    offsets = dict(key)
                    offsets[a] = d
                    where = number(key, rest)
                    if phase == 0:
                        src = block_of(j, offsets)
                    else:
                        src = bufs[j][0][phase].at[d - 1, where]
                        src[...] = total_of(j, offsets, phase).astype(src.dtype)
                    dst = bufs[j][1][phase].at[d - 1, where]
                    copy = remote(src, dst, send_sems.at[sem], recv_sems.at[sem], a, d, sizes)
                    copy.start()
                    sends.append(copy)
                    arrivals[j][(phase, d, where)] = sem
                    sem += 1
        if between is not None:
            between(phase)
    late = []
    for j, (i, rows, layout, phases, swap) in enumerate(plans):
        total = total_of(j, {}, len(phases))
        if swap:
            hold, out = bufs[j][0][0], outs[i]
            hold[...] = total.astype(hold.dtype)
            me = lax.axis_index("head")
            copy = pltpu.make_async_copy(hold.at[me], out.at[me], local_sems.at[j])
            copy.start()
            late.append((copy, None))
            for d in range(1, sizes["head"]):
                to = lax.rem(me + d, sizes["head"])
                copy = remote(
                    hold.at[to], out.at[me], send_sems.at[sem], recv_sems.at[sem], "head", d, sizes
                )
                copy.start()
                sends.append(copy)
                late.append((out.at[lax.rem(me + sizes["head"] - d, sizes["head"])], sem))
                sem += 1
        elif rows is None:
            outs[i][...] = total.astype(outs[i].dtype)
        else:
            outs[i][pl.ds(*rows)] = total.astype(outs[i].dtype)
    for item, s in late:
        if s is None:
            item.wait()
        else:
            remote(item, item, send_sems.at[s], recv_sems.at[s], "head", 0, sizes).wait_recv()
    for copy in sends:
        copy.wait_send()


def scatter_scratch(arrays, plans, out_types, sizes):
    scratch, total = [], 0
    for i, rows, layout, phases, swap in plans:
        x, kind = arrays[i], out_types[i]
        block = x.shape[1:] if rows is None else (rows[1],) + x.shape[2:]
        send_bufs, recv_bufs = [], []
        for p, a in enumerate(phases):
            rest = int(np.prod([sizes[b] for b in phases[p + 1 :]], dtype=int))
            shape = (sizes[a] - 1, rest) + block
            recv_bufs.append(pltpu.VMEM(shape, x.dtype))
            if p == 0:
                send_bufs.append(pltpu.VMEM(block if swap else (8, LANES), kind if swap else F32))
            else:
                send_bufs.append(pltpu.VMEM(shape, x.dtype))
            total += (sizes[a] - 1) * rest
        scratch += send_bufs + recv_bufs
        if swap:
            total += sizes["head"] - 1
    return scratch + [
        pltpu.SemaphoreType.DMA((total,)),
        pltpu.SemaphoreType.DMA((total,)),
        pltpu.SemaphoreType.DMA((len(plans),)),
    ]


def held_scratch(arrays, plans, far, sizes):
    count = 0
    for i, _, _, phases, _ in plans:
        if i in far:
            count += int(np.prod([sizes[a] for a in phases[1:]], dtype=int))
    return [pltpu.VMEM(arrays[i].shape, arrays[i].dtype) for i in far] + [
        pltpu.SemaphoreType.DMA((count,))
    ]


def alive(plans, sizes):
    return [
        (i, rows, live(layout, sizes), live(phases, sizes), flag)
        for i, rows, layout, phases, flag in plans
    ]


def scatter_and_wait_kernel(plans, sizes, arrays, waited, carried, far, *refs):
    xs, refs = refs[:arrays], refs[arrays + waited :]
    outs, refs, held = refs[:arrays], refs[arrays + carried :], {}
    if far:
        held = dict(zip(far, refs[-len(far) - 1 : -1]))
        refs, held_sems = refs[: -len(far) - 1], refs[-1]
        scatter_kernel(plans, sizes, *xs, *outs, *refs, held=held, held_sems=held_sems)
    else:
        scatter_kernel(plans, sizes, *xs, *outs, *refs)


def scatter(arrays, plans, out_types, sizes, collective_id, after=(), carried=()):
    plans = alive(plans, sizes)
    shapes = [jax.ShapeDtypeStruct(x.shape[1:], kind) for x, kind in zip(arrays, out_types)]
    spec = pl.BlockSpec(memory_space=pltpu.VMEM)
    far = pl.BlockSpec(memory_space=pl.ANY)
    big = tuple(i for i, x in enumerate(arrays) if x.dtype == BF)
    moved = sum(int(np.prod(x.shape)) * x.dtype.itemsize for x in arrays)
    return pl.pallas_call(
        functools.partial(
            scatter_and_wait_kernel,
            plans,
            sizes,
            len(arrays),
            len(after) + len(carried),
            len(carried),
            big,
        ),
        out_shape=shapes + [jax.ShapeDtypeStruct(x.shape, x.dtype) for x in carried],
        in_specs=[far if i in big else spec for i in range(len(arrays))] + [far] * (len(after) + len(carried)),
        out_specs=[spec] * len(arrays) + [far] * len(carried),
        input_output_aliases={
            len(arrays) + len(after) + i: len(arrays) + i for i in range(len(carried))
        },
        scratch_shapes=scatter_scratch(arrays, plans, out_types, sizes)
        + (held_scratch(arrays, plans, big, sizes) if big else []),
        compiler_params=pltpu.CompilerParams(
            collective_id=collective_id, has_side_effects=True, vmem_limit_bytes=VMEM_LIMIT
        ),
        cost_estimate=pl.CostEstimate(flops=0, bytes_accessed=20 * moved, transcendentals=0),
    )(*arrays, *after, *carried)


def swap_kernel(count, *refs):
    items = swaps_of(refs[:count], refs[count + 1 : 2 * count + 1], refs[2 * count + 1 :])
    greet(("y", "c"), {"y": 2, "c": 2}, True)
    for item in items:
        item.start()
    for item in items:
        item.wait()


def swap(xs, last, collective_id):
    far = pl.BlockSpec(memory_space=pl.ANY)
    n = len(xs)
    return pl.pallas_call(
        functools.partial(swap_kernel, n),
        out_shape=[jax.ShapeDtypeStruct(x.shape, x.dtype) for x in xs],
        in_specs=[far] * (n + 1),
        out_specs=[far] * n,
        scratch_shapes=swap_scratch(xs),
        compiler_params=pltpu.CompilerParams(
            collective_id=collective_id, has_side_effects=True, vmem_limit_bytes=VMEM_LIMIT
        ),
    )(*xs, last)


def outputs_kernel(*refs):
    w_ref, dnormed_ref, branch_ref, dmixed_ref, x_ref, mixed_ref, gain_ref = refs[:7]
    parts, refs = refs[7:9], refs[9:]
    q_ref, k_ref, v_ref, out_ref, hidden_ref = refs[:5]
    feeds = refs[5:]
    heads = w_ref.shape[0]
    q_cols = q_ref.shape[1] // heads
    for i in range(heads):
        cols = slice(i * HEAD_DIM, (i + 1) * HEAD_DIM)
        q_ref[:, i * q_cols : (i + 1) * q_cols] = w_ref[i, :, :q_cols]
        k_ref[:, cols] = w_ref[i, :, q_cols : q_cols + HEAD_DIM]
        v_ref[:, cols] = w_ref[i, :, q_cols + HEAD_DIM :]
    out_ref[...] = (mixed_ref[...] + branch_ref[...]).astype(BF)
    x = x_ref[...].astype(F32)
    scale = inverse_rms(x)
    z = x * scale
    u = gain_ref[...] * dnormed_ref[...]
    hidden_ref[...] = (
        dmixed_ref[...] + scale * (u - z * jnp.mean(z * u, axis=-1, keepdims=True))
    ).astype(BF)
    width = feeds[0].shape[1]
    lanes = sum(part.shape[-1] for part in parts)
    for m, feed_ref in enumerate(feeds):
        for i in range(parts[0].shape[1]):
            low = i * lanes
            for part in parts:
                n = part.shape[-1]
                real = min(n, width - low)
                if real > 0:
                    feed_ref[:, low : low + real] = part[m, i, :, :real].astype(F32)
                low += n


def write_outputs(w, dnormed, branch, dmixed, x, mixed, gain, parts, width):
    heads, rows, inner = w.shape
    tok, ff_rows = x.shape[0], parts[0].shape[2]
    steps = 2 if rows % 16 == 0 and ff_rows % 32 == 0 else 1

    def rows_of(shape, dim):
        block = tuple(n // steps if i == dim else n for i, n in enumerate(shape))
        return pl.BlockSpec(block, lambda i: tuple(i if k == dim else 0 for k in range(len(shape))))

    kinds = [
        ((rows, heads * (inner - 2 * HEAD_DIM)), F32),
        ((rows, heads * HEAD_DIM), F32),
        ((rows, heads * HEAD_DIM), F32),
        (x.shape, BF),
        (x.shape, BF),
    ] + [((ff_rows, width), F32)] * 3
    return pl.pallas_call(
        outputs_kernel,
        grid=(steps,),
        out_shape=[jax.ShapeDtypeStruct(*k) for k in kinds],
        in_specs=[rows_of(w.shape, 1)]
        + [rows_of(x.shape, 0)] * 5
        + [pl.BlockSpec(gain.shape, lambda i: (0, 0))]
        + [rows_of(part.shape, 2) for part in parts],
        out_specs=[rows_of(shape, 0) for shape, _ in kinds],
        compiler_params=pltpu.CompilerParams(vmem_limit_bytes=VMEM_LIMIT),
        cost_estimate=pl.CostEstimate(flops=0, bytes_accessed=20 * 2**20, transcendentals=0),
    )(w, dnormed, branch, dmixed, x, mixed, gain, *parts)


def feed_kernel(chunks, added, t_ref, c_ref, w_ref, *refs):
    act_ref, dgate_ref, dup_ref, branch_ref, dtok_ref = refs[-5:]
    before = refs[:added]
    tokens, cot = t_ref[...], c_ref[...]
    places, _, rows, width = w_ref.shape
    per = max(1, LANES * 3 // rows)

    def products(j):
        low, n = chunks[j]

        def weight(m):
            return w_ref[:, m, :, low : low + n].reshape(D, n)

        return dot_nn(tokens, weight(1)), dot_nn(tokens, weight(2)), dot_nn(cot, weight(0))

    ready = [products(0)]
    for j, (low, n) in enumerate(chunks):
        gate, up, dact = ready[j]
        if j + 1 < len(chunks):
            ready.append(products(j + 1))
        sig = 1.0 / (1.0 + jnp.exp(-gate))
        silu = gate * sig
        act_ref[:, low : low + n] = (silu * up).astype(BF)
        dgate_ref[:, low : low + n] = (dact * up * (sig + silu * (1.0 - sig))).astype(BF)
        dup_ref[:, low : low + n] = (dact * silu).astype(BF)
    for z in range(0, places, per):
        cols = slice(z * rows, (z + per) * rows)

        def weight(m):
            return w_ref[z : z + per, m].reshape(per * rows, width)

        dtok = dot_nt(dgate_ref[...], weight(1)) + dot_nt(dup_ref[...], weight(2))
        branch = dot_nt(act_ref[...], weight(0))
        if before:
            branch = branch + before[0][:, cols].astype(F32)
            dtok = dtok + before[1][:, cols].astype(F32)
        dtok_ref[:, cols] = dtok.astype(BF)
        branch_ref[:, cols] = branch.astype(BF)


def feed(tokens, cot, weights, before=(), after=()):
    n, width, tile = tokens.shape[0], weights.shape[-1], 256
    chunks = [(i, min(256, width - i)) for i in range(0, width, 256)]
    wide = pl.BlockSpec((tile, D), lambda i: (i, 0))
    inner = pl.BlockSpec((tile, width), lambda i: (i, 0))
    return pl.pallas_call(
        functools.partial(feed_kernel, chunks, len(before)),
        grid=(n // tile,),
        in_specs=[wide, wide, pl.BlockSpec(memory_space=pltpu.VMEM)]
        + [wide] * len(before)
        + [pl.BlockSpec(memory_space=pl.ANY)] * len(after),
        out_specs=[inner, inner, inner, wide, wide],
        out_shape=[jax.ShapeDtypeStruct((n, k), BF) for k in (width, width, width, D, D)],
        compiler_params=pltpu.CompilerParams(vmem_limit_bytes=VMEM_LIMIT),
        cost_estimate=pl.CostEstimate(
            flops=12 * n * D * width, bytes_accessed=40 * 2**20, transcendentals=n * width
        ),
    )(tokens, cot, weights, *before, *after)


def plain_grads_kernel(t_ref, c_ref, act_ref, dgate_ref, dup_ref, grad_ref):
    per, _, rows, width = grad_ref.shape
    for m, (left, right) in enumerate(((c_ref, act_ref), (t_ref, dgate_ref), (t_ref, dup_ref))):
        made = dot_tn(left[...], right[...]).astype(BF)
        grad_ref[:, m] = made.reshape(per, rows, width)


def plain_grads(tokens, cot, act, dgate, dup, places):
    n, width = act.shape
    rows = D // places
    per = max(1, LANES * 3 // rows)
    left = pl.BlockSpec((n, per * rows), lambda k: (0, k))
    right = pl.BlockSpec(memory_space=pltpu.VMEM)
    return pl.pallas_call(
        plain_grads_kernel,
        grid=(places // per,),
        in_specs=[left, left, right, right, right],
        out_specs=pl.BlockSpec((per, 3, rows, width), lambda k: (k, 0, 0, 0)),
        out_shape=jax.ShapeDtypeStruct((places, 3, rows, width), BF),
        compiler_params=pltpu.CompilerParams(vmem_limit_bytes=VMEM_LIMIT),
        cost_estimate=pl.CostEstimate(
            flops=6 * n * D * width, bytes_accessed=40 * 2**20, transcendentals=0
        ),
    )(tokens, cot, act, dgate, dup)


def grads_kernel(plans, sizes, dtok_ref, mixed_ref, cot_ref, gain_ref, *refs):
    t_hbm, c_hbm, act_hbm, dgate_hbm, dup_hbm = refs[:5]
    dmixed_ref, dproj_ref, gain_grad_ref, grad_hbm = refs[5:9]
    sum_ref, left_s, right_s, made_s, load_sems, made_sems = refs[9:15]
    held, held_sems = {0: refs[-2]}, refs[-1]
    per, rows = made_s.shape[1:3]
    cols = per * rows
    loads = [
        pltpu.make_async_copy(c_hbm, left_s.at[0], load_sems.at[0]),
        pltpu.make_async_copy(act_hbm, right_s.at[0], load_sems.at[1]),
        pltpu.make_async_copy(t_hbm, left_s.at[1], load_sems.at[2]),
        pltpu.make_async_copy(dgate_hbm, right_s.at[1], load_sems.at[3]),
        pltpu.make_async_copy(dup_hbm, right_s.at[0], load_sems.at[4]),
    ]
    for copy in loads[:4]:
        copy.start()

    def stored(m, k, slot):
        return pltpu.make_async_copy(
            made_s.at[slot], grad_hbm.at[pl.ds(k * per, per), m], made_sems.at[slot]
        )

    def some(m, low, high, left, right, fresh):
        def one(k, carry):
            slot = lax.rem(k, 2)
            if fresh:
                pl.when(k >= 2)(lambda: stored(m, k, slot).wait())
            else:
                stored(m, k, slot).wait()
            part = left_s[left, :, pl.ds(pl.multiple_of(k * cols, LANES), cols)]
            made_s[slot] = dot_tn(part, right_s[right]).astype(BF).reshape(made_s.shape[1:])
            stored(m, k, slot).start()
            return carry

        lax.fori_loop(low, high, one, 0)

    chunks = D // cols

    def between(phase):
        if phase == 0:
            loads[0].wait()
            loads[1].wait()
            some(0, 0, chunks // 2, 0, 0, True)
        elif phase == 1:
            some(0, chunks // 2, chunks, 0, 0, False)
            loads[4].start()
            loads[2].wait()
            loads[3].wait()
            some(1, 0, chunks, 1, 1, False)
        else:
            loads[4].wait()
            some(2, 0, chunks, 1, 0, False)

    scatter_kernel(
        plans,
        sizes,
        dtok_ref,
        sum_ref,
        *refs[15:-2],
        between=between,
        held=held,
        held_sems=held_sems,
    )
    mixed, dnormed = mixed_ref[...], sum_ref[...]
    scale = inverse_rms(mixed)
    z = mixed * scale
    u = gain_ref[...] * dnormed
    gain_grad_ref[...] = jnp.sum(dnormed * z, axis=0, keepdims=True)
    dmixed = cot_ref[...].astype(F32) + scale * (
        u - z * jnp.mean(z * u, axis=-1, keepdims=True)
    )
    dmixed_ref[...] = dmixed
    dproj_ref[...] = dmixed.astype(BF)
    for slot in range(2):
        stored(2, slot, slot).wait()


def feed_grads(dtok, mixed, cot_own, gain, tokens, cot, act, dgate, dup, places, plans, sizes, collective_id):
    plans = alive(plans, sizes)
    n, width = act.shape
    rows = D // places
    per = max(1, LANES * 3 // rows)
    spec = pl.BlockSpec(memory_space=pltpu.VMEM)
    far = pl.BlockSpec(memory_space=pl.ANY)
    return pl.pallas_call(
        functools.partial(grads_kernel, plans, sizes),
        out_shape=[
            jax.ShapeDtypeStruct(dtok.shape[1:], F32),
            jax.ShapeDtypeStruct(dtok.shape[1:], BF),
            jax.ShapeDtypeStruct((1, D), F32),
            jax.ShapeDtypeStruct((places, 3, rows, width), BF),
        ],
        in_specs=[far] + [spec] * 3 + [far] * 5,
        out_specs=[spec] * 3 + [far],
        scratch_shapes=[
            pltpu.VMEM(dtok.shape[1:], F32),
            pltpu.VMEM((2, n, D), BF),
            pltpu.VMEM((2, n, width), BF),
            pltpu.VMEM((2, per, rows, width), BF),
            pltpu.SemaphoreType.DMA((5,)),
            pltpu.SemaphoreType.DMA((2,)),
        ]
        + scatter_scratch([dtok], plans, [F32], sizes)
        + held_scratch([dtok], plans, (0,), sizes),
        compiler_params=pltpu.CompilerParams(
            collective_id=collective_id, has_side_effects=True, vmem_limit_bytes=VMEM_LIMIT
        ),
        cost_estimate=pl.CostEstimate(
            flops=6 * n * D * width, bytes_accessed=100 * 2**20, transcendentals=0
        ),
    )(dtok, mixed, cot_own, gain, tokens, cot, act, dgate, dup)


def forward_kernel(heads, slots, tops, q_ref, kv_ref, o_ref, lse_ref, top_s, sum_s, acc_s):
    def score(keys, a, h):
        return dot_nt(keys, q_ref[a * BLOCK : (a + 1) * BLOCK, h * HEAD_DIM : (h + 1) * HEAD_DIM])

    for a in range(2):
        top_s[...] = jnp.full(top_s.shape, -1e30, F32)
        sum_s[...] = jnp.zeros(sum_s.shape, F32)
        acc_s[...] = jnp.zeros(acc_s.shape, F32)
        count = tops[a] + 1

        def step(keys, values_t):
            ahead = min(3, heads)
            ready = [score(keys, a, h) for h in range(ahead)]
            for h in range(heads):
                s = ready[h]
                if h + ahead < heads:
                    ready.append(score(keys, a, h + ahead))
                old = top_s[h : h + 1, :]
                new = jnp.maximum(old, jnp.max(s, axis=0, keepdims=True))
                p = jnp.exp2((s - new) * SCALE2)
                fade = jnp.exp2((old - new) * SCALE2)
                sum_s[h : h + 1, :] = sum_s[h : h + 1, :] * fade + jnp.sum(p, axis=0, keepdims=True)
                top_s[h : h + 1, :] = new
                acc_s[h] = acc_s[h] * fade + dot_nn(values_t, p.astype(BF))

        def two(i, carry):
            first, second = slots[2 * i], slots[2 * i + 1]
            both = jnp.concatenate([kv_ref[first], kv_ref[second]], axis=0)
            step(both[:, :HEAD_DIM], both[:, HEAD_DIM:].T)
            return carry

        lax.fori_loop(0, count // 2, two, 0)

        @pl.when(count % 2 == 1)
        def _():
            last = kv_ref[slots[count - 1]]
            step(last[:, :HEAD_DIM], last[:, HEAD_DIM:].T)

        for h in range(heads):
            total = sum_s[h : h + 1, :]
            o_ref[a * BLOCK : (a + 1) * BLOCK, h * HEAD_DIM : (h + 1) * HEAD_DIM] = (
                acc_s[h] / total
            ).T
            lse_ref[a, h : h + 1, :] = top_s[h : h + 1, :] * SCALE2 + jnp.log2(total)
        lse_ref[a, heads:8, :] = jnp.zeros((8 - heads, BLOCK), F32)


def attend(slots, tops, q, kv):
    heads = q.shape[1] // HEAD_DIM
    spec = pl.BlockSpec(memory_space=pltpu.VMEM)
    pairs = 33 * BLOCK * BLOCK * heads
    return pl.pallas_call(
        functools.partial(forward_kernel, heads),
        grid_spec=pltpu.PrefetchScalarGridSpec(
            num_scalar_prefetch=2,
            grid=(1,),
            in_specs=[spec] * 2,
            out_specs=[spec] * 2,
            scratch_shapes=[
                pltpu.VMEM((8, BLOCK), F32),
                pltpu.VMEM((8, BLOCK), F32),
                pltpu.VMEM((heads, HEAD_DIM, BLOCK), F32),
            ],
        ),
        out_shape=(
            jax.ShapeDtypeStruct(q.shape, F32),
            jax.ShapeDtypeStruct((2, 8, BLOCK), F32),
        ),
        compiler_params=pltpu.CompilerParams(vmem_limit_bytes=VMEM_LIMIT),
        cost_estimate=pl.CostEstimate(
            flops=pairs * 4 * HEAD_DIM, bytes_accessed=80 * 2**20, transcendentals=pairs
        ),
    )(slots, tops, q, kv)


def backward_kernel(
    heads,
    slots,
    tops,
    q_ref,
    kv_ref,
    do_ref,
    lse_ref,
    o_ref,
    dq_ref,
    dkv_ref,
    dq_s,
    dkv_s,
    delta_s,
):
    dkv_s[...] = jnp.zeros(dkv_s.shape, F32)
    for a in range(2):
        dq_s[...] = jnp.zeros(dq_s.shape, F32)

        def part(ref, h):
            return ref[a * BLOCK : (a + 1) * BLOCK, h * HEAD_DIM : (h + 1) * HEAD_DIM]

        for h in range(heads):
            product = part(do_ref, h).astype(F32) * part(o_ref, h)
            delta_s[h : h + 1, :] = jnp.sum(product.T, axis=0, keepdims=True)

        def one(n, carry):
            slot = slots[n]
            keys, values = kv_ref[slot, :, :HEAD_DIM], kv_ref[slot, :, HEAD_DIM:]
            keys_t = keys.T

            def products(h):
                return dot_nt(keys, part(q_ref, h)), dot_nt(values, part(do_ref, h))

            dk = jnp.zeros((BLOCK, HEAD_DIM), F32)
            dv = jnp.zeros((BLOCK, HEAD_DIM), F32)
            ahead = min(2, heads)
            ready = [products(h) for h in range(ahead)]
            for h in range(heads):
                s, dp = ready[h]
                if h + ahead < heads:
                    ready.append(products(h + ahead))
                p = jnp.exp2(s * SCALE2 - lse_ref[a, h : h + 1, :])
                dv = dv + dot_nn(p.astype(BF), part(do_ref, h))
                ds = (p * (dp - delta_s[h : h + 1, :])).astype(BF)
                dk = dk + dot_nn(ds, part(q_ref, h))
                dq_s[h] = dq_s[h] + dot_nn(keys_t, ds)
            dkv_s[slot, :, :HEAD_DIM] = dkv_s[slot, :, :HEAD_DIM] + dk
            dkv_s[slot, :, HEAD_DIM:] = dkv_s[slot, :, HEAD_DIM:] + dv
            return carry

        lax.fori_loop(0, tops[a] + 1, one, 0)
        for h in range(heads):
            dq_ref[a * BLOCK : (a + 1) * BLOCK, h * HEAD_DIM : (h + 1) * HEAD_DIM] = (
                (dq_s[h] * SCALE).T
            ).astype(BF)
    dkv_ref[:, :, :HEAD_DIM] = (dkv_s[:, :, :HEAD_DIM] * SCALE).astype(BF)
    dkv_ref[:, :, HEAD_DIM:] = dkv_s[:, :, HEAD_DIM:].astype(BF)


def attend_back(slots, tops, q, kv, do, lse, attended):
    heads = q.shape[1] // HEAD_DIM
    spec = pl.BlockSpec(memory_space=pltpu.VMEM)
    pairs = 33 * BLOCK * BLOCK * heads
    return pl.pallas_call(
        functools.partial(backward_kernel, heads),
        grid_spec=pltpu.PrefetchScalarGridSpec(
            num_scalar_prefetch=2,
            grid=(1,),
            in_specs=[spec] * 5,
            out_specs=[spec] * 2,
            scratch_shapes=[
                pltpu.VMEM((heads, HEAD_DIM, BLOCK), F32),
                pltpu.VMEM(kv.shape, F32),
                pltpu.VMEM((8, BLOCK), F32),
            ],
        ),
        out_shape=(
            jax.ShapeDtypeStruct(q.shape, BF),
            jax.ShapeDtypeStruct(kv.shape, BF),
        ),
        compiler_params=pltpu.CompilerParams(vmem_limit_bytes=VMEM_LIMIT),
        cost_estimate=pl.CostEstimate(
            flops=pairs * 10 * HEAD_DIM, bytes_accessed=120 * 2**20, transcendentals=pairs
        ),
    )(slots, tops, q, kv, do, lse, attended)


def inverse_rms(value):
    return lax.rsqrt(jnp.mean(value * value, axis=-1, keepdims=True) + EPS)


def turned(value, cosine, sine):
    return value * cosine + pltpu.roll(value, HEAD_DIM // 2, 1) * sine


def project_kernel(plans, sizes, x_ref, w_hbm, gain_ref, bias_ref, cos_ref, sin_ref, *refs):
    packed_ref, _, kv_all_ref, swapped_ref, q_ref, normed_ref, kv_s, w_ref, w_sems = refs[:9]
    q_width = q_ref.shape[1]
    loads = []
    for i, (low, n) in enumerate(((q_width, 2 * HEAD_DIM), (0, q_width))):
        span = (slice(None), pl.ds(low, n))
        loads.append(pltpu.make_async_copy(w_hbm.at[span], w_ref.at[span], w_sems.at[i]))
        loads[i].start()
    x = x_ref[...].astype(F32)
    normed_ref[...] = (x * inverse_rms(x) * gain_ref[...]).astype(BF)
    cosine, sine = cos_ref[...], sin_ref[...]
    heads = q_ref.shape[1] // HEAD_DIM

    def product(low, n):
        cols = slice(low * HEAD_DIM, (low + n) * HEAD_DIM)
        return dot_nn(normed_ref[...], w_ref[:, cols]) + bias_ref[:, cols]

    loads[0].wait()
    made = product(heads, 2)
    kv_s[:, :HEAD_DIM] = turned(made[:, :HEAD_DIM], cosine, sine).astype(BF)
    kv_s[:, HEAD_DIM:] = made[:, HEAD_DIM:].astype(BF)

    def queries():
        loads[1].wait()
        for low in range(0, heads, 2):
            made = product(low, 2)
            for i in range(2):
                part = made[:, i * HEAD_DIM : (i + 1) * HEAD_DIM]
                q_ref[:, (low + i) * HEAD_DIM : (low + i + 1) * HEAD_DIM] = turned(
                    part, cosine, sine
                ).astype(BF)

    gather_kernel(
        plans, sizes, 1, 0, 0, kv_s, packed_ref, kv_all_ref, swapped_ref, *refs[9:], behind=queries
    )


def project(x, w, gain, bias, cosine, sine, packed, after, plans, sizes, collective_id):
    plans = alive(plans, sizes)
    n, width = x.shape[0], w.shape[1]
    spec = pl.BlockSpec(memory_space=pltpu.VMEM)
    far = pl.BlockSpec(memory_space=pl.ANY)
    count = int(np.prod([sizes[a] for a in plans[0][2]]))
    kv = (n, 2 * HEAD_DIM)
    return pl.pallas_call(
        functools.partial(project_kernel, plans, sizes),
        in_specs=[spec, far] + [spec] * 4 + [far] * 2,
        out_specs=[far, far, spec, spec],
        out_shape=[
            jax.ShapeDtypeStruct(s, BF)
            for s in ((count,) + kv, packed.shape, (n, width - 2 * HEAD_DIM), (n, D))
        ],
        scratch_shapes=[
            pltpu.VMEM(kv, BF),
            pltpu.VMEM(w.shape, BF),
            pltpu.SemaphoreType.DMA((2,)),
            pltpu.SemaphoreType.DMA((count - 1,)),
            pltpu.SemaphoreType.DMA((count - 1,)),
            pltpu.SemaphoreType.DMA((1,)),
        ]
        + swap_scratch([packed]),
        compiler_params=pltpu.CompilerParams(
            collective_id=collective_id, has_side_effects=True, vmem_limit_bytes=VMEM_LIMIT
        ),
        cost_estimate=pl.CostEstimate(
            flops=2 * n * D * width, bytes_accessed=80 * 2**20, transcendentals=0
        ),
    )(x, w, gain, bias, cosine, sine, packed, after)


def project_back_kernel(
    dq_ref,
    dkv_ref,
    normed_ref,
    x_ref,
    w_ref,
    cos_ref,
    sin_ref,
    back_ref,
    grad_ref,
    dnormed_ref,
    gain_grad_ref,
    bias_grad_ref,
    swapped_ref,
    dpre_s,
    *sems,
):
    (item,) = swaps_of([back_ref], [swapped_ref], sems)
    greet(("y", "c"), {"y": 2, "c": 2}, True)
    item.start()
    cosine, sine = cos_ref[...], -sin_ref[...]
    heads = dq_ref.shape[1] // HEAD_DIM
    for h in range(heads + 1):
        cols = slice(h * HEAD_DIM, (h + 1) * HEAD_DIM)
        part = dq_ref[:, cols] if h < heads else dkv_ref[:, :HEAD_DIM]
        dpre_s[:, cols] = turned(part.astype(F32), cosine, sine).astype(BF)
    dpre_s[:, (heads + 1) * HEAD_DIM :] = dkv_ref[:, HEAD_DIM:]
    bias_grad_ref[...] = jnp.sum(dpre_s[...].astype(F32), axis=0, keepdims=True)
    x = x_ref[...].astype(F32)
    scale = inverse_rms(x)
    step = 2 * HEAD_DIM
    for low in range(0, D, step):
        cols = slice(low, low + step)
        dnormed = dot_nt(dpre_s[...], w_ref[cols, :])
        dnormed_ref[:, cols] = dnormed.astype(BF)
        gain_grad_ref[:, cols] = jnp.sum(
            dnormed * (x[:, cols] * scale), axis=0, keepdims=True
        )
        if len(grad_ref.shape) == 2:
            grad_ref[cols, :] = dot_tn(normed_ref[:, cols], dpre_s[...]).astype(BF)
    if len(grad_ref.shape) == 4:
        blk, heads, rows, width = grad_ref.shape
        step = 3 * LANES
        for low in range(0, D, step):
            made = dot_tn(normed_ref[:, low : low + step], dpre_s[...]).astype(BF)
            half, start = divmod(low // rows, blk)
            grad_ref[start : start + step // rows, half] = made.reshape(step // rows, rows, width)
    item.wait()


def project_back(dq, dkv, normed, x, w, cosine, sine, back, blk, rows, collective_id):
    n, width = x.shape[0], w.shape[1]
    split = rows % 16 == 0
    made = (blk, 2, rows, width) if split else (D, width)
    spec = pl.BlockSpec(memory_space=pltpu.VMEM)
    far = pl.BlockSpec(memory_space=pl.ANY)
    return pl.pallas_call(
        project_back_kernel,
        in_specs=[spec] * 7 + [far],
        out_specs=[spec] * 4 + [far],
        out_shape=[
            jax.ShapeDtypeStruct(made, BF),
            jax.ShapeDtypeStruct((n, D), BF),
            jax.ShapeDtypeStruct((1, D), F32),
            jax.ShapeDtypeStruct((1, width), F32),
            jax.ShapeDtypeStruct(back.shape, back.dtype),
        ],
        scratch_shapes=[pltpu.VMEM((n, width), BF)] + swap_scratch([back]),
        compiler_params=pltpu.CompilerParams(
            collective_id=collective_id, has_side_effects=True, vmem_limit_bytes=VMEM_LIMIT
        ),
        cost_estimate=pl.CostEstimate(
            flops=4 * n * D * width, bytes_accessed=16 * 2**20, transcendentals=0
        ),
    )(dq, dkv, normed, x, w, cosine, sine, back)


def exchange_back_kernel(sizes, dproj_ref, w_hbm, attn_hbm, dout_ref, o_ref, pair_s, sum_s, *refs):
    w_ref, attn_ref, load_sems, send_sems, recv_sems = refs
    loads = [
        pltpu.make_async_copy(w_hbm, w_ref, load_sems.at[0]),
        pltpu.make_async_copy(attn_hbm, attn_ref, load_sems.at[1]),
    ]
    for copy in loads:
        copy.start()
    greet(("head",), sizes)
    me, count = lax.axis_index("head"), sizes["head"]
    tok = dproj_ref.shape[0]
    copies = []
    for d in range(1, count):
        copy = remote(
            dproj_ref, pair_s.at[me], send_sems.at[d - 1], recv_sems.at[d - 1], "head", d, sizes
        )
        copy.start()
        copies.append(copy)
    cols = 2 * LANES

    def use(place, grads, fresh, last):
        rows = pl.ds(pl.multiple_of(place * tok, tok), tok)
        for low in range(0, w_ref.shape[0], cols):
            part = slice(low, low + cols)
            dout_ref[rows, part] = dot_nt(grads, w_ref[part, :]).astype(BF)
            made = dot_tn(attn_ref[rows, part], grads)
            if not fresh:
                made = made + sum_s[part, :]
            if last:
                o_ref[part, :] = made.astype(BF)
            else:
                sum_s[part, :] = made

    for copy in loads:
        copy.wait()
    use(me, dproj_ref[...], True, count == 1)
    for d in range(1, count):
        copies[d - 1].wait_recv()
        place = lax.rem(me + count - d, count)
        use(place, pair_s[place], False, d == count - 1)
    for copy in copies:
        copy.wait_send()


def exchange_back(dproj, w, attn, sizes, collective_id):
    spec = pl.BlockSpec(memory_space=pltpu.VMEM)
    count = sizes["head"]
    return pl.pallas_call(
        functools.partial(exchange_back_kernel, sizes),
        in_specs=[spec] + [pl.BlockSpec(memory_space=pl.ANY)] * 2,
        out_specs=[spec] * 2,
        out_shape=[
            jax.ShapeDtypeStruct(attn.shape, BF),
            jax.ShapeDtypeStruct(w.shape, BF),
        ],
        scratch_shapes=[
            pltpu.VMEM((count,) + dproj.shape, BF),
            pltpu.VMEM(w.shape, F32),
            pltpu.VMEM(w.shape, BF),
            pltpu.VMEM(attn.shape, BF),
            pltpu.SemaphoreType.DMA((2,)),
            pltpu.SemaphoreType.DMA((count - 1,)),
            pltpu.SemaphoreType.DMA((count - 1,)),
        ],
        compiler_params=pltpu.CompilerParams(
            collective_id=collective_id, has_side_effects=True, vmem_limit_bytes=VMEM_LIMIT
        ),
        cost_estimate=pl.CostEstimate(
            flops=4 * w.size * attn.shape[0], bytes_accessed=40 * 2**20, transcendentals=0
        ),
    )(dproj, w, attn)


def shards(
    sizes,
    hidden,
    cotangent,
    block_order,
    norm1,
    q_weight,
    q_bias,
    k_weight,
    k_bias,
    v_weight,
    v_bias,
    o_weight,
    norm2,
    gate_weight,
    up_weight,
    down_weight,
):
    tok = hidden.shape[0]
    pair = sizes["head"] * tok
    blk = int(np.prod([sizes[a] for a in BLK]))
    seqs = blk // SEQ_SPAN
    place_axes = {1: BLK, 2: BLK[:3], 4: BLK[:2]}[seqs]
    seq_axes = BLK[len(place_axes) :]
    head = lax.axis_index("head")
    place = place_of({}, place_axes, sizes)
    seq = place_of({}, seq_axes, sizes) if seq_axes else 0
    order = lax.dynamic_index_in_dim(block_order, seq, 0, keepdims=False)
    tops = lax.dynamic_slice_in_dim(order, place * 2, 2)
    slots = jnp.argsort(order).astype(jnp.int32)
    positions = (tops[:, None] * tok + jnp.arange(tok, dtype=jnp.int32)[None, :]).reshape(pair)
    frequency = THETA ** (-(jnp.arange(HEAD_DIM // 2, dtype=F32) * 2.0) / HEAD_DIM)
    angles = positions.astype(F32)[:, None] * frequency[None, :]
    cosine, sine = jnp.cos(angles), jnp.sin(angles)
    cosine = jnp.concatenate([cosine, cosine], axis=1)
    sine = jnp.concatenate([-sine, sine], axis=1)

    q_cols = D // 2
    kv_cols = HEAD_DIM
    rows = q_weight.shape[0]
    small = lax.reduce_precision(jnp.concatenate([norm1, norm2, q_bias, k_bias, v_bias]), 8, 7)
    small = jnp.pad(small, (0, 8 * LANES - small.shape[0])).reshape(8, LANES)
    parts = sizes["y"] * sizes["c"]
    width = gate_weight.shape[1]
    lanes = -(-width // (LANES * parts)) * LANES
    first = lanes * 6 // 9 // LANES * LANES
    ff_rows = gate_weight.shape[0]

    def along_z(part):
        part = part.reshape(1, 3, parts * ff_rows, part.shape[-1])
        return lax.all_gather(part, live(("g", "z"), sizes), axis=0, tiled=True)

    w_qkv, x_pair, small_all, w_out, packed_one, packed_two = front(
        (q_weight, k_weight, v_weight, o_weight),
        hidden,
        small,
        (down_weight, gate_weight, up_weight),
        first,
        lanes - first,
        [
            (0, None, AXES, AXES, True),
            (1, None, ("head",), ("head",), False),
            (2, None, AXES, AXES, False),
            (3, None, BLK, ("y", "z", "g", "c"), False),
        ],
        sizes,
        1,
    )
    w_out = w_out.reshape(q_cols, D)
    w_qkv = w_qkv.reshape(D, q_cols + 2 * kv_cols)
    x_pair = x_pair.reshape(pair, D)
    small_all = small_all.reshape(-1, 8 * LANES)
    kn = k_bias.shape[0]
    long = small_all[:, : 3 * rows].reshape(-1, 3, rows).transpose(1, 0, 2).reshape(3, D)
    short = small_all[:, 3 * rows : 3 * rows + 2 * kn].reshape(-1, 2, kn)
    short = short.transpose(1, 0, 2).reshape(2, 2 * kv_cols)
    gain_one, gain_two = long[:1], long[1:2]
    bias = jnp.concatenate(
        [
            lax.dynamic_slice_in_dim(v, head * n, n)
            for v, n in ((long[2], q_cols), (short[0], kv_cols), (short[1], kv_cols))
        ]
    )[None]
    far_axes, near_axes = place_axes[:2], place_axes[2:]
    group = ("head", "y", "c")
    cot_all = lax.all_gather(cotangent, group, axis=0, tiled=True)
    kv, mine_one, queries, normed = project(
        x_pair,
        w_qkv,
        gain_one,
        bias,
        cosine,
        sine,
        packed_one,
        cot_all,
        [(0, None, far_axes, far_axes, False)],
        sizes,
        2,
    )
    half = tok // 2
    crossed = [
        ((0, half), group, ("head", "y", "c"), False),
        ((half, half), group, ("y", "head", "c"), False),
    ]
    summed = [
        ((0, half), group, ("c", "head", "y"), False),
        ((half, half), group, ("c", "y", "head"), False),
    ]
    w_feed_one = along_z(mine_one)
    if near_axes:
        (kv,) = gather([kv], [(0, None, near_axes, near_axes, False)], sizes, 10)
    near_count = int(np.prod([sizes[a] for a in near_axes], dtype=int))
    far_count = SEQ_SPAN // near_count
    where = slots // 2
    slots = ((where % near_count) * far_count + where // near_count) * 2 + slots % 2
    kv = kv.reshape(2 * SEQ_SPAN, tok, 2 * HEAD_DIM)
    attended, lse = attend(slots, tops, queries, kv)
    attn_local = attended.astype(BF)
    inputs = hidden.astype(F32)
    mixed_part = dot_nn(attn_local, w_out).reshape(2, tok, D)
    mixed_got, mine_two = gather(
        [mixed_part.astype(BF)],
        [(0, None, ("head",), ("head",), True)],
        sizes,
        3,
        [packed_two],
    )
    w_feed_two = along_z(mine_two)
    mixed = (
        inputs
        + lax.dynamic_index_in_dim(mixed_part, head, 0, keepdims=False)
        + lax.dynamic_index_in_dim(mixed_got, 1 - head, 0, keepdims=False).astype(F32)
    )
    scale_two = inverse_rms(mixed)
    normed_two = (mixed * scale_two * gain_two).astype(BF)
    (tokens,) = gather([normed_two], [(0,) + c for c in crossed], sizes, 4)
    tokens = tokens.reshape(-1, D)

    places = w_feed_one.shape[0]
    act, dgate, dup, branch, dtokens = feed(tokens, cot_all, w_feed_one)
    parts_one = plain_grads(tokens, cot_all, act, dgate, dup, places)
    act, dgate, dup, branch, dtokens = feed(
        tokens, cot_all, w_feed_two, (branch, dtokens), (parts_one,)
    )
    dmixed, dproj, norm2_part, parts_two = feed_grads(
        dtokens.reshape(-1, tok, D),
        mixed,
        cotangent,
        gain_two,
        tokens,
        cot_all,
        act,
        dgate,
        dup,
        places,
        [(0,) + c for c in summed],
        sizes,
        5,
    )
    def collect(grad):
        total = lax.psum_scatter(grad, live(("g", "z"), sizes), scatter_dimension=0, tiled=True)
        return total.reshape(3, parts, ff_rows, grad.shape[-1])

    back_one = collect(parts_one)

    dout, o_part = exchange_back(dproj, w_out, attn_local, sizes, 6)

    dq, dkv_parts = attend_back(slots, tops, queries, kv, dout, lse, attended)
    dkv, d_out_weight, parts_two = scatter(
        [dkv_parts.reshape(SEQ_SPAN, pair, 2 * HEAD_DIM), o_part.reshape(blk, -1, D)],
        [
            (0, None, near_axes + far_axes, place_axes[::-1], False),
            (1, None, BLK, BLK[::-1], False),
        ],
        [BF, F32],
        sizes,
        7,
        carried=[parts_two],
    )
    back_two = collect(parts_two)
    w_part, dnormed, norm1_part, bias_part, back_one = project_back(
        dq, dkv, normed, x_pair, w_qkv, cosine, sine, back_one, blk, rows, 11
    )
    if w_part.ndim == 2:
        w_part = w_part.reshape(2, blk, rows, -1).transpose(1, 0, 2, 3)
    norm1_part, bias_part = norm1_part[0], bias_part[0]
    own = (jnp.arange(2) == head).astype(F32)[:, None]

    def owners(vector):
        return vector.reshape(2, blk, -1).transpose(1, 0, 2)

    def owned(vector):
        return owners((own * vector[None, :]).reshape(-1))

    small_grads = jnp.stack(
        [
            jnp.pad(part, ((0, 0), (0, 0), (0, LANES - part.shape[2])))
            for part in (
                owners(norm1_part),
                owners(norm2_part[0]),
                owned(bias_part[:q_cols]),
                owned(bias_part[q_cols : q_cols + kv_cols]),
                owned(bias_part[q_cols + kv_cols :]),
            )
        ]
        + [jnp.zeros((blk, 2, LANES), F32)] * 3,
        axis=2,
    )
    small_grads = small_grads.transpose(1, 0, 2, 3).reshape(2 * blk, 8, LANES)
    w_grads, small_sum, dnormed_sum, branch_sum = scatter(
        [
            w_part,
            small_grads,
            dnormed.reshape(2, tok, D),
            branch.reshape(-1, tok, D),
        ],
        [
            (0, None, BLK, BLK[::-1], True),
            (1, None, AXES, AXES[::-1], False),
            (2, None, ("head",), ("head",), False),
        ]
        + [(3,) + c for c in summed],
        [F32] * 4,
        sizes,
        8,
    )
    d_query, d_key, d_value, output, hidden_grad, d_down, d_gate, d_up = write_outputs(
        w_grads,
        dnormed_sum,
        branch_sum,
        dmixed,
        hidden,
        mixed,
        gain_one,
        [back_one] + list(swap([back_two], w_grads, 9)),
        width,
    )
    return (
        output,
        hidden_grad,
        small_sum[0, :rows],
        d_query,
        small_sum[2, :rows],
        d_key,
        small_sum[3, :kn],
        d_value,
        small_sum[4, :kn],
        d_out_weight,
        small_sum[1, :rows],
        d_gate,
        d_up,
        d_down,
    )


def solution(mesh):
    heads, blk = mesh.devices.shape
    split = jax.sharding.Mesh(mesh.devices.reshape(heads, blk // 16, 4, 2, 2), AXES)
    sizes = dict(split.shape)
    rows = P(AXES, None)
    vector = P(AXES)
    feed = P(BLK, "head")
    return jax.shard_map(
        functools.partial(shards, sizes),
        mesh=split,
        in_specs=(
            rows,
            rows,
            P(),
            vector,
            rows,
            vector,
            rows,
            vector,
            rows,
            vector,
            rows,
            vector,
            feed,
            feed,
            feed,
        ),
        out_specs=(
            rows,
            rows,
            vector,
            rows,
            vector,
            rows,
            vector,
            rows,
            vector,
            rows,
            vector,
            feed,
            feed,
            feed,
        ),
        check_vma=False,
    )
```
